32 devices in a mesh: dp: 8 (over z, x), seq: 4 (over y, core).
Axes of the slice: x: 2, y: 2, z: 4, core: 2. Of those that a mesh axis runs over, the one named last changes fastest.
Arguments:
- tokens: float32 [8, 1024, 768], P('dp', 'seq'), may hold values from -6 to 6
- cotangent: float32 [8, 1024, 768], P('dp', 'seq'), may hold values from -6 to 6
- segment_ids: int32 [8, 1024], P('dp', 'seq'), may hold values from 0 to 3, never falling along the last dimension, each value on 1 to 896 neighbouring positions
- valid: int32 [8, 1024], P('dp', 'seq'), may hold values from 0 to 1, as said below
- vectors: float32 [9216], P('dp'), may hold values from -1 to 3
- vec_first: float32 [9216], P('dp'), may hold values from -1 to 1
- vec_second: float32 [9216], P('dp'), may hold values from 0 to 1, as said below
- w_qkv: float32 [768, 2304], P('dp'), may hold values from -0.21875 to 0.21875
- qkv_first: float32 [768, 2304], P('dp'), may hold values from -1 to 1
- qkv_second: float32 [768, 2304], P('dp'), may hold values from 0 to 1, as said below
- w_proj: float32 [768, 768], P('dp'), may hold values from -0.875 to 0.875
- proj_first: float32 [768, 768], P('dp'), may hold values from -1 to 1
- proj_second: float32 [768, 768], P('dp'), may hold values from 0 to 1, as said below
- w_in: float32 [768, 3072], P('dp'), may hold values from -0.21875 to 0.21875
- in_first: float32 [768, 3072], P('dp'), may hold values from -1 to 1
- in_second: float32 [768, 3072], P('dp'), may hold values from 0 to 1, as said below
- w_out: float32 [3072, 768], P('dp'), may hold values from -0.109375 to 0.109375
- out_first: float32 [3072, 768], P('dp'), may hold values from -1 to 1
- out_second: float32 [3072, 768], P('dp'), may hold values from 0 to 1, as said below
Outputs:
- output: float32 [8, 1024, 768], P('dp', 'seq')
- input_grad: float32 [8, 1024, 768], P('dp', 'seq')
- clip_norm: float32 [], replicated
- new_vec_first: float32 [9216], P('dp')
- new_vec_second: float32 [9216], P('dp')
- new_vectors: float32 [9216], P('dp')
- new_qkv_first: float32 [768, 2304], P('dp')
- new_qkv_second: float32 [768, 2304], P('dp')
- new_w_qkv: float32 [768, 2304], P('dp')
- new_proj_first: float32 [768, 768], P('dp')
- new_proj_second: float32 [768, 768], P('dp')
- new_w_proj: float32 [768, 768], P('dp')
- new_in_first: float32 [768, 3072], P('dp')
- new_in_second: float32 [768, 3072], P('dp')
- new_w_in: float32 [768, 3072], P('dp')
- new_out_first: float32 [3072, 768], P('dp')
- new_out_second: float32 [3072, 768], P('dp')
- new_w_out: float32 [3072, 768], P('dp')
The draws below stay inside these ranges and needn't reach their ends.
Inputs may be any that keep to these rules, and one draw needn't show every extreme that they name: `valid`: in each row the positions from some point to the row's end are 0, at most the last 128 of them; all others are 1. `vec_second`: positive. `qkv_second`: positive. `proj_second`: positive. `in_second`: positive. `out_second`: positive.
All inputs are finite; a program needn't handle non-finite values.
Results may differ from the reference program's by a relative error of at most 0.0003.
Values sent between devices are 32-bit elements; how exact they have to be, the bound alone decides.
No kernel may reach another device: no remote copies, remote signals or barrier semaphores. Data moves between devices by JAX's collectives and lax.ppermute only.
A program may use at most 256 MiB of HBM per device.

```python
import math
import jax
import jax.numpy as jnp
import numpy as np
from jax import lax

D = 768
HEADS = 12
HEAD = 64
FF = 3072
LEN = 1024
STEP = 10
CH = 256
ROWS = 8
VEC = 9216


def entry_size(weight):
    weighted = VEC + 0.36 * D * D + 0.5 * D * FF
    return weight / math.sqrt(weighted)


def first_moment(key, extent, weight):
    sign_key, size_key = jax.random.split(key)
    sign_values = jnp.where(jax.random.bernoulli(sign_key, 0.5, extent), 1.0, -1.0)
    magnitude = jax.random.uniform(size_key, extent, jnp.float32, 0.5, 2.0)
    return sign_values * magnitude * (0.111 * entry_size(weight))


def second_moment(key, extent, weight):
    factor = jax.random.uniform(key, extent, jnp.float32, 1.0, 4.0)
    return factor * (0.001001 * entry_size(weight) ** 2)


def draw_valid(key, part):
    key = jax.random.fold_in(key, 2)
    padding = jax.random.randint(key, (ROWS, 1), 0, CH // 2 + 1)
    places = jnp.arange(LEN, dtype=jnp.int32)[None, :]
    return (places < LEN - padding).astype(jnp.int32)


def draw_vectors(key, part):
    key = jax.random.fold_in(key, 1)
    gain_key, bias_key = jax.random.split(key)
    places = jnp.arange(VEC, dtype=jnp.int32)
    block = places // D
    column = (places % D).astype(jnp.float32) / D
    ramp = 0.5 + column
    noise = jax.random.uniform(gain_key, (VEC,), jnp.float32, 0.8, 1.25)
    biases = jnp.clip(0.2 * jax.random.normal(bias_key, (VEC,), jnp.float32), -1.0, 1.0)
    is_gain = (block == 0) | (block == 5)
    return jnp.where(is_gain, ramp * noise, biases)


def draw_vec_first(key, part):
    key = jax.random.fold_in(key, 11)
    return first_moment(key, (VEC,), 1.0)


def draw_vec_second(key, part):
    key = jax.random.fold_in(key, 12)
    return second_moment(key, (VEC,), 1.0)


def draw_qkv_first(key, part):
    key = jax.random.fold_in(key, 13)
    return first_moment(key, (D, 3 * D), 0.3)


def draw_qkv_second(key, part):
    key = jax.random.fold_in(key, 14)
    return second_moment(key, (D, 3 * D), 0.3)


def draw_proj_first(key, part):
    key = jax.random.fold_in(key, 15)
    return first_moment(key, (D, D), 0.3)


def draw_proj_second(key, part):
    key = jax.random.fold_in(key, 16)
    return second_moment(key, (D, D), 0.3)


def draw_in_first(key, part):
    key = jax.random.fold_in(key, 17)
    return first_moment(key, (D, FF), 0.5)


def draw_in_second(key, part):
    key = jax.random.fold_in(key, 18)
    return second_moment(key, (D, FF), 0.5)


def draw_out_first(key, part):
    key = jax.random.fold_in(key, 19)
    return first_moment(key, (FF, D), 0.5)


def draw_out_second(key, part):
    key = jax.random.fold_in(key, 20)
    return second_moment(key, (FF, D), 0.5)


def block_levels(rng, dims, shards, least, largest):
    level, own = 1.0, jax.random.fold_in(rng, 6)
    for axis_at, shards_of in shards:
        draws = jnp.exp(jax.random.uniform(jax.random.fold_in(own, axis_at), (shards_of,), jnp.float32, least / len(shards), largest / len(shards)))
        level = level * jnp.repeat(draws, dims[axis_at] // shards_of).reshape([-1 if axis == axis_at else 1 for axis in range(len(dims))])
    return level


def length_profile(number_of, total, most, lean):
    portions = [(1 << 20) // math.isqrt(standing ** lean) + 1 for standing in range(2, number_of + 1)]
    rest, counts = total - most - (number_of - 1), [1] * (number_of - 1)
    while rest > 0:
        movable = [i for i in range(number_of - 1) if counts[i] < most]
        mass, left = sum([portions[i] for i in movable]), rest
        for i in movable:
            more = min(most - counts[i], max(1, left * portions[i] // mass), rest)
            counts[i] = counts[i] + more
            rest = rest - more
    return np.array([most] + counts)


def uneven(stream_key, count, total, bound, slope):
    if count == 2:
        one = jax.random.randint(stream_key, (), max(1, total - bound), min(bound, total - 1) + 1)
        return jnp.stack([one, total - one])
    lengths = jnp.asarray(length_profile(count, total, bound, slope), jnp.int32)
    twos = (count - 1) // 2
    giver, receiver = lengths[1:1 + 2 * twos:2], lengths[2:2 + 2 * twos:2]
    room = jnp.minimum(giver - 1, bound - receiver)
    shifted = jax.random.randint(jax.random.fold_in(stream_key, 1), (twos,), 0, 1 << 20) % (room + 1)
    lengths = lengths.at[1:1 + 2 * twos:2].set(giver - shifted).at[2:2 + 2 * twos:2].set(receiver + shifted)
    return lengths[jax.random.permutation(jax.random.fold_in(stream_key, 2), count)]


def bell_draw(rng, dims, scale, limit, cuts=(), held_as=jnp.bfloat16):
    loudness = block_levels(rng, dims, cuts, -0.22, 0.18) if cuts else 1.0
    values = jax.random.normal(rng, dims, jnp.float32) * scale * loudness
    return jnp.minimum(jnp.maximum(values, -limit), limit).astype(held_as)


def setup_inputs(seed: int = 0) -> dict:
    splits = jax.random.split(jax.random.key(seed), 20)
    tokens = bell_draw(splits[0], (ROWS, LEN, D), 1.0, 6.0, ((0, 8), (1, 4)), jnp.float32)
    cotangent = bell_draw(splits[1], (ROWS, LEN, D), 1.0, 6.0, ((0, 8), (1, 4)), jnp.float32)
    segment_ids = jax.vmap(lambda own: jnp.searchsorted(jnp.cumsum(uneven(own, 4, LEN, 3 * CH + CH // 2, 0)), jnp.arange(LEN), side="right"))(jax.random.split(splits[2], ROWS)).reshape((ROWS, LEN)).astype(jnp.int32)
    valid = draw_valid(jax.random.fold_in(splits[19], 71), 0)
    vectors = draw_vectors(jax.random.fold_in(splits[19], 71), 0)
    vec_first = draw_vec_first(jax.random.fold_in(splits[19], 71), 0)
    vec_second = draw_vec_second(jax.random.fold_in(splits[19], 71), 0)
    w_qkv = bell_draw(splits[7], (D, 3 * D), D ** -0.5, 0.21875, ((0, 8),), jnp.float32)
    qkv_first = draw_qkv_first(jax.random.fold_in(splits[19], 71), 0)
    qkv_second = draw_qkv_second(jax.random.fold_in(splits[19], 71), 0)
    w_proj = bell_draw(splits[10], (D, D), (D // 16) ** -0.5, 0.875, ((0, 8),), jnp.float32)
    proj_first = draw_proj_first(jax.random.fold_in(splits[19], 71), 0)
    proj_second = draw_proj_second(jax.random.fold_in(splits[19], 71), 0)
    w_in = bell_draw(splits[13], (D, FF), D ** -0.5, 0.21875, ((0, 8),), jnp.float32)
    in_first = draw_in_first(jax.random.fold_in(splits[19], 71), 0)
    in_second = draw_in_second(jax.random.fold_in(splits[19], 71), 0)
    w_out = bell_draw(splits[16], (FF, D), FF ** -0.5, 0.109375, ((0, 8),), jnp.float32)
    out_first = draw_out_first(jax.random.fold_in(splits[19], 71), 0)
    out_second = draw_out_second(jax.random.fold_in(splits[19], 71), 0)
    return {"tokens": tokens, "cotangent": cotangent, "segment_ids": segment_ids, "valid": valid, "vectors": vectors, "vec_first": vec_first, "vec_second": vec_second, "w_qkv": w_qkv, "qkv_first": qkv_first, "qkv_second": qkv_second, "w_proj": w_proj, "proj_first": proj_first, "proj_second": proj_second, "w_in": w_in, "in_first": in_first, "in_second": in_second, "w_out": w_out, "out_first": out_first, "out_second": out_second}


highest = lax.Precision.HIGHEST
masked_score = -1e+30
norm_eps = 1e-05
clip_limit = 1.0
beta_one = 0.9
beta_two = 0.999
adam_eps = 1e-08
matrix_rate = 0.02
vector_rate = 0.4
weight_decay = 0.01

@jax.custom_vjp
def low(v):
    return lax.optimization_barrier(v.astype(jnp.bfloat16)).astype(jnp.float32)

@jax.custom_vjp
def low_back(v):
    return v

def low_keep(v):
    return (low(v), None)

def low_pass(kept, grad):
    return (grad,)

def back_keep(v):
    return (v, None)

def back_low(kept, grad):
    return (low(grad),)
low.defvjp(low_keep, low_pass)
low_back.defvjp(back_keep, back_low)

def split_vector(vectors):
    pieces = [vectors[number * D:(number + 1) * D] for number in range(8)]
    return pieces + [vectors[8 * D:]]

def layer_norm(inputs, gain, shift):
    center = inputs - lax.optimization_barrier(jnp.mean(inputs, axis=-1, keepdims=True))
    spread = lax.optimization_barrier(jnp.mean(center * center, axis=-1, keepdims=True))
    return center * lax.rsqrt(spread + norm_eps) * gain + shift

def pre_attention(flat_in, vectors, w_qkv):
    pieces = split_vector(vectors)
    normed = layer_norm(flat_in, pieces[0], pieces[1])
    joined = jnp.dot(normed, w_qkv, precision=highest)
    queries = (joined[:, :D] + pieces[2]) * HEAD ** (-0.5)
    return (queries, joined[:, D:2 * D], joined[:, 2 * D:] + pieces[3])

def attention_out(flat_in, flat_heads, vectors, w_proj):
    pieces = split_vector(vectors)
    return flat_in + jnp.dot(flat_heads, w_proj, precision=highest) + pieces[4]

def feed_forward(mixed, vectors, w_in, w_out):
    pieces = split_vector(vectors)
    normed = layer_norm(mixed, pieces[5], pieces[6])
    hidden = jnp.dot(normed, w_in, precision=highest) + pieces[8]
    activated = jax.nn.gelu(hidden, approximate=True)
    return mixed + jnp.dot(activated, w_out, precision=highest) + pieces[7]

def row_attention(items):
    queries, keys_all, values_all, query_keys, key_keys = items
    places = jnp.arange(queries.shape[0], dtype=jnp.int32)
    same = query_keys[:, None] == key_keys[None, :]
    earlier = places[None, :] <= places[:, None]
    itself = places[None, :] == places[:, None]
    allow = same & earlier | itself
    scores = jnp.einsum('qhd,khd->hqk', queries, keys_all, precision=highest)
    scores = jnp.where(allow[None], scores, masked_score)
    probs = jax.nn.softmax(scores, axis=-1)
    return jnp.einsum('hqk,khd->qhd', probs, values_all, precision=highest)

def group_forward(block_in, vectors, w_qkv, w_proj, w_in, w_out, query_keys, key_keys):
    group_rows = block_in.shape[0]
    flat_in = block_in.reshape(group_rows * LEN, D)
    queries, keys_flat, values_flat = pre_attention(flat_in, vectors, w_qkv)
    layout = (group_rows, LEN, HEADS, HEAD)
    heads_out = lax.map(jax.checkpoint(row_attention), (queries.reshape(layout), keys_flat.reshape(layout), values_flat.reshape(layout), query_keys, key_keys))
    mixed = attention_out(flat_in, heads_out.reshape(group_rows * LEN, D), vectors, w_proj)
    return feed_forward(mixed, vectors, w_in, w_out).reshape(group_rows, LEN, D)

def adamw_update(weight, first, second, grad, rate, decay):
    new_first = beta_one * first + (1.0 - beta_one) * grad
    new_second = beta_two * second + (1.0 - beta_two) * grad * grad
    first_hat = new_first / (1.0 - beta_one ** STEP)
    second_hat = new_second / (1.0 - beta_two ** STEP)
    new_weight = weight - rate * (first_hat / (jnp.sqrt(second_hat) + adam_eps) + decay * weight)
    return (new_first, new_second, new_weight)

def reference(tokens, cotangent, segment_ids, valid, vectors, vec_first, vec_second, w_qkv, qkv_first, qkv_second, w_proj, proj_first, proj_second, w_in, in_first, in_second, w_out, out_first, out_second):
    per_group = 4 if ROWS % 4 == 0 else 1
    blocks = ROWS // per_group
    query_keys = jnp.where(valid > 0, segment_ids, -2).astype(jnp.float32)
    key_keys = jnp.where(valid > 0, segment_ids, -1).astype(jnp.float32)
    live = valid.astype(jnp.float32)

    def group_step(totals, items):
        block_in, block_cot, block_qk, block_kk, block_live = items

        def forward(inputs, vec_arg, qkv_arg, proj_arg, in_arg, out_arg):
            return group_forward(inputs, vec_arg, qkv_arg, proj_arg, in_arg, out_arg, block_qk, block_kk)
        result, back = jax.vjp(forward, block_in, vectors, w_qkv, w_proj, w_in, w_out)
        grads = back(block_cot * block_live[..., None])
        totals = tuple((total + grad for total, grad in zip(totals, grads[1:])))
        return (totals, (result, grads[0]))
    items = (tokens.reshape(blocks, per_group, LEN, D), cotangent.reshape(blocks, per_group, LEN, D), query_keys.reshape(blocks, per_group, LEN), key_keys.reshape(blocks, per_group, LEN), live.reshape(blocks, per_group, LEN))
    start = tuple((jnp.zeros_like(weight) for weight in (vectors, w_qkv, w_proj, w_in, w_out)))
    totals, (results, input_grads) = lax.scan(group_step, start, items)
    output = results.reshape(ROWS, LEN, D)
    input_grad = input_grads.reshape(ROWS, LEN, D)
    squares = jnp.sum(totals[0] * totals[0]) + jnp.sum(totals[1] * totals[1]) + jnp.sum(totals[2] * totals[2]) + jnp.sum(totals[3] * totals[3]) + jnp.sum(totals[4] * totals[4])
    clip_norm = jnp.sqrt(squares)
    factor = clip_limit / jnp.maximum(clip_norm, clip_limit)
    vec_a, vec_b, vec_c = adamw_update(vectors, vec_first, vec_second, factor * totals[0], vector_rate, 0.0)
    qkv_a, qkv_b, qkv_c = adamw_update(w_qkv, qkv_first, qkv_second, factor * totals[1], matrix_rate, weight_decay)
    proj_a, proj_b, proj_c = adamw_update(w_proj, proj_first, proj_second, factor * totals[2], matrix_rate, weight_decay)
    in_a, in_b, in_c = adamw_update(w_in, in_first, in_second, factor * totals[3], matrix_rate, weight_decay)
    out_a, out_b, out_c = adamw_update(w_out, out_first, out_second, factor * totals[4], matrix_rate, weight_decay)
    return (output, input_grad, clip_norm, vec_a, vec_b, vec_c, qkv_a, qkv_b, qkv_c, proj_a, proj_b, proj_c, in_a, in_b, in_c, out_a, out_b, out_c)
```

```python
import jax
import jax.numpy as jnp
from jax import lax
from jax.sharding import PartitionSpec as P

D = 768
HEADS = 12
HEAD = 64
STEP = 10

high = lax.Precision.HIGH
masked_score = -1e30
norm_eps = 1e-05
clip_limit = 1.0
beta_one = 0.9
beta_two = 0.999
adam_eps = 1e-08
matrix_rate = 0.02
vector_rate = 0.4
weight_decay = 0.01
gelu_scale = 0.7978845608028654
gelu_cubic = 0.044715


def adamw_update(weight, first, second, grad, rate, decay):
    new_first = beta_one * first + (1.0 - beta_one) * grad
    new_second = beta_two * second + (1.0 - beta_two) * grad * grad
    first_hat = new_first / (1.0 - beta_one**STEP)
    second_hat = new_second / (1.0 - beta_two**STEP)
    new_weight = weight - rate * (first_hat / (jnp.sqrt(second_hat) + adam_eps) + decay * weight)
    return (new_first, new_second, new_weight)


def dot(left, right, dims):
    return lax.dot_general(left, right, (dims, ((), ())), precision=high)


def ring_order(count):
    evens = [2 * i for i in range(count // 2)]
    return evens + [i + 1 for i in reversed(evens)]


def ring_tables(count):
    order = ring_order(count)
    place = [0] * count
    for position, device in enumerate(order):
        place[device] = position
    right = [(order[i], order[(i + 1) % count]) for i in range(count)]
    left = [(b, a) for a, b in right]
    return jnp.array(order, jnp.int32), jnp.array(place, jnp.int32), right, left


def use_ring(count):
    return count % 2 == 0 and 4 <= count <= 8


def gather_dp(block):
    count = lax.axis_size("dp")
    if not use_ring(count):
        return lax.all_gather(block, "dp", axis=0, tiled=False)
    order, place, right, left = ring_tables(count)
    mine = place[lax.axis_index("dp")]
    half = count // 2
    cut = block.shape[0] // 16 * 8
    got = {0: block}
    forth = back = block
    for step in range(1, half):
        forth = lax.ppermute(forth, "dp", right)
        back = lax.ppermute(back, "dp", left)
        got[count - step] = forth
        got[step] = back
    top = lax.ppermute(forth[:cut], "dp", right)
    bottom = lax.ppermute(back[cut:], "dp", left)
    got[half] = jnp.concatenate([top, bottom], axis=0)
    out = jnp.zeros((count,) + block.shape, block.dtype)
    for step in range(count):
        out = lax.dynamic_update_index_in_dim(out, got[step], order[(mine + step) % count], 0)
    return out


def scatter_dp(parts):
    count = lax.axis_size("dp")
    if not use_ring(count):
        return lax.psum_scatter(parts, "dp", scatter_dimension=0, tiled=False)
    order, place, right, left = ring_tables(count)
    mine = place[lax.axis_index("dp")]
    half = count // 2
    cut = parts.shape[1] // 16 * 8

    def own(step):
        return lax.dynamic_index_in_dim(parts, order[(mine + step) % count], 0, keepdims=False)

    far = own(half)
    top = lax.ppermute(far[:cut], "dp", right)
    bottom = lax.ppermute(far[cut:], "dp", left)
    forth, back = own(half - 1), own(count - half + 1)
    forth = jnp.concatenate([forth[:cut] + top, forth[cut:]], axis=0)
    back = jnp.concatenate([back[:cut], back[cut:] + bottom], axis=0)
    for step in range(half - 1, 0, -1):
        forth = lax.ppermute(forth, "dp", right)
        back = lax.ppermute(back, "dp", left)
        if step > 1:
            forth = forth + own(step - 1)
            back = back + own(count - step + 1)
    return own(0) + forth + back


def swap(block, bit):
    count = lax.axis_size("seq")
    return lax.ppermute(block, "seq", [(i, i ^ bit) for i in range(count)])


def gather_seq(block):
    core = swap(block, 1)
    across = swap(block, 2)
    return [block, core, across, swap(across, 1)]


def scatter_seq(parts):
    near = swap(parts[1], 1)
    far = swap(parts[3], 1)
    across = swap(parts[2] + far, 2)
    return parts[0] + near + across


def ordered(blocks, mine):
    stack = jnp.stack(blocks, axis=0)
    return [lax.dynamic_index_in_dim(stack, mine ^ j, 0, keepdims=False) for j in range(len(blocks))]


def norm_stats(inputs):
    center = inputs - jnp.mean(inputs, axis=-1, keepdims=True)
    spread = jnp.mean(center * center, axis=-1, keepdims=True)
    scale = lax.rsqrt(spread + norm_eps)
    return center * scale, scale


def norm_back(hat, scale, gain, grad):
    inner = grad * gain
    return scale * (
        inner
        - jnp.mean(inner, axis=-1, keepdims=True)
        - hat * jnp.mean(inner * hat, axis=-1, keepdims=True)
    )


def local(
    tokens,
    cotangent,
    segment_ids,
    valid,
    vectors,
    vec_first,
    vec_second,
    w_qkv,
    qkv_first,
    qkv_second,
    w_proj,
    proj_first,
    proj_second,
    w_in,
    in_first,
    in_second,
    w_out,
    out_first,
    out_second,
):
    _, chunk, features = tokens.shape
    dp_parts = lax.axis_size("dp")
    seq_parts = lax.axis_size("seq")
    mine = lax.axis_index("seq")
    length = chunk * seq_parts
    width = features // seq_parts
    heads = HEADS // seq_parts
    rows = w_qkv.shape[0]
    unit_rows = w_out.shape[0] // seq_parts

    def columns(array, base):
        return lax.dynamic_slice_in_dim(array, base + mine * width, width, 1)

    vec_size = vectors.shape[0]
    vec_rows = -(-vec_size // features)
    vec_block = jnp.pad(vectors, (0, vec_rows * features - vec_size)).reshape(vec_rows, features)
    first_block = jnp.concatenate(
        [columns(w_qkv, 0), columns(w_qkv, features), columns(w_qkv, 2 * features), columns(w_proj, 0)],
        axis=1,
    )
    first_all = gather_dp(jnp.concatenate([first_block, vec_block], axis=0))
    in_block = lax.dynamic_index_in_dim(
        w_in.reshape(rows, dp_parts, seq_parts, unit_rows), mine, 2, keepdims=False
    ).reshape(rows, dp_parts * unit_rows)
    out_block = lax.dynamic_slice_in_dim(w_out, mine * unit_rows, unit_rows, 0)
    win = gather_dp(in_block).reshape(features, dp_parts * unit_rows)
    wout = gather_dp(out_block).reshape(dp_parts * unit_rows, features)
    wqkv = first_all[:, :rows, : 3 * width].reshape(features, 3 * width)
    proj_part = first_all[:, :rows, 3 * width :].reshape(features, width)
    full_vec = first_all[:, rows:].reshape(dp_parts, vec_rows * features)[:, :vec_size].reshape(-1)
    pieces = [full_vec[i * features : (i + 1) * features] for i in range(8)]
    in_bias = lax.dynamic_index_in_dim(
        full_vec[8 * features :].reshape(dp_parts, seq_parts, unit_rows), mine, 1, keepdims=False
    ).reshape(-1)
    gain_one, shift_one, query_bias, value_bias, proj_bias, gain_two, shift_two, out_bias = pieces
    wproj = jnp.concatenate(ordered(gather_seq(proj_part), mine), axis=1)

    flat_in = tokens.reshape(chunk, features)
    hat_one, scale_one = norm_stats(flat_in)
    hat_row = jnp.concatenate(ordered(gather_seq(hat_one), mine), axis=0)
    normed_row = hat_row * gain_one + shift_one
    joined = dot(normed_row, wqkv, ((1,), (0,)))
    own_bias = lambda piece: lax.dynamic_slice_in_dim(piece, mine * width, width, 0)
    split = lambda part: part.reshape(length, heads, HEAD).transpose(1, 0, 2)
    merge = lambda part: part.transpose(1, 0, 2).reshape(length, width)
    queries = split((joined[:, :width] + own_bias(query_bias)) * HEAD ** (-0.5))
    keys = split(joined[:, width : 2 * width])
    values = split(joined[:, 2 * width :] + own_bias(value_bias))
    labels = lax.all_gather(
        jnp.where(valid > 0, segment_ids, -1).astype(jnp.int32).reshape(-1), "seq", axis=0, tiled=True
    )
    place = jnp.arange(length, dtype=jnp.int32)
    earlier = place[None, :] <= place[:, None]
    same = (labels[:, None] == labels[None, :]) & (labels[:, None] >= 0)
    mask = (same & earlier) | (place[None, :] == place[:, None])
    scores = jnp.einsum("hqd,hkd->hqk", queries, keys, precision=high)
    scores = jnp.where(mask[None], scores, masked_score)
    peak = jnp.max(scores, axis=-1, keepdims=True)
    weights = jnp.where(mask[None], jnp.exp(scores - peak), 0.0)
    probs = weights / jnp.sum(weights, axis=-1, keepdims=True)
    heads_row = jnp.einsum("hqk,hkd->hqd", probs, values, precision=high)
    heads_parts = merge(heads_row).reshape(seq_parts, chunk, width)

    def to_tokens(parts):
        rel = [lax.dynamic_index_in_dim(parts, mine ^ r, 0, keepdims=False) for r in range(seq_parts)]
        got = [rel[0]] + [swap(rel[r], r) for r in range(1, seq_parts)]
        return jnp.concatenate(ordered(got, mine), axis=1)

    def to_heads(block):
        parts = [lax.dynamic_slice_in_dim(block, (mine ^ r) * width, width, 1) for r in range(seq_parts)]
        got = [parts[0]] + [swap(parts[r], r) for r in range(1, seq_parts)]
        return jnp.concatenate(ordered(got, mine), axis=0)

    heads_flat = to_tokens(heads_parts)
    mixed = flat_in + dot(heads_flat, wproj, ((1,), (0,))) + proj_bias

    hat_two, scale_two = norm_stats(mixed)
    hat_all = jnp.concatenate(gather_seq(hat_two), axis=0)
    live = valid.reshape(chunk, 1).astype(jnp.float32)
    grad_out = cotangent.reshape(chunk, features) * live
    grad_all = jnp.concatenate(gather_seq(grad_out), axis=0)
    normed_all = hat_all * gain_two + shift_two
    hidden = dot(normed_all, win, ((1,), (0,))) + in_bias
    inner = jnp.tanh(gelu_scale * (hidden + gelu_cubic * hidden * hidden * hidden))
    activated = 0.5 * hidden * (1.0 + inner)
    slope = 0.5 * (1.0 + inner) + 0.5 * hidden * (1.0 - inner * inner) * gelu_scale * (
        1.0 + 3.0 * gelu_cubic * hidden * hidden
    )
    out_part = dot(activated, wout, ((1,), (0,)))
    rel = lambda part: [part[r * chunk : (r + 1) * chunk] for r in range(seq_parts)]
    output = mixed + scatter_seq(rel(out_part)) + out_bias

    grad_hidden = dot(grad_all, wout, ((1,), (1,))) * slope
    grad_wout = dot(activated, grad_all, ((0,), (0,)))
    shard_out = scatter_dp(grad_wout.reshape(dp_parts, unit_rows, features))
    grad_win = dot(normed_all, grad_hidden, ((0,), (0,)))
    shard_in = scatter_dp(grad_win.reshape(dp_parts, rows, dp_parts * unit_rows))
    grad_bias_in = jnp.sum(grad_hidden, axis=0)
    norm_part = dot(grad_hidden, win, ((1,), (1,)))
    grad_normed = scatter_seq(rel(norm_part))
    grad_gain_two = jnp.sum(grad_normed * hat_two, axis=0)
    grad_shift_two = jnp.sum(grad_normed, axis=0)
    grad_mixed = grad_out + norm_back(hat_two, scale_two, gain_two, grad_normed)
    grad_heads = dot(grad_mixed, wproj, ((1,), (1,)))
    grad_wproj = dot(heads_flat, grad_mixed, ((0,), (0,)))
    proj_parts = [lax.dynamic_slice_in_dim(grad_wproj, (mine ^ r) * width, width, 1) for r in range(seq_parts)]
    proj_part_sum = scatter_seq(proj_parts)
    head_grads = split(to_heads(grad_heads))
    row_dots = jnp.sum(head_grads * heads_row, axis=-1, keepdims=True)
    weight_grads = jnp.einsum("hqd,hkd->hqk", head_grads, values, precision=high)
    score_grads = probs * (weight_grads - row_dots)
    value_grads = jnp.einsum("hqk,hqd->hkd", probs, head_grads, precision=high)
    query_grads = jnp.einsum("hqk,hkd->hqd", score_grads, keys, precision=high)
    key_grads = jnp.einsum("hqk,hqd->hkd", score_grads, queries, precision=high)
    joined_grads = jnp.concatenate(
        [merge(query_grads) * HEAD ** (-0.5), merge(key_grads), merge(value_grads)], axis=1
    )
    grad_wqkv = dot(normed_row, joined_grads, ((0,), (0,)))
    first_grads = jnp.concatenate([grad_wqkv, proj_part_sum], axis=1)
    shard_first = scatter_dp(first_grads.reshape(dp_parts, rows, features))
    joined_sums = jnp.sum(joined_grads, axis=0)
    pre_part = dot(joined_grads, wqkv, ((1,), (1,)))
    grad_gain_one = jnp.sum(pre_part * hat_row, axis=0)
    grad_shift_one = jnp.sum(pre_part, axis=0)
    pre_parts = pre_part.reshape(seq_parts, chunk, features)
    grad_pre = scatter_seq(
        [lax.dynamic_index_in_dim(pre_parts, mine ^ r, 0, keepdims=False) for r in range(seq_parts)]
    )
    input_grad = grad_mixed + norm_back(hat_one, scale_one, gain_one, grad_pre)

    def spread(part):
        return lax.dynamic_update_slice_in_dim(jnp.zeros((features,), jnp.float32), part, mine * width, 0)

    bias_blocks = lax.dynamic_update_index_in_dim(
        jnp.zeros((dp_parts, seq_parts, unit_rows), jnp.float32),
        grad_bias_in.reshape(dp_parts, unit_rows),
        mine,
        1,
    )
    grad_vec = jnp.concatenate(
        [
            grad_gain_one,
            grad_shift_one,
            spread(joined_sums[:width]),
            spread(joined_sums[2 * width :]),
            jnp.sum(grad_mixed, axis=0),
            grad_gain_two,
            grad_shift_two,
            jnp.sum(grad_out, axis=0),
            bias_blocks.reshape(-1),
        ]
    )
    all_vec = lax.psum(grad_vec, ("dp", "seq"))
    shard_vec = lax.dynamic_slice_in_dim(all_vec, lax.axis_index("dp") * vec_size, vec_size, 0)

    squares = jnp.sum(shard_out * shard_out) + jnp.sum(shard_in * shard_in) + jnp.sum(shard_first * shard_first)
    clip_norm = jnp.sqrt(lax.psum(squares, ("dp", "seq")) + jnp.sum(all_vec * all_vec))
    factor = clip_limit / jnp.maximum(clip_norm, clip_limit)

    out_grad = jnp.concatenate(ordered(gather_seq(shard_out), mine), axis=0)
    in_grad = jnp.stack(
        [part.reshape(rows, dp_parts, unit_rows) for part in ordered(gather_seq(shard_in), mine)], axis=2
    ).reshape(rows, -1)
    first_parts = ordered(gather_seq(shard_first), mine)
    qkv_grad = jnp.concatenate(
        [part[:, i * width : (i + 1) * width] for i in range(3) for part in first_parts], axis=1
    )
    proj_grad = jnp.concatenate([part[:, 3 * width :] for part in first_parts], axis=1)

    vec_a, vec_b, vec_c = adamw_update(vectors, vec_first, vec_second, factor * shard_vec, vector_rate, 0.0)
    qkv_a, qkv_b, qkv_c = adamw_update(
        w_qkv, qkv_first, qkv_second, factor * qkv_grad, matrix_rate, weight_decay
    )
    proj_a, proj_b, proj_c = adamw_update(
        w_proj, proj_first, proj_second, factor * proj_grad, matrix_rate, weight_decay
    )
    in_a, in_b, in_c = adamw_update(w_in, in_first, in_second, factor * in_grad, matrix_rate, weight_decay)
    out_a, out_b, out_c = adamw_update(
        w_out, out_first, out_second, factor * out_grad, matrix_rate, weight_decay
    )
    return (
        output.reshape(tokens.shape),
        input_grad.reshape(tokens.shape),
        clip_norm,
        vec_a,
        vec_b,
        vec_c,
        qkv_a,
        qkv_b,
        qkv_c,
        proj_a,
        proj_b,
        proj_c,
        in_a,
        in_b,
        in_c,
        out_a,
        out_b,
        out_c,
    )


def solution(mesh):
    row = P("dp", "seq", None)
    mark = P("dp", "seq")
    vec = P("dp")
    mat = P("dp", None)
    return jax.shard_map(
        local,
        mesh=mesh,
        in_specs=(row, row, mark, mark) + (vec,) * 3 + (mat,) * 12,
        out_specs=(row, row, P()) + (vec,) * 3 + (mat,) * 12,
        check_vma=False,
    )
```

```python
import functools

import jax
import jax.numpy as jnp
from jax import lax
from jax.experimental import pallas as pl
from jax.experimental.pallas import tpu as pltpu
from jax.sharding import PartitionSpec as P

D = 768
HEADS = 12
HEAD = 64
STEP = 10
CH = 256
LEN = 1024
SEQ = 4
QUARTER = D // SEQ
OWN = HEADS // SEQ
GROUPS = 8
ROWS = D // GROUPS
SUB = ROWS // SEQ
HALF_VEC = D // 2
VEC_ROWS = 24

f32 = jnp.float32
bf16 = jnp.bfloat16
masked_score = -1e30
norm_eps = 1e-05
clip_limit = 1.0
beta_one = 0.9
beta_two = 0.999
adam_eps = 1e-08
matrix_rate = 0.02
vector_rate = 0.4
weight_decay = 0.01
gelu_scale = 0.7978845608028654
gelu_cubic = 0.044715

WHOLE = pl.BlockSpec(memory_space=pltpu.VMEM)
SCALARS = pl.BlockSpec(memory_space=pltpu.SMEM)
NN = ((1,), (0,))
NT = ((1,), (1,))
TN = ((0,), (0,))


def shape(*dims, kind=f32):
    return jax.ShapeDtypeStruct(dims, kind)


def run(kernel, scal, args, outs, scratch=(), work=0, name=None):
    moved = sum(a.size * a.dtype.itemsize for a in args) + sum(
        o.size * o.dtype.itemsize for o in outs
    )
    return pl.pallas_call(
        kernel,
        out_shape=tuple(outs),
        in_specs=[SCALARS] + [WHOLE] * len(args),
        out_specs=tuple([WHOLE] * len(outs)),
        scratch_shapes=list(scratch),
        compiler_params=pltpu.CompilerParams(vmem_limit_bytes=56 << 20),
        cost_estimate=pl.CostEstimate(flops=work, bytes_accessed=moved, transcendentals=0),
        name=name,
    )(scal, *args)


def halves(value):
    top = value.astype(bf16)
    return top, (value - top.astype(f32)).astype(bf16)


def dot(left, right, dims):
    return lax.dot_general(left, right, (dims, ((), ())), preferred_element_type=f32)


def dot3(lh, ll, rh, rl, dims):
    return dot(lh, rh, dims) + (dot(lh, rl, dims) + dot(ll, rh, dims))


def rows_at(index, size):
    return pl.ds(pl.multiple_of(index * size, size), size)


def piece(vec, number):
    a, b = 2 * number, 2 * number + 1
    return jnp.concatenate(
        [vec[a // 3, a % 3 : a % 3 + 1, :], vec[b // 3, b % 3 : b % 3 + 1, :]], axis=1
    )


def norm_stats(inputs):
    center = inputs - jnp.mean(inputs, axis=-1, keepdims=True)
    spread = jnp.mean(center * center, axis=-1, keepdims=True)
    scale = lax.rsqrt(spread + norm_eps)
    return center * scale, scale


def norm_back(hat, scale, gain, grad):
    inner = grad * gain
    return scale * (
        inner
        - jnp.mean(inner, axis=-1, keepdims=True)
        - hat * jnp.mean(inner * hat, axis=-1, keepdims=True)
    )


def low_lanes(dims):
    return lax.broadcasted_iota(jnp.int32, dims, 1) < HEAD


def lane_pairs(pair, last):
    low = low_lanes(pair.shape)
    roll = lambda v: pltpu.roll(v, HEAD, 1)
    ph = pair.astype(bf16).astype(f32)
    pl_ = pair - ph
    lh = last.astype(bf16).astype(f32)
    ll = last - lh
    return [
        jnp.where(low, ph, roll(pl_)).astype(bf16),
        jnp.where(low, roll(ph), pl_).astype(bf16),
        jnp.where(low, lh, roll(ll)).astype(bf16),
    ]


def row_halves(turned, head):
    part = turned[HEAD * head : HEAD * (head + 1)]
    return halves(part)


def pack_first_kernel(scal, wqkv, wproj, vec, seg, valid, tokens, first, packed):
    mine = scal[0]
    proj = wproj[pl.ds(pl.multiple_of(mine * SUB, 8), SUB), :]
    turn = lax.rem(D - mine * QUARTER, D)
    for part in range(3):
        turned = pltpu.roll(wqkv[:, part * D : (part + 1) * D], turn, 1)
        first[:ROWS, part * CH : part * CH + QUARTER] = turned[:, :QUARTER]
        for group in range(SEQ):
            lane = HEAD * (3 * group + part)
            first[group * SUB : (group + 1) * SUB, part * CH + QUARTER : (part + 1) * CH] = proj[
                :, lane : lane + HEAD
            ]
    first[ROWS:, :] = jnp.zeros((8, D), f32)
    first[ROWS : ROWS + 3, :HALF_VEC] = vec[...]
    packed[:CH, :] = tokens[...]
    packed[CH:, :] = jnp.zeros((8, D), f32)
    packed[CH : CH + 1, :CH] = jnp.where(valid[...] > 0, seg[...], -1).astype(f32)


def pack_second_kernel(scal, win, wout, second):
    mine = scal[0]
    turn = lax.rem(HALF_VEC - mine * ROWS, HALF_VEC)
    for part in range(GROUPS):
        turned = pltpu.roll(win[:, part * HALF_VEC : (part + 1) * HALF_VEC], turn, 1)
        second[:ROWS, part * ROWS : (part + 1) * ROWS] = turned[:, :ROWS]
    second[ROWS:, :] = wout[pl.ds(pl.multiple_of(mine * ROWS, 8), ROWS), :]


def front_kernel(ring, scal, *refs):
    blocks = refs[: GROUPS if ring else 2]
    refs = refs[len(blocks) :]
    toks, refs = refs[:4], refs[4:]
    (wh, wl, xh, xl, kcat, qturn, vcat, qpair, kturn, outs_turn, lse, low_row, vec, proj) = refs[:14]
    heads, refs = refs[14:18], refs[18:]
    vturn, label = refs
    mine = scal[0]

    if ring:
        for k in range(GROUPS):
            at = scal[1 + k]
            block = blocks[k][:ROWS, :]
            top, rest = halves(block)
            wh[rows_at(at, ROWS), :] = top
            wl[rows_at(at, ROWS), :] = rest
            vec[at] = blocks[k][ROWS:, :HALF_VEC]
            for group in range(SEQ):
                for part in range(3):
                    lane = HEAD * (3 * group + part)
                    proj[pl.ds(pl.multiple_of(at * SUB, 8), SUB), lane : lane + HEAD] = block[
                        group * SUB : (group + 1) * SUB, part * CH + QUARTER : (part + 1) * CH
                    ]
    else:
        wh[...], wl[...] = halves(blocks[0][...])
        vec[...] = blocks[1][...]
        proj[...] = jnp.zeros_like(proj)

    gain, shift = piece(vec, 0), piece(vec, 1)
    turn = lax.rem(D - mine * QUARTER, D)
    own = lambda number: pltpu.roll(jnp.broadcast_to(piece(vec, number), (8, D)), turn, 1)[:1, :CH]
    query_bias, value_bias = own(2), own(3)

    for r in range(SEQ):
        nat = jnp.bitwise_xor(mine, r)
        at = rows_at(nat, CH)
        label[nat] = toks[r][CH:, :CH]
        hat, _ = norm_stats(toks[r][:CH, :])
        xh[at, :], xl[at, :] = halves(hat)
        nh, nl = halves(hat * gain + shift)
        joined = dot3(nh, nl, wh[...], wl[...], NN)
        query = (joined[:, :CH] + query_bias) * HEAD ** (-0.5)
        key = joined[:, CH : 2 * CH]
        value = joined[:, 2 * CH :] + value_bias
        keys = lane_pairs(key[:, :128], key[:, 128:])
        values = lane_pairs(value[:, :128], value[:, 128:])
        queries = lane_pairs(query[:, :128], query[:, 128:])
        key_t, value_t, query_t = key.T, value.T, query.T
        for h in range(OWN):
            kcat[h, at, :] = jnp.concatenate([keys[h], keys[h]], axis=1)
            vcat[h, at, :] = jnp.concatenate([values[h], values[h]], axis=1)
            qpair[h, at, :] = queries[h]
            a, b = row_halves(query_t, h)
            qturn[h, :, at] = jnp.concatenate([a, a, b, b], axis=0)
            a, b = row_halves(key_t, h)
            kturn[h, :, at] = jnp.concatenate([a, b], axis=0)
            a, b = row_halves(value_t, h)
            vturn[h, :, at] = jnp.concatenate([a, b], axis=0)

    labels = jnp.concatenate([label[c][:1, :] for c in range(SEQ)], axis=1)
    spot = lax.broadcasted_iota(jnp.int32, (1, LEN), 1).astype(f32)
    begin = jnp.zeros((1, LEN), f32)
    for segment in range(3):
        held = jnp.sum(jnp.where(labels == float(segment), 1.0, 0.0), axis=1, keepdims=True)
        begin = begin + jnp.where(labels > float(segment), held, 0.0)
    begin = jnp.where(labels < 0.0, spot, begin)
    low_row[...] = jnp.broadcast_to(begin, (8, LEN))

    def one_head(h, carry):
        for c in range(SEQ):
            size = CH * (c + 1)
            lanes = slice(c * CH, (c + 1) * CH)
            score = dot(kcat[h, :size, :], qturn[h, :, lanes], NN)
            mask = allowed(low_row, c, size)
            score = jnp.where(mask, score, masked_score)
            peak = jnp.max(score, axis=0, keepdims=True)
            weight = jnp.exp(score - peak)
            total = jnp.sum(weight, axis=0, keepdims=True)
            top, rest = halves(weight)
            both = dot(vturn[h, :, :size], top, NN)
            extra = dot(vturn[h, :HEAD, :size], rest, NN)
            result = (both[:HEAD] + both[HEAD:] + extra) / total
            outs_turn[h, :, lanes] = result
            lse[h, :, lanes] = jnp.broadcast_to(peak + jnp.log(total), (8, CH))
        return carry

    lax.fori_loop(0, OWN, one_head, 0)
    for r in range(SEQ):
        at = rows_at(jnp.bitwise_xor(mine, r), CH)
        stacked = jnp.concatenate([outs_turn[h, :, at] for h in range(OWN)], axis=0)
        heads[r][...] = stacked.T


def allowed(low_row, c, size):
    key_at = lax.broadcasted_iota(jnp.int32, (size, CH), 0).astype(f32)
    query_at = (lax.broadcasted_iota(jnp.int32, (1, CH), 1) + c * CH).astype(f32)
    begin = low_row[:1, c * CH : (c + 1) * CH]
    return (key_at >= begin) & (key_at <= query_at)


def proj_kernel(ring, scal, tokens, *refs):
    heads, refs = refs[:4], refs[4:]
    parts, refs = refs[: 4 if ring else 1], refs[4 if ring else 1 :]
    vec, wh, wl, mixed, hat, scale, weight = refs
    mine = scal[0]
    if ring:
        for r in range(SEQ):
            at = jnp.bitwise_xor(mine, r)
            for d in range(GROUPS):
                weight[pl.ds(pl.multiple_of(d * ROWS + at * SUB, 8), SUB), :] = parts[r][
                    d * SUB : (d + 1) * SUB, :
                ]
        wh[...], wl[...] = halves(weight[...])
    else:
        wh[...], wl[...] = halves(parts[0][...])
    total = tokens[...] + piece(vec, 4)
    for r in range(SEQ):
        at = rows_at(jnp.bitwise_xor(mine, r), QUARTER)
        a, b = halves(heads[r][...])
        total = total + dot3(a, b, wh[at, :], wl[at, :], NN)
    mixed[...] = total
    normed, size = norm_stats(total)
    hat[...] = normed
    scale[...] = jnp.broadcast_to(size, (CH, 128))


def ffn_kernel(scal, *refs):
    hats, grads, refs = refs[:4], refs[4:8], refs[8:]
    weights, vec = refs[:2]
    acts_h, acts_l, hid_h, hid_l, norm_h, norm_l, out_h, out_l, bias_sum = refs[2:11]
    parts, refs = refs[11:15], refs[15:]
    wouth, woutl, winh, winl = refs
    mine = scal[0]
    for d in range(GROUPS):
        at = slice(d * ROWS, (d + 1) * ROWS)
        winh[at, :], winl[at, :] = halves(weights[d, :ROWS, :])
        wouth[at, :], woutl[at, :] = halves(weights[d, ROWS:, :])
    gain, shift = piece(vec, 5), piece(vec, 6)
    marks = [16 + d for d in range(GROUPS)]
    table = jnp.concatenate([vec[m // 3, m % 3 : m % 3 + 1, :] for m in marks], axis=0)
    table = pltpu.roll(table, lax.rem(HALF_VEC - mine * ROWS, HALF_VEC), 1)[:, :ROWS]
    bias = jnp.concatenate([table[d : d + 1] for d in range(GROUPS)], axis=1)
    sums = jnp.zeros((1, D), f32)
    for r in (1, 3, 2, 0):
        at = slice(r * CH, (r + 1) * CH)
        nh, nl = halves(hats[r][...] * gain + shift)
        norm_h[at, :], norm_l[at, :] = nh, nl
        hidden = dot3(nh, nl, winh[...], winl[...], NN) + bias
        inner = jnp.tanh(gelu_scale * (hidden + gelu_cubic * hidden * hidden * hidden))
        acts_h[at, :], acts_l[at, :] = halves(0.5 * hidden * (1.0 + inner))
        slope = 0.5 * (1.0 + inner) + 0.5 * hidden * (1.0 - inner * inner) * gelu_scale * (
            1.0 + 3.0 * gelu_cubic * hidden * hidden
        )
        gh, gl = halves(grads[r][...])
        out_h[at, :], out_l[at, :] = gh, gl
        back = dot3(gh, gl, wouth[...], woutl[...], NT) * slope
        sums = sums + jnp.sum(back, axis=0, keepdims=True)
        bh, bl = halves(back)
        hid_h[at, :], hid_l[at, :] = bh, bl
        parts[r][...] = dot3(bh, bl, winh[...], winl[...], NT)
    bias_sum[...] = jnp.broadcast_to(sums, (8, D))


def ffn_grad_kernel(scal, norm_h, norm_l, hid_h, hid_l, acts_h, acts_l, out_h, out_l, grads):
    win = dot3(norm_h[...], norm_l[...], hid_h[...], hid_l[...], TN)
    for d in range(GROUPS):
        grads[d, :ROWS, :] = win[d * ROWS : (d + 1) * ROWS]
    wout = dot3(acts_h[...], acts_l[...], out_h[...], out_l[...], TN)
    for d in range(GROUPS):
        grads[d, ROWS:, :] = wout[d * ROWS : (d + 1) * ROWS]


def ffn_out_kernel(scal, acts_h, acts_l, weights, *refs):
    parts, refs = refs[:4], refs[4:]
    wouth, woutl = refs
    for d in range(GROUPS):
        at = slice(d * ROWS, (d + 1) * ROWS)
        wouth[at, :], woutl[at, :] = halves(weights[d, ROWS:, :])
    for r in (1, 3, 2, 0):
        at = slice(r * CH, (r + 1) * CH)
        parts[r][...] = dot3(acts_h[at, :], acts_l[at, :], wouth[...], woutl[...], NN)


def output_kernel(scal, mixed, one, two, three, vec, output):
    output[...] = mixed[...] + (one[...] + two[...] + three[...]) + piece(vec, 7)


def proj_back_kernel(scal, one, two, three, hat, scale, vec, grad_out, wh, wl, mixed_grad, sums, *parts):
    mine = scal[0]
    normed = one[...] + two[...] + three[...]
    back = norm_back(hat[...], scale[:, :1], piece(vec, 5), normed)
    total = grad_out[...] + back
    mixed_grad[...] = total
    a, b = halves(total)
    for r in range(SEQ):
        at = rows_at(jnp.bitwise_xor(mine, r), QUARTER)
        parts[r][...] = dot3(a, b, wh[at, :], wl[at, :], NT)
    add = lambda v: jnp.sum(v, axis=0, keepdims=True)
    sums[...] = jnp.concatenate(
        [add(total), add(normed * hat[...]), add(normed), add(grad_out[...]), jnp.zeros((4, D), f32)],
        axis=0,
    )


def proj_grad_kernel(ring, scal, *refs):
    heads, refs = refs[:4], refs[4:]
    mixed_grad, outs, whole = refs[0], refs[1:-1], refs[-1]
    mine = scal[0]
    gh, gl = halves(mixed_grad[...])
    for r in range(SEQ):
        at = rows_at(jnp.bitwise_xor(mine, r), QUARTER)
        a, b = halves(heads[r][...])
        whole[at, :] = dot3(a, b, gh, gl, TN)
    if not ring:
        outs[0][...] = whole[...]
        return
    for r in range(SEQ):
        at = jnp.bitwise_xor(mine, r)
        for d in range(GROUPS):
            outs[r][d * SUB : (d + 1) * SUB, :] = whole[
                pl.ds(pl.multiple_of(d * ROWS + at * SUB, 8), SUB), :
            ]


def back_kernel(ring, scal, *refs):
    grads, refs = refs[:4], refs[4:]
    kcat, qturn, vcat, qpair, kturn, outs_turn, lse, low_row, xh, xl, wh, wl, vec = refs[:13]
    proj_one, proj_two, proj_three, sums, bias_sum = refs[13:18]
    joined_h, joined_l = refs[18:20]
    outs = refs[20 : 20 + (GROUPS if ring else 2)]
    gturn, gpair, dots, key_sum, value_sum, query_turn, whole, rows = refs[20 + len(outs) :]
    mine = scal[0]

    for r in range(SEQ):
        at = rows_at(jnp.bitwise_xor(mine, r), CH)
        grad = jnp.concatenate([grads[r][...], jnp.zeros((CH, HEAD), f32)], axis=1)
        pairs = lane_pairs(grad[:, :128], grad[:, 128:])
        turned = grad.T
        for h in range(OWN):
            gpair[h, at, :] = pairs[h]
            part = turned[HEAD * h : HEAD * (h + 1)]
            dots[h, :, at] = jnp.broadcast_to(
                jnp.sum(part * outs_turn[h, :, at], axis=0, keepdims=True), (8, CH)
            )
            a, b = halves(part)
            gturn[h, :, at] = jnp.concatenate([a, a, b, b], axis=0)

    key_sum[...] = jnp.zeros_like(key_sum)
    value_sum[...] = jnp.zeros_like(value_sum)

    def one_head(h, carry):
        for c in range(SEQ):
            size = CH * (c + 1)
            lanes = slice(c * CH, (c + 1) * CH)
            score = dot(kcat[h, :size, :], qturn[h, :, lanes], NN)
            weight = jnp.where(allowed(low_row, c, size), jnp.exp(score - lse[h, :1, lanes]), 0.0)
            back = dot(vcat[h, :size, :], gturn[h, :, lanes], NN)
            score_back = weight * (back - dots[h, :1, lanes])
            a, b = halves(weight)
            pair = gpair[h, lanes, :]
            value_sum[h, :size, :] += dot(a, pair, NN) + dot(b, pair, NN)
            a, b = halves(score_back)
            pair = qpair[h, lanes, :]
            key_sum[h, :size, :] += dot(a, pair, NN) + dot(b, pair, NN)
            turned = dot(kturn[h, :, :size], a, NN) + dot(kturn[h, :, :size], b, NN)
            query_turn[h, :, lanes] = (turned[:HEAD] + turned[HEAD:]) * HEAD ** (-0.5)
        return carry

    lax.fori_loop(0, OWN, one_head, 0)

    column_sums = jnp.zeros((1, D), f32)
    low = low_lanes((CH, 128))
    for c in range(SEQ):
        at = slice(c * CH, (c + 1) * CH)
        blank = jnp.zeros((HEAD, CH), f32)
        query = jnp.concatenate([query_turn[h, :, at] for h in range(OWN)] + [blank], axis=0).T
        done = [query]
        for kept in (key_sum, value_sum):
            full = [kept[h, at, :] for h in range(OWN)]
            full = [v + pltpu.roll(v, HEAD, 1) for v in full]
            done.append(jnp.where(low, full[0], full[1]))
            done.append(jnp.where(low, full[2], 0.0))
        joined = jnp.concatenate(done, axis=1)
        column_sums = column_sums + jnp.sum(joined, axis=0, keepdims=True)
        joined_h[at, :], joined_l[at, :] = halves(joined)

    core = dot3(xh[...], xl[...], joined_h[...], joined_l[...], TN)
    gain, shift = piece(vec, 0), piece(vec, 1)
    as_column = lambda v: jnp.broadcast_to(v, (128, D)).T[:, :1]
    whole[...] = as_column(gain) * core + as_column(shift) * column_sums
    weights = wh[...].astype(f32) + wl[...].astype(f32)
    gain_grad = jnp.sum(weights * core, axis=1, keepdims=True)
    shift_grad = jnp.sum(weights * column_sums, axis=1, keepdims=True)
    lane = lax.broadcasted_iota(jnp.int32, (D, 128), 1)
    norm_grads = jnp.where(lane == 0, gain_grad, shift_grad).T

    def place(part, scale):
        wide = jnp.concatenate([part[:, :QUARTER], jnp.zeros((1, D - QUARTER), f32)], axis=1)
        wide = jnp.broadcast_to(wide, (8, D))
        return pltpu.roll(wide, mine * QUARTER, 1)[:1]

    entries = [
        norm_grads[0:1],
        norm_grads[1:2],
        place(column_sums[:, :CH], 1.0),
        place(column_sums[:, 2 * CH :], 1.0),
        sums[0:1],
        sums[1:2],
        sums[2:3],
        sums[3:4],
    ]
    lines = [e[:, i * HALF_VEC : (i + 1) * HALF_VEC] for e in entries for i in range(2)]
    bias = jnp.concatenate(
        [bias_sum[:1, d * ROWS : (d + 1) * ROWS] for d in range(GROUPS)], axis=0
    )
    bias = jnp.concatenate([bias, jnp.zeros((GROUPS, HALF_VEC - ROWS), f32)], axis=1)
    bias = pltpu.roll(bias, mine * ROWS, 1)
    lines = lines + [bias[d : d + 1] for d in range(GROUPS)]
    filler = jnp.zeros((5, HALF_VEC), f32)
    for d in range(GROUPS):
        rows[d] = jnp.concatenate(lines[3 * d : 3 * d + 3] + [filler], axis=0)

    if not ring:
        outs[0][...] = whole[...]
        outs[1][...] = rows[...]
        return
    for k in range(GROUPS):
        at = scal[1 + k]
        outs[k][:ROWS, :] = whole[rows_at(at, ROWS), :]
        here = pl.ds(pl.multiple_of(at * SUB, 8), SUB)
        proj = proj_one[here, :] + proj_two[here, :] + proj_three[here, :]
        for group in range(SEQ):
            for part in range(3):
                lane_at = HEAD * (3 * group + part)
                outs[k][
                    group * SUB : (group + 1) * SUB, part * CH + QUARTER : (part + 1) * CH
                ] = proj[:, lane_at : lane_at + HEAD]
        outs[k][ROWS:, :HALF_VEC] = rows[at]
        outs[k][ROWS:, HALF_VEC:] = jnp.zeros((8, HALF_VEC), f32)


def pre_back_kernel(scal, joined_h, joined_l, wh, wl, *parts):
    mine = scal[0]
    for r in (1, 3, 2, 0):
        at = rows_at(jnp.bitwise_xor(mine, r), CH)
        parts[r][...] = dot3(joined_h[at, :], joined_l[at, :], wh[...], wl[...], NT)


def input_grad_kernel(scal, tokens, one, two, three, vec, mixed_grad, result):
    hat, scale = norm_stats(tokens[...])
    grad = one[...] + two[...] + three[...]
    result[...] = mixed_grad[...] + norm_back(hat, scale, piece(vec, 0), grad)


def shard_kernel(scal, *refs):
    firsts, seconds, refs = refs[:4], refs[4:8], refs[8:]
    qkv, proj, win, wout, vec, squares, first, second = refs
    mine = scal[0]
    for r in range(SEQ):
        first[jnp.bitwise_xor(mine, r)] = firsts[r][:ROWS, :]
        second[jnp.bitwise_xor(mine, r)] = seconds[r][...]
    for part in range(3):
        qkv[:, part * D : (part + 1) * D] = jnp.concatenate(
            [first[j][:, part * CH : part * CH + QUARTER] for j in range(SEQ)], axis=1
        )
    for j in range(SEQ):
        for group in range(SEQ):
            for part in range(3):
                lane = HEAD * (3 * group + part)
                proj[j * SUB : (j + 1) * SUB, lane : lane + HEAD] = first[j][
                    group * SUB : (group + 1) * SUB, part * CH + QUARTER : (part + 1) * CH
                ]
        wout[j * ROWS : (j + 1) * ROWS, :] = second[j][ROWS:, :]
    for d in range(GROUPS):
        win[:, d * HALF_VEC : (d + 1) * HALF_VEC] = jnp.concatenate(
            [second[j][:ROWS, d * ROWS : (d + 1) * ROWS] for j in range(SEQ)], axis=1
        )
    line = sum(firsts[r][ROWS:, :HALF_VEC] for r in range(SEQ))
    vec[...] = line
    square = lambda v: jnp.sum(jnp.sum(v * v, axis=0, keepdims=True), axis=1, keepdims=True)
    total = square(qkv[...]) + square(proj[...]) + square(win[...]) + square(wout[...]) + square(line)
    squares[...] = jnp.broadcast_to(total, (8, 128))


def adamw_update(weight, first, second, grad, rate, decay):
    new_first = beta_one * first + (1.0 - beta_one) * grad
    new_second = beta_two * second + (1.0 - beta_two) * grad * grad
    first_hat = new_first / (1.0 - beta_one**STEP)
    second_hat = new_second / (1.0 - beta_two**STEP)
    new_weight = weight - rate * (first_hat / (jnp.sqrt(second_hat) + adam_eps) + decay * weight)
    return (new_first, new_second, new_weight)


def ring_tables(count):
    evens = [2 * i for i in range(count // 2)]
    order = evens + [i + 1 for i in reversed(evens)]
    place = [0] * count
    for position, device in enumerate(order):
        place[device] = position
    right = [(order[i], order[(i + 1) % count]) for i in range(count)]
    left = [(b, a) for a, b in right]
    return order, place, right, left


def ring_gather(block):
    _, _, right, left = ring_tables(GROUPS)
    got = {0: block}
    forth = back = block
    for step in range(1, GROUPS // 2 + 1):
        forth = lax.ppermute(forth, "dp", right)
        got[GROUPS - step] = forth
        if step < GROUPS // 2:
            back = lax.ppermute(back, "dp", left)
            got[step] = back
    return [got[k] for k in range(GROUPS)]


def ring_scatter(blocks):
    _, _, right, left = ring_tables(GROUPS)
    half = GROUPS // 2
    forth = lax.ppermute(blocks[half], "dp", right)
    back = lax.ppermute(blocks[half + 1], "dp", left)
    for step in range(half - 1, 0, -1):
        forth = lax.ppermute(forth + blocks[step], "dp", right)
        if step > 1:
            back = lax.ppermute(back + blocks[GROUPS + 1 - step], "dp", left)
    return forth + back + blocks[0]


def swap(block, bits):
    return lax.ppermute(block, "seq", [(i, i ^ bits) for i in range(SEQ)])


def gather_seq(block):
    across = swap(block, 2)
    core = swap(block, 1)
    return [block, core, across, swap(across, 1)]


def exchange_seq(parts):
    return [parts[0]] + [swap(parts[r], r) for r in range(1, SEQ)]


def scatter_seq(parts):
    near = swap(parts[1], 1)
    far = swap(parts[3], 1)
    return parts[0], near, swap(parts[2] + far, 2)


def local(
    tokens,
    cotangent,
    segment_ids,
    valid,
    vectors,
    vec_first,
    vec_second,
    w_qkv,
    qkv_first,
    qkv_second,
    w_proj,
    proj_first,
    proj_second,
    w_in,
    in_first,
    in_second,
    w_out,
    out_first,
    out_second,
):
    dp_parts = lax.axis_size("dp")
    ring = dp_parts == GROUPS
    mine = lax.axis_index("seq")
    home = lax.axis_index("dp")
    rows = w_qkv.shape[0]
    units = w_out.shape[0] // SEQ
    if ring:
        order, place, _, _ = ring_tables(GROUPS)
        position = jnp.array(place, jnp.int32)[home]
        table = jnp.array(order + order, jnp.int32)
        scal = jnp.concatenate([mine[None], lax.dynamic_slice_in_dim(table, position, GROUPS)])
    else:
        scal = jnp.concatenate([mine[None], jnp.zeros((GROUPS,), jnp.int32)])
    scal = scal.astype(jnp.int32)
    flat_in = tokens.reshape(CH, D)
    wide = (D, D)

    if ring:
        first, packed = run(
            pack_first_kernel,
            scal,
            [w_qkv, w_proj, vectors.reshape(3, HALF_VEC), segment_ids, valid, flat_in],
            [shape(ROWS + 8, D), shape(CH + 8, D)],
            name="pack_first",
        )
        (second,) = run(
            pack_second_kernel, scal, [w_in, w_out], [shape(2 * ROWS, D)], name="pack_second"
        )
        blocks = ring_gather(first)
        weights = lax.all_gather(second, "dp", axis=0, tiled=False)
    else:
        own = lambda part: lax.dynamic_slice_in_dim(w_qkv, part * D + mine * QUARTER, CH, 1)
        padded = jnp.pad(w_qkv, ((0, 0), (0, CH)))
        own = lambda part: lax.dynamic_slice_in_dim(padded, part * D + mine * QUARTER, CH, 1)
        first = jnp.concatenate([own(0), own(1), own(2)], axis=1)
        all_vec = lax.all_gather(vectors, "dp", axis=0, tiled=True).reshape(GROUPS, 3, HALF_VEC)
        blocks = [
            lax.all_gather(first, "dp", axis=0, tiled=True),
            jnp.pad(all_vec, ((0, 0), (0, 5), (0, 0))),
        ]
        in_part = lax.dynamic_index_in_dim(
            w_in.reshape(rows, dp_parts, SEQ, units), mine, 2, keepdims=False
        ).reshape(rows, D)
        out_part = lax.dynamic_slice_in_dim(w_out, mine * units, units, 0)
        weights = jnp.concatenate(
            [
                lax.all_gather(part, "dp", axis=0, tiled=True).reshape(GROUPS, ROWS, D)
                for part in (in_part, out_part)
            ],
            axis=1,
        )
        marks = jnp.where(valid > 0, segment_ids, -1).astype(f32)
        packed = jnp.concatenate(
            [flat_in, jnp.pad(marks, ((0, 7), (0, D - CH)))], axis=0
        )
    toks = gather_seq(packed)
    grad_out = (cotangent * valid[..., None].astype(f32)).reshape(CH, D)
    grads_row = gather_seq(grad_out)

    big = shape(LEN, D, kind=bf16)
    square = shape(*wide, kind=bf16)
    done = run(
        functools.partial(front_kernel, ring),
        scal,
        blocks + toks,
        [
            square,
            square,
            big,
            big,
            shape(OWN, LEN, 256, kind=bf16),
            shape(OWN, 256, LEN, kind=bf16),
            shape(OWN, LEN, 256, kind=bf16),
            shape(OWN, LEN, 128, kind=bf16),
            shape(OWN, 128, LEN, kind=bf16),
            shape(OWN, HEAD, LEN),
            shape(OWN, 8, LEN),
            shape(8, LEN),
            shape(GROUPS, 8, HALF_VEC),
            shape(GROUPS * SUB, D),
        ]
        + [shape(CH, QUARTER)] * SEQ,
        scratch=[pltpu.VMEM((OWN, 128, LEN), bf16), pltpu.VMEM((SEQ, 8, CH), f32)],
        work=10_000_000_000,
        name="front",
    )
    qkv_h, qkv_l, hat_h, hat_l, kcat, qturn, vcat, qpair, kturn, outs_turn, lse, low_row, vec, proj = done[:14]
    heads = exchange_seq(list(done[14:]))
    if ring:
        proj_parts = gather_seq(proj)
    else:
        proj_parts = [lax.all_gather(w_proj, "dp", axis=0, tiled=True)]
    proj_h, proj_l, mixed, hat_two, scale_two = run(
        functools.partial(proj_kernel, ring),
        scal,
        [flat_in] + heads + proj_parts + [vec],
        [square, square, shape(CH, D), shape(CH, D), shape(CH, 128)],
        scratch=[pltpu.VMEM(wide, f32)],
        work=1_000_000_000,
        name="proj",
    )

    hats = gather_seq(hat_two)
    done = run(
        ffn_kernel,
        scal,
        hats + grads_row + [weights, vec],
        [big] * 8 + [shape(8, D)] + [shape(CH, D)] * SEQ,
        scratch=[pltpu.VMEM(wide, bf16)] * 4,
        work=11_000_000_000,
        name="ffn",
    )
    acts_h, acts_l, hid_h, hid_l, norm_h, norm_l, out_h, out_l, bias_sum = done[:9]
    norm_sums = scatter_seq(done[9:])
    (ffn_grads,) = run(
        ffn_grad_kernel,
        scal,
        [norm_h, norm_l, hid_h, hid_l, acts_h, acts_l, out_h, out_l],
        [shape(GROUPS, 2 * ROWS, D)],
        work=7_000_000_000,
        name="ffn_grad",
    )
    if ring:
        shard_second = lax.psum_scatter(ffn_grads, "dp", scatter_dimension=0, tiled=False)
    else:
        shard_in = lax.psum_scatter(
            ffn_grads[:, :ROWS].reshape(D, D), "dp", scatter_dimension=0, tiled=True
        )
        shard_out = lax.psum_scatter(
            ffn_grads[:, ROWS:].reshape(D, D), "dp", scatter_dimension=0, tiled=True
        )
    out_parts = run(
        ffn_out_kernel,
        scal,
        [acts_h, acts_l, weights],
        [shape(CH, D)] * SEQ,
        scratch=[pltpu.VMEM(wide, bf16)] * 2,
        work=3_600_000_000,
        name="ffn_out",
    )
    (output,) = run(
        output_kernel, scal, [mixed, *scatter_seq(out_parts), vec], [shape(CH, D)], name="output"
    )

    done = run(
        proj_back_kernel,
        scal,
        [*norm_sums, hat_two, scale_two, vec, grad_out, proj_h, proj_l],
        [shape(CH, D), shape(8, D)] + [shape(CH, QUARTER)] * SEQ,
        work=1_000_000_000,
        name="proj_back",
    )
    mixed_grad, sums = done[:2]
    head_grads = exchange_seq(list(done[2:]))
    proj_grads = run(
        functools.partial(proj_grad_kernel, ring),
        scal,
        heads + [mixed_grad],
        [shape(GROUPS * SUB, D)] * SEQ if ring else [shape(*wide)],
        scratch=[pltpu.VMEM(wide, f32)],
        work=1_000_000_000,
        name="proj_grad",
    )
    proj_sums = list(scatter_seq(proj_grads)) if ring else [jnp.zeros((8, 128), f32)] * 3
    done = run(
        functools.partial(back_kernel, ring),
        scal,
        head_grads
        + [kcat, qturn, vcat, qpair, kturn, outs_turn, lse, low_row, hat_h, hat_l, qkv_h, qkv_l, vec]
        + proj_sums
        + [sums, bias_sum],
        [big, big]
        + ([shape(ROWS + 8, D)] * GROUPS if ring else [shape(*wide), shape(GROUPS, 8, HALF_VEC)]),
        scratch=[
            pltpu.VMEM((OWN, 256, LEN), bf16),
            pltpu.VMEM((OWN, LEN, 128), bf16),
            pltpu.VMEM((OWN, 8, LEN), f32),
            pltpu.VMEM((OWN, LEN, 128), f32),
            pltpu.VMEM((OWN, LEN, 128), f32),
            pltpu.VMEM((OWN, HEAD, LEN), f32),
            pltpu.VMEM(wide, f32),
            pltpu.VMEM((GROUPS, 8, HALF_VEC), f32),
        ],
        work=14_000_000_000,
        name="back",
    )
    joined_h, joined_l = done[:2]
    pre_parts = run(
        pre_back_kernel,
        scal,
        [joined_h, joined_l, qkv_h, qkv_l],
        [shape(CH, D)] * SEQ,
        work=3_600_000_000,
        name="pre_back",
    )
    (input_grad,) = run(
        input_grad_kernel,
        scal,
        [flat_in, *scatter_seq(pre_parts), vec, mixed_grad],
        [shape(CH, D)],
        name="input_grad",
    )

    if ring:
        shard_first = ring_scatter(list(done[2:]))
        qkv_grad, proj_grad, in_grad, out_grad, vec_rows, squares = run(
            shard_kernel,
            scal,
            gather_seq(shard_first) + gather_seq(shard_second),
            [
                shape(ROWS, 3 * D),
                shape(ROWS, D),
                shape(ROWS, SEQ * D),
                shape(SEQ * ROWS, D),
                shape(8, HALF_VEC),
                shape(8, 128),
            ],
            scratch=[pltpu.VMEM((SEQ, ROWS, D), f32), pltpu.VMEM((SEQ, 2 * ROWS, D), f32)],
            name="shard",
        )
        vec_grad = vec_rows[:3].reshape(-1)
        clip_norm = jnp.sqrt(lax.psum(squares[0, 0], "dp"))
    else:
        shard_first = lax.psum_scatter(done[2], "dp", scatter_dimension=0, tiled=True)
        proj_grad = lax.psum(
            lax.psum_scatter(proj_grads[0], "dp", scatter_dimension=0, tiled=True), "seq"
        )
        all_vec = lax.psum(done[3], ("dp", "seq"))[:, :3].reshape(-1)
        vec_grad = lax.dynamic_slice_in_dim(all_vec, home * vectors.shape[0], vectors.shape[0])
        joined = lax.all_gather(shard_first, "seq", axis=0, tiled=False)
        qkv_grad = jnp.concatenate(
            [joined[j, :, i * CH : i * CH + QUARTER] for i in range(3) for j in range(SEQ)], axis=1
        )
        in_all = lax.all_gather(shard_in, "seq", axis=0, tiled=False)
        in_grad = in_all.reshape(SEQ, rows, dp_parts, units).transpose(1, 2, 0, 3).reshape(rows, -1)
        out_grad = lax.all_gather(shard_out, "seq", axis=0, tiled=True)
        total = sum(jnp.sum(g * g) for g in (qkv_grad, proj_grad, in_grad, out_grad, vec_grad))
        clip_norm = jnp.sqrt(lax.psum(total, "dp"))

    factor = clip_limit / jnp.maximum(clip_norm, clip_limit)
    new = []
    for weight, one, two, grad, rate, decay in (
        (vectors, vec_first, vec_second, vec_grad, vector_rate, 0.0),
        (w_qkv, qkv_first, qkv_second, qkv_grad, matrix_rate, weight_decay),
        (w_proj, proj_first, proj_second, proj_grad, matrix_rate, weight_decay),
        (w_in, in_first, in_second, in_grad, matrix_rate, weight_decay),
        (w_out, out_first, out_second, out_grad, matrix_rate, weight_decay),
    ):
        new.extend(adamw_update(weight, one, two, factor * grad, rate, decay))
    return (output.reshape(tokens.shape), input_grad.reshape(tokens.shape), clip_norm, *new)


def solution(mesh):
    row = P("dp", "seq", None)
    mark = P("dp", "seq")
    vec = P("dp")
    mat = P("dp", None)
    return jax.shard_map(
        local,
        mesh=mesh,
        in_specs=(row, row, mark, mark) + (vec,) * 3 + (mat,) * 12,
        out_specs=(row, row, P()) + (vec,) * 3 + (mat,) * 12,
        check_vma=False,
    )
```

```python
import functools

import jax
import jax.numpy as jnp
from jax import lax
from jax.experimental import pallas as pl
from jax.experimental.pallas import tpu as pltpu
from jax.sharding import PartitionSpec as P

D = 768
HEADS = 12
HEAD = 64
STEP = 10
CH = 256
LEN = 1024
SEQ = 4
QUARTER = D // SEQ
OWN = HEADS // SEQ
GROUPS = 8
ROWS = D // GROUPS
SUB = ROWS // SEQ
HALF = GROUPS // 2
CUT = ROWS // 2
HALF_VEC = D // 2
VEC_ROWS = 24

f32 = jnp.float32
bf16 = jnp.bfloat16
masked_score = -1e30
norm_eps = 1e-05
clip_limit = 1.0
beta_one = 0.9
beta_two = 0.999
adam_eps = 1e-08
matrix_rate = 0.02
vector_rate = 0.4
weight_decay = 0.01
gelu_scale = 0.7978845608028654
gelu_cubic = 0.044715

WHOLE = pl.BlockSpec(memory_space=pltpu.VMEM)
SCALARS = pl.BlockSpec(memory_space=pltpu.SMEM)
NN = ((1,), (0,))
NT = ((1,), (1,))
TN = ((0,), (0,))


def shape(*dims, kind=f32):
    return jax.ShapeDtypeStruct(dims, kind)


def run(kernel, scal, args, outs, scratch=(), work=0, name=None, after=()):
    moved = sum(a.size * a.dtype.itemsize for a in args) + sum(
        o.size * o.dtype.itemsize for o in outs
    )
    args, after = list(args), list(after)

    def body(scal_ref, *refs):
        kernel(scal_ref, *refs[: len(args)], *refs[len(args) + len(after) :])

    return pl.pallas_call(
        body,
        out_shape=tuple(outs),
        in_specs=[SCALARS] + [WHOLE] * len(args) + [pl.BlockSpec(memory_space=pl.ANY)] * len(after),
        out_specs=tuple([WHOLE] * len(outs)),
        scratch_shapes=list(scratch),
        compiler_params=pltpu.CompilerParams(vmem_limit_bytes=56 << 20),
        cost_estimate=pl.CostEstimate(flops=work, bytes_accessed=moved, transcendentals=0),
        name=name,
    )(scal, *args, *after)


def halves(value):
    top = value.astype(bf16)
    return top, (value - top.astype(f32)).astype(bf16)


def dot(left, right, dims):
    return lax.dot_general(left, right, (dims, ((), ())), preferred_element_type=f32)


def dot3(lh, ll, rh, rl, dims):
    return dot(lh, rh, dims) + (dot(lh, rl, dims) + dot(ll, rh, dims))


def rows_at(index, size):
    return pl.ds(pl.multiple_of(index * size, size), size)


def piece(vec, number):
    a, b = 2 * number, 2 * number + 1
    return jnp.concatenate(
        [vec[a // 3, a % 3 : a % 3 + 1, :], vec[b // 3, b % 3 : b % 3 + 1, :]], axis=1
    )


def norm_stats(inputs):
    center = inputs - jnp.mean(inputs, axis=-1, keepdims=True)
    spread = jnp.mean(center * center, axis=-1, keepdims=True)
    scale = lax.rsqrt(spread + norm_eps)
    return center * scale, scale


def norm_back(hat, scale, gain, grad):
    inner = grad * gain
    return scale * (
        inner
        - jnp.mean(inner, axis=-1, keepdims=True)
        - hat * jnp.mean(inner * hat, axis=-1, keepdims=True)
    )


def low_lanes(dims):
    return lax.broadcasted_iota(jnp.int32, dims, 1) < HEAD


def lane_pairs(pair, last):
    low = low_lanes(pair.shape)
    roll = lambda v: pltpu.roll(v, HEAD, 1)
    ph = pair.astype(bf16).astype(f32)
    pl_ = pair - ph
    lh = last.astype(bf16).astype(f32)
    ll = last - lh
    return [
        jnp.where(low, ph, roll(pl_)).astype(bf16),
        jnp.where(low, roll(ph), pl_).astype(bf16),
        jnp.where(low, lh, roll(ll)).astype(bf16),
    ]


def row_halves(turned, head):
    part = turned[HEAD * head : HEAD * (head + 1)]
    return halves(part)


def pack_first_kernel(scal, wqkv, wproj, vec, seg, valid, tokens, first, packed):
    mine = scal[0]
    proj = wproj[pl.ds(pl.multiple_of(mine * SUB, 8), SUB), :]
    turn = lax.rem(D - mine * QUARTER, D)
    for part in range(3):
        turned = pltpu.roll(wqkv[:, part * D : (part + 1) * D], turn, 1)
        first[:ROWS, part * CH : part * CH + QUARTER] = turned[:, :QUARTER]
        for group in range(SEQ):
            lane = HEAD * (3 * group + part)
            first[group * SUB : (group + 1) * SUB, part * CH + QUARTER : (part + 1) * CH] = proj[
                :, lane : lane + HEAD
            ]
    first[ROWS:, :] = jnp.zeros((8, D), f32)
    first[ROWS : ROWS + 3, :HALF_VEC] = vec[...]
    packed[:CH, :] = tokens[...]
    packed[CH:, :] = jnp.zeros((8, D), f32)
    packed[CH : CH + 1, :CH] = jnp.where(valid[...] > 0, seg[...], -1).astype(f32)


def pack_second_kernel(scal, win, wout, second):
    mine = scal[0]
    turn = lax.rem(HALF_VEC - mine * ROWS, HALF_VEC)
    for part in range(GROUPS):
        turned = pltpu.roll(win[:, part * HALF_VEC : (part + 1) * HALF_VEC], turn, 1)
        second[:ROWS, part * ROWS : (part + 1) * ROWS] = turned[:, :ROWS]
    second[ROWS:, :] = wout[pl.ds(pl.multiple_of(mine * ROWS, 8), ROWS), :]


def mask_kernel(scal, cotangent, valid, result):
    keep = jnp.where(valid[...] > 0, 1.0, 0.0).astype(f32)
    column = jnp.broadcast_to(keep, (128, CH)).T[:, :1]
    result[...] = cotangent[...] * column


def weights_kernel(scal, *refs):
    blocks, (wh, wl, vec, proj) = refs[: GROUPS + 1], refs[GROUPS + 1 :]
    spans = [(k, 0, ROWS + 8) for k in range(GROUPS)]
    spans[HALF : HALF + 1] = [(HALF, 0, CUT), (HALF, CUT, ROWS + 8)]
    for ref, (k, first, last) in zip(blocks, spans):
        at = scal[1 + k]
        size = min(last, ROWS) - first
        block = ref[:size, :]
        here = pl.ds(pl.multiple_of(at * ROWS + first, 16), size)
        wh[here, :], wl[here, :] = halves(block)
        if last > ROWS:
            vec[at] = ref[size:, :HALF_VEC]
        for group in range(SEQ):
            top, end = group * SUB, (group + 1) * SUB
            if top < first or end > first + size:
                continue
            for part in range(3):
                lane = HEAD * (3 * group + part)
                proj[pl.ds(pl.multiple_of(at * SUB, 8), SUB), lane : lane + HEAD] = block[
                    top - first : end - first, part * CH + QUARTER : (part + 1) * CH
                ]


def front_kernel(scal, *refs):
    toks, refs = refs[:4], refs[4:]
    wh, wl, vec = refs[:3]
    (xh, xl, kcat, qturn, vcat, qpair, kturn, outs_turn, lse, low_row) = refs[3:13]
    vturn, label = refs[13:]
    mine = scal[0]

    gain, shift = piece(vec, 0), piece(vec, 1)
    turn = lax.rem(D - mine * QUARTER, D)
    own = lambda number: pltpu.roll(jnp.broadcast_to(piece(vec, number), (8, D)), turn, 1)[:1, :CH]
    query_bias, value_bias = own(2), own(3)

    for r in range(SEQ):
        nat = jnp.bitwise_xor(mine, r)
        at = rows_at(nat, CH)
        label[nat] = toks[r][CH:, :CH]
        hat, _ = norm_stats(toks[r][:CH, :])
        xh[at, :], xl[at, :] = halves(hat)
        nh, nl = halves(hat * gain + shift)
        joined = dot3(nh, nl, wh[...], wl[...], NN)
        query = (joined[:, :CH] + query_bias) * HEAD ** (-0.5)
        key = joined[:, CH : 2 * CH]
        value = joined[:, 2 * CH :] + value_bias
        keys = lane_pairs(key[:, :128], key[:, 128:])
        values = lane_pairs(value[:, :128], value[:, 128:])
        queries = lane_pairs(query[:, :128], query[:, 128:])
        key_t, value_t, query_t = key.T, value.T, query.T
        for h in range(OWN):
            kcat[h, at, :] = jnp.concatenate([keys[h], keys[h]], axis=1)
            vcat[h, at, :] = jnp.concatenate([values[h], values[h]], axis=1)
            qpair[h, at, :] = queries[h]
            a, b = row_halves(query_t, h)
            qturn[h, :, at] = jnp.concatenate([a, a, b, b], axis=0)
            a, b = row_halves(key_t, h)
            kturn[h, :, at] = jnp.concatenate([a, b], axis=0)
            a, b = row_halves(value_t, h)
            vturn[h, :, at] = jnp.concatenate([a, b], axis=0)

    labels = jnp.concatenate([label[c][:1, :] for c in range(SEQ)], axis=1)
    spot = lax.broadcasted_iota(jnp.int32, (1, LEN), 1).astype(f32)
    begin = jnp.zeros((1, LEN), f32)
    for segment in range(3):
        held = jnp.sum(jnp.where(labels == float(segment), 1.0, 0.0), axis=1, keepdims=True)
        begin = begin + jnp.where(labels > float(segment), held, 0.0)
    begin = jnp.where(labels < 0.0, spot, begin)
    low_row[...] = jnp.broadcast_to(begin, (8, LEN))

    def one_head(h, carry):
        for c in range(SEQ):
            size = CH * (c + 1)
            lanes = slice(c * CH, (c + 1) * CH)
            score = dot(kcat[h, :size, :], qturn[h, :, lanes], NN)
            mask = allowed(low_row, c, size)
            score = jnp.where(mask, score, masked_score)
            peak = jnp.max(score, axis=0, keepdims=True)
            weight = jnp.exp(score - peak)
            total = jnp.sum(weight, axis=0, keepdims=True)
            top, rest = halves(weight)
            both = dot(vturn[h, :, :size], top, NN)
            extra = dot(vturn[h, :HEAD, :size], rest, NN)
            result = (both[:HEAD] + both[HEAD:] + extra) / total
            outs_turn[pl.ds(pl.multiple_of(h * HEAD, HEAD), HEAD), lanes] = result
            lse[h, :, lanes] = jnp.broadcast_to(peak + jnp.log(total), (8, CH))
        return carry

    lax.fori_loop(0, OWN, one_head, 0)


def allowed(low_row, c, size):
    key_at = lax.broadcasted_iota(jnp.int32, (size, CH), 0).astype(f32)
    query_at = (lax.broadcasted_iota(jnp.int32, (1, CH), 1) + c * CH).astype(f32)
    begin = low_row[:1, c * CH : (c + 1) * CH]
    return (key_at >= begin) & (key_at <= query_at)


def proj_kernel(scal, *refs):
    toks, heads, parts, refs = refs[:4], refs[4:8], refs[8:12], refs[12:]
    vec, wh, wl, heads_h, heads_l, norm_h, norm_l, mixed, hat, scale, weight = refs
    mine = scal[0]
    for r in range(SEQ):
        at = jnp.bitwise_xor(mine, r)
        for d in range(GROUPS):
            weight[pl.ds(pl.multiple_of(d * ROWS + at * SUB, 8), SUB), :] = parts[r][
                d * SUB : (d + 1) * SUB, :
            ]
        here = rows_at(at, QUARTER)
        heads_h[here, :], heads_l[here, :] = halves(heads[r][...])
    wh[...], wl[...] = halves(weight[...])
    gain, shift = piece(vec, 5), piece(vec, 6)
    for r in range(SEQ):
        at = rows_at(jnp.bitwise_xor(mine, r), CH)
        total = toks[r][:CH, :] + dot3(heads_h[:, at], heads_l[:, at], wh[...], wl[...], TN)
        total = total + piece(vec, 4)
        normed, size = norm_stats(total)
        norm_h[r], norm_l[r] = halves(normed * gain + shift)
        if r == 0:
            mixed[...] = total
            hat[...] = normed
            scale[...] = jnp.broadcast_to(size, (CH, 128))


def ffn_kernel(scal, norm_h, norm_l, *refs):
    grads, blocks, refs = refs[:4], refs[4 : 5 + GROUPS], refs[5 + GROUPS :]
    vec = refs[0]
    acts_h, acts_l, hid_h, hid_l, out_h, out_l, wouth, woutl, bias_sum = refs[1:10]
    parts, (winh, winl) = refs[10:14], refs[14:]
    mine = scal[0]
    for k in range(GROUPS):
        at = rows_at(scal[1 + k], ROWS)
        if k == HALF:
            first, second = blocks[k][...], blocks[GROUPS][...]
        else:
            first, second = blocks[k][:ROWS, :], blocks[k][ROWS:, :]
        winh[at, :], winl[at, :] = halves(first)
        wouth[at, :], woutl[at, :] = halves(second)
    marks = [16 + d for d in range(GROUPS)]
    table = jnp.concatenate([vec[m // 3, m % 3 : m % 3 + 1, :] for m in marks], axis=0)
    table = pltpu.roll(table, lax.rem(HALF_VEC - mine * ROWS, HALF_VEC), 1)[:, :ROWS]
    bias = jnp.concatenate([table[d : d + 1] for d in range(GROUPS)], axis=1)
    sums = jnp.zeros((1, D), f32)
    for r in (1, 3, 2, 0):
        at = slice(r * CH, (r + 1) * CH)
        hidden = dot3(norm_h[r], norm_l[r], winh[...], winl[...], NN) + bias
        inner = jnp.tanh(gelu_scale * (hidden + gelu_cubic * hidden * hidden * hidden))
        acts_h[at, :], acts_l[at, :] = halves(0.5 * hidden * (1.0 + inner))
        slope = 0.5 * (1.0 + inner) + 0.5 * hidden * (1.0 - inner * inner) * gelu_scale * (
            1.0 + 3.0 * gelu_cubic * hidden * hidden
        )
        gh, gl = halves(grads[r][...])
        out_h[at, :], out_l[at, :] = gh, gl
        back = dot3(gh, gl, wouth[...], woutl[...], NT) * slope
        sums = sums + jnp.sum(back, axis=0, keepdims=True)
        bh, bl = halves(back)
        hid_h[at, :], hid_l[at, :] = bh, bl
        parts[r][...] = dot3(bh, bl, winh[...], winl[...], NT)
    bias_sum[...] = jnp.broadcast_to(sums, (8, D))


def ffn_grad_kernel(scal, norm_h, norm_l, hid_h, hid_l, acts_h, acts_l, out_h, out_l, *refs):
    outs, whole = refs[:-1], refs[-1]

    def emit(first):
        for k in range(GROUPS):
            at = rows_at(scal[1 + k], ROWS)
            if k == HALF:
                outs[HALF if first else GROUPS][...] = whole[at, :]
            elif first:
                outs[k][:ROWS, :] = whole[at, :]
            else:
                outs[k][ROWS:, :] = whole[at, :]

    flat = lambda ref: ref[...].reshape(LEN, D)
    whole[...] = dot3(flat(norm_h), flat(norm_l), hid_h[...], hid_l[...], TN)
    emit(True)
    whole[...] = dot3(acts_h[...], acts_l[...], out_h[...], out_l[...], TN)
    emit(False)


def ffn_out_kernel(scal, acts_h, acts_l, wouth, woutl, *parts):
    for r in (1, 3, 2, 0):
        at = slice(r * CH, (r + 1) * CH)
        parts[r][...] = dot3(acts_h[at, :], acts_l[at, :], wouth[...], woutl[...], NN)


def add_kernel(scal, one, two, result):
    result[...] = one[...] + two[...]


def ring_add_kernel(top, scal, forth, back, ahead, behind, forth_out, back_out):
    if forth.shape == forth_out.shape:
        forth_out[...] = forth[...] + ahead[...]
        back_out[...] = back[...] + behind[...]
        return
    forth_out[:top, :] = forth[...] + ahead[:top, :]
    forth_out[top:, :] = ahead[top:, :]
    back_out[:top, :] = behind[:top, :]
    back_out[top:, :] = back[...] + behind[top:, :]


def sum_kernel(scal, one, two, three, result):
    result[...] = one[...] + two[...] + three[...]


def output_kernel(scal, mixed, one, two, three, vec, output):
    output[...] = mixed[...] + (one[...] + two[...] + three[...]) + piece(vec, 7)


def proj_back_kernel(scal, one, two, three, hat, scale, vec, grad_out, wh, wl, mixed_grad, sums, *parts):
    mine = scal[0]
    normed = one[...] + two[...] + three[...]
    back = norm_back(hat[...], scale[:, :1], piece(vec, 5), normed)
    total = grad_out[...] + back
    mixed_grad[...] = total
    a, b = halves(total)
    for r in range(SEQ):
        at = rows_at(jnp.bitwise_xor(mine, r), QUARTER)
        parts[r][...] = dot3(wh[at, :], wl[at, :], a, b, NT)
    add = lambda v: jnp.sum(v, axis=0, keepdims=True)
    sums[...] = jnp.concatenate(
        [add(total), add(normed * hat[...]), add(normed), add(grad_out[...]), jnp.zeros((4, D), f32)],
        axis=0,
    )


def proj_grad_kernel(scal, heads_h, heads_l, mixed_grad, *refs):
    outs, whole = refs[:-1], refs[-1]
    mine = scal[0]
    gh, gl = halves(mixed_grad[...])
    own = rows_at(mine, CH)
    whole[...] = dot3(heads_h[:, own], heads_l[:, own], gh, gl, NN)
    for r in range(SEQ):
        at = jnp.bitwise_xor(mine, r)
        for d in range(GROUPS):
            outs[r][d * SUB : (d + 1) * SUB, :] = whole[
                pl.ds(pl.multiple_of(d * ROWS + at * SUB, 8), SUB), :
            ]


def back_kernel(scal, *refs):
    grads, refs = refs[:4], refs[4:]
    kcat, qturn, vcat, qpair, kturn, outs_turn, lse, low_row = refs[:8]
    joined_h, joined_l, joined_sums = refs[8:11]
    gturn, gpair, dots, key_sum, value_sum, query_turn = refs[11:]
    mine = scal[0]

    for r in range(SEQ):
        at = rows_at(jnp.bitwise_xor(mine, r), CH)
        turned = grads[r][...]
        grad = jnp.concatenate([turned, jnp.zeros((HEAD, CH), f32)], axis=0).T
        pairs = lane_pairs(grad[:, :128], grad[:, 128:])
        for h in range(OWN):
            gpair[h, at, :] = pairs[h]
            part = turned[HEAD * h : HEAD * (h + 1)]
            dots[h, :, at] = jnp.broadcast_to(
                jnp.sum(part * outs_turn[HEAD * h : HEAD * (h + 1), at], axis=0, keepdims=True), (8, CH)
            )
            a, b = halves(part)
            gturn[h, :, at] = jnp.concatenate([a, a, b, b], axis=0)

    key_sum[...] = jnp.zeros_like(key_sum)
    value_sum[...] = jnp.zeros_like(value_sum)

    def one_head(h, carry):
        for c in range(SEQ):
            size = CH * (c + 1)
            lanes = slice(c * CH, (c + 1) * CH)
            score = dot(kcat[h, :size, :], qturn[h, :, lanes], NN)
            weight = jnp.where(allowed(low_row, c, size), jnp.exp(score - lse[h, :1, lanes]), 0.0)
            back = dot(vcat[h, :size, :], gturn[h, :, lanes], NN)
            score_back = weight * (back - dots[h, :1, lanes])
            a, b = halves(weight)
            pair = gpair[h, lanes, :]
            value_sum[h, :size, :] += dot(a, pair, NN) + dot(b, pair, NN)
            a, b = halves(score_back)
            pair = qpair[h, lanes, :]
            key_sum[h, :size, :] += dot(a, pair, NN) + dot(b, pair, NN)
            turned = dot(kturn[h, :, :size], a, NN) + dot(kturn[h, :, :size], b, NN)
            query_turn[h, :, lanes] = (turned[:HEAD] + turned[HEAD:]) * HEAD ** (-0.5)
        return carry

    lax.fori_loop(0, OWN, one_head, 0)

    column_sums = jnp.zeros((1, D), f32)
    low = low_lanes((CH, 128))
    for c in range(SEQ):
        at = slice(c * CH, (c + 1) * CH)
        blank = jnp.zeros((HEAD, CH), f32)
        query = jnp.concatenate([query_turn[h, :, at] for h in range(OWN)] + [blank], axis=0).T
        done = [query]
        for kept in (key_sum, value_sum):
            full = [kept[h, at, :] for h in range(OWN)]
            full = [v + pltpu.roll(v, HEAD, 1) for v in full]
            done.append(jnp.where(low, full[0], full[1]))
            done.append(jnp.where(low, full[2], 0.0))
        joined = jnp.concatenate(done, axis=1)
        column_sums = column_sums + jnp.sum(joined, axis=0, keepdims=True)
        joined_h[at, :], joined_l[at, :] = halves(joined)

    joined_sums[...] = jnp.broadcast_to(column_sums, (8, D))


def qkv_grad_kernel(scal, xh, xl, joined_h, joined_l, joined_sums, wh, wl, vec, *refs):
    proj_one, proj_two, proj_three, sums, bias_sum = refs[:5]
    outs, (whole, rows) = refs[5 : 6 + GROUPS], refs[6 + GROUPS :]
    mine = scal[0]
    column_sums = joined_sums[:1, :]
    core = dot3(xh[...], xl[...], joined_h[...], joined_l[...], TN)
    gain, shift = piece(vec, 0), piece(vec, 1)
    as_column = lambda v: jnp.broadcast_to(v, (128, D)).T[:, :1]
    whole[...] = as_column(gain) * core + as_column(shift) * column_sums
    weights = wh[...].astype(f32) + wl[...].astype(f32)
    gain_grad = jnp.sum(weights * core, axis=1, keepdims=True)
    shift_grad = jnp.sum(weights * column_sums, axis=1, keepdims=True)
    lane = lax.broadcasted_iota(jnp.int32, (D, 128), 1)
    norm_grads = jnp.where(lane == 0, gain_grad, shift_grad).T

    def place(part, scale):
        wide = jnp.concatenate([part[:, :QUARTER], jnp.zeros((1, D - QUARTER), f32)], axis=1)
        wide = jnp.broadcast_to(wide, (8, D))
        return pltpu.roll(wide, mine * QUARTER, 1)[:1]

    entries = [
        norm_grads[0:1],
        norm_grads[1:2],
        place(column_sums[:, :CH], 1.0),
        place(column_sums[:, 2 * CH :], 1.0),
        sums[0:1],
        sums[1:2],
        sums[2:3],
        sums[3:4],
    ]
    lines = [e[:, i * HALF_VEC : (i + 1) * HALF_VEC] for e in entries for i in range(2)]
    bias = jnp.concatenate(
        [bias_sum[:1, d * ROWS : (d + 1) * ROWS] for d in range(GROUPS)], axis=0
    )
    bias = jnp.concatenate([bias, jnp.zeros((GROUPS, HALF_VEC - ROWS), f32)], axis=1)
    bias = pltpu.roll(bias, mine * ROWS, 1)
    lines = lines + [bias[d : d + 1] for d in range(GROUPS)]
    filler = jnp.zeros((5, HALF_VEC), f32)
    for d in range(GROUPS):
        rows[d] = jnp.concatenate(lines[3 * d : 3 * d + 3] + [filler], axis=0)

    spans = [(k, 0, ROWS + 8) for k in range(GROUPS)]
    spans[HALF : HALF + 1] = [(HALF, 0, CUT), (HALF, CUT, ROWS + 8)]
    for ref, (k, first, last) in zip(outs, spans):
        at = scal[1 + k]
        size = min(last, ROWS) - first
        ref[:size, :] = whole[pl.ds(pl.multiple_of(at * ROWS + first, 8), size), :]
        here = pl.ds(pl.multiple_of(at * SUB, 8), SUB)
        proj = proj_one[here, :] + proj_two[here, :] + proj_three[here, :]
        for group in range(SEQ):
            top, end = group * SUB - first, (group + 1) * SUB - first
            if top < 0 or end > size:
                continue
            for part in range(3):
                lane_at = HEAD * (3 * group + part)
                ref[top:end, part * CH + QUARTER : (part + 1) * CH] = proj[:, lane_at : lane_at + HEAD]
        if last > ROWS:
            ref[size:, :HALF_VEC] = rows[at]
            ref[size:, HALF_VEC:] = jnp.zeros((8, HALF_VEC), f32)


def pre_back_kernel(scal, joined_h, joined_l, wh, wl, *parts):
    mine = scal[0]
    for r in (1, 3, 2, 0):
        at = rows_at(jnp.bitwise_xor(mine, r), CH)
        parts[r][...] = dot3(joined_h[at, :], joined_l[at, :], wh[...], wl[...], NT)


def input_grad_kernel(scal, tokens, one, two, three, vec, mixed_grad, result):
    hat, scale = norm_stats(tokens[...])
    grad = one[...] + two[...] + three[...]
    result[...] = mixed_grad[...] + norm_back(hat, scale, piece(vec, 0), grad)


def total_square(value):
    return jnp.sum(jnp.sum(value * value, axis=0, keepdims=True), axis=1, keepdims=True)


def shard_second_kernel(scal, *refs):
    seconds, (win, wout, squares, second) = refs[:4], refs[4:]
    mine = scal[0]
    total = jnp.zeros((1, 1), f32)
    for r in range(SEQ):
        part = seconds[r][...]
        total = total + total_square(part)
        second[jnp.bitwise_xor(mine, r)] = part
    for j in range(SEQ):
        wout[j * ROWS : (j + 1) * ROWS, :] = second[j][ROWS:, :]
    for d in range(GROUPS):
        win[:, d * HALF_VEC : (d + 1) * HALF_VEC] = jnp.concatenate(
            [second[j][:ROWS, d * ROWS : (d + 1) * ROWS] for j in range(SEQ)], axis=1
        )
    squares[...] = jnp.broadcast_to(total, (8, 128))


def shard_first_kernel(scal, *refs):
    firsts, (before, qkv, proj, vec, squares, first) = refs[:4], refs[4:]
    mine = scal[0]
    total = jnp.zeros((1, 1), f32)
    for r in range(SEQ):
        part = firsts[r][:ROWS, :]
        total = total + total_square(part)
        first[jnp.bitwise_xor(mine, r)] = part
    line = sum(firsts[r][ROWS:, :HALF_VEC] for r in range(SEQ))
    vec[...] = line
    squares[...] = before[...] + total + total_square(line)
    for part in range(3):
        qkv[:, part * D : (part + 1) * D] = jnp.concatenate(
            [first[j][:, part * CH : part * CH + QUARTER] for j in range(SEQ)], axis=1
        )
    for j in range(SEQ):
        for group in range(SEQ):
            for part in range(3):
                lane = HEAD * (3 * group + part)
                proj[j * SUB : (j + 1) * SUB, lane : lane + HEAD] = first[j][
                    group * SUB : (group + 1) * SUB, part * CH + QUARTER : (part + 1) * CH
                ]


def adamw_update(weight, first, second, grad, rate, decay):
    new_first = beta_one * first + (1.0 - beta_one) * grad
    new_second = beta_two * second + (1.0 - beta_two) * grad * grad
    first_hat = new_first / (1.0 - beta_one**STEP)
    second_hat = new_second / (1.0 - beta_two**STEP)
    new_weight = weight - rate * (first_hat / (jnp.sqrt(second_hat) + adam_eps) + decay * weight)
    return (new_first, new_second, new_weight)


def ring_tables(count):
    evens = [2 * i for i in range(count // 2)]
    order = evens + [i + 1 for i in reversed(evens)]
    place = [0] * count
    for position, device in enumerate(order):
        place[device] = position
    right = [(order[i], order[(i + 1) % count]) for i in range(count)]
    left = [(b, a) for a, b in right]
    return order, place, right, left


def ring_gather(block, cut):
    _, _, right, left = ring_tables(GROUPS)
    got = {0: block}
    forth = back = block
    for step in range(1, HALF):
        forth = got[GROUPS - step] = lax.ppermute(forth, "dp", right)
        back = got[step] = lax.ppermute(back, "dp", left)
    top = lax.ppermute(forth[:cut], "dp", right)
    rest = lax.ppermute(back[cut:], "dp", left)
    return [got[k] if k != HALF else top for k in range(GROUPS)], rest


def ring_scatter(scal, blocks, top, rest, name):
    _, _, right, left = ring_tables(GROUPS)
    cut = top.shape[0]
    forth = lax.ppermute(top, "dp", right)
    back = lax.ppermute(rest, "dp", left)
    for step in range(HALF - 1, 0, -1):
        like = shape(*blocks[step].shape)
        forth, back = run(
            functools.partial(ring_add_kernel, cut),
            scal,
            [forth, back, blocks[step], blocks[GROUPS - step]],
            [like, like],
            name=name,
        )
        forth = lax.ppermute(forth, "dp", right)
        back = lax.ppermute(back, "dp", left)
    (own,) = run(sum_kernel, scal, [forth, back, blocks[0]], [shape(*blocks[0].shape)], name=name)
    return own


def swap(block, bits):
    return lax.ppermute(block, "seq", [(i, i ^ bits) for i in range(SEQ)])


def gather_seq(block):
    across = swap(block, 2)
    core = swap(block, 1)
    return [block, core, across, swap(across, 1)]


def exchange_seq(parts):
    return [parts[0]] + [swap(parts[r], r) for r in range(1, SEQ)]


def scatter_core(parts):
    return parts[0], swap(parts[1], 1), parts[2], swap(parts[3], 1)


def ordered(blocks, mine):
    stack = jnp.stack(blocks, axis=0)
    return [lax.dynamic_index_in_dim(stack, mine ^ j, 0, keepdims=False) for j in range(len(blocks))]


def local(
    tokens,
    cotangent,
    segment_ids,
    valid,
    vectors,
    vec_first,
    vec_second,
    w_qkv,
    qkv_first,
    qkv_second,
    w_proj,
    proj_first,
    proj_second,
    w_in,
    in_first,
    in_second,
    w_out,
    out_first,
    out_second,
):
    dp_parts = lax.axis_size("dp")
    ring = dp_parts == GROUPS
    mine = lax.axis_index("seq")
    home = lax.axis_index("dp")
    rows = w_qkv.shape[0]
    units = w_out.shape[0] // SEQ
    if ring:
        order, place, _, _ = ring_tables(GROUPS)
        position = jnp.array(place, jnp.int32)[home]
        table = jnp.array(order + order, jnp.int32)
        table = lax.dynamic_slice_in_dim(table, position, GROUPS)
    else:
        table = jnp.arange(GROUPS, dtype=jnp.int32)
    scal = jnp.concatenate([mine[None].astype(jnp.int32), table])
    flat_in = tokens.reshape(CH, D)
    chunk, tall, square = shape(CH, D), shape(LEN, D, kind=bf16), shape(D, D, kind=bf16)

    def add(one, two, after=()):
        (total,) = run(add_kernel, scal, [one, two], [shape(*one.shape)], name="add", after=after)
        return total

    if ring:
        first, packed = run(
            pack_first_kernel,
            scal,
            [w_qkv, w_proj, vectors.reshape(3, HALF_VEC), segment_ids, valid, flat_in],
            [shape(ROWS + 8, D), shape(CH + 8, D)],
            name="pack_first",
        )
        firsts, first_rest = ring_gather(first, CUT)
        (second,) = run(
            pack_second_kernel,
            scal,
            [w_in, w_out],
            [shape(2 * ROWS, D)],
            name="pack_second",
            after=[firsts[HALF + 1]],
        )
        seconds, second_rest = ring_gather(second, ROWS)
    else:
        padded = jnp.pad(w_qkv, ((0, 0), (0, CH)))
        own = lambda part: lax.dynamic_slice_in_dim(padded, part * D + mine * QUARTER, CH, 1)
        first = jnp.concatenate([own(0), own(1), own(2)], axis=1)
        first = lax.all_gather(first, "dp", axis=0, tiled=True).reshape(GROUPS, ROWS, D)
        all_vec = lax.all_gather(vectors, "dp", axis=0, tiled=True).reshape(GROUPS, 3, HALF_VEC)
        first = jnp.concatenate([first, jnp.pad(all_vec, ((0, 0), (0, 5), (0, D - HALF_VEC)))], axis=1)
        firsts = [first[k] for k in range(GROUPS)]
        firsts[HALF], first_rest = first[HALF, :CUT], first[HALF, CUT:]
        in_part = lax.dynamic_index_in_dim(
            w_in.reshape(rows, dp_parts, SEQ, units), mine, 2, keepdims=False
        ).reshape(rows, D)
        out_part = lax.dynamic_slice_in_dim(w_out, mine * units, units, 0)
        second = jnp.concatenate(
            [
                lax.all_gather(part, "dp", axis=0, tiled=True).reshape(GROUPS, ROWS, D)
                for part in (in_part, out_part)
            ],
            axis=1,
        )
        seconds = [second[k] for k in range(GROUPS)]
        seconds[HALF], second_rest = second[HALF, :ROWS], second[HALF, ROWS:]
        marks = jnp.where(valid > 0, segment_ids, -1).astype(f32)
        packed = jnp.concatenate([flat_in, jnp.pad(marks, ((0, 7), (0, D - CH)))], axis=0)
    toks = gather_seq(packed)
    (grad_out,) = run(
        mask_kernel, scal, [cotangent.reshape(CH, D), valid], [chunk], name="mask", after=[toks[2]]
    )
    grads_row = gather_seq(grad_out)

    qkv_h, qkv_l, vec, proj = run(
        weights_kernel,
        scal,
        firsts[: HALF + 1] + [first_rest] + firsts[HALF + 1 :],
        [square, square, shape(GROUPS, 8, HALF_VEC), shape(GROUPS * SUB, D)],
        name="weights",
    )
    if ring:
        proj_parts = gather_seq(proj)
    else:
        full = lax.all_gather(w_proj, "dp", axis=0, tiled=True).reshape(GROUPS, SEQ, SUB, D)
        proj_parts = [
            lax.dynamic_index_in_dim(full, mine ^ r, 1, keepdims=False).reshape(GROUPS * SUB, D)
            for r in range(SEQ)
        ]
    hat_h, hat_l, kcat, qturn, vcat, qpair, kturn, heads, lse, low_row = run(
        front_kernel,
        scal,
        toks + [qkv_h, qkv_l, vec],
        [
            tall,
            tall,
            shape(OWN, LEN, 256, kind=bf16),
            shape(OWN, 256, LEN, kind=bf16),
            shape(OWN, LEN, 256, kind=bf16),
            shape(OWN, LEN, 128, kind=bf16),
            shape(OWN, 128, LEN, kind=bf16),
            shape(QUARTER, LEN),
            shape(OWN, 8, LEN),
            shape(8, LEN),
        ],
        scratch=[pltpu.VMEM((OWN, 128, LEN), bf16), pltpu.VMEM((SEQ, 8, CH), f32)],
        work=10_000_000_000,
        name="front",
    )
    wide = shape(D, LEN, kind=bf16)
    split = shape(SEQ, CH, D, kind=bf16)
    proj_h, proj_l, heads_h, heads_l, norm_h, norm_l, mixed, hat_two, scale_two = run(
        proj_kernel,
        scal,
        toks + gather_seq(heads) + proj_parts + [vec],
        [square, square, wide, wide, split, split, chunk, chunk, shape(CH, 128)],
        scratch=[pltpu.VMEM((D, D), f32)],
        work=3_600_000_000,
        name="proj",
    )

    done = run(
        ffn_kernel,
        scal,
        [norm_h, norm_l] + grads_row + seconds + [second_rest, vec],
        [tall] * 6 + [square] * 2 + [shape(8, D)] + [chunk] * SEQ,
        scratch=[pltpu.VMEM((D, D), bf16)] * 2,
        work=11_000_000_000,
        name="ffn",
    )
    acts_h, acts_l, hid_h, hid_l, out_h, out_l, out_wh, out_wl, bias_sum = done[:9]
    norm_own, norm_near, norm_across, norm_far = scatter_core(done[9:])
    norm_pair = add(norm_across, norm_far)
    norm_last = swap(norm_pair, 2)
    done = run(
        ffn_grad_kernel,
        scal,
        [norm_h, norm_l, hid_h, hid_l, acts_h, acts_l, out_h, out_l],
        [shape(2 * ROWS, D) if k != HALF else shape(ROWS, D) for k in range(GROUPS)] + [shape(ROWS, D)],
        scratch=[pltpu.VMEM((D, D), f32)],
        work=7_000_000_000,
        name="ffn_grad",
        after=[norm_pair],
    )
    second_grads, second_grad_rest = list(done[:-1]), done[-1]
    if ring:
        shard_second = ring_scatter(
            scal, second_grads, second_grads[HALF], second_grad_rest, "ring_second"
        )
    out_parts = run(
        ffn_out_kernel,
        scal,
        [acts_h, acts_l, out_wh, out_wl],
        [chunk] * SEQ,
        work=3_600_000_000,
        name="ffn_out",
        after=[done[0]],
    )
    done = run(
        proj_back_kernel,
        scal,
        [norm_own, norm_near, norm_last, hat_two, scale_two, vec, grad_out, proj_h, proj_l],
        [chunk, shape(8, D)] + [shape(QUARTER, CH)] * SEQ,
        work=1_000_000_000,
        name="proj_back",
        after=[out_parts[0]],
    )
    mixed_grad, sums = done[:2]
    head_grads = exchange_seq(list(done[2:]))
    proj_grads = run(
        proj_grad_kernel,
        scal,
        [heads_h, heads_l, mixed_grad],
        [shape(GROUPS * SUB, D)] * SEQ,
        scratch=[pltpu.VMEM((D, D), f32)],
        work=1_000_000_000,
        name="proj_grad",
    )
    wait = [head_grads[3], head_grads[2]]
    if ring:
        proj_own, proj_near, proj_across, proj_far = scatter_core(proj_grads)
        proj_pair = add(proj_across, proj_far, after=wait)
        proj_last = swap(proj_pair, 2)
    else:
        proj_own = proj_near = proj_last = proj_pair = proj_grads[0]
    out_own, out_near, out_across, out_far = scatter_core(out_parts)
    out_pair = add(out_across, out_far, after=wait)
    out_last = swap(out_pair, 2)
    joined_h, joined_l, joined_sums = run(
        back_kernel,
        scal,
        head_grads + [kcat, qturn, vcat, qpair, kturn, heads, lse, low_row],
        [tall, tall, shape(8, D)],
        scratch=[
            pltpu.VMEM((OWN, 256, LEN), bf16),
            pltpu.VMEM((OWN, LEN, 128), bf16),
            pltpu.VMEM((OWN, 8, LEN), f32),
            pltpu.VMEM((OWN, LEN, 128), f32),
            pltpu.VMEM((OWN, LEN, 128), f32),
            pltpu.VMEM((OWN, HEAD, LEN), f32),
        ],
        work=10_000_000_000,
        name="back",
        after=[proj_pair, out_pair],
    )
    done = run(
        qkv_grad_kernel,
        scal,
        [hat_h, hat_l, joined_h, joined_l, joined_sums, qkv_h, qkv_l, vec]
        + [proj_own, proj_near, proj_last, sums, bias_sum],
        [shape(ROWS + 8, D)] * HALF
        + [shape(CUT, D), shape(ROWS + 8 - CUT, D)]
        + [shape(ROWS + 8, D)] * (HALF - 1),
        scratch=[pltpu.VMEM((D, D), f32), pltpu.VMEM((GROUPS, 8, HALF_VEC), f32)],
        work=4_000_000_000,
        name="qkv_grad",
    )
    first_grads = list(done[: HALF + 1]) + list(done[HALF + 2 :])
    first_grad_rest = done[HALF + 1]
    if ring:
        shard_first = ring_scatter(scal, first_grads, first_grads[HALF], first_grad_rest, "ring_first")
    pre_parts = run(
        pre_back_kernel,
        scal,
        [joined_h, joined_l, qkv_h, qkv_l],
        [chunk] * SEQ,
        work=3_600_000_000,
        name="pre_back",
        after=[done[0], out_last],
    )
    pre_own, pre_near, pre_across, pre_far = scatter_core(pre_parts)
    pre_last = swap(add(pre_across, pre_far), 2)
    (output,) = run(
        output_kernel, scal, [mixed, out_own, out_near, out_last, vec], [chunk], name="output"
    )
    (input_grad,) = run(
        input_grad_kernel,
        scal,
        [flat_in, pre_own, pre_near, pre_last, vec, mixed_grad],
        [chunk],
        name="input_grad",
    )

    if ring:
        in_grad, out_grad, squares = run(
            shard_second_kernel,
            scal,
            gather_seq(shard_second),
            [shape(ROWS, SEQ * D), shape(SEQ * ROWS, D), shape(8, 128)],
            scratch=[pltpu.VMEM((SEQ, 2 * ROWS, D), f32)],
            name="shard_second",
        )
        qkv_grad, proj_grad, vec_rows, squares = run(
            shard_first_kernel,
            scal,
            gather_seq(shard_first) + [squares],
            [shape(ROWS, 3 * D), shape(ROWS, D), shape(8, HALF_VEC), shape(8, 128)],
            scratch=[pltpu.VMEM((SEQ, ROWS, D), f32)],
            name="shard_first",
        )
        vec_grad = vec_rows[:3].reshape(-1)
        for bits in (1, 2, 4):
            pairs = [(i, i ^ bits) for i in range(GROUPS)]
            squares = squares + lax.ppermute(squares, "dp", pairs)
        total = squares[0, 0]
    else:
        by_group = jnp.stack(first_grads[:HALF] + [first_grads[0]] + first_grads[HALF + 1 :])
        by_group = by_group.at[HALF].set(jnp.concatenate([first_grads[HALF], first_grad_rest], axis=0))
        shard_first = lax.psum_scatter(
            by_group[:, :ROWS].reshape(D, D), "dp", scatter_dimension=0, tiled=True
        )
        proj_full = jnp.stack([p.reshape(GROUPS, SUB, D) for p in ordered(proj_grads, mine)], axis=1)
        proj_grad = lax.psum(
            lax.psum_scatter(proj_full.reshape(D, D), "dp", scatter_dimension=0, tiled=True), "seq"
        )
        all_vec = lax.psum(by_group[:, ROWS : ROWS + 3, :HALF_VEC], ("dp", "seq")).reshape(-1)
        vec_grad = lax.dynamic_slice_in_dim(all_vec, home * vectors.shape[0], vectors.shape[0])
        joined = lax.all_gather(shard_first, "seq", axis=0, tiled=False)
        qkv_grad = jnp.concatenate(
            [joined[j, :, i * CH : i * CH + QUARTER] for i in range(3) for j in range(SEQ)], axis=1
        )
        halved = jnp.concatenate([second_grads[HALF], second_grad_rest], axis=0)
        by_group = jnp.stack(second_grads[:HALF] + [halved] + second_grads[HALF + 1 :])
        shard_in, shard_out = (
            lax.psum_scatter(part.reshape(D, D), "dp", scatter_dimension=0, tiled=True)
            for part in (by_group[:, :ROWS], by_group[:, ROWS:])
        )
        in_all = lax.all_gather(shard_in, "seq", axis=0, tiled=False)
        in_grad = in_all.reshape(SEQ, rows, dp_parts, units).transpose(1, 2, 0, 3).reshape(rows, -1)
        out_grad = lax.all_gather(shard_out, "seq", axis=0, tiled=True)
        total = sum(jnp.sum(g * g) for g in (qkv_grad, proj_grad, in_grad, out_grad, vec_grad))
        total = lax.psum(total, "dp")

    clip_norm = jnp.sqrt(total)
    factor = clip_limit / jnp.maximum(clip_norm, clip_limit)
    new = []
    for weight, one, two, grad, rate, decay in (
        (vectors, vec_first, vec_second, vec_grad, vector_rate, 0.0),
        (w_qkv, qkv_first, qkv_second, qkv_grad, matrix_rate, weight_decay),
        (w_proj, proj_first, proj_second, proj_grad, matrix_rate, weight_decay),
        (w_in, in_first, in_second, in_grad, matrix_rate, weight_decay),
        (w_out, out_first, out_second, out_grad, matrix_rate, weight_decay),
    ):
        new.extend(adamw_update(weight, one, two, factor * grad, rate, decay))
    return (output.reshape(tokens.shape), input_grad.reshape(tokens.shape), clip_norm, *new)


def solution(mesh):
    row = P("dp", "seq", None)
    mark = P("dp", "seq")
    vec = P("dp")
    mat = P("dp", None)
    return jax.shard_map(
        local,
        mesh=mesh,
        in_specs=(row, row, mark, mark) + (vec,) * 3 + (mat,) * 12,
        out_specs=(row, row, P()) + (vec,) * 3 + (mat,) * 12,
        check_vma=False,
    )
```

```python
import functools
import math

import jax
import jax.numpy as jnp
from jax import lax
from jax.experimental import pallas as pl
from jax.experimental.pallas import tpu as pltpu
from jax.sharding import PartitionSpec as P

D = 768
HEADS = 12
HEAD = 64
STEP = 10
CH = 256
LEN = 1024
SEQ = 4
QUARTER = D // SEQ
OWN = HEADS // SEQ
GROUPS = 8
ROWS = D // GROUPS
SUB = ROWS // SEQ
HALF = GROUPS // 2
HALF_VEC = D // 2
VEC_ROWS = 24

f32 = jnp.float32
bf16 = jnp.bfloat16
masked_score = -1e30
norm_eps = 1e-05
clip_limit = 1.0
beta_one = 0.9
beta_two = 0.999
adam_eps = 1e-08
matrix_rate = 0.02
vector_rate = 0.4
weight_decay = 0.01
gelu_scale = 0.7978845608028654
gelu_cubic = 0.044715

WHOLE = pl.BlockSpec(memory_space=pltpu.VMEM)
SCALARS = pl.BlockSpec(memory_space=pltpu.SMEM)
NN = ((1,), (0,))
NT = ((1,), (1,))
TN = ((0,), (0,))


def shape(*dims, kind=f32):
    return jax.ShapeDtypeStruct(dims, kind)


def run(kernel, scal, args, outs, scratch=(), room=4, work=1.0, name=None, after=()):
    moved = sum(a.size * a.dtype.itemsize for a in args) + sum(
        o.size * o.dtype.itemsize for o in outs
    )
    args, after = list(args), list(after)
    held = moved + sum(math.prod(v.shape) * jnp.dtype(v.dtype).itemsize for v in scratch)

    def body(scal_ref, *refs):
        kernel(scal_ref, *refs[: len(args)], *refs[len(args) + len(after) :])

    return pl.pallas_call(
        body,
        out_shape=tuple(outs),
        in_specs=[SCALARS] + [WHOLE] * len(args) + [pl.BlockSpec(memory_space=pl.ANY)] * len(after),
        out_specs=tuple([WHOLE] * len(outs)),
        scratch_shapes=list(scratch),
        compiler_params=pltpu.CompilerParams(vmem_limit_bytes=held + (room << 20)),
        cost_estimate=pl.CostEstimate(
            flops=int(work * 1e9), bytes_accessed=1, transcendentals=0
        ),
        name=name,
    )(scal, *args, *after)


def gate(value, after):
    anywhere = pl.BlockSpec(memory_space=pl.ANY)
    return pl.pallas_call(
        lambda *refs: None,
        out_shape=shape(*value.shape, kind=value.dtype),
        in_specs=[anywhere] * (1 + len(after)),
        out_specs=anywhere,
        input_output_aliases={0: 0},
        name="gate",
    )(value, *after)


def owner(scal, k):
    spot = jnp.bitwise_and(scal[1] + k, GROUPS - 1)
    return jnp.where(scal[2] > 0, jnp.where(spot < HALF, 2 * spot, 2 * GROUPS - 1 - 2 * spot), k)


def halves(value):
    top = value.astype(bf16)
    return top, (value - top.astype(f32)).astype(bf16)


def dot(left, right, dims):
    return lax.dot_general(left, right, (dims, ((), ())), preferred_element_type=f32)


def dot3(lh, ll, rh, rl, dims):
    return dot(lh, rh, dims) + (dot(lh, rl, dims) + dot(ll, rh, dims))


def rows_at(index, size):
    return pl.ds(pl.multiple_of(index * size, size), size)


def piece(vec, number):
    a, b = 2 * number, 2 * number + 1
    return jnp.concatenate(
        [vec[a // 3, a % 3 : a % 3 + 1, :], vec[b // 3, b % 3 : b % 3 + 1, :]], axis=1
    )


def norm_stats(inputs):
    center = inputs - jnp.mean(inputs, axis=-1, keepdims=True)
    spread = jnp.mean(center * center, axis=-1, keepdims=True)
    scale = lax.rsqrt(spread + norm_eps)
    return center * scale, scale


def norm_back(hat, scale, gain, grad):
    inner = grad * gain
    return scale * (
        inner
        - jnp.mean(inner, axis=-1, keepdims=True)
        - hat * jnp.mean(inner * hat, axis=-1, keepdims=True)
    )


def low_lanes(dims):
    return lax.broadcasted_iota(jnp.int32, dims, 1) < HEAD


def lane_pairs(pair, last):
    low = low_lanes(pair.shape)
    roll = lambda v: pltpu.roll(v, HEAD, 1)
    ph = pair.astype(bf16).astype(f32)
    pl_ = pair - ph
    lh = last.astype(bf16).astype(f32)
    ll = last - lh
    return [
        jnp.where(low, ph, roll(pl_)).astype(bf16),
        jnp.where(low, roll(ph), pl_).astype(bf16),
        jnp.where(low, lh, roll(ll)).astype(bf16),
    ]


def row_halves(turned, head):
    part = turned[HEAD * head : HEAD * (head + 1)]
    return halves(part)


def wide_row(vec, line):
    return jnp.concatenate([vec[3 * line + i : 3 * line + i + 1, :] for i in range(3)], axis=1)


def pack_first_kernel(scal, wqkv, wproj, vec, seg, valid, tokens, first, packed):
    mine = scal[0]
    proj = wproj[pl.ds(pl.multiple_of(mine * SUB, 8), SUB), :]
    turn = lax.rem(D - mine * QUARTER, D)
    for part in range(3):
        turned = pltpu.roll(wqkv[:, part * D : (part + 1) * D], turn, 1)
        first[:ROWS, part * CH : part * CH + QUARTER] = turned[:, :QUARTER]
        for group in range(SEQ):
            lane = HEAD * (3 * group + part)
            first[group * SUB : (group + 1) * SUB, part * CH + QUARTER : (part + 1) * CH] = proj[
                :, lane : lane + HEAD
            ]
    first[ROWS:, :] = jnp.zeros((8, D), f32)
    for line in range(3):
        first[ROWS + line : ROWS + line + 1, :HALF_VEC] = wide_row(vec, line)
    packed[:CH, :] = tokens[...]
    packed[CH:, :] = jnp.zeros((8, D), f32)
    packed[CH : CH + 1, :CH] = jnp.where(valid[...] > 0, seg[...], -1).astype(f32)


def pack_second_kernel(scal, win, wout, second):
    mine = scal[0]
    turn = lax.rem(HALF_VEC - mine * ROWS, HALF_VEC)
    for part in range(GROUPS):
        turned = pltpu.roll(win[:, part * HALF_VEC : (part + 1) * HALF_VEC], turn, 1)
        second[:ROWS, part * ROWS : (part + 1) * ROWS] = turned[:, :ROWS]
    second[ROWS:, :] = wout[pl.ds(pl.multiple_of(mine * ROWS, 8), ROWS), :]


def mask_kernel(scal, cotangent, valid, result):
    keep = jnp.where(valid[...] > 0, 1.0, 0.0).astype(f32)
    column = jnp.broadcast_to(keep, (128, CH)).T[:, :1]
    result[...] = cotangent[...] * column


def weights_kernel(scal, *refs):
    blocks, (wh, wl, vec, proj) = refs[:GROUPS], refs[GROUPS:]
    for k in range(GROUPS):
        at = owner(scal, k)
        block = blocks[k][:ROWS, :]
        here = rows_at(at, ROWS)
        wh[here, :], wl[here, :] = halves(block)
        vec[at] = blocks[k][ROWS:, :HALF_VEC]
        for group in range(SEQ):
            for part in range(3):
                lane = HEAD * (3 * group + part)
                proj[pl.ds(pl.multiple_of(at * SUB, 8), SUB), lane : lane + HEAD] = block[
                    group * SUB : (group + 1) * SUB, part * CH + QUARTER : (part + 1) * CH
                ]


def front_kernel(scal, *refs):
    toks, refs = refs[:4], refs[4:]
    wh, wl, vec = refs[:3]
    xh, xl, kcat, qturn, vcat, qpair, kturn, vturn, low_row, label = refs[3:]
    mine = scal[0]

    gain, shift = piece(vec, 0), piece(vec, 1)
    turn = lax.rem(D - mine * QUARTER, D)
    own = lambda number: pltpu.roll(jnp.broadcast_to(piece(vec, number), (8, D)), turn, 1)[:1, :CH]
    query_bias, value_bias = own(2), own(3)

    for r in range(SEQ):
        nat = jnp.bitwise_xor(mine, r)
        at = rows_at(nat, CH)
        label[nat] = toks[r][CH:, :CH]
        hat, _ = norm_stats(toks[r][:CH, :])
        xh[at, :], xl[at, :] = halves(hat)
        nh, nl = halves(hat * gain + shift)
        joined = dot3(nh, nl, wh[...], wl[...], NN)
        query = (joined[:, :CH] + query_bias) * HEAD ** (-0.5)
        key = joined[:, CH : 2 * CH]
        value = joined[:, 2 * CH :] + value_bias
        keys = lane_pairs(key[:, :128], key[:, 128:])
        values = lane_pairs(value[:, :128], value[:, 128:])
        queries = lane_pairs(query[:, :128], query[:, 128:])
        key_t, value_t, query_t = key.T, value.T, query.T
        for h in range(OWN):
            kcat[h, at, :] = jnp.concatenate([keys[h], keys[h]], axis=1)
            vcat[h, at, :] = jnp.concatenate([values[h], values[h]], axis=1)
            qpair[h, at, :] = queries[h]
            a, b = row_halves(query_t, h)
            qturn[h, :, at] = jnp.concatenate([a, a, b, b], axis=0)
            a, b = row_halves(key_t, h)
            kturn[h, :, at] = jnp.concatenate([a, b], axis=0)
            a, b = row_halves(value_t, h)
            vturn[h, :, at] = jnp.concatenate([a, b], axis=0)

    labels = jnp.concatenate([label[c][:1, :] for c in range(SEQ)], axis=1)
    spot = lax.broadcasted_iota(jnp.int32, (1, LEN), 1).astype(f32)
    begin = jnp.zeros((1, LEN), f32)
    for segment in range(3):
        held = jnp.sum(jnp.where(labels == float(segment), 1.0, 0.0), axis=1, keepdims=True)
        begin = begin + jnp.where(labels > float(segment), held, 0.0)
    begin = jnp.where(labels < 0.0, spot, begin)
    low_row[...] = jnp.broadcast_to(begin, (8, LEN))


def attend_kernel(scal, kcat, qturn, vturn, low_row, outs_turn, lse):
    def one_head(h, carry):
        for c in range(SEQ):
            size = CH * (c + 1)
            lanes = slice(c * CH, (c + 1) * CH)
            score = dot(kcat[h, :size, :], qturn[h, :, lanes], NN)
            mask = allowed(low_row, c, size)
            score = jnp.where(mask, score, masked_score)
            peak = jnp.max(score, axis=0, keepdims=True)
            weight = jnp.exp(score - peak)
            total = jnp.sum(weight, axis=0, keepdims=True)
            top, rest = halves(weight)
            both = dot(vturn[h, :, :size], top, NN)
            extra = dot(vturn[h, :HEAD, :size], rest, NN)
            result = (both[:HEAD] + both[HEAD:] + extra) / total
            outs_turn[pl.ds(pl.multiple_of(h * HEAD, HEAD), HEAD), lanes] = result
            lse[h, :, lanes] = jnp.broadcast_to(peak + jnp.log(total), (8, CH))
        return carry

    lax.fori_loop(0, OWN, one_head, 0)


def allowed(low_row, c, size):
    key_at = lax.broadcasted_iota(jnp.int32, (size, CH), 0).astype(f32)
    query_at = (lax.broadcasted_iota(jnp.int32, (1, CH), 1) + c * CH).astype(f32)
    begin = low_row[:1, c * CH : (c + 1) * CH]
    return (key_at >= begin) & (key_at <= query_at)


def proj_kernel(scal, *refs):
    toks, heads, parts, refs = refs[:4], refs[4:8], refs[8:12], refs[12:]
    vec, wh, wl, heads_h, heads_l, norm_h, norm_l, mixed, hat, scale, weight, joined = refs
    mine = scal[0]
    for r in range(SEQ):
        at = jnp.bitwise_xor(mine, r)
        for d in range(GROUPS):
            weight[pl.ds(pl.multiple_of(d * ROWS + at * SUB, 8), SUB), :] = parts[r][
                d * SUB : (d + 1) * SUB, :
            ]
        joined[rows_at(at, QUARTER), :] = heads[r][...]
    wh[...], wl[...] = halves(weight[...])
    heads_h[...], heads_l[...] = halves(joined[:, rows_at(mine, CH)])
    gain, shift = piece(vec, 5), piece(vec, 6)
    for r in range(SEQ):
        at = rows_at(jnp.bitwise_xor(mine, r), CH)
        a, b = halves(joined[:, at].T)
        total = toks[r][:CH, :] + dot3(a, b, wh[...], wl[...], NN)
        total = total + piece(vec, 4)
        normed, size = norm_stats(total)
        norm_h[r], norm_l[r] = halves(normed * gain + shift)
        if r == 0:
            mixed[...] = total
            hat[...] = normed
            scale[...] = jnp.broadcast_to(size, (CH, 128))


def ffn_kernel(scal, norm_h, norm_l, *refs):
    grads, blocks, refs = refs[:4], refs[4 : 5 + GROUPS], refs[5 + GROUPS :]
    vec = refs[0]
    acts_h, acts_l, hid_h, hid_l, out_h, out_l, wouth, woutl, bias_sum = refs[1:10]
    parts, (winh, winl) = refs[10:14], refs[14:]
    mine = scal[0]
    for k in range(GROUPS):
        at = rows_at(owner(scal, k), ROWS)
        if k == HALF:
            first, second = blocks[k][...], blocks[GROUPS][...]
        else:
            first, second = blocks[k][:ROWS, :], blocks[k][ROWS:, :]
        winh[at, :], winl[at, :] = halves(first)
        wouth[at, :], woutl[at, :] = halves(second)
    marks = [16 + d for d in range(GROUPS)]
    table = jnp.concatenate([vec[m // 3, m % 3 : m % 3 + 1, :] for m in marks], axis=0)
    table = pltpu.roll(table, lax.rem(HALF_VEC - mine * ROWS, HALF_VEC), 1)[:, :ROWS]
    bias = jnp.concatenate([table[d : d + 1] for d in range(GROUPS)], axis=1)
    sums = jnp.zeros((1, D), f32)
    for r in (1, 3, 2, 0):
        at = slice(r * CH, (r + 1) * CH)
        hidden = dot3(norm_h[r], norm_l[r], winh[...], winl[...], NN) + bias
        inner = jnp.tanh(gelu_scale * (hidden + gelu_cubic * hidden * hidden * hidden))
        acts_h[at, :], acts_l[at, :] = halves(0.5 * hidden * (1.0 + inner))
        slope = 0.5 * (1.0 + inner) + 0.5 * hidden * (1.0 - inner * inner) * gelu_scale * (
            1.0 + 3.0 * gelu_cubic * hidden * hidden
        )
        gh, gl = halves(grads[r][...])
        out_h[at, :], out_l[at, :] = gh, gl
        back = dot3(gh, gl, wouth[...], woutl[...], NT) * slope
        sums = sums + jnp.sum(back, axis=0, keepdims=True)
        bh, bl = halves(back)
        hid_h[at, :], hid_l[at, :] = bh, bl
        parts[r][...] = dot3(bh, bl, winh[...], winl[...], NT)
    bias_sum[...] = jnp.broadcast_to(sums, (8, D))


def ffn_grad_kernel(scal, norm_h, norm_l, hid_h, hid_l, acts_h, acts_l, out_h, out_l, *refs):
    outs, whole = refs[:-1], refs[-1]

    def emit(first):
        for k in range(GROUPS):
            at = rows_at(owner(scal, k), ROWS)
            if k == HALF:
                outs[HALF if first else GROUPS][...] = whole[at, :]
            elif first:
                outs[k][:ROWS, :] = whole[at, :]
            else:
                outs[k][ROWS:, :] = whole[at, :]

    flat = lambda ref: ref[...].reshape(LEN, D)
    whole[...] = dot3(flat(norm_h), flat(norm_l), hid_h[...], hid_l[...], TN)
    emit(True)
    whole[...] = dot3(acts_h[...], acts_l[...], out_h[...], out_l[...], TN)
    emit(False)


def ffn_out_kernel(scal, acts_h, acts_l, wouth, woutl, *parts):
    for r in (1, 3, 2, 0):
        at = slice(r * CH, (r + 1) * CH)
        parts[r][...] = dot3(acts_h[at, :], acts_l[at, :], wouth[...], woutl[...], NN)


def output_kernel(scal, mixed, one, two, three, vec, output):
    output[...] = mixed[...] + (one[...] + two[...] + three[...]) + piece(vec, 7)


def proj_back_kernel(scal, one, two, three, hat, scale, vec, grad_out, wh, wl, mixed_grad, sums, *parts):
    mine = scal[0]
    normed = one[...] + two[...] + three[...]
    back = norm_back(hat[...], scale[:, :1], piece(vec, 5), normed)
    total = grad_out[...] + back
    mixed_grad[...] = total
    a, b = halves(total)
    for r in range(SEQ):
        at = rows_at(jnp.bitwise_xor(mine, r), QUARTER)
        parts[r][...] = dot3(wh[at, :], wl[at, :], a, b, NT)
    add = lambda v: jnp.sum(v, axis=0, keepdims=True)
    sums[...] = jnp.concatenate(
        [add(total), add(normed * hat[...]), add(normed), add(grad_out[...]), jnp.zeros((4, D), f32)],
        axis=0,
    )


def proj_grad_kernel(scal, heads_h, heads_l, mixed_grad, *refs):
    outs, whole = refs[:-1], refs[-1]
    mine = scal[0]
    gh, gl = halves(mixed_grad[...])
    whole[...] = dot3(heads_h[...], heads_l[...], gh, gl, NN)
    for r in range(SEQ):
        at = jnp.bitwise_xor(mine, r)
        for d in range(GROUPS):
            outs[r][d * SUB : (d + 1) * SUB, :] = whole[
                pl.ds(pl.multiple_of(d * ROWS + at * SUB, 8), SUB), :
            ]


def back_kernel(scal, *refs):
    grads, refs = refs[:4], refs[4:]
    kcat, qturn, vcat, qpair, kturn, outs_turn, lse, low_row = refs[:8]
    joined_h, joined_l, joined_sums = refs[8:11]
    gturn, gpair, dots, key_sum, value_sum, query_turn = refs[11:]
    mine = scal[0]

    for r in range(SEQ):
        at = rows_at(jnp.bitwise_xor(mine, r), CH)
        turned = grads[r][...]
        grad = jnp.concatenate([turned, jnp.zeros((HEAD, CH), f32)], axis=0).T
        pairs = lane_pairs(grad[:, :128], grad[:, 128:])
        for h in range(OWN):
            gpair[h, at, :] = pairs[h]
            part = turned[HEAD * h : HEAD * (h + 1)]
            dots[h, :, at] = jnp.broadcast_to(
                jnp.sum(part * outs_turn[HEAD * h : HEAD * (h + 1), at], axis=0, keepdims=True), (8, CH)
            )
            a, b = halves(part)
            gturn[h, :, at] = jnp.concatenate([a, a, b, b], axis=0)

    key_sum[...] = jnp.zeros_like(key_sum)
    value_sum[...] = jnp.zeros_like(value_sum)

    def one_head(h, carry):
        for c in range(SEQ):
            size = CH * (c + 1)
            lanes = slice(c * CH, (c + 1) * CH)
            score = dot(kcat[h, :size, :], qturn[h, :, lanes], NN)
            weight = jnp.where(allowed(low_row, c, size), jnp.exp(score - lse[h, :1, lanes]), 0.0)
            back = dot(vcat[h, :size, :], gturn[h, :, lanes], NN)
            score_back = weight * (back - dots[h, :1, lanes])
            a, b = halves(weight)
            pair = gpair[h, lanes, :]
            value_sum[h, :size, :] += dot(a, pair, NN) + dot(b, pair, NN)
            a, b = halves(score_back)
            pair = qpair[h, lanes, :]
            key_sum[h, :size, :] += dot(a, pair, NN) + dot(b, pair, NN)
            turned = dot(kturn[h, :, :size], a, NN) + dot(kturn[h, :, :size], b, NN)
            query_turn[h, :, lanes] = (turned[:HEAD] + turned[HEAD:]) * HEAD ** (-0.5)
        return carry

    lax.fori_loop(0, OWN, one_head, 0)

    column_sums = jnp.zeros((1, D), f32)
    low = low_lanes((CH, 128))
    for c in range(SEQ):
        at = slice(c * CH, (c + 1) * CH)
        blank = jnp.zeros((HEAD, CH), f32)
        query = jnp.concatenate([query_turn[h, :, at] for h in range(OWN)] + [blank], axis=0).T
        done = [query]
        for kept in (key_sum, value_sum):
            full = [kept[h, at, :] for h in range(OWN)]
            full = [v + pltpu.roll(v, HEAD, 1) for v in full]
            done.append(jnp.where(low, full[0], full[1]))
            done.append(jnp.where(low, full[2], 0.0))
        joined = jnp.concatenate(done, axis=1)
        column_sums = column_sums + jnp.sum(joined, axis=0, keepdims=True)
        joined_h[at, :], joined_l[at, :] = halves(joined)

    joined_sums[...] = jnp.broadcast_to(column_sums, (8, D))


def qkv_grad_kernel(scal, xh, xl, joined_h, joined_l, joined_sums, wh, wl, vec, *refs):
    proj_one, proj_two, proj_three, sums, bias_sum = refs[:5]
    outs, (whole, rows) = refs[5 : 5 + GROUPS], refs[5 + GROUPS :]
    mine = scal[0]
    column_sums = joined_sums[:1, :]
    core = dot3(xh[...], xl[...], joined_h[...], joined_l[...], TN)
    gain, shift = piece(vec, 0), piece(vec, 1)
    as_column = lambda v: jnp.broadcast_to(v, (128, D)).T[:, :1]
    whole[...] = as_column(gain) * core + as_column(shift) * column_sums
    weights = wh[...].astype(f32) + wl[...].astype(f32)
    gain_grad = jnp.sum(weights * core, axis=1, keepdims=True)
    shift_grad = jnp.sum(weights * column_sums, axis=1, keepdims=True)
    lane = lax.broadcasted_iota(jnp.int32, (D, 128), 1)
    norm_grads = jnp.where(lane == 0, gain_grad, shift_grad).T

    def place(part, scale):
        wide = jnp.concatenate([part[:, :QUARTER], jnp.zeros((1, D - QUARTER), f32)], axis=1)
        wide = jnp.broadcast_to(wide, (8, D))
        return pltpu.roll(wide, mine * QUARTER, 1)[:1]

    entries = [
        norm_grads[0:1],
        norm_grads[1:2],
        place(column_sums[:, :CH], 1.0),
        place(column_sums[:, 2 * CH :], 1.0),
        sums[0:1],
        sums[1:2],
        sums[2:3],
        sums[3:4],
    ]
    lines = [e[:, i * HALF_VEC : (i + 1) * HALF_VEC] for e in entries for i in range(2)]
    bias = jnp.concatenate(
        [bias_sum[:1, d * ROWS : (d + 1) * ROWS] for d in range(GROUPS)], axis=0
    )
    bias = jnp.concatenate([bias, jnp.zeros((GROUPS, HALF_VEC - ROWS), f32)], axis=1)
    bias = pltpu.roll(bias, mine * ROWS, 1)
    lines = lines + [bias[d : d + 1] for d in range(GROUPS)]
    filler = jnp.zeros((5, HALF_VEC), f32)
    for d in range(GROUPS):
        rows[d] = jnp.concatenate(lines[3 * d : 3 * d + 3] + [filler], axis=0)

    for k in range(GROUPS):
        at = owner(scal, k)
        outs[k][:ROWS, :] = whole[rows_at(at, ROWS), :]
        here = pl.ds(pl.multiple_of(at * SUB, 8), SUB)
        proj = proj_one[here, :] + proj_two[here, :] + proj_three[here, :]
        for group in range(SEQ):
            for part in range(3):
                lane_at = HEAD * (3 * group + part)
                outs[k][
                    group * SUB : (group + 1) * SUB, part * CH + QUARTER : (part + 1) * CH
                ] = proj[:, lane_at : lane_at + HEAD]
        outs[k][ROWS:, :HALF_VEC] = rows[at]
        outs[k][ROWS:, HALF_VEC:] = jnp.zeros((8, HALF_VEC), f32)


def pre_back_kernel(scal, joined_h, joined_l, wh, wl, *parts):
    mine = scal[0]
    for r in (1, 3, 2, 0):
        at = rows_at(jnp.bitwise_xor(mine, r), CH)
        parts[r][...] = dot3(joined_h[at, :], joined_l[at, :], wh[...], wl[...], NT)


def input_grad_kernel(scal, tokens, one, two, three, vec, mixed_grad, result):
    hat, scale = norm_stats(tokens[...])
    grad = one[...] + two[...] + three[...]
    result[...] = mixed_grad[...] + norm_back(hat, scale, piece(vec, 0), grad)


def total_square(value):
    return jnp.sum(jnp.sum(value * value, axis=0, keepdims=True), axis=1, keepdims=True)


def second_squares_kernel(scal, one, two, three, four, squares):
    total = sum(total_square(part[...]) for part in (one, two, three, four))
    squares[...] = jnp.broadcast_to(total, (8, 128))


def first_squares_kernel(scal, one, two, three, four, before, squares):
    parts = (one, two, three, four)
    total = sum(total_square(part[:ROWS, :]) for part in parts)
    line = sum(part[ROWS:, :HALF_VEC] for part in parts)
    squares[...] = before[...] + (total + total_square(line))


def adamw_kernel(scal, squares, *refs):
    firsts, seconds, refs = refs[:4], refs[4:8], refs[8:]
    states, clip, news, (first, second) = refs[:15], refs[15], refs[16:31], refs[31:]
    mine = scal[0]
    norm = jnp.sqrt(squares[...])
    clip[...] = norm
    factor = (clip_limit / jnp.maximum(norm, clip_limit))[:1, :1]
    for r in range(SEQ):
        at = jnp.bitwise_xor(mine, r)
        first[at] = firsts[r][:ROWS, :]
        second[at] = seconds[r][...]

    def update(number, spot, grad, rate, decay):
        held = [states[3 * number + i][spot] for i in range(3)]
        fresh = adamw_update(*held, factor * grad, rate, decay)
        for i in range(3):
            news[3 * number + i][spot] = fresh[i]

    line = sum(firsts[r][ROWS:, :HALF_VEC] for r in range(SEQ))
    for i in range(3):
        for j in range(3):
            spot = (slice(3 * i + j, 3 * i + j + 1), slice(None))
            update(0, spot, line[i : i + 1, 128 * j : 128 * (j + 1)], vector_rate, 0.0)
    every = slice(None)
    for part in range(3):
        grad = jnp.concatenate(
            [first[j][:, part * CH : part * CH + QUARTER] for j in range(SEQ)], axis=1
        )
        update(1, (every, slice(part * D, (part + 1) * D)), grad, matrix_rate, weight_decay)
    for j in range(SEQ):
        grad = jnp.concatenate(
            [
                first[j][group * SUB : (group + 1) * SUB, part * CH + QUARTER : (part + 1) * CH]
                for group in range(SEQ)
                for part in range(3)
            ],
            axis=1,
        )
        update(2, (slice(j * SUB, (j + 1) * SUB), every), grad, matrix_rate, weight_decay)
    for d in range(GROUPS):
        grad = jnp.concatenate(
            [second[j][:ROWS, d * ROWS : (d + 1) * ROWS] for j in range(SEQ)], axis=1
        )
        update(3, (every, slice(d * HALF_VEC, (d + 1) * HALF_VEC)), grad, matrix_rate, weight_decay)
    for j in range(SEQ):
        update(
            4, (slice(j * ROWS, (j + 1) * ROWS), every), second[j][ROWS:, :], matrix_rate, weight_decay
        )


def adamw_update(weight, first, second, grad, rate, decay):
    new_first = beta_one * first + (1.0 - beta_one) * grad
    new_second = beta_two * second + (1.0 - beta_two) * grad * grad
    first_hat = new_first / (1.0 - beta_one**STEP)
    second_hat = new_second / (1.0 - beta_two**STEP)
    new_weight = weight - rate * (first_hat / (jnp.sqrt(second_hat) + adam_eps) + decay * weight)
    return (new_first, new_second, new_weight)


def ring_tables(count):
    evens = [2 * i for i in range(count // 2)]
    order = evens + [i + 1 for i in reversed(evens)]
    place = [0] * count
    for position, device in enumerate(order):
        place[device] = position
    right = [(order[i], order[(i + 1) % count]) for i in range(count)]
    left = [(b, a) for a, b in right]
    return order, place, right, left


def ring_gather(block, cut=0, holds=()):
    _, _, right, left = ring_tables(GROUPS)
    got = {0: block}
    forth = back = block
    for step in range(1, HALF):
        if step <= len(holds):
            forth, back = gate(forth, holds[step - 1][0]), gate(back, holds[step - 1][1])
        forth = got[GROUPS - step] = lax.ppermute(forth, "dp", right)
        back = got[step] = lax.ppermute(back, "dp", left)
    if not cut:
        got[HALF] = lax.ppermute(forth, "dp", right)
        return [got[k] for k in range(GROUPS)]
    got[HALF] = lax.ppermute(forth[:cut], "dp", right)
    return [got[k] for k in range(GROUPS)], lax.ppermute(back[cut:], "dp", left)


def ring_scatter(blocks, rest=None, hold=()):
    _, _, right, left = ring_tables(GROUPS)
    forth = lax.ppermute(blocks[HALF], "dp", right)
    back = None if rest is None else lax.ppermute(rest, "dp", left)
    for step in range(HALF - 1, 0, -1):
        ahead, behind = blocks[step], blocks[GROUPS - step]
        if step == HALF - 1 and back is not None:
            cut = forth.shape[0]
            ahead, behind = gate(ahead, hold), gate(behind, hold)
            forth = lax.dynamic_update_slice(ahead, ahead[:cut] + forth, (0, 0))
            back = lax.dynamic_update_slice(behind, behind[cut:] + back, (cut, 0))
        else:
            forth, back = forth + ahead, behind if back is None else back + behind
        sent = [forth, back]
        forth = lax.ppermute(forth, "dp", right)
        back = lax.ppermute(back, "dp", left)
    return forth + back + blocks[0], sent


def swap(block, bits):
    return lax.ppermute(block, "seq", [(i, i ^ bits) for i in range(SEQ)])


def gather_seq(block):
    across = swap(block, 2)
    core = swap(block, 1)
    return [block, core, across, swap(across, 1)]


def exchange_seq(parts):
    return [parts[0]] + [swap(parts[r], r) for r in range(1, SEQ)]


def scatter_core(parts):
    return parts[0], swap(parts[1], 1), parts[2], swap(parts[3], 1)


def ordered(blocks, mine):
    stack = jnp.stack(blocks, axis=0)
    return [lax.dynamic_index_in_dim(stack, mine ^ j, 0, keepdims=False) for j in range(len(blocks))]


def local(
    tokens,
    cotangent,
    segment_ids,
    valid,
    vectors,
    vec_first,
    vec_second,
    w_qkv,
    qkv_first,
    qkv_second,
    w_proj,
    proj_first,
    proj_second,
    w_in,
    in_first,
    in_second,
    w_out,
    out_first,
    out_second,
):
    dp_parts = lax.axis_size("dp")
    ring = dp_parts == GROUPS
    mine = lax.axis_index("seq")
    home = lax.axis_index("dp")
    rows = w_qkv.shape[0]
    units = w_out.shape[0] // SEQ
    far, near = home // 2, home % 2
    position = jnp.where(near > 0, GROUPS - 1 - far, far)
    scal = jnp.stack([mine, position, jnp.full_like(mine, 1 if ring else 0)]).astype(jnp.int32)
    flat_in = tokens.reshape(CH, D)
    chunk, tall, square = shape(CH, D), shape(LEN, D, kind=bf16), shape(D, D, kind=bf16)

    if ring:
        first, packed = run(
            pack_first_kernel,
            scal,
            [w_qkv, w_proj, vectors.reshape(9, 128), segment_ids, valid, flat_in],
            [shape(ROWS + 8, D), shape(CH + 8, D)],
            name="pack_first", work=3.0,
        )
        firsts = ring_gather(first)
        (second,) = run(
            pack_second_kernel,
            scal,
            [w_in, w_out],
            [shape(2 * ROWS, D)],
            name="pack_second", work=3.0,
            after=[firsts[GROUPS - 1]],
        )
    else:
        padded = jnp.pad(w_qkv, ((0, 0), (0, CH)))
        own = lambda part: lax.dynamic_slice_in_dim(padded, part * D + mine * QUARTER, CH, 1)
        first = jnp.concatenate([own(0), own(1), own(2)], axis=1)
        first = lax.all_gather(first, "dp", axis=0, tiled=True).reshape(GROUPS, ROWS, D)
        all_vec = lax.all_gather(vectors, "dp", axis=0, tiled=True).reshape(GROUPS, 3, HALF_VEC)
        first = jnp.concatenate([first, jnp.pad(all_vec, ((0, 0), (0, 5), (0, D - HALF_VEC)))], axis=1)
        firsts = [first[k] for k in range(GROUPS)]
        in_part = lax.dynamic_index_in_dim(
            w_in.reshape(rows, dp_parts, SEQ, units), mine, 2, keepdims=False
        ).reshape(rows, D)
        out_part = lax.dynamic_slice_in_dim(w_out, mine * units, units, 0)
        second = jnp.concatenate(
            [
                lax.all_gather(part, "dp", axis=0, tiled=True).reshape(GROUPS, ROWS, D)
                for part in (in_part, out_part)
            ],
            axis=1,
        )
        seconds = [second[k] for k in range(GROUPS)]
        seconds[HALF], second_rest = second[HALF, :ROWS], second[HALF, ROWS:]
        marks = jnp.where(valid > 0, segment_ids, -1).astype(f32)
        packed = jnp.concatenate([flat_in, jnp.pad(marks, ((0, 7), (0, D - CH)))], axis=0)
    toks = gather_seq(packed)
    (grad_out,) = run(
        mask_kernel, scal, [cotangent.reshape(CH, D), valid], [chunk], name="mask", work=2.0, after=[toks[2]]
    )
    grads_row = gather_seq(grad_out)

    qkv_h, qkv_l, vec, proj = run(
        weights_kernel,
        scal,
        firsts,
        [square, square, shape(GROUPS, 8, HALF_VEC), shape(GROUPS * SUB, D)],
        name="weights", work=3.0,
    )
    if ring:
        proj_parts = gather_seq(proj)
    else:
        full = lax.all_gather(w_proj, "dp", axis=0, tiled=True).reshape(GROUPS, SEQ, SUB, D)
        proj_parts = [
            lax.dynamic_index_in_dim(full, mine ^ r, 1, keepdims=False).reshape(GROUPS * SUB, D)
            for r in range(SEQ)
        ]
    hat_h, hat_l, kcat, qturn, vcat, qpair, kturn, vturn, low_row = run(
        front_kernel,
        scal,
        toks + [qkv_h, qkv_l, vec],
        [
            tall,
            tall,
            shape(OWN, LEN, 256, kind=bf16),
            shape(OWN, 256, LEN, kind=bf16),
            shape(OWN, LEN, 256, kind=bf16),
            shape(OWN, LEN, 128, kind=bf16),
            shape(OWN, 128, LEN, kind=bf16),
            shape(OWN, 128, LEN, kind=bf16),
            shape(8, LEN),
        ],
        scratch=[pltpu.VMEM((SEQ, 8, CH), f32)],
        name="front", work=8.0,
        after=[grads_row[2]],
    )
    heads, lse = run(
        attend_kernel,
        scal,
        [kcat, qturn, vturn, low_row],
        [shape(QUARTER, LEN), shape(OWN, 8, LEN)],
        name="attend", work=8.0,
        after=[proj_parts[2]],
    )
    if ring:
        holds = [([firsts[HALF]], [firsts[HALF - 1]]), ([low_row], [low_row]), ([lse], [lse])]
        seconds, second_rest = ring_gather(second, ROWS, holds)
    wide = shape(D, CH, kind=bf16)
    split = shape(SEQ, CH, D, kind=bf16)
    proj_h, proj_l, heads_h, heads_l, norm_h, norm_l, mixed, hat_two, scale_two = run(
        proj_kernel,
        scal,
        toks + gather_seq(heads) + proj_parts + [vec],
        [square, square, wide, wide, split, split, chunk, chunk, shape(CH, 128)],
        scratch=[pltpu.VMEM((D, D), f32), pltpu.VMEM((D, LEN), f32)],
        name="proj", work=8.0,
    )

    done = run(
        ffn_kernel,
        scal,
        [norm_h, norm_l] + grads_row + seconds + [second_rest, vec],
        [tall] * 6 + [square] * 2 + [shape(8, D)] + [chunk] * SEQ,
        scratch=[pltpu.VMEM((D, D), bf16)] * 2,
        name="ffn", work=20.0,
    )
    acts_h, acts_l, hid_h, hid_l, out_h, out_l, out_wh, out_wl, bias_sum = done[:9]
    norm_own, norm_near, norm_across, norm_far = scatter_core(done[9:])
    norm_pair = norm_across + norm_far
    norm_last = swap(norm_pair, 2)
    done = run(
        ffn_grad_kernel,
        scal,
        [norm_h, norm_l, hid_h, hid_l, acts_h, acts_l, out_h, out_l],
        [shape(2 * ROWS, D) if k != HALF else shape(ROWS, D) for k in range(GROUPS)] + [shape(ROWS, D)],
        scratch=[pltpu.VMEM((D, D), f32)],
        name="ffn_grad", work=14.0,
        after=[norm_pair],
    )
    second_grads, second_grad_rest = list(done[:-1]), done[-1]
    done = run(
        proj_back_kernel,
        scal,
        [norm_own, norm_near, norm_last, hat_two, scale_two, vec, grad_out, proj_h, proj_l],
        [chunk, shape(8, D)] + [shape(QUARTER, CH)] * SEQ,
        name="proj_back", work=5.0,
    )
    mixed_grad, sums = done[:2]
    head_grads = exchange_seq(list(done[2:]))
    if ring:
        shard_second, second_sent = ring_scatter(
            second_grads, second_grad_rest, [mixed_grad]
        )
        second_all = gather_seq(shard_second)
    proj_grads = run(
        proj_grad_kernel,
        scal,
        [heads_h, heads_l, mixed_grad],
        [shape(GROUPS * SUB, D)] * SEQ,
        scratch=[pltpu.VMEM((D, D), f32)],
        name="proj_grad", work=4.0,
    )
    wait = [head_grads[3], head_grads[2]]
    if ring:
        proj_own, proj_near, proj_across, proj_far = scatter_core(proj_grads)
        proj_pair = gate(proj_across, wait) + proj_far
        proj_last = swap(proj_pair, 2)
    else:
        proj_own = proj_near = proj_last = proj_pair = proj_grads[0]
    joined_h, joined_l, joined_sums = run(
        back_kernel,
        scal,
        head_grads + [kcat, qturn, vcat, qpair, kturn, heads, lse, low_row],
        [tall, tall, shape(8, D)],
        scratch=[
            pltpu.VMEM((OWN, 256, LEN), bf16),
            pltpu.VMEM((OWN, LEN, 128), bf16),
            pltpu.VMEM((OWN, 8, LEN), f32),
            pltpu.VMEM((OWN, LEN, 128), f32),
            pltpu.VMEM((OWN, LEN, 128), f32),
            pltpu.VMEM((OWN, HEAD, LEN), f32),
        ],
        name="back", work=16.0,
        after=[proj_grads[0]],
    )
    done = run(
        qkv_grad_kernel,
        scal,
        [hat_h, hat_l, joined_h, joined_l, joined_sums, qkv_h, qkv_l, vec]
        + [proj_own, proj_near, proj_last, sums, bias_sum],
        [shape(ROWS + 8, D)] * GROUPS,
        scratch=[pltpu.VMEM((D, D), f32), pltpu.VMEM((GROUPS, 8, HALF_VEC), f32)],
        name="qkv_grad", work=9.0,
        after=second_sent if ring else [],
    )
    first_grads = list(done)
    if ring:
        shard_first, _ = ring_scatter(first_grads)
    pre_parts = run(
        pre_back_kernel,
        scal,
        [joined_h, joined_l, qkv_h, qkv_l],
        [chunk] * SEQ,
        name="pre_back", work=7.0,
        after=[done[0], shard_second] if ring else [],
    )
    pre_own, pre_near, pre_across, pre_far = scatter_core(pre_parts)
    if ring:
        pre_across = gate(pre_across, [second_all[2]])
    pre_last = swap(pre_across + pre_far, 2)
    out_parts = run(
        ffn_out_kernel,
        scal,
        [acts_h, acts_l, out_wh, out_wl],
        [chunk] * SEQ,
        name="ffn_out", work=7.0,
        after=[pre_parts[0]],
    )
    out_own, out_near, out_across, out_far = scatter_core(out_parts)
    out_pair = out_across + out_far
    (input_grad,) = run(
        input_grad_kernel,
        scal,
        [flat_in, pre_own, pre_near, pre_last, vec, mixed_grad],
        [chunk],
        name="input_grad", work=3.0,
    )

    flat = lambda v: v.reshape(9, 128)
    states = [vectors, vec_first, vec_second, w_qkv, qkv_first, qkv_second, w_proj, proj_first, proj_second]
    states = states + [w_in, in_first, in_second, w_out, out_first, out_second]
    if ring:
        (squares,) = run(
            second_squares_kernel, scal, second_all, [shape(8, 128)], name="second_squares", work=2.0
        )
        first_all = gather_seq(gate(shard_first, [pre_last, out_parts[0]]))
        out_pair = gate(out_pair, [first_all[2]])
        (squares,) = run(
            first_squares_kernel,
            scal,
            first_all + [squares],
            [shape(8, 128)],
            name="first_squares", work=2.0,
            after=[input_grad],
        )
        out_last = swap(out_pair, 2)
        for bits in (1, 2, 4):
            pairs = [(i, i ^ bits) for i in range(GROUPS)]
            squares = squares + lax.ppermute(squares, "dp", pairs)
        held = [flat(v) for v in states[:3]] + states[3:]
        done = run(
            adamw_kernel,
            scal,
            [squares] + first_all + second_all + held,
            [shape(8, 128)] + [shape(*v.shape) for v in held],
            scratch=[pltpu.VMEM((SEQ, ROWS, D), f32), pltpu.VMEM((SEQ, 2 * ROWS, D), f32)],
            name="adamw", work=10.0,
        )
        new = [v.reshape(-1) for v in done[1:4]] + list(done[4:])
        clip_norm = done[0][0, 0]
    else:
        out_last = swap(out_pair, 2)
        by_group = jnp.stack(first_grads)
        shard_first = lax.psum_scatter(
            by_group[:, :ROWS].reshape(D, D), "dp", scatter_dimension=0, tiled=True
        )
        proj_full = jnp.stack([p.reshape(GROUPS, SUB, D) for p in ordered(proj_grads, mine)], axis=1)
        proj_grad = lax.psum(
            lax.psum_scatter(proj_full.reshape(D, D), "dp", scatter_dimension=0, tiled=True), "seq"
        )
        all_vec = lax.psum(by_group[:, ROWS : ROWS + 3, :HALF_VEC], ("dp", "seq")).reshape(-1)
        vec_grad = lax.dynamic_slice_in_dim(all_vec, home * vectors.shape[0], vectors.shape[0])
        joined = lax.all_gather(shard_first, "seq", axis=0, tiled=False)
        qkv_grad = jnp.concatenate(
            [joined[j, :, i * CH : i * CH + QUARTER] for i in range(3) for j in range(SEQ)], axis=1
        )
        halved = jnp.concatenate([second_grads[HALF], second_grad_rest], axis=0)
        by_group = jnp.stack(second_grads[:HALF] + [halved] + second_grads[HALF + 1 :])
        shard_in, shard_out = (
            lax.psum_scatter(part.reshape(D, D), "dp", scatter_dimension=0, tiled=True)
            for part in (by_group[:, :ROWS], by_group[:, ROWS:])
        )
        in_all = lax.all_gather(shard_in, "seq", axis=0, tiled=False)
        in_grad = in_all.reshape(SEQ, rows, dp_parts, units).transpose(1, 2, 0, 3).reshape(rows, -1)
        out_grad = lax.all_gather(shard_out, "seq", axis=0, tiled=True)
        total = sum(jnp.sum(g * g) for g in (qkv_grad, proj_grad, in_grad, out_grad, vec_grad))
        total = lax.psum(total, "dp")
        clip_norm = jnp.sqrt(total)
        factor = clip_limit / jnp.maximum(clip_norm, clip_limit)
        grads = (vec_grad, qkv_grad, proj_grad, in_grad, out_grad)
        new = []
        for number, grad in enumerate(grads):
            rate, decay = (matrix_rate, weight_decay) if number else (vector_rate, 0.0)
            new.extend(adamw_update(*states[3 * number : 3 * number + 3], factor * grad, rate, decay))
    (output,) = run(
        output_kernel, scal, [mixed, out_own, out_near, out_last, vec], [chunk], name="output", work=2.0
    )
    return (output.reshape(tokens.shape), input_grad.reshape(tokens.shape), clip_norm, *new)


def solution(mesh):
    row = P("dp", "seq", None)
    mark = P("dp", "seq")
    vec = P("dp")
    mat = P("dp", None)
    return jax.shard_map(
        local,
        mesh=mesh,
        in_specs=(row, row, mark, mark) + (vec,) * 3 + (mat,) * 12,
        out_specs=(row, row, P()) + (vec,) * 3 + (mat,) * 12,
        check_vma=False,
    )
```

```python
import functools
import math

import jax
import jax.numpy as jnp
from jax import lax
from jax.experimental import pallas as pl
from jax.experimental.pallas import tpu as pltpu
from jax.sharding import PartitionSpec as P

D = 768
HEADS = 12
HEAD = 64
STEP = 10
CH = 256
LEN = 1024
SEQ = 4
QUARTER = D // SEQ
OWN = HEADS // SEQ
GROUPS = 8
ROWS = D // GROUPS
SUB = ROWS // SEQ
HALF = GROUPS // 2
HALF_VEC = D // 2
VEC_ROWS = 24

f32 = jnp.float32
bf16 = jnp.bfloat16
masked_score = -1e30
norm_eps = 1e-05
clip_limit = 1.0
beta_one = 0.9
beta_two = 0.999
adam_eps = 1e-08
matrix_rate = 0.02
vector_rate = 0.4
weight_decay = 0.01
gelu_scale = 0.7978845608028654
gelu_cubic = 0.044715

COST = 1e9

WHOLE = pl.BlockSpec(memory_space=pltpu.VMEM)
SCALARS = pl.BlockSpec(memory_space=pltpu.SMEM)
NN = ((1,), (0,))
NT = ((1,), (1,))
TN = ((0,), (0,))


def shape(*dims, kind=f32):
    return jax.ShapeDtypeStruct(dims, kind)


def run(
    kernel, scal, args, outs, scratch=(), sems=0, far_args=(), far_outs=(), room=10, work=1.0, name=None, after=()
):
    args, after = list(args), list(after)
    held = sum(math.prod(v.shape) * jnp.dtype(v.dtype).itemsize for v in scratch)
    anywhere, far = pl.BlockSpec(memory_space=pl.ANY), pl.BlockSpec(memory_space=pltpu.HBM)
    scratch = list(scratch) + ([pltpu.SemaphoreType.DMA((sems,))] if sems else [])

    def body(scal_ref, *refs):
        kernel(scal_ref, *refs[: len(args)], *refs[len(args) + len(after) :])

    return pl.pallas_call(
        body,
        out_shape=tuple(outs),
        in_specs=[SCALARS]
        + [far if i in far_args else WHOLE for i in range(len(args))]
        + [anywhere] * len(after),
        out_specs=tuple(far if i in far_outs else WHOLE for i in range(len(outs))),
        scratch_shapes=scratch,
        compiler_params=pltpu.CompilerParams(vmem_limit_bytes=held + (room << 20)),
        cost_estimate=pl.CostEstimate(
            flops=int(work * COST), bytes_accessed=1, transcendentals=0
        ),
        name=name,
    )(scal, *args, *after)


def gate(value, after):
    anywhere = pl.BlockSpec(memory_space=pl.ANY)
    return pl.pallas_call(
        lambda *refs: None,
        out_shape=shape(*value.shape, kind=value.dtype),
        in_specs=[anywhere] * (1 + len(after)),
        out_specs=anywhere,
        input_output_aliases={0: 0},
        name="gate",
    )(value, *after)


def owner(scal, k):
    spot = jnp.bitwise_and(scal[1] + k, GROUPS - 1)
    return jnp.where(scal[2] > 0, jnp.where(spot < HALF, 2 * spot, 2 * GROUPS - 1 - 2 * spot), k)


def halves(value):
    top = value.astype(bf16)
    return top, (value - top.astype(f32)).astype(bf16)


def dot(left, right, dims):
    return lax.dot_general(left, right, (dims, ((), ())), preferred_element_type=f32)


def dot3(lh, ll, rh, rl, dims):
    return dot(lh, rh, dims) + (dot(lh, rl, dims) + dot(ll, rh, dims))


def rows_at(index, size):
    return pl.ds(pl.multiple_of(index * size, size), size)


def piece(vec, number):
    a, b = 2 * number, 2 * number + 1
    return jnp.concatenate(
        [vec[a // 3, a % 3 : a % 3 + 1, :], vec[b // 3, b % 3 : b % 3 + 1, :]], axis=1
    )


def norm_stats(inputs):
    center = inputs - jnp.mean(inputs, axis=-1, keepdims=True)
    spread = jnp.mean(center * center, axis=-1, keepdims=True)
    scale = lax.rsqrt(spread + norm_eps)
    return center * scale, scale


def norm_back(hat, scale, gain, grad):
    inner = grad * gain
    return scale * (
        inner
        - jnp.mean(inner, axis=-1, keepdims=True)
        - hat * jnp.mean(inner * hat, axis=-1, keepdims=True)
    )


def low_lanes(dims):
    return lax.broadcasted_iota(jnp.int32, dims, 1) < HEAD


def lane_pairs(pair, last):
    low = low_lanes(pair.shape)
    roll = lambda v: pltpu.roll(v, HEAD, 1)
    ph = pair.astype(bf16).astype(f32)
    pl_ = pair - ph
    lh = last.astype(bf16).astype(f32)
    ll = last - lh
    return [
        jnp.where(low, ph, roll(pl_)).astype(bf16),
        jnp.where(low, roll(ph), pl_).astype(bf16),
        jnp.where(low, lh, roll(ll)).astype(bf16),
    ]


def row_halves(turned, head):
    part = turned[HEAD * head : HEAD * (head + 1)]
    return halves(part)


def pack_first_kernel(scal, wqkv, wproj, vec, seg, valid, tokens, first, packed, *refs):
    bands, proj, lines, marks, sems = refs
    mine = scal[0]
    aligned = pl.multiple_of(jnp.bitwise_and(mine * QUARTER, -128), 128)
    copies = [
        pltpu.make_async_copy(wqkv.at[:, pl.ds(part * D + aligned, CH)], bands.at[part], sems.at[part])
        for part in range(3)
    ]
    sub = pl.ds(pl.multiple_of(mine * SUB, 8), SUB)
    copies.append(pltpu.make_async_copy(wproj.at[sub, :], proj, sems.at[3]))
    copies.append(pltpu.make_async_copy(vec, lines, sems.at[4]))
    copies.append(pltpu.make_async_copy(seg, marks.at[0], sems.at[5]))
    copies.append(pltpu.make_async_copy(valid, marks.at[1], sems.at[6]))
    copies.append(pltpu.make_async_copy(tokens, packed.at[:CH, :], sems.at[7]))
    for copy in copies:
        copy.start()
    first[ROWS:, :] = jnp.zeros((8, D), f32)
    packed[CH:, :] = jnp.zeros((8, D), f32)
    for copy in copies[:5]:
        copy.wait()
    turn = jnp.where(jnp.bitwise_and(mine, 1) > 0, CH - HEAD, 0)
    for part in range(3):
        turned = pltpu.roll(bands[part], turn, 1)
        first[:ROWS, part * CH : part * CH + QUARTER] = turned[:, :QUARTER]
        for group in range(SEQ):
            lane = HEAD * (3 * group + part)
            first[group * SUB : (group + 1) * SUB, part * CH + QUARTER : (part + 1) * CH] = proj[
                :, lane : lane + HEAD
            ]
        first[ROWS + part : ROWS + part + 1, :HALF_VEC] = jnp.concatenate(
            [lines[3 * part + i : 3 * part + i + 1, :] for i in range(3)], axis=1
        )
    for copy in copies[5:]:
        copy.wait()
    packed[CH : CH + 1, :CH] = jnp.where(marks[1] > 0, marks[0], -1).astype(f32)


def pack_second_kernel(scal, win, wout, second):
    mine = scal[0]
    turn = lax.rem(HALF_VEC - mine * ROWS, HALF_VEC)
    for part in range(GROUPS):
        turned = pltpu.roll(win[:, part * HALF_VEC : (part + 1) * HALF_VEC], turn, 1)
        second[:ROWS, part * ROWS : (part + 1) * ROWS] = turned[:, :ROWS]
    second[ROWS:, :] = wout[pl.ds(pl.multiple_of(mine * ROWS, 8), ROWS), :]


def mask_kernel(scal, cotangent, valid, result):
    keep = jnp.where(valid[...] > 0, 1.0, 0.0).astype(f32)
    column = jnp.broadcast_to(keep, (128, CH)).T[:, :1]
    result[...] = cotangent[...] * column


def weights_kernel(scal, *refs):
    blocks, (wh, wl, vec, proj) = refs[:GROUPS], refs[GROUPS:]
    for k in range(GROUPS):
        at = owner(scal, k)
        block = blocks[k][:ROWS, :]
        here = rows_at(at, ROWS)
        wh[here, :], wl[here, :] = halves(block)
        vec[at] = blocks[k][ROWS:, :HALF_VEC]
        for group in range(SEQ):
            for part in range(3):
                lane = HEAD * (3 * group + part)
                proj[pl.ds(pl.multiple_of(at * SUB, 8), SUB), lane : lane + HEAD] = block[
                    group * SUB : (group + 1) * SUB, part * CH + QUARTER : (part + 1) * CH
                ]


def front_kernel(scal, *refs):
    toks, refs = refs[:4], refs[4:]
    wh, wl, vec = refs[:3]
    xh, xl, kcat, qturn, vcat, qpair, kturn, vturn, low_row, label = refs[3:]
    mine = scal[0]

    gain, shift = piece(vec, 0), piece(vec, 1)
    turn = lax.rem(D - mine * QUARTER, D)
    own = lambda number: pltpu.roll(jnp.broadcast_to(piece(vec, number), (8, D)), turn, 1)[:1, :CH]
    query_bias, value_bias = own(2), own(3)

    for r in range(SEQ):
        nat = jnp.bitwise_xor(mine, r)
        at = rows_at(nat, CH)
        label[nat] = toks[r][CH:, :CH]
        hat, _ = norm_stats(toks[r][:CH, :])
        xh[at, :], xl[at, :] = halves(hat)
        nh, nl = halves(hat * gain + shift)
        joined = dot3(nh, nl, wh[...], wl[...], NN)
        query = (joined[:, :CH] + query_bias) * HEAD ** (-0.5)
        key = joined[:, CH : 2 * CH]
        value = joined[:, 2 * CH :] + value_bias
        keys = lane_pairs(key[:, :128], key[:, 128:])
        values = lane_pairs(value[:, :128], value[:, 128:])
        queries = lane_pairs(query[:, :128], query[:, 128:])
        key_t, value_t, query_t = key.T, value.T, query.T
        for h in range(OWN):
            kcat[h, at, :] = jnp.concatenate([keys[h], keys[h]], axis=1)
            vcat[h, at, :] = jnp.concatenate([values[h], values[h]], axis=1)
            qpair[h, at, :] = queries[h]
            a, b = row_halves(query_t, h)
            qturn[h, :, at] = jnp.concatenate([a, a, b, b], axis=0)
            a, b = row_halves(key_t, h)
            kturn[h, :, at] = jnp.concatenate([a, b], axis=0)
            a, b = row_halves(value_t, h)
            vturn[h, :, at] = jnp.concatenate([a, b], axis=0)

    labels = jnp.concatenate([label[c][:1, :] for c in range(SEQ)], axis=1)
    spot = lax.broadcasted_iota(jnp.int32, (1, LEN), 1).astype(f32)
    begin = jnp.zeros((1, LEN), f32)
    for segment in range(3):
        held = jnp.sum(jnp.where(labels == float(segment), 1.0, 0.0), axis=1, keepdims=True)
        begin = begin + jnp.where(labels > float(segment), held, 0.0)
    begin = jnp.where(labels < 0.0, spot, begin)
    low_row[...] = jnp.broadcast_to(begin, (8, LEN))


def attend_kernel(scal, kcat, qturn, vturn, low_row, outs_turn, lse):
    def one_head(h, carry):
        for c in range(SEQ):
            size = CH * (c + 1)
            lanes = slice(c * CH, (c + 1) * CH)
            score = dot(kcat[h, :size, :], qturn[h, :, lanes], NN)
            mask = allowed(low_row, c, size)
            score = jnp.where(mask, score, masked_score)
            peak = jnp.max(score, axis=0, keepdims=True)
            weight = jnp.exp(score - peak)
            total = jnp.sum(weight, axis=0, keepdims=True)
            top, rest = halves(weight)
            both = dot(vturn[h, :, :size], top, NN)
            extra = dot(vturn[h, :HEAD, :size], rest, NN)
            result = (both[:HEAD] + both[HEAD:] + extra) / total
            outs_turn[pl.ds(pl.multiple_of(h * HEAD, HEAD), HEAD), lanes] = result
            lse[h, :, lanes] = jnp.broadcast_to(peak + jnp.log(total), (8, CH))
        return carry

    lax.fori_loop(0, OWN, one_head, 0)


def allowed(low_row, c, size):
    key_at = lax.broadcasted_iota(jnp.int32, (size, CH), 0).astype(f32)
    query_at = (lax.broadcasted_iota(jnp.int32, (1, CH), 1) + c * CH).astype(f32)
    begin = low_row[:1, c * CH : (c + 1) * CH]
    return (key_at >= begin) & (key_at <= query_at)


def proj_kernel(scal, *refs):
    toks, heads, parts, refs = refs[:4], refs[4:8], refs[8:12], refs[12:]
    vec, wh, wl, heads_h, heads_l, norm_h, norm_l, mixed, hat, scale, weight, joined = refs
    mine = scal[0]
    for r in range(SEQ):
        at = jnp.bitwise_xor(mine, r)
        for d in range(GROUPS):
            weight[pl.ds(pl.multiple_of(d * ROWS + at * SUB, 8), SUB), :] = parts[r][
                d * SUB : (d + 1) * SUB, :
            ]
        joined[rows_at(at, QUARTER), :] = heads[r][...]
    wh[...], wl[...] = halves(weight[...])
    heads_h[...], heads_l[...] = halves(joined[:, rows_at(mine, CH)])
    gain, shift = piece(vec, 5), piece(vec, 6)
    for r in range(SEQ):
        at = rows_at(jnp.bitwise_xor(mine, r), CH)
        a, b = halves(joined[:, at].T)
        total = toks[r][:CH, :] + dot3(a, b, wh[...], wl[...], NN)
        total = total + piece(vec, 4)
        normed, size = norm_stats(total)
        norm_h[r], norm_l[r] = halves(normed * gain + shift)
        if r == 0:
            mixed[...] = total
            hat[...] = normed
            scale[...] = jnp.broadcast_to(size, (CH, 128))


def hidden_kernel(scal, norm_h, norm_l, *refs):
    blocks, vec, acts_h, acts_l, slope, winh, winl = refs[:GROUPS], *refs[GROUPS:]
    mine = scal[0]
    for k in range(GROUPS):
        at = rows_at(owner(scal, k), ROWS)
        winh[at, :], winl[at, :] = halves(blocks[k][:ROWS, :])
    marks = [16 + d for d in range(GROUPS)]
    table = jnp.concatenate([vec[m // 3, m % 3 : m % 3 + 1, :] for m in marks], axis=0)
    table = pltpu.roll(table, lax.rem(HALF_VEC - mine * ROWS, HALF_VEC), 1)[:, :ROWS]
    bias = jnp.concatenate([table[d : d + 1] for d in range(GROUPS)], axis=1)
    for r in range(SEQ):
        at = slice(r * CH, (r + 1) * CH)
        hidden = dot3(norm_h[r], norm_l[r], winh[...], winl[...], NN) + bias
        inner = jnp.tanh(gelu_scale * (hidden + gelu_cubic * hidden * hidden * hidden))
        acts_h[at, :], acts_l[at, :] = halves(0.5 * hidden * (1.0 + inner))
        slope[at, :] = 0.5 * (1.0 + inner) + 0.5 * hidden * (1.0 - inner * inner) * gelu_scale * (
            1.0 + 3.0 * gelu_cubic * hidden * hidden
        )


def emit_blocks(scal, outs, whole):
    for k in range(GROUPS):
        outs[k][...] = whole[rows_at(owner(scal, k), ROWS), :]


def out_grad_kernel(scal, acts_h, acts_l, *refs):
    grads, (out_h, out_l), outs, whole = refs[:4], refs[4:6], refs[6 : 6 + GROUPS], refs[6 + GROUPS]
    for r in range(SEQ):
        at = slice(r * CH, (r + 1) * CH)
        out_h[at, :], out_l[at, :] = halves(grads[r][...])
    whole[...] = dot3(acts_h[...], acts_l[...], out_h[...], out_l[...], TN)
    emit_blocks(scal, outs, whole)


def hidden_back_kernel(scal, out_h, out_l, slope, winh, winl, *refs):
    blocks, rest, refs = refs[:GROUPS], refs[GROUPS], refs[GROUPS + 1 :]
    hid_h, hid_l, wouth, woutl, bias_sum = refs[:5]
    parts = refs[5:]
    for k in range(GROUPS):
        at = rows_at(owner(scal, k), ROWS)
        block = rest[...] if k == HALF else blocks[k][ROWS:, :]
        wouth[at, :], woutl[at, :] = halves(block)
    sums = jnp.zeros((1, D), f32)
    for r in (1, 3, 2, 0):
        at = slice(r * CH, (r + 1) * CH)
        back = dot3(out_h[at, :], out_l[at, :], wouth[...], woutl[...], NT) * slope[at, :]
        sums = sums + jnp.sum(back, axis=0, keepdims=True)
        bh, bl = halves(back)
        hid_h[at, :], hid_l[at, :] = bh, bl
        parts[r][...] = dot3(bh, bl, winh[...], winl[...], NT)
    bias_sum[...] = jnp.broadcast_to(sums, (8, D))


def in_grad_kernel(scal, norm_h, norm_l, hid_h, hid_l, *refs):
    outs, whole = refs[:GROUPS], refs[GROUPS]
    flat = lambda ref: ref[...].reshape(LEN, D)
    whole[...] = dot3(flat(norm_h), flat(norm_l), hid_h[...], hid_l[...], TN)
    emit_blocks(scal, outs, whole)


def ffn_out_kernel(scal, acts_h, acts_l, wouth, woutl, *parts):
    for r in (1, 3, 2, 0):
        at = slice(r * CH, (r + 1) * CH)
        parts[r][...] = dot3(acts_h[at, :], acts_l[at, :], wouth[...], woutl[...], NN)


def output_kernel(scal, mixed, one, two, three, vec, output):
    output[...] = mixed[...] + (one[...] + two[...] + three[...]) + piece(vec, 7)


def proj_back_kernel(scal, one, two, three, hat, scale, vec, grad_out, wh, wl, mixed_grad, sums, *parts):
    mine = scal[0]
    normed = one[...] + two[...] + three[...]
    back = norm_back(hat[...], scale[:, :1], piece(vec, 5), normed)
    total = grad_out[...] + back
    mixed_grad[...] = total
    a, b = halves(total)
    for r in range(SEQ):
        at = rows_at(jnp.bitwise_xor(mine, r), QUARTER)
        parts[r][...] = dot3(wh[at, :], wl[at, :], a, b, NT)
    add = lambda v: jnp.sum(v, axis=0, keepdims=True)
    sums[...] = jnp.concatenate(
        [add(total), add(normed * hat[...]), add(normed), add(grad_out[...]), jnp.zeros((4, D), f32)],
        axis=0,
    )


def proj_grad_kernel(scal, heads_h, heads_l, mixed_grad, *refs):
    outs, whole = refs[:-1], refs[-1]
    mine = scal[0]
    gh, gl = halves(mixed_grad[...])
    whole[...] = dot3(heads_h[...], heads_l[...], gh, gl, NN)
    for r in range(SEQ):
        at = jnp.bitwise_xor(mine, r)
        for d in range(GROUPS):
            outs[r][d * SUB : (d + 1) * SUB, :] = whole[
                pl.ds(pl.multiple_of(d * ROWS + at * SUB, 8), SUB), :
            ]


def back_kernel(scal, *refs):
    grads, refs = refs[:4], refs[4:]
    kcat, qturn, vcat, qpair, kturn, outs_turn, lse, low_row = refs[:8]
    joined_h, joined_l, joined_sums = refs[8:11]
    gturn, gpair, dots, key_sum, value_sum, query_turn = refs[11:]
    mine = scal[0]

    for r in range(SEQ):
        at = rows_at(jnp.bitwise_xor(mine, r), CH)
        turned = grads[r][...]
        grad = jnp.concatenate([turned, jnp.zeros((HEAD, CH), f32)], axis=0).T
        pairs = lane_pairs(grad[:, :128], grad[:, 128:])
        for h in range(OWN):
            gpair[h, at, :] = pairs[h]
            part = turned[HEAD * h : HEAD * (h + 1)]
            dots[h, :, at] = jnp.broadcast_to(
                jnp.sum(part * outs_turn[HEAD * h : HEAD * (h + 1), at], axis=0, keepdims=True), (8, CH)
            )
            a, b = halves(part)
            gturn[h, :, at] = jnp.concatenate([a, a, b, b], axis=0)

    key_sum[...] = jnp.zeros_like(key_sum)
    value_sum[...] = jnp.zeros_like(value_sum)

    def one_head(h, carry):
        for c in range(SEQ):
            size = CH * (c + 1)
            lanes = slice(c * CH, (c + 1) * CH)
            score = dot(kcat[h, :size, :], qturn[h, :, lanes], NN)
            weight = jnp.where(allowed(low_row, c, size), jnp.exp(score - lse[h, :1, lanes]), 0.0)
            back = dot(vcat[h, :size, :], gturn[h, :, lanes], NN)
            score_back = weight * (back - dots[h, :1, lanes])
            a, b = halves(weight)
            pair = gpair[h, lanes, :]
            value_sum[h, :size, :] += dot(a, pair, NN) + dot(b, pair, NN)
            a, b = halves(score_back)
            pair = qpair[h, lanes, :]
            key_sum[h, :size, :] += dot(a, pair, NN) + dot(b, pair, NN)
            turned = dot(kturn[h, :, :size], a, NN) + dot(kturn[h, :, :size], b, NN)
            query_turn[h, :, lanes] = (turned[:HEAD] + turned[HEAD:]) * HEAD ** (-0.5)
        return carry

    lax.fori_loop(0, OWN, one_head, 0)

    column_sums = jnp.zeros((1, D), f32)
    low = low_lanes((CH, 128))
    for c in range(SEQ):
        at = slice(c * CH, (c + 1) * CH)
        blank = jnp.zeros((HEAD, CH), f32)
        query = jnp.concatenate([query_turn[h, :, at] for h in range(OWN)] + [blank], axis=0).T
        done = [query]
        for kept in (key_sum, value_sum):
            full = [kept[h, at, :] for h in range(OWN)]
            full = [v + pltpu.roll(v, HEAD, 1) for v in full]
            done.append(jnp.where(low, full[0], full[1]))
            done.append(jnp.where(low, full[2], 0.0))
        joined = jnp.concatenate(done, axis=1)
        column_sums = column_sums + jnp.sum(joined, axis=0, keepdims=True)
        joined_h[at, :], joined_l[at, :] = halves(joined)

    joined_sums[...] = jnp.broadcast_to(column_sums, (8, D))


def qkv_grad_kernel(scal, xh, xl, joined_h, joined_l, joined_sums, wh, wl, vec, *refs):
    proj_one, proj_two, proj_three, sums, bias_sum = refs[:5]
    outs, (whole, rows) = refs[5 : 5 + GROUPS], refs[5 + GROUPS :]
    mine = scal[0]
    column_sums = joined_sums[:1, :]
    core = dot3(xh[...], xl[...], joined_h[...], joined_l[...], TN)
    gain, shift = piece(vec, 0), piece(vec, 1)
    as_column = lambda v: jnp.broadcast_to(v, (128, D)).T[:, :1]
    whole[...] = as_column(gain) * core + as_column(shift) * column_sums
    weights = wh[...].astype(f32) + wl[...].astype(f32)
    gain_grad = jnp.sum(weights * core, axis=1, keepdims=True)
    shift_grad = jnp.sum(weights * column_sums, axis=1, keepdims=True)
    lane = lax.broadcasted_iota(jnp.int32, (D, 128), 1)
    norm_grads = jnp.where(lane == 0, gain_grad, shift_grad).T

    def place(part, scale):
        wide = jnp.concatenate([part[:, :QUARTER], jnp.zeros((1, D - QUARTER), f32)], axis=1)
        wide = jnp.broadcast_to(wide, (8, D))
        return pltpu.roll(wide, mine * QUARTER, 1)[:1]

    entries = [
        norm_grads[0:1],
        norm_grads[1:2],
        place(column_sums[:, :CH], 1.0),
        place(column_sums[:, 2 * CH :], 1.0),
        sums[0:1],
        sums[1:2],
        sums[2:3],
        sums[3:4],
    ]
    lines = [e[:, i * HALF_VEC : (i + 1) * HALF_VEC] for e in entries for i in range(2)]
    bias = jnp.concatenate(
        [bias_sum[:1, d * ROWS : (d + 1) * ROWS] for d in range(GROUPS)], axis=0
    )
    bias = jnp.concatenate([bias, jnp.zeros((GROUPS, HALF_VEC - ROWS), f32)], axis=1)
    bias = pltpu.roll(bias, mine * ROWS, 1)
    lines = lines + [bias[d : d + 1] for d in range(GROUPS)]
    filler = jnp.zeros((5, HALF_VEC), f32)
    for d in range(GROUPS):
        rows[d] = jnp.concatenate(lines[3 * d : 3 * d + 3] + [filler], axis=0)

    for k in range(GROUPS):
        at = owner(scal, k)
        outs[k][:ROWS, :] = whole[rows_at(at, ROWS), :]
        here = pl.ds(pl.multiple_of(at * SUB, 8), SUB)
        proj = proj_one[here, :] + proj_two[here, :] + proj_three[here, :]
        for group in range(SEQ):
            for part in range(3):
                lane_at = HEAD * (3 * group + part)
                outs[k][
                    group * SUB : (group + 1) * SUB, part * CH + QUARTER : (part + 1) * CH
                ] = proj[:, lane_at : lane_at + HEAD]
        outs[k][ROWS:, :HALF_VEC] = rows[at]
        outs[k][ROWS:, HALF_VEC:] = jnp.zeros((8, HALF_VEC), f32)


def pre_back_kernel(scal, joined_h, joined_l, wh, wl, *parts):
    mine = scal[0]
    for r in (1, 3, 2, 0):
        at = rows_at(jnp.bitwise_xor(mine, r), CH)
        parts[r][...] = dot3(joined_h[at, :], joined_l[at, :], wh[...], wl[...], NT)


def input_grad_kernel(scal, tokens, one, two, three, vec, mixed_grad, result):
    hat, scale = norm_stats(tokens[...])
    grad = one[...] + two[...] + three[...]
    result[...] = mixed_grad[...] + norm_back(hat, scale, piece(vec, 0), grad)


def total_square(value):
    return jnp.sum(jnp.sum(value * value, axis=0, keepdims=True), axis=1, keepdims=True)


def second_squares_kernel(scal, *refs):
    parts, squares = refs[:8], refs[8]
    total = sum(total_square(part[...]) for part in parts)
    squares[...] = jnp.broadcast_to(total, (8, 128))


def first_squares_kernel(scal, one, two, three, four, before, squares):
    parts = (one, two, three, four)
    total = sum(total_square(part[:ROWS, :]) for part in parts)
    line = sum(part[ROWS:, :HALF_VEC] for part in parts)
    squares[...] = before[...] + (total + total_square(line))


def stage_kernel(scal, *refs):
    sources, targets, sems = refs[:15], refs[15:30], refs[30]
    copies = [
        pltpu.make_async_copy(source, target, sems.at[i])
        for i, (source, target) in enumerate(zip(sources, targets))
    ]
    for copy in copies:
        copy.start()
    for copy in copies:
        copy.wait()


def adamw_kernel(scal, squares, *refs):
    firsts, ins, outs, refs = refs[:4], refs[4:8], refs[8:12], refs[12:]
    states, clip, finals, news = refs[:15], refs[15], refs[16:31], refs[31:46]
    first, second, sems = refs[46:]
    send = lambda number: [
        pltpu.make_async_copy(news[i], finals[i], sems.at[i]) for i in range(3 * number, 3 * number + 3)
    ]
    mine = scal[0]
    norm = jnp.sqrt(squares[...])
    clip[...] = norm
    factor = (clip_limit / jnp.maximum(norm, clip_limit))[:1, :1]
    for r in range(SEQ):
        at = jnp.bitwise_xor(mine, r)
        first[at] = firsts[r][:ROWS, :]
        second[at, :ROWS] = ins[r][...]
        second[at, ROWS:] = outs[r][...]

    def update(number, spot, grad, rate, decay):
        held = [states[3 * number + i][spot] for i in range(3)]
        fresh = adamw_update(*held, factor * grad, rate, decay)
        for i in range(3):
            news[3 * number + i][spot] = fresh[i]

    def finish(number):
        for copy in send(number):
            copy.start()

    line = sum(firsts[r][ROWS:, :HALF_VEC] for r in range(SEQ))
    for i in range(3):
        for j in range(3):
            spot = (slice(3 * i + j, 3 * i + j + 1), slice(None))
            update(0, spot, line[i : i + 1, 128 * j : 128 * (j + 1)], vector_rate, 0.0)
    finish(0)
    every = slice(None)
    for part in range(3):
        grad = jnp.concatenate(
            [first[j][:, part * CH : part * CH + QUARTER] for j in range(SEQ)], axis=1
        )
        update(1, (every, slice(part * D, (part + 1) * D)), grad, matrix_rate, weight_decay)
    finish(1)
    for j in range(SEQ):
        grad = jnp.concatenate(
            [
                first[j][group * SUB : (group + 1) * SUB, part * CH + QUARTER : (part + 1) * CH]
                for group in range(SEQ)
                for part in range(3)
            ],
            axis=1,
        )
        update(2, (slice(j * SUB, (j + 1) * SUB), every), grad, matrix_rate, weight_decay)
    finish(2)
    for d in range(GROUPS):
        grad = jnp.concatenate(
            [second[j][:ROWS, d * ROWS : (d + 1) * ROWS] for j in range(SEQ)], axis=1
        )
        update(3, (every, slice(d * HALF_VEC, (d + 1) * HALF_VEC)), grad, matrix_rate, weight_decay)
    finish(3)
    for j in range(SEQ):
        update(
            4, (slice(j * ROWS, (j + 1) * ROWS), every), second[j][ROWS:, :], matrix_rate, weight_decay
        )
    finish(4)
    for number in range(5):
        for copy in send(number):
            copy.wait()


def adamw_update(weight, first, second, grad, rate, decay):
    new_first = beta_one * first + (1.0 - beta_one) * grad
    new_second = beta_two * second + (1.0 - beta_two) * grad * grad
    first_hat = new_first / (1.0 - beta_one**STEP)
    second_hat = new_second / (1.0 - beta_two**STEP)
    new_weight = weight - rate * (first_hat / (jnp.sqrt(second_hat) + adam_eps) + decay * weight)
    return (new_first, new_second, new_weight)


def ring_tables(count):
    evens = [2 * i for i in range(count // 2)]
    order = evens + [i + 1 for i in reversed(evens)]
    place = [0] * count
    for position, device in enumerate(order):
        place[device] = position
    right = [(order[i], order[(i + 1) % count]) for i in range(count)]
    left = [(b, a) for a, b in right]
    return order, place, right, left


class RingGather:
    def __init__(self, block, name):
        _, _, self.right, self.left = ring_tables(GROUPS)
        self.got, self.name, self.at = {0: block}, name, 0

    def step(self, after=()):
        places = (-self.at % GROUPS, self.at)
        if after:
            for place in set(places):
                self.got[place] = gate(self.got[place], after)
        forth, back = (self.got[place] for place in places)
        self.at += 1
        self.got[GROUPS - self.at] = move(forth, "dp", self.right, f"{self.name}_right_{self.at}")
        self.got[self.at] = move(back, "dp", self.left, f"{self.name}_left_{self.at}")
        return [forth, back]

    def last(self, cut=0):
        forth, back = self.got[GROUPS - self.at], self.got[self.at]
        if not cut:
            self.got[HALF] = move(forth, "dp", self.right, f"{self.name}_right_{HALF}")
            return None
        self.got[HALF] = move(forth[:cut], "dp", self.right, f"{self.name}_right_{HALF}")
        return move(back[cut:], "dp", self.left, f"{self.name}_left_{HALF}")

    def blocks(self):
        return [self.got[k] for k in range(GROUPS)]


class RingScatter:
    def __init__(self, blocks, name, flip=False):
        _, _, self.right, self.left = ring_tables(GROUPS)
        self.blocks = blocks
        if flip:
            self.right, self.left = self.left, self.right
            self.blocks = [blocks[-k % GROUPS] for k in range(GROUPS)]
        self.name, self.back, self.at = name, None, HALF
        self.forth = move(self.blocks[HALF], "dp", self.right, f"{name}_right_1")

    def step(self, after=()):
        hold = lambda block: gate(block, after) if after else block
        self.at -= 1
        forth = self.forth + hold(self.blocks[self.at])
        back = hold(self.blocks[GROUPS - self.at])
        if self.back is not None:
            back = self.back + back
        number = HALF + 1 - self.at
        self.forth = move(forth, "dp", self.right, f"{self.name}_right_{number}")
        self.back = move(back, "dp", self.left, f"{self.name}_left_{number}")
        return [forth, back]

    def result(self, after=()):
        return self.forth + self.back + (gate(self.blocks[0], after) if after else self.blocks[0])


def move(block, axis, pairs, name):
    with jax.named_scope(name):
        return lax.ppermute(block, axis, pairs)


def swap(block, bits, name):
    return move(block, "seq", [(i, i ^ bits) for i in range(SEQ)], f"{name}_{bits}")


def gather_seq(block, name):
    across = swap(block, 2, name)
    core = swap(block, 1, name)
    return [block, core, across, swap(across, 1, f"{name}_2")]


def exchange_seq(parts, name):
    return [parts[0]] + [swap(parts[r], r, name) for r in range(1, SEQ)]


def scatter_core(parts, name):
    return parts[0], swap(parts[1], 1, f"{name}_own"), parts[2], swap(parts[3], 1, f"{name}_across")


def ordered(blocks, mine):
    stack = jnp.stack(blocks, axis=0)
    return [lax.dynamic_index_in_dim(stack, mine ^ j, 0, keepdims=False) for j in range(len(blocks))]


def local(
    tokens,
    cotangent,
    segment_ids,
    valid,
    vectors,
    vec_first,
    vec_second,
    w_qkv,
    qkv_first,
    qkv_second,
    w_proj,
    proj_first,
    proj_second,
    w_in,
    in_first,
    in_second,
    w_out,
    out_first,
    out_second,
):
    dp_parts = lax.axis_size("dp")
    ring = dp_parts == GROUPS
    mine = lax.axis_index("seq")
    home = lax.axis_index("dp")
    rows = w_qkv.shape[0]
    units = w_out.shape[0] // SEQ
    far, near = home // 2, home % 2
    position = jnp.where(near > 0, GROUPS - 1 - far, far)
    scal = jnp.stack([mine, position, jnp.full_like(mine, 1 if ring else 0)]).astype(jnp.int32)
    flat_in = tokens.reshape(CH, D)
    chunk, tall, square = shape(CH, D), shape(LEN, D, kind=bf16), shape(D, D, kind=bf16)

    if ring:
        first, packed = run(
            pack_first_kernel,
            scal,
            [w_qkv, w_proj, vectors.reshape(9, 128), segment_ids, valid, flat_in],
            [shape(ROWS + 8, D), shape(CH + 8, D)],
            scratch=[
                pltpu.VMEM((3, ROWS, CH), f32),
                pltpu.VMEM((SUB, D), f32),
                pltpu.VMEM((9, 128), f32),
                pltpu.VMEM((2, 1, CH), jnp.int32),
            ],
            sems=8,
            far_args=range(6),
            room=54,
            name="pack_first", work=3.0,
        )
        ring_first = RingGather(first, "first")
        for _ in range(HALF - 1):
            ring_first.step()
        ring_first.last()
        firsts = ring_first.blocks()
        (second,) = run(
            pack_second_kernel,
            scal,
            [w_in, w_out],
            [shape(2 * ROWS, D)],
            name="pack_second", work=3.0,
            after=[firsts[GROUPS - 1]],
        )
        ring_second = RingGather(second, "second")
        ring_second.step([firsts[HALF]])
    else:
        padded = jnp.pad(w_qkv, ((0, 0), (0, CH)))
        own = lambda part: lax.dynamic_slice_in_dim(padded, part * D + mine * QUARTER, CH, 1)
        first = jnp.concatenate([own(0), own(1), own(2)], axis=1)
        first = lax.all_gather(first, "dp", axis=0, tiled=True).reshape(GROUPS, ROWS, D)
        all_vec = lax.all_gather(vectors, "dp", axis=0, tiled=True).reshape(GROUPS, 3, HALF_VEC)
        first = jnp.concatenate([first, jnp.pad(all_vec, ((0, 0), (0, 5), (0, D - HALF_VEC)))], axis=1)
        firsts = [first[k] for k in range(GROUPS)]
        in_part = lax.dynamic_index_in_dim(
            w_in.reshape(rows, dp_parts, SEQ, units), mine, 2, keepdims=False
        ).reshape(rows, D)
        out_part = lax.dynamic_slice_in_dim(w_out, mine * units, units, 0)
        second = jnp.concatenate(
            [
                lax.all_gather(part, "dp", axis=0, tiled=True).reshape(GROUPS, ROWS, D)
                for part in (in_part, out_part)
            ],
            axis=1,
        )
        seconds = [second[k] for k in range(GROUPS)]
        seconds[HALF], second_rest = second[HALF, :ROWS], second[HALF, ROWS:]
        marks = jnp.where(valid > 0, segment_ids, -1).astype(f32)
        packed = jnp.concatenate([flat_in, jnp.pad(marks, ((0, 7), (0, D - CH)))], axis=0)
    toks = gather_seq(packed, "tokens")
    (grad_out,) = run(
        mask_kernel, scal, [cotangent.reshape(CH, D), valid], [chunk], name="mask", work=2.0, after=[toks[2]]
    )
    grads_row = gather_seq(grad_out, "cotangent")

    qkv_h, qkv_l, vec, proj = run(
        weights_kernel,
        scal,
        firsts,
        [square, square, shape(GROUPS, 8, HALF_VEC), shape(GROUPS * SUB, D)],
        name="weights", work=3.0,
    )
    if ring:
        proj_parts = gather_seq(proj, "w_proj")
    else:
        full = lax.all_gather(w_proj, "dp", axis=0, tiled=True).reshape(GROUPS, SEQ, SUB, D)
        proj_parts = [
            lax.dynamic_index_in_dim(full, mine ^ r, 1, keepdims=False).reshape(GROUPS * SUB, D)
            for r in range(SEQ)
        ]
    hat_h, hat_l, kcat, qturn, vcat, qpair, kturn, vturn, low_row = run(
        front_kernel,
        scal,
        toks + [qkv_h, qkv_l, vec],
        [
            tall,
            tall,
            shape(OWN, LEN, 256, kind=bf16),
            shape(OWN, 256, LEN, kind=bf16),
            shape(OWN, LEN, 256, kind=bf16),
            shape(OWN, LEN, 128, kind=bf16),
            shape(OWN, 128, LEN, kind=bf16),
            shape(OWN, 128, LEN, kind=bf16),
            shape(8, LEN),
        ],
        scratch=[pltpu.VMEM((SEQ, 8, CH), f32)],
        name="front", work=8.0,
        after=[grads_row[2]],
    )
    if ring:
        second_sent = ring_second.step([low_row])
    heads, lse = run(
        attend_kernel,
        scal,
        [kcat, qturn, vturn, low_row],
        [shape(QUARTER, LEN), shape(OWN, 8, LEN)],
        name="attend", work=8.0,
        after=[proj_parts[2], *second_sent] if ring else [],
    )
    if ring:
        ring_second.step([lse])
        second_rest = ring_second.last(ROWS)
        seconds = ring_second.blocks()
    wide = shape(D, CH, kind=bf16)
    split = shape(SEQ, CH, D, kind=bf16)
    proj_h, proj_l, heads_h, heads_l, norm_h, norm_l, mixed, hat_two, scale_two = run(
        proj_kernel,
        scal,
        toks + gather_seq(heads, "heads") + proj_parts + [vec],
        [square, square, wide, wide, split, split, chunk, chunk, shape(CH, 128)],
        scratch=[pltpu.VMEM((D, D), f32), pltpu.VMEM((D, LEN), f32)],
        name="proj", work=8.0,
    )

    block = shape(ROWS, D)
    acts_h, acts_l, slope, in_wh, in_wl = run(
        hidden_kernel,
        scal,
        [norm_h, norm_l] + seconds + [vec],
        [tall, tall, shape(LEN, D), square, square],
        name="hidden", work=8.0,
    )
    done = run(
        out_grad_kernel,
        scal,
        [acts_h, acts_l] + grads_row,
        [tall, tall] + [block] * GROUPS,
        scratch=[pltpu.VMEM((D, D), f32)],
        name="out_grad", work=5.0,
    )
    out_h, out_l = done[:2]
    out_grads = list(done[2:])
    if ring:
        ring_out = RingScatter(out_grads, "out_grad")
    done = run(
        hidden_back_kernel,
        scal,
        [out_h, out_l, slope, in_wh, in_wl] + seconds + [second_rest],
        [tall, tall, square, square, shape(8, D)] + [chunk] * SEQ,
        name="hidden_back", work=11.0,
        after=out_grads[:1],
    )
    hid_h, hid_l, out_wh, out_wl, bias_sum = done[:5]
    parts = list(done[5:])
    if ring:
        parts[3] = gate(parts[3], ring_out.step())
    norm_own, norm_near, norm_across, norm_far = scatter_core(parts, "norm_grad")
    norm_pair = norm_across + norm_far
    norm_last = swap(norm_pair, 2, "norm_grad")
    in_grads = list(
        run(
            in_grad_kernel,
            scal,
            [norm_h, norm_l, hid_h, hid_l],
            [block] * GROUPS,
            scratch=[pltpu.VMEM((D, D), f32)],
            name="in_grad", work=5.0,
            after=[norm_pair],
        )
    )
    if ring:
        ring_in = RingScatter(in_grads, "in_grad", flip=True)
        out_sent = ring_out.step()
        in_sent = ring_in.step()
    done = run(
        proj_back_kernel,
        scal,
        [norm_own, norm_near, norm_last, hat_two, scale_two, vec, grad_out, proj_h, proj_l],
        [chunk, shape(8, D)] + [shape(QUARTER, CH)] * SEQ,
        name="proj_back", work=5.0,
        after=out_sent + in_sent if ring else [],
    )
    mixed_grad, sums = done[:2]
    head_grads = exchange_seq(list(done[2:]), "head_grad")
    if ring:
        out_sent = ring_out.step([mixed_grad])
        in_sent = ring_in.step([mixed_grad])
    proj_grads = run(
        proj_grad_kernel,
        scal,
        [heads_h, heads_l, mixed_grad],
        [shape(GROUPS * SUB, D)] * SEQ,
        scratch=[pltpu.VMEM((D, D), f32)],
        name="proj_grad", work=4.0,
        after=[*head_grads[1:], *out_sent, *in_sent] if ring else [],
    )
    wait = [head_grads[3], head_grads[2]]
    if ring:
        proj_own, proj_near, proj_across, proj_far = scatter_core(proj_grads, "proj_grad")
        proj_pair = gate(proj_across, wait) + proj_far
        proj_last = swap(proj_pair, 2, "proj_grad")
    else:
        proj_own = proj_near = proj_last = proj_pair = proj_grads[0]
    joined_h, joined_l, joined_sums = run(
        back_kernel,
        scal,
        head_grads + [kcat, qturn, vcat, qpair, kturn, heads, lse, low_row],
        [tall, tall, shape(8, D)],
        scratch=[
            pltpu.VMEM((OWN, 256, LEN), bf16),
            pltpu.VMEM((OWN, LEN, 128), bf16),
            pltpu.VMEM((OWN, 8, LEN), f32),
            pltpu.VMEM((OWN, LEN, 128), f32),
            pltpu.VMEM((OWN, LEN, 128), f32),
            pltpu.VMEM((OWN, HEAD, LEN), f32),
        ],
        name="back", work=16.0,
        after=[proj_grads[0]],
    )
    if ring:
        shard_out = ring_out.result([joined_sums])
        in_sent = ring_in.step([joined_sums])
    done = run(
        qkv_grad_kernel,
        scal,
        [hat_h, hat_l, joined_h, joined_l, joined_sums, qkv_h, qkv_l, vec]
        + [proj_own, proj_near, proj_last, sums, bias_sum],
        [shape(ROWS + 8, D)] * GROUPS,
        scratch=[pltpu.VMEM((D, D), f32), pltpu.VMEM((GROUPS, 8, HALF_VEC), f32)],
        name="qkv_grad", work=9.0,
        after=[*in_sent, shard_out] if ring else [],
    )
    first_grads = list(done)
    if ring:
        ring_first = RingScatter(first_grads, "first_grad")
        shard_in = ring_in.result([first_grads[0]])
        out_all = gather_seq(shard_out, "out_shard")
        in_all = gather_seq(shard_in, "in_shard")
        first_sent = ring_first.step()
    pre_parts = run(
        pre_back_kernel,
        scal,
        [joined_h, joined_l, qkv_h, qkv_l],
        [chunk] * SEQ,
        name="pre_back", work=7.0,
        after=[shard_in, *first_sent] if ring else [],
    )
    pre_parts = list(pre_parts)
    if ring:
        first_sent = ring_first.step()
        pre_parts[3] = gate(pre_parts[3], first_sent)
    pre_own, pre_near, pre_across, pre_far = scatter_core(pre_parts, "pre_grad")
    if ring:
        pre_across = gate(pre_across, [in_all[2]])
    pre_last = swap(pre_across + pre_far, 2, "pre_grad")
    states = [vectors, vec_first, vec_second, w_qkv, qkv_first, qkv_second, w_proj, proj_first, proj_second]
    states = states + [w_in, in_first, in_second, w_out, out_first, out_second]
    if ring:
        held = [v.reshape(9, 128) for v in states[:3]] + states[3:]
        held = run(
            stage_kernel,
            scal,
            held,
            [shape(*v.shape) for v in held],
            sems=15,
            far_args=range(15),
            name="stage", work=4.0,
            after=[pre_parts[0]],
        )
    out_parts = run(
        ffn_out_kernel,
        scal,
        [acts_h, acts_l, out_wh, out_wl],
        [chunk] * SEQ,
        name="ffn_out", work=7.0,
        after=first_sent if ring else [],
    )
    out_parts = list(out_parts)
    if ring:
        ring_first.step()
        shard_first = ring_first.result()
        out_parts[3] = gate(out_parts[3], [shard_first])
    out_own, out_near, out_across, out_far = scatter_core(out_parts, "output")
    out_pair = out_across + out_far
    (input_grad,) = run(
        input_grad_kernel,
        scal,
        [flat_in, pre_own, pre_near, pre_last, vec, mixed_grad],
        [chunk],
        name="input_grad", work=3.0,
    )

    if ring:
        (squares,) = run(
            second_squares_kernel, scal, in_all + out_all, [shape(8, 128)], name="second_squares", work=2.0
        )
        first_all = gather_seq(gate(shard_first, [pre_last, out_parts[0], held[3]]), "first_shard")
        out_pair = gate(out_pair, [first_all[2]])
        (squares,) = run(
            first_squares_kernel,
            scal,
            first_all + [squares],
            [shape(8, 128)],
            name="first_squares", work=2.0,
            after=[input_grad],
        )
        out_last = swap(out_pair, 2, "output")
        for bits in (1, 2, 4):
            pairs = [(i, i ^ bits) for i in range(GROUPS)]
            squares = squares + move(squares, "dp", pairs, "squares")
        done = run(
            adamw_kernel,
            scal,
            [squares] + first_all + in_all + out_all + list(held),
            [shape(8, 128)] + [shape(*v.shape) for v in held],
            scratch=[pltpu.VMEM(v.shape, f32) for v in held]
            + [pltpu.VMEM((SEQ, ROWS, D), f32), pltpu.VMEM((SEQ, 2 * ROWS, D), f32)],
            sems=15,
            far_outs=range(1, 16),
            name="adamw", work=10.0,
        )
        new = [v.reshape(-1) for v in done[1:4]] + list(done[4:])
        clip_norm = done[0][0, 0]
    else:
        out_last = swap(out_pair, 2, "output")
        by_group = jnp.stack(first_grads)
        shard_first = lax.psum_scatter(
            by_group[:, :ROWS].reshape(D, D), "dp", scatter_dimension=0, tiled=True
        )
        proj_full = jnp.stack([p.reshape(GROUPS, SUB, D) for p in ordered(proj_grads, mine)], axis=1)
        proj_grad = lax.psum(
            lax.psum_scatter(proj_full.reshape(D, D), "dp", scatter_dimension=0, tiled=True), "seq"
        )
        all_vec = lax.psum(by_group[:, ROWS : ROWS + 3, :HALF_VEC], ("dp", "seq")).reshape(-1)
        vec_grad = lax.dynamic_slice_in_dim(all_vec, home * vectors.shape[0], vectors.shape[0])
        joined = lax.all_gather(shard_first, "seq", axis=0, tiled=False)
        qkv_grad = jnp.concatenate(
            [joined[j, :, i * CH : i * CH + QUARTER] for i in range(3) for j in range(SEQ)], axis=1
        )
        shard_in, shard_out = (
            lax.psum_scatter(jnp.concatenate(parts, axis=0), "dp", scatter_dimension=0, tiled=True)
            for parts in (in_grads, out_grads)
        )
        in_all = lax.all_gather(shard_in, "seq", axis=0, tiled=False)
        in_grad = in_all.reshape(SEQ, rows, dp_parts, units).transpose(1, 2, 0, 3).reshape(rows, -1)
        out_grad = lax.all_gather(shard_out, "seq", axis=0, tiled=True)
        total = sum(jnp.sum(g * g) for g in (qkv_grad, proj_grad, in_grad, out_grad, vec_grad))
        total = lax.psum(total, "dp")
        clip_norm = jnp.sqrt(total)
        factor = clip_limit / jnp.maximum(clip_norm, clip_limit)
        grads = (vec_grad, qkv_grad, proj_grad, in_grad, out_grad)
        new = []
        for number, grad in enumerate(grads):
            rate, decay = (matrix_rate, weight_decay) if number else (vector_rate, 0.0)
            new.extend(adamw_update(*states[3 * number : 3 * number + 3], factor * grad, rate, decay))
    (output,) = run(
        output_kernel, scal, [mixed, out_own, out_near, out_last, vec], [chunk], name="output", work=2.0
    )
    return (output.reshape(tokens.shape), input_grad.reshape(tokens.shape), clip_norm, *new)


def solution(mesh):
    row = P("dp", "seq", None)
    mark = P("dp", "seq")
    vec = P("dp")
    mat = P("dp", None)
    return jax.shard_map(
        local,
        mesh=mesh,
        in_specs=(row, row, mark, mark) + (vec,) * 3 + (mat,) * 12,
        out_specs=(row, row, P()) + (vec,) * 3 + (mat,) * 12,
        check_vma=False,
    )
```

```python
import functools
import math

import jax
import jax.numpy as jnp
from jax import lax
from jax.experimental import pallas as pl
from jax.experimental.pallas import tpu as pltpu
from jax.sharding import PartitionSpec as P

D = 768
HEADS = 12
HEAD = 64
STEP = 10
CH = 256
LEN = 1024
SEQ = 4
QUARTER = D // SEQ
OWN = HEADS // SEQ
GROUPS = 8
ROWS = D // GROUPS
SUB = ROWS // SEQ
HALF = GROUPS // 2
HALF_VEC = D // 2
VEC_ROWS = 24

f32 = jnp.float32
bf16 = jnp.bfloat16
masked_score = -1e30
norm_eps = 1e-05
clip_limit = 1.0
beta_one = 0.9
beta_two = 0.999
adam_eps = 1e-08
matrix_rate = 0.02
vector_rate = 0.4
weight_decay = 0.01
gelu_scale = 0.7978845608028654
gelu_cubic = 0.044715

COST = 1e9

WHOLE = pl.BlockSpec(memory_space=pltpu.VMEM)
SCALARS = pl.BlockSpec(memory_space=pltpu.SMEM)
NN = ((1,), (0,))
NT = ((1,), (1,))
TN = ((0,), (0,))


def shape(*dims, kind=f32):
    return jax.ShapeDtypeStruct(dims, kind)


def run(
    kernel, scal, args, outs, scratch=(), sems=0, far_args=(), far_outs=(), room=10, work=1.0, name=None, after=()
):
    args, after = list(args), list(after)
    held = sum(math.prod(v.shape) * jnp.dtype(v.dtype).itemsize for v in scratch)
    anywhere, far = pl.BlockSpec(memory_space=pl.ANY), pl.BlockSpec(memory_space=pltpu.HBM)
    scratch = list(scratch) + ([pltpu.SemaphoreType.DMA((sems,))] if sems else [])

    def body(scal_ref, *refs):
        kernel(scal_ref, *refs[: len(args)], *refs[len(args) + len(after) :])

    return pl.pallas_call(
        body,
        out_shape=tuple(outs),
        in_specs=[SCALARS]
        + [far if i in far_args else WHOLE for i in range(len(args))]
        + [anywhere] * len(after),
        out_specs=tuple(far if i in far_outs else WHOLE for i in range(len(outs))),
        scratch_shapes=scratch,
        compiler_params=pltpu.CompilerParams(vmem_limit_bytes=held + (room << 20)),
        cost_estimate=pl.CostEstimate(
            flops=int(work * COST), bytes_accessed=1, transcendentals=0
        ),
        name=name,
    )(scal, *args, *after)


def gate(value, after):
    anywhere = pl.BlockSpec(memory_space=pl.ANY)
    return pl.pallas_call(
        lambda *refs: None,
        out_shape=shape(*value.shape, kind=value.dtype),
        in_specs=[anywhere] * (1 + len(after)),
        out_specs=anywhere,
        input_output_aliases={0: 0},
        compiler_params=pltpu.CompilerParams(vmem_limit_bytes=1 << 20),
        name="gate",
    )(value, *after)


def plus(*terms, after=()):
    def body(*refs):
        refs[-1][...] = sum((ref[...] for ref in refs[1 : len(terms)]), refs[0][...])

    return pl.pallas_call(
        body,
        out_shape=shape(*terms[0].shape),
        in_specs=[WHOLE] * len(terms) + [pl.BlockSpec(memory_space=pl.ANY)] * len(after),
        out_specs=WHOLE,
        compiler_params=pltpu.CompilerParams(vmem_limit_bytes=4 << 20),
        cost_estimate=pl.CostEstimate(flops=int(COST), bytes_accessed=1, transcendentals=0),
        name="plus",
    )(*terms, *after)


def split_rows(one, two, cut):
    def body(one_ref, two_ref, top, rest):
        top[...] = one_ref[:cut, :]
        rest[...] = two_ref[cut:, :]

    return pl.pallas_call(
        body,
        out_shape=(shape(cut, one.shape[1]), shape(two.shape[0] - cut, two.shape[1])),
        in_specs=[WHOLE] * 2,
        out_specs=(WHOLE, WHOLE),
        compiler_params=pltpu.CompilerParams(vmem_limit_bytes=4 << 20),
        cost_estimate=pl.CostEstimate(flops=int(COST), bytes_accessed=1, transcendentals=0),
        name="split_rows",
    )(one, two)


def owner(scal, k):
    spot = jnp.bitwise_and(scal[1] + k, GROUPS - 1)
    return jnp.where(scal[2] > 0, jnp.where(spot < HALF, 2 * spot, 2 * GROUPS - 1 - 2 * spot), k)


def halves(value):
    top = value.astype(bf16)
    return top, (value - top.astype(f32)).astype(bf16)


def dot(left, right, dims):
    return lax.dot_general(left, right, (dims, ((), ())), preferred_element_type=f32)


def dot3(lh, ll, rh, rl, dims):
    return dot(lh, rh, dims) + (dot(lh, rl, dims) + dot(ll, rh, dims))


def rows_at(index, size):
    return pl.ds(pl.multiple_of(index * size, size), size)


def piece(vec, number):
    a, b = 2 * number, 2 * number + 1
    return jnp.concatenate(
        [vec[a // 3, a % 3 : a % 3 + 1, :], vec[b // 3, b % 3 : b % 3 + 1, :]], axis=1
    )


def norm_stats(inputs):
    center = inputs - jnp.mean(inputs, axis=-1, keepdims=True)
    spread = jnp.mean(center * center, axis=-1, keepdims=True)
    scale = lax.rsqrt(spread + norm_eps)
    return center * scale, scale


def norm_back(hat, scale, gain, grad):
    inner = grad * gain
    return scale * (
        inner
        - jnp.mean(inner, axis=-1, keepdims=True)
        - hat * jnp.mean(inner * hat, axis=-1, keepdims=True)
    )


def low_lanes(dims):
    return lax.broadcasted_iota(jnp.int32, dims, 1) < HEAD


def lane_pairs(pair, last):
    low = low_lanes(pair.shape)
    roll = lambda v: pltpu.roll(v, HEAD, 1)
    ph = pair.astype(bf16).astype(f32)
    pl_ = pair - ph
    lh = last.astype(bf16).astype(f32)
    ll = last - lh
    return [
        jnp.where(low, ph, roll(pl_)).astype(bf16),
        jnp.where(low, roll(ph), pl_).astype(bf16),
        jnp.where(low, lh, roll(ll)).astype(bf16),
    ]


def row_halves(turned, head):
    part = turned[HEAD * head : HEAD * (head + 1)]
    return halves(part)


def pack_first_kernel(scal, wqkv, wproj, vec, seg, valid, tokens, first, packed, *refs):
    bands, proj, lines, marks, sems = refs
    mine = scal[0]
    aligned = pl.multiple_of(jnp.bitwise_and(mine * QUARTER, -128), 128)
    copies = [
        pltpu.make_async_copy(wqkv.at[:, pl.ds(part * D + aligned, CH)], bands.at[part], sems.at[part])
        for part in range(3)
    ]
    sub = pl.ds(pl.multiple_of(mine * SUB, 8), SUB)
    copies.append(pltpu.make_async_copy(wproj.at[sub, :], proj, sems.at[3]))
    copies.append(pltpu.make_async_copy(vec, lines, sems.at[4]))
    copies.append(pltpu.make_async_copy(seg, marks.at[0], sems.at[5]))
    copies.append(pltpu.make_async_copy(valid, marks.at[1], sems.at[6]))
    copies.append(pltpu.make_async_copy(tokens, packed.at[:CH, :], sems.at[7]))
    for copy in copies:
        copy.start()
    first[ROWS:, :] = jnp.zeros((8, D), f32)
    packed[CH:, :] = jnp.zeros((8, D), f32)
    for copy in copies[:5]:
        copy.wait()
    turn = jnp.where(jnp.bitwise_and(mine, 1) > 0, CH - HEAD, 0)
    for part in range(3):
        turned = pltpu.roll(bands[part], turn, 1)
        first[:ROWS, part * CH : part * CH + QUARTER] = turned[:, :QUARTER]
        for group in range(SEQ):
            lane = HEAD * (3 * group + part)
            first[group * SUB : (group + 1) * SUB, part * CH + QUARTER : (part + 1) * CH] = proj[
                :, lane : lane + HEAD
            ]
        first[ROWS + part : ROWS + part + 1, :HALF_VEC] = jnp.concatenate(
            [lines[3 * part + i : 3 * part + i + 1, :] for i in range(3)], axis=1
        )
    for copy in copies[5:]:
        copy.wait()
    packed[CH : CH + 1, :CH] = jnp.where(marks[1] > 0, marks[0], -1).astype(f32)


def pack_second_kernel(scal, win, wout, second):
    mine = scal[0]
    turn = lax.rem(HALF_VEC - mine * ROWS, HALF_VEC)
    for part in range(GROUPS):
        turned = pltpu.roll(win[:, part * HALF_VEC : (part + 1) * HALF_VEC], turn, 1)
        second[:ROWS, part * ROWS : (part + 1) * ROWS] = turned[:, :ROWS]
    second[ROWS:, :] = wout[pl.ds(pl.multiple_of(mine * ROWS, 8), ROWS), :]


def mask_kernel(scal, cotangent, valid, result):
    keep = jnp.where(valid[...] > 0, 1.0, 0.0).astype(f32)
    column = jnp.broadcast_to(keep, (128, CH)).T[:, :1]
    result[...] = cotangent[...] * column


def weights_kernel(scal, *refs):
    blocks, (wh, wl, vec, proj) = refs[:GROUPS], refs[GROUPS:]
    for k in range(GROUPS):
        at = owner(scal, k)
        block = blocks[k][:ROWS, :]
        here = rows_at(at, ROWS)
        wh[here, :], wl[here, :] = halves(block)
        vec[at] = blocks[k][ROWS:, :HALF_VEC]
        for group in range(SEQ):
            for part in range(3):
                lane = HEAD * (3 * group + part)
                proj[pl.ds(pl.multiple_of(at * SUB, 8), SUB), lane : lane + HEAD] = block[
                    group * SUB : (group + 1) * SUB, part * CH + QUARTER : (part + 1) * CH
                ]


def front_kernel(scal, *refs):
    toks, refs = refs[:4], refs[4:]
    wh, wl, vec = refs[:3]
    xh, xl, kcat, qturn, vcat, qpair, kturn, vturn, low_row, label = refs[3:]
    mine = scal[0]

    gain, shift = piece(vec, 0), piece(vec, 1)
    turn = lax.rem(D - mine * QUARTER, D)
    own = lambda number: pltpu.roll(jnp.broadcast_to(piece(vec, number), (8, D)), turn, 1)[:1, :CH]
    query_bias, value_bias = own(2), own(3)

    for r in range(SEQ):
        nat = jnp.bitwise_xor(mine, r)
        at = rows_at(nat, CH)
        label[nat] = toks[r][CH:, :CH]
        hat, _ = norm_stats(toks[r][:CH, :])
        xh[at, :], xl[at, :] = halves(hat)
        nh, nl = halves(hat * gain + shift)
        joined = dot3(nh, nl, wh[...], wl[...], NN)
        query = (joined[:, :CH] + query_bias) * HEAD ** (-0.5)
        key = joined[:, CH : 2 * CH]
        value = joined[:, 2 * CH :] + value_bias
        keys = lane_pairs(key[:, :128], key[:, 128:])
        values = lane_pairs(value[:, :128], value[:, 128:])
        queries = lane_pairs(query[:, :128], query[:, 128:])
        key_t, value_t, query_t = key.T, value.T, query.T
        for h in range(OWN):
            kcat[h, at, :] = jnp.concatenate([keys[h], keys[h]], axis=1)
            vcat[h, at, :] = jnp.concatenate([values[h], values[h]], axis=1)
            qpair[h, at, :] = queries[h]
            a, b = row_halves(query_t, h)
            qturn[h, :, at] = jnp.concatenate([a, a, b, b], axis=0)
            a, b = row_halves(key_t, h)
            kturn[h, :, at] = jnp.concatenate([a, b], axis=0)
            a, b = row_halves(value_t, h)
            vturn[h, :, at] = jnp.concatenate([a, b], axis=0)

    labels = jnp.concatenate([label[c][:1, :] for c in range(SEQ)], axis=1)
    spot = lax.broadcasted_iota(jnp.int32, (1, LEN), 1).astype(f32)
    begin = jnp.zeros((1, LEN), f32)
    for segment in range(3):
        held = jnp.sum(jnp.where(labels == float(segment), 1.0, 0.0), axis=1, keepdims=True)
        begin = begin + jnp.where(labels > float(segment), held, 0.0)
    begin = jnp.where(labels < 0.0, spot, begin)
    low_row[...] = jnp.broadcast_to(begin, (8, LEN))


def attend_kernel(scal, kcat, qturn, vturn, low_row, outs_turn, lse):
    def one_head(h, carry):
        for c in range(SEQ):
            size = CH * (c + 1)
            lanes = slice(c * CH, (c + 1) * CH)
            score = dot(kcat[h, :size, :], qturn[h, :, lanes], NN)
            mask = allowed(low_row, c, size)
            score = jnp.where(mask, score, masked_score)
            peak = jnp.max(score, axis=0, keepdims=True)
            weight = jnp.exp(score - peak)
            total = jnp.sum(weight, axis=0, keepdims=True)
            top, rest = halves(weight)
            both = dot(vturn[h, :, :size], top, NN)
            extra = dot(vturn[h, :HEAD, :size], rest, NN)
            result = (both[:HEAD] + both[HEAD:] + extra) / total
            outs_turn[pl.ds(pl.multiple_of(h * HEAD, HEAD), HEAD), lanes] = result
            lse[h, :, lanes] = jnp.broadcast_to(peak + jnp.log(total), (8, CH))
        return carry

    lax.fori_loop(0, OWN, one_head, 0)


def allowed(low_row, c, size):
    key_at = lax.broadcasted_iota(jnp.int32, (size, CH), 0).astype(f32)
    query_at = (lax.broadcasted_iota(jnp.int32, (1, CH), 1) + c * CH).astype(f32)
    begin = low_row[:1, c * CH : (c + 1) * CH]
    return (key_at >= begin) & (key_at <= query_at)


def proj_kernel(scal, *refs):
    toks, heads, parts, refs = refs[:4], refs[4:8], refs[8:12], refs[12:]
    vec, wh, wl, heads_h, heads_l, norm_h, norm_l, mixed, hat, scale, weight, joined = refs
    mine = scal[0]
    for r in range(SEQ):
        at = jnp.bitwise_xor(mine, r)
        for d in range(GROUPS):
            weight[pl.ds(pl.multiple_of(d * ROWS + at * SUB, 8), SUB), :] = parts[r][
                d * SUB : (d + 1) * SUB, :
            ]
        joined[rows_at(at, QUARTER), :] = heads[r][...]
    wh[...], wl[...] = halves(weight[...])
    heads_h[...], heads_l[...] = halves(joined[:, rows_at(mine, CH)])
    gain, shift = piece(vec, 5), piece(vec, 6)
    for r in range(SEQ):
        at = rows_at(jnp.bitwise_xor(mine, r), CH)
        a, b = halves(joined[:, at].T)
        total = toks[r][:CH, :] + dot3(a, b, wh[...], wl[...], NN)
        total = total + piece(vec, 4)
        normed, size = norm_stats(total)
        norm_h[r], norm_l[r] = halves(normed * gain + shift)
        if r == 0:
            mixed[...] = total
            hat[...] = normed
            scale[...] = jnp.broadcast_to(size, (CH, 128))


def hidden_kernel(scal, norm_h, norm_l, *refs):
    blocks, vec, acts_h, acts_l, slope, winh, winl = refs[:GROUPS], *refs[GROUPS:]
    mine = scal[0]
    for k in range(GROUPS):
        at = rows_at(owner(scal, k), ROWS)
        winh[at, :], winl[at, :] = halves(blocks[k][:ROWS, :])
    marks = [16 + d for d in range(GROUPS)]
    table = jnp.concatenate([vec[m // 3, m % 3 : m % 3 + 1, :] for m in marks], axis=0)
    table = pltpu.roll(table, lax.rem(HALF_VEC - mine * ROWS, HALF_VEC), 1)[:, :ROWS]
    bias = jnp.concatenate([table[d : d + 1] for d in range(GROUPS)], axis=1)
    for r in range(SEQ):
        at = slice(r * CH, (r + 1) * CH)
        hidden = dot3(norm_h[r], norm_l[r], winh[...], winl[...], NN) + bias
        inner = jnp.tanh(gelu_scale * (hidden + gelu_cubic * hidden * hidden * hidden))
        acts_h[at, :], acts_l[at, :] = halves(0.5 * hidden * (1.0 + inner))
        slope[at, :] = 0.5 * (1.0 + inner) + 0.5 * hidden * (1.0 - inner * inner) * gelu_scale * (
            1.0 + 3.0 * gelu_cubic * hidden * hidden
        )


def emit_blocks(scal, outs, whole):
    for k in range(GROUPS):
        outs[k][...] = whole[rows_at(owner(scal, k), ROWS), :]


def out_grad_kernel(scal, acts_h, acts_l, *refs):
    grads, (out_h, out_l), outs, whole = refs[:4], refs[4:6], refs[6 : 6 + GROUPS], refs[6 + GROUPS]
    for r in range(SEQ):
        at = slice(r * CH, (r + 1) * CH)
        out_h[at, :], out_l[at, :] = halves(grads[r][...])
    whole[...] = dot3(acts_h[...], acts_l[...], out_h[...], out_l[...], TN)
    emit_blocks(scal, outs, whole)


def hidden_back_kernel(scal, out_h, out_l, slope, winh, winl, *refs):
    blocks, rest, refs = refs[:GROUPS], refs[GROUPS], refs[GROUPS + 1 :]
    hid_h, hid_l, wouth, woutl, bias_sum = refs[:5]
    parts = refs[5:]
    for k in range(GROUPS):
        at = rows_at(owner(scal, k), ROWS)
        block = rest[...] if k == HALF else blocks[k][ROWS:, :]
        wouth[at, :], woutl[at, :] = halves(block)
    sums = jnp.zeros((1, D), f32)
    for r in (1, 3, 2, 0):
        at = slice(r * CH, (r + 1) * CH)
        back = dot3(out_h[at, :], out_l[at, :], wouth[...], woutl[...], NT) * slope[at, :]
        sums = sums + jnp.sum(back, axis=0, keepdims=True)
        bh, bl = halves(back)
        hid_h[at, :], hid_l[at, :] = bh, bl
        parts[r][...] = dot3(bh, bl, winh[...], winl[...], NT)
    bias_sum[...] = jnp.broadcast_to(sums, (8, D))


def in_grad_kernel(scal, norm_h, norm_l, hid_h, hid_l, *refs):
    outs, whole = refs[:GROUPS], refs[GROUPS]
    flat = lambda ref: ref[...].reshape(LEN, D)
    whole[...] = dot3(flat(norm_h), flat(norm_l), hid_h[...], hid_l[...], TN)
    emit_blocks(scal, outs, whole)


def ffn_out_kernel(scal, acts_h, acts_l, wouth, woutl, *parts):
    for r in (1, 3, 2, 0):
        at = slice(r * CH, (r + 1) * CH)
        parts[r][...] = dot3(acts_h[at, :], acts_l[at, :], wouth[...], woutl[...], NN)


def output_kernel(scal, mixed, one, two, three, vec, output):
    output[...] = mixed[...] + (one[...] + two[...] + three[...]) + piece(vec, 7)


def proj_back_kernel(scal, one, two, three, hat, scale, vec, grad_out, wh, wl, mixed_grad, sums, *parts):
    mine = scal[0]
    normed = one[...] + two[...] + three[...]
    back = norm_back(hat[...], scale[:, :1], piece(vec, 5), normed)
    total = grad_out[...] + back
    mixed_grad[...] = total
    a, b = halves(total)
    for r in range(SEQ):
        at = rows_at(jnp.bitwise_xor(mine, r), QUARTER)
        parts[r][...] = dot3(wh[at, :], wl[at, :], a, b, NT)
    add = lambda v: jnp.sum(v, axis=0, keepdims=True)
    sums[...] = jnp.concatenate(
        [add(total), add(normed * hat[...]), add(normed), add(grad_out[...]), jnp.zeros((4, D), f32)],
        axis=0,
    )


def proj_grad_kernel(scal, heads_h, heads_l, mixed_grad, *refs):
    outs, whole = refs[:-1], refs[-1]
    mine = scal[0]
    gh, gl = halves(mixed_grad[...])
    whole[...] = dot3(heads_h[...], heads_l[...], gh, gl, NN)
    for r in range(SEQ):
        at = jnp.bitwise_xor(mine, r)
        for d in range(GROUPS):
            outs[r][d * SUB : (d + 1) * SUB, :] = whole[
                pl.ds(pl.multiple_of(d * ROWS + at * SUB, 8), SUB), :
            ]


def back_kernel(scal, *refs):
    grads, refs = refs[:4], refs[4:]
    kcat, qturn, vcat, qpair, kturn, outs_turn, lse, low_row = refs[:8]
    joined_h, joined_l, joined_sums = refs[8:11]
    gturn, gpair, dots, key_sum, value_sum, query_turn = refs[11:]
    mine = scal[0]

    for r in range(SEQ):
        at = rows_at(jnp.bitwise_xor(mine, r), CH)
        turned = grads[r][...]
        grad = jnp.concatenate([turned, jnp.zeros((HEAD, CH), f32)], axis=0).T
        pairs = lane_pairs(grad[:, :128], grad[:, 128:])
        for h in range(OWN):
            gpair[h, at, :] = pairs[h]
            part = turned[HEAD * h : HEAD * (h + 1)]
            dots[h, :, at] = jnp.broadcast_to(
                jnp.sum(part * outs_turn[HEAD * h : HEAD * (h + 1), at], axis=0, keepdims=True), (8, CH)
            )
            a, b = halves(part)
            gturn[h, :, at] = jnp.concatenate([a, a, b, b], axis=0)

    key_sum[...] = jnp.zeros_like(key_sum)
    value_sum[...] = jnp.zeros_like(value_sum)

    def one_head(h, carry):
        for c in range(SEQ):
            size = CH * (c + 1)
            lanes = slice(c * CH, (c + 1) * CH)
            score = dot(kcat[h, :size, :], qturn[h, :, lanes], NN)
            weight = jnp.where(allowed(low_row, c, size), jnp.exp(score - lse[h, :1, lanes]), 0.0)
            back = dot(vcat[h, :size, :], gturn[h, :, lanes], NN)
            score_back = weight * (back - dots[h, :1, lanes])
            a, b = halves(weight)
            pair = gpair[h, lanes, :]
            value_sum[h, :size, :] += dot(a, pair, NN) + dot(b, pair, NN)
            a, b = halves(score_back)
            pair = qpair[h, lanes, :]
            key_sum[h, :size, :] += dot(a, pair, NN) + dot(b, pair, NN)
            turned = dot(kturn[h, :, :size], a, NN) + dot(kturn[h, :, :size], b, NN)
            query_turn[h, :, lanes] = (turned[:HEAD] + turned[HEAD:]) * HEAD ** (-0.5)
        return carry

    lax.fori_loop(0, OWN, one_head, 0)

    column_sums = jnp.zeros((1, D), f32)
    low = low_lanes((CH, 128))
    for c in range(SEQ):
        at = slice(c * CH, (c + 1) * CH)
        blank = jnp.zeros((HEAD, CH), f32)
        query = jnp.concatenate([query_turn[h, :, at] for h in range(OWN)] + [blank], axis=0).T
        done = [query]
        for kept in (key_sum, value_sum):
            full = [kept[h, at, :] for h in range(OWN)]
            full = [v + pltpu.roll(v, HEAD, 1) for v in full]
            done.append(jnp.where(low, full[0], full[1]))
            done.append(jnp.where(low, full[2], 0.0))
        joined = jnp.concatenate(done, axis=1)
        column_sums = column_sums + jnp.sum(joined, axis=0, keepdims=True)
        joined_h[at, :], joined_l[at, :] = halves(joined)

    joined_sums[...] = jnp.broadcast_to(column_sums, (8, D))


def qkv_grad_kernel(scal, xh, xl, joined_h, joined_l, joined_sums, wh, wl, vec, *refs):
    proj_one, proj_two, proj_three, sums, bias_sum = refs[:5]
    outs, (whole, rows) = refs[5 : 5 + GROUPS], refs[5 + GROUPS :]
    mine = scal[0]
    column_sums = joined_sums[:1, :]
    core = dot3(xh[...], xl[...], joined_h[...], joined_l[...], TN)
    gain, shift = piece(vec, 0), piece(vec, 1)
    as_column = lambda v: jnp.broadcast_to(v, (128, D)).T[:, :1]
    whole[...] = as_column(gain) * core + as_column(shift) * column_sums
    weights = wh[...].astype(f32) + wl[...].astype(f32)
    gain_grad = jnp.sum(weights * core, axis=1, keepdims=True)
    shift_grad = jnp.sum(weights * column_sums, axis=1, keepdims=True)
    lane = lax.broadcasted_iota(jnp.int32, (D, 128), 1)
    norm_grads = jnp.where(lane == 0, gain_grad, shift_grad).T

    def place(part, scale):
        wide = jnp.concatenate([part[:, :QUARTER], jnp.zeros((1, D - QUARTER), f32)], axis=1)
        wide = jnp.broadcast_to(wide, (8, D))
        return pltpu.roll(wide, mine * QUARTER, 1)[:1]

    entries = [
        norm_grads[0:1],
        norm_grads[1:2],
        place(column_sums[:, :CH], 1.0),
        place(column_sums[:, 2 * CH :], 1.0),
        sums[0:1],
        sums[1:2],
        sums[2:3],
        sums[3:4],
    ]
    lines = [e[:, i * HALF_VEC : (i + 1) * HALF_VEC] for e in entries for i in range(2)]
    bias = jnp.concatenate(
        [bias_sum[:1, d * ROWS : (d + 1) * ROWS] for d in range(GROUPS)], axis=0
    )
    bias = jnp.concatenate([bias, jnp.zeros((GROUPS, HALF_VEC - ROWS), f32)], axis=1)
    bias = pltpu.roll(bias, mine * ROWS, 1)
    lines = lines + [bias[d : d + 1] for d in range(GROUPS)]
    filler = jnp.zeros((5, HALF_VEC), f32)
    for d in range(GROUPS):
        rows[d] = jnp.concatenate(lines[3 * d : 3 * d + 3] + [filler], axis=0)

    for k in range(GROUPS):
        at = owner(scal, k)
        outs[k][:ROWS, :] = whole[rows_at(at, ROWS), :]
        here = pl.ds(pl.multiple_of(at * SUB, 8), SUB)
        proj = proj_one[here, :] + proj_two[here, :] + proj_three[here, :]
        for group in range(SEQ):
            for part in range(3):
                lane_at = HEAD * (3 * group + part)
                outs[k][
                    group * SUB : (group + 1) * SUB, part * CH + QUARTER : (part + 1) * CH
                ] = proj[:, lane_at : lane_at + HEAD]
        outs[k][ROWS:, :HALF_VEC] = rows[at]
        outs[k][ROWS:, HALF_VEC:] = jnp.zeros((8, HALF_VEC), f32)


def pre_back_kernel(scal, joined_h, joined_l, wh, wl, *parts):
    mine = scal[0]
    for r in (1, 3, 2, 0):
        at = rows_at(jnp.bitwise_xor(mine, r), CH)
        parts[r][...] = dot3(joined_h[at, :], joined_l[at, :], wh[...], wl[...], NT)


def input_grad_kernel(scal, tokens, one, two, three, vec, mixed_grad, result):
    hat, scale = norm_stats(tokens[...])
    grad = one[...] + two[...] + three[...]
    result[...] = mixed_grad[...] + norm_back(hat, scale, piece(vec, 0), grad)


def total_square(value):
    return jnp.sum(jnp.sum(value * value, axis=0, keepdims=True), axis=1, keepdims=True)


def second_squares_kernel(scal, *refs):
    parts, squares = refs[:8], refs[8]
    total = sum(total_square(part[...]) for part in parts)
    squares[...] = jnp.broadcast_to(total, (8, 128))


def first_squares_kernel(scal, one, two, three, four, before, squares):
    parts = (one, two, three, four)
    total = sum(total_square(part[:ROWS, :]) for part in parts)
    line = sum(part[ROWS:, :HALF_VEC] for part in parts)
    squares[...] = before[...] + (total + total_square(line))


def stage_kernel(scal, *refs):
    sources, targets, sems = refs[:15], refs[15:30], refs[30]
    copies = [
        pltpu.make_async_copy(source, target, sems.at[i])
        for i, (source, target) in enumerate(zip(sources, targets))
    ]
    for copy in copies:
        copy.start()
    for copy in copies:
        copy.wait()


def adamw_kernel(scal, squares, *refs):
    firsts, ins, outs, refs = refs[:4], refs[4:8], refs[8:12], refs[12:]
    states, clip, finals, news = refs[:15], refs[15], refs[16:31], refs[31:46]
    first, second, sems = refs[46:]
    send = lambda number: [
        pltpu.make_async_copy(news[i], finals[i], sems.at[i]) for i in range(3 * number, 3 * number + 3)
    ]
    mine = scal[0]
    norm = jnp.sqrt(squares[...])
    clip[...] = norm
    factor = (clip_limit / jnp.maximum(norm, clip_limit))[:1, :1]
    for r in range(SEQ):
        at = jnp.bitwise_xor(mine, r)
        first[at] = firsts[r][:ROWS, :]
        second[at, :ROWS] = ins[r][...]
        second[at, ROWS:] = outs[r][...]

    def update(number, spot, grad, rate, decay):
        held = [states[3 * number + i][spot] for i in range(3)]
        fresh = adamw_update(*held, factor * grad, rate, decay)
        for i in range(3):
            news[3 * number + i][spot] = fresh[i]

    def finish(number):
        for copy in send(number):
            copy.start()

    line = sum(firsts[r][ROWS:, :HALF_VEC] for r in range(SEQ))
    for i in range(3):
        for j in range(3):
            spot = (slice(3 * i + j, 3 * i + j + 1), slice(None))
            update(0, spot, line[i : i + 1, 128 * j : 128 * (j + 1)], vector_rate, 0.0)
    finish(0)
    every = slice(None)
    for part in range(3):
        grad = jnp.concatenate(
            [first[j][:, part * CH : part * CH + QUARTER] for j in range(SEQ)], axis=1
        )
        update(1, (every, slice(part * D, (part + 1) * D)), grad, matrix_rate, weight_decay)
    finish(1)
    for j in range(SEQ):
        grad = jnp.concatenate(
            [
                first[j][group * SUB : (group + 1) * SUB, part * CH + QUARTER : (part + 1) * CH]
                for group in range(SEQ)
                for part in range(3)
            ],
            axis=1,
        )
        update(2, (slice(j * SUB, (j + 1) * SUB), every), grad, matrix_rate, weight_decay)
    finish(2)
    for d in range(GROUPS):
        grad = jnp.concatenate(
            [second[j][:ROWS, d * ROWS : (d + 1) * ROWS] for j in range(SEQ)], axis=1
        )
        update(3, (every, slice(d * HALF_VEC, (d + 1) * HALF_VEC)), grad, matrix_rate, weight_decay)
    finish(3)
    for j in range(SEQ):
        update(
            4, (slice(j * ROWS, (j + 1) * ROWS), every), second[j][ROWS:, :], matrix_rate, weight_decay
        )
    finish(4)
    for number in range(5):
        for copy in send(number):
            copy.wait()


def adamw_update(weight, first, second, grad, rate, decay):
    new_first = beta_one * first + (1.0 - beta_one) * grad
    new_second = beta_two * second + (1.0 - beta_two) * grad * grad
    first_hat = new_first / (1.0 - beta_one**STEP)
    second_hat = new_second / (1.0 - beta_two**STEP)
    new_weight = weight - rate * (first_hat / (jnp.sqrt(second_hat) + adam_eps) + decay * weight)
    return (new_first, new_second, new_weight)


def ring_tables(count):
    evens = [2 * i for i in range(count // 2)]
    order = evens + [i + 1 for i in reversed(evens)]
    place = [0] * count
    for position, device in enumerate(order):
        place[device] = position
    right = [(order[i], order[(i + 1) % count]) for i in range(count)]
    left = [(b, a) for a, b in right]
    return order, place, right, left


class RingGather:
    def __init__(self, block, name):
        _, _, self.right, self.left = ring_tables(GROUPS)
        self.got, self.name, self.at = {0: block}, name, 0

    def step(self, after=()):
        places = (-self.at % GROUPS, self.at)
        if after:
            for place in set(places):
                self.got[place] = gate(self.got[place], after)
        forth, back = (self.got[place] for place in places)
        self.at += 1
        self.got[GROUPS - self.at] = move(forth, "dp", self.right, f"{self.name}_right_{self.at}")
        self.got[self.at] = move(back, "dp", self.left, f"{self.name}_left_{self.at}")
        return [forth, back]

    def last(self, cut=0):
        forth, back = self.got[GROUPS - self.at], self.got[self.at]
        if not cut:
            self.got[HALF] = move(forth, "dp", self.right, f"{self.name}_right_{HALF}")
            return None
        top, rest = split_rows(forth, back, cut)
        self.got[HALF] = move(top, "dp", self.right, f"{self.name}_right_{HALF}")
        return move(rest, "dp", self.left, f"{self.name}_left_{HALF}")

    def blocks(self):
        return [self.got[k] for k in range(GROUPS)]


class RingScatter:
    def __init__(self, blocks, name, flip=False):
        _, _, self.right, self.left = ring_tables(GROUPS)
        self.blocks = blocks
        if flip:
            self.right, self.left = self.left, self.right
            self.blocks = [blocks[-k % GROUPS] for k in range(GROUPS)]
        self.name, self.back, self.at = name, None, HALF
        self.forth = move(self.blocks[HALF], "dp", self.right, f"{name}_right_1")

    def step(self, after=()):
        self.at -= 1
        forth = plus(self.forth, self.blocks[self.at], after=after)
        back = self.blocks[GROUPS - self.at]
        if self.back is not None:
            back = plus(self.back, back, after=after)
        number = HALF + 1 - self.at
        self.forth = move(forth, "dp", self.right, f"{self.name}_right_{number}")
        self.back = move(back, "dp", self.left, f"{self.name}_left_{number}")
        return [forth, back]

    def result(self, after=()):
        return plus(self.forth, self.back, self.blocks[0], after=after)


def move(block, axis, pairs, name):
    with jax.named_scope(name):
        return lax.ppermute(block, axis, pairs)


def swap(block, bits, name):
    return move(block, "seq", [(i, i ^ bits) for i in range(SEQ)], f"{name}_{bits}")


def gather_seq(block, name):
    across = swap(block, 2, name)
    core = swap(block, 1, name)
    return [block, core, across, swap(across, 1, f"{name}_2")]


def exchange_seq(parts, name):
    return [parts[0]] + [swap(parts[r], r, name) for r in range(1, SEQ)]


def scatter_core(parts, name):
    return parts[0], swap(parts[1], 1, f"{name}_own"), parts[2], swap(parts[3], 1, f"{name}_across")


def ordered(blocks, mine):
    stack = jnp.stack(blocks, axis=0)
    return [lax.dynamic_index_in_dim(stack, mine ^ j, 0, keepdims=False) for j in range(len(blocks))]


def local(
    tokens,
    cotangent,
    segment_ids,
    valid,
    vectors,
    vec_first,
    vec_second,
    w_qkv,
    qkv_first,
    qkv_second,
    w_proj,
    proj_first,
    proj_second,
    w_in,
    in_first,
    in_second,
    w_out,
    out_first,
    out_second,
):
    dp_parts = lax.axis_size("dp")
    ring = dp_parts == GROUPS
    mine = lax.axis_index("seq")
    home = lax.axis_index("dp")
    rows = w_qkv.shape[0]
    units = w_out.shape[0] // SEQ
    far, near = home // 2, home % 2
    position = jnp.where(near > 0, GROUPS - 1 - far, far)
    scal = jnp.stack([mine, position, jnp.full_like(mine, 1 if ring else 0)]).astype(jnp.int32)
    flat_in = tokens.reshape(CH, D)
    chunk, tall, square = shape(CH, D), shape(LEN, D, kind=bf16), shape(D, D, kind=bf16)

    if ring:
        first, packed = run(
            pack_first_kernel,
            scal,
            [w_qkv, w_proj, vectors.reshape(9, 128), segment_ids, valid, flat_in],
            [shape(ROWS + 8, D), shape(CH + 8, D)],
            scratch=[
                pltpu.VMEM((3, ROWS, CH), f32),
                pltpu.VMEM((SUB, D), f32),
                pltpu.VMEM((9, 128), f32),
                pltpu.VMEM((2, 1, CH), jnp.int32),
            ],
            sems=8,
            far_args=range(6),
            room=54,
            name="pack_first", work=3.0,
        )
        ring_first = RingGather(first, "first")
        for _ in range(HALF - 1):
            ring_first.step()
        ring_first.last()
        firsts = ring_first.blocks()
        (second,) = run(
            pack_second_kernel,
            scal,
            [w_in, w_out],
            [shape(2 * ROWS, D)],
            name="pack_second", work=3.0,
            after=[firsts[GROUPS - 1]],
        )
        ring_second = RingGather(second, "second")
        ring_second.step([firsts[HALF]])
    else:
        padded = jnp.pad(w_qkv, ((0, 0), (0, CH)))
        own = lambda part: lax.dynamic_slice_in_dim(padded, part * D + mine * QUARTER, CH, 1)
        first = jnp.concatenate([own(0), own(1), own(2)], axis=1)
        first = lax.all_gather(first, "dp", axis=0, tiled=True).reshape(GROUPS, ROWS, D)
        all_vec = lax.all_gather(vectors, "dp", axis=0, tiled=True).reshape(GROUPS, 3, HALF_VEC)
        first = jnp.concatenate([first, jnp.pad(all_vec, ((0, 0), (0, 5), (0, D - HALF_VEC)))], axis=1)
        firsts = [first[k] for k in range(GROUPS)]
        in_part = lax.dynamic_index_in_dim(
            w_in.reshape(rows, dp_parts, SEQ, units), mine, 2, keepdims=False
        ).reshape(rows, D)
        out_part = lax.dynamic_slice_in_dim(w_out, mine * units, units, 0)
        second = jnp.concatenate(
            [
                lax.all_gather(part, "dp", axis=0, tiled=True).reshape(GROUPS, ROWS, D)
                for part in (in_part, out_part)
            ],
            axis=1,
        )
        seconds = [second[k] for k in range(GROUPS)]
        seconds[HALF], second_rest = second[HALF, :ROWS], second[HALF, ROWS:]
        marks = jnp.where(valid > 0, segment_ids, -1).astype(f32)
        packed = jnp.concatenate([flat_in, jnp.pad(marks, ((0, 7), (0, D - CH)))], axis=0)
    toks = gather_seq(packed, "tokens")
    (grad_out,) = run(
        mask_kernel, scal, [cotangent.reshape(CH, D), valid], [chunk], name="mask", work=2.0, after=[toks[2]]
    )
    grads_row = gather_seq(grad_out, "cotangent")

    qkv_h, qkv_l, vec, proj = run(
        weights_kernel,
        scal,
        firsts,
        [square, square, shape(GROUPS, 8, HALF_VEC), shape(GROUPS * SUB, D)],
        name="weights", work=3.0,
    )
    if ring:
        proj_parts = gather_seq(proj, "w_proj")
    else:
        full = lax.all_gather(w_proj, "dp", axis=0, tiled=True).reshape(GROUPS, SEQ, SUB, D)
        proj_parts = [
            lax.dynamic_index_in_dim(full, mine ^ r, 1, keepdims=False).reshape(GROUPS * SUB, D)
            for r in range(SEQ)
        ]
    hat_h, hat_l, kcat, qturn, vcat, qpair, kturn, vturn, low_row = run(
        front_kernel,
        scal,
        toks + [qkv_h, qkv_l, vec],
        [
            tall,
            tall,
            shape(OWN, LEN, 256, kind=bf16),
            shape(OWN, 256, LEN, kind=bf16),
            shape(OWN, LEN, 256, kind=bf16),
            shape(OWN, LEN, 128, kind=bf16),
            shape(OWN, 128, LEN, kind=bf16),
            shape(OWN, 128, LEN, kind=bf16),
            shape(8, LEN),
        ],
        scratch=[pltpu.VMEM((SEQ, 8, CH), f32)],
        name="front", work=8.0,
        after=[grads_row[2]],
    )
    if ring:
        second_sent = ring_second.step([low_row])
    heads, lse = run(
        attend_kernel,
        scal,
        [kcat, qturn, vturn, low_row],
        [shape(QUARTER, LEN), shape(OWN, 8, LEN)],
        name="attend", work=8.0,
        after=[proj_parts[2], *second_sent] if ring else [],
    )
    if ring:
        ring_second.step([lse])
        second_rest = ring_second.last(ROWS)
        seconds = ring_second.blocks()
    wide = shape(D, CH, kind=bf16)
    split = shape(SEQ, CH, D, kind=bf16)
    proj_h, proj_l, heads_h, heads_l, norm_h, norm_l, mixed, hat_two, scale_two = run(
        proj_kernel,
        scal,
        toks + gather_seq(heads, "heads") + proj_parts + [vec],
        [square, square, wide, wide, split, split, chunk, chunk, shape(CH, 128)],
        scratch=[pltpu.VMEM((D, D), f32), pltpu.VMEM((D, LEN), f32)],
        name="proj", work=8.0,
    )

    block = shape(ROWS, D)
    acts_h, acts_l, slope, in_wh, in_wl = run(
        hidden_kernel,
        scal,
        [norm_h, norm_l] + seconds + [vec],
        [tall, tall, shape(LEN, D), square, square],
        name="hidden", work=8.0,
    )
    done = run(
        out_grad_kernel,
        scal,
        [acts_h, acts_l] + grads_row,
        [tall, tall] + [block] * GROUPS,
        scratch=[pltpu.VMEM((D, D), f32)],
        name="out_grad", work=5.0,
    )
    out_h, out_l = done[:2]
    out_grads = list(done[2:])
    if ring:
        ring_out = RingScatter(out_grads, "out_grad")
    done = run(
        hidden_back_kernel,
        scal,
        [out_h, out_l, slope, in_wh, in_wl] + seconds + [second_rest],
        [tall, tall, square, square, shape(8, D)] + [chunk] * SEQ,
        name="hidden_back", work=11.0,
        after=out_grads[:1],
    )
    hid_h, hid_l, out_wh, out_wl, bias_sum = done[:5]
    parts = list(done[5:])
    if ring:
        parts[3] = gate(parts[3], ring_out.step())
    norm_own, norm_near, norm_across, norm_far = scatter_core(parts, "norm_grad")
    norm_pair = plus(norm_across, norm_far)
    norm_last = swap(norm_pair, 2, "norm_grad")
    in_grads = list(
        run(
            in_grad_kernel,
            scal,
            [norm_h, norm_l, hid_h, hid_l],
            [block] * GROUPS,
            scratch=[pltpu.VMEM((D, D), f32)],
            name="in_grad", work=5.0,
            after=[norm_pair],
        )
    )
    if ring:
        ring_in = RingScatter(in_grads, "in_grad", flip=True)
        out_sent = ring_out.step()
        in_sent = ring_in.step()
    done = run(
        proj_back_kernel,
        scal,
        [norm_own, norm_near, norm_last, hat_two, scale_two, vec, grad_out, proj_h, proj_l],
        [chunk, shape(8, D)] + [shape(QUARTER, CH)] * SEQ,
        name="proj_back", work=5.0,
        after=out_sent + in_sent if ring else [],
    )
    mixed_grad, sums = done[:2]
    head_grads = exchange_seq(list(done[2:]), "head_grad")
    if ring:
        out_sent = ring_out.step([mixed_grad])
        in_sent = ring_in.step([mixed_grad])
    proj_grads = run(
        proj_grad_kernel,
        scal,
        [heads_h, heads_l, mixed_grad],
        [shape(GROUPS * SUB, D)] * SEQ,
        scratch=[pltpu.VMEM((D, D), f32)],
        name="proj_grad", work=4.0,
        after=[*head_grads[1:], *out_sent, *in_sent] if ring else [],
    )
    wait = [head_grads[3], head_grads[2]]
    if ring:
        proj_own, proj_near, proj_across, proj_far = scatter_core(proj_grads, "proj_grad")
        proj_pair = plus(proj_across, proj_far, after=wait)
        proj_last = swap(proj_pair, 2, "proj_grad")
    else:
        proj_own = proj_near = proj_last = proj_pair = proj_grads[0]
    joined_h, joined_l, joined_sums = run(
        back_kernel,
        scal,
        head_grads + [kcat, qturn, vcat, qpair, kturn, heads, lse, low_row],
        [tall, tall, shape(8, D)],
        scratch=[
            pltpu.VMEM((OWN, 256, LEN), bf16),
            pltpu.VMEM((OWN, LEN, 128), bf16),
            pltpu.VMEM((OWN, 8, LEN), f32),
            pltpu.VMEM((OWN, LEN, 128), f32),
            pltpu.VMEM((OWN, LEN, 128), f32),
            pltpu.VMEM((OWN, HEAD, LEN), f32),
        ],
        name="back", work=16.0,
        after=[proj_grads[0]],
    )
    if ring:
        shard_out = ring_out.result([joined_sums])
        in_sent = ring_in.step([joined_sums])
    done = run(
        qkv_grad_kernel,
        scal,
        [hat_h, hat_l, joined_h, joined_l, joined_sums, qkv_h, qkv_l, vec]
        + [proj_own, proj_near, proj_last, sums, bias_sum],
        [shape(ROWS + 8, D)] * GROUPS,
        scratch=[pltpu.VMEM((D, D), f32), pltpu.VMEM((GROUPS, 8, HALF_VEC), f32)],
        name="qkv_grad", work=9.0,
        after=[*in_sent, shard_out] if ring else [],
    )
    first_grads = list(done)
    if ring:
        ring_first = RingScatter(first_grads, "first_grad")
        shard_in = ring_in.result([first_grads[0]])
        out_all = gather_seq(shard_out, "out_shard")
        in_all = gather_seq(shard_in, "in_shard")
        first_sent = ring_first.step()
    pre_parts = run(
        pre_back_kernel,
        scal,
        [joined_h, joined_l, qkv_h, qkv_l],
        [chunk] * SEQ,
        name="pre_back", work=7.0,
        after=[shard_in, *first_sent] if ring else [],
    )
    pre_parts = list(pre_parts)
    if ring:
        first_sent = ring_first.step()
        pre_parts[3] = gate(pre_parts[3], first_sent)
    pre_own, pre_near, pre_across, pre_far = scatter_core(pre_parts, "pre_grad")
    pre_pair = plus(pre_across, pre_far, after=[in_all[2]] if ring else [])
    pre_last = swap(pre_pair, 2, "pre_grad")
    states = [vectors, vec_first, vec_second, w_qkv, qkv_first, qkv_second, w_proj, proj_first, proj_second]
    states = states + [w_in, in_first, in_second, w_out, out_first, out_second]
    if ring:
        held = [v.reshape(9, 128) for v in states[:3]] + states[3:]
        held = run(
            stage_kernel,
            scal,
            held,
            [shape(*v.shape) for v in held],
            sems=15,
            far_args=range(15),
            name="stage", work=4.0,
            after=[pre_parts[0]],
        )
    out_parts = run(
        ffn_out_kernel,
        scal,
        [acts_h, acts_l, out_wh, out_wl],
        [chunk] * SEQ,
        name="ffn_out", work=7.0,
        after=first_sent if ring else [],
    )
    out_parts = list(out_parts)
    if ring:
        ring_first.step()
        shard_first = ring_first.result()
        out_parts[3] = gate(out_parts[3], [shard_first])
    out_own, out_near, out_across, out_far = scatter_core(out_parts, "output")
    if not ring:
        out_pair = plus(out_across, out_far)
    (input_grad,) = run(
        input_grad_kernel,
        scal,
        [flat_in, pre_own, pre_near, pre_last, vec, mixed_grad],
        [chunk],
        name="input_grad", work=3.0,
    )

    if ring:
        (squares,) = run(
            second_squares_kernel, scal, in_all + out_all, [shape(8, 128)], name="second_squares", work=2.0
        )
        first_all = gather_seq(gate(shard_first, [pre_last, out_parts[0], held[3]]), "first_shard")
        out_pair = plus(out_across, out_far, after=[first_all[2]])
        (squares,) = run(
            first_squares_kernel,
            scal,
            first_all + [squares],
            [shape(8, 128)],
            name="first_squares", work=2.0,
            after=[input_grad],
        )
        out_last = swap(out_pair, 2, "output")
        for bits in (1, 2, 4):
            pairs = [(i, i ^ bits) for i in range(GROUPS)]
            squares = plus(squares, move(squares, "dp", pairs, "squares"))
        done = run(
            adamw_kernel,
            scal,
            [squares] + first_all + in_all + out_all + list(held),
            [shape(8, 128)] + [shape(*v.shape) for v in held],
            scratch=[pltpu.VMEM(v.shape, f32) for v in held]
            + [pltpu.VMEM((SEQ, ROWS, D), f32), pltpu.VMEM((SEQ, 2 * ROWS, D), f32)],
            sems=15,
            far_outs=range(1, 16),
            name="adamw", work=10.0,
        )
        new = [v.reshape(-1) for v in done[1:4]] + list(done[4:])
        clip_norm = done[0][0, 0]
    else:
        out_last = swap(out_pair, 2, "output")
        by_group = jnp.stack(first_grads)
        shard_first = lax.psum_scatter(
            by_group[:, :ROWS].reshape(D, D), "dp", scatter_dimension=0, tiled=True
        )
        proj_full = jnp.stack([p.reshape(GROUPS, SUB, D) for p in ordered(proj_grads, mine)], axis=1)
        proj_grad = lax.psum(
            lax.psum_scatter(proj_full.reshape(D, D), "dp", scatter_dimension=0, tiled=True), "seq"
        )
        all_vec = lax.psum(by_group[:, ROWS : ROWS + 3, :HALF_VEC], ("dp", "seq")).reshape(-1)
        vec_grad = lax.dynamic_slice_in_dim(all_vec, home * vectors.shape[0], vectors.shape[0])
        joined = lax.all_gather(shard_first, "seq", axis=0, tiled=False)
        qkv_grad = jnp.concatenate(
            [joined[j, :, i * CH : i * CH + QUARTER] for i in range(3) for j in range(SEQ)], axis=1
        )
        shard_in, shard_out = (
            lax.psum_scatter(jnp.concatenate(parts, axis=0), "dp", scatter_dimension=0, tiled=True)
            for parts in (in_grads, out_grads)
        )
        in_all = lax.all_gather(shard_in, "seq", axis=0, tiled=False)
        in_grad = in_all.reshape(SEQ, rows, dp_parts, units).transpose(1, 2, 0, 3).reshape(rows, -1)
        out_grad = lax.all_gather(shard_out, "seq", axis=0, tiled=True)
        total = sum(jnp.sum(g * g) for g in (qkv_grad, proj_grad, in_grad, out_grad, vec_grad))
        total = lax.psum(total, "dp")
        clip_norm = jnp.sqrt(total)
        factor = clip_limit / jnp.maximum(clip_norm, clip_limit)
        grads = (vec_grad, qkv_grad, proj_grad, in_grad, out_grad)
        new = []
        for number, grad in enumerate(grads):
            rate, decay = (matrix_rate, weight_decay) if number else (vector_rate, 0.0)
            new.extend(adamw_update(*states[3 * number : 3 * number + 3], factor * grad, rate, decay))
    (output,) = run(
        output_kernel, scal, [mixed, out_own, out_near, out_last, vec], [chunk], name="output", work=2.0
    )
    return (output.reshape(tokens.shape), input_grad.reshape(tokens.shape), clip_norm, *new)


def solution(mesh):
    row = P("dp", "seq", None)
    mark = P("dp", "seq")
    vec = P("dp")
    mat = P("dp", None)
    return jax.shard_map(
        local,
        mesh=mesh,
        in_specs=(row, row, mark, mark) + (vec,) * 3 + (mat,) * 12,
        out_specs=(row, row, P()) + (vec,) * 3 + (mat,) * 12,
        check_vma=False,
    )
```

```python
import functools
import math

import jax
import jax.numpy as jnp
from jax import lax
from jax.experimental import pallas as pl
from jax.experimental.pallas import tpu as pltpu
from jax.sharding import PartitionSpec as P

D = 768
HEADS = 12
HEAD = 64
STEP = 10
CH = 256
LEN = 1024
SEQ = 4
QUARTER = D // SEQ
OWN = HEADS // SEQ
GROUPS = 8
ROWS = D // GROUPS
SUB = ROWS // SEQ
HALF = GROUPS // 2
HALF_VEC = D // 2
VEC_ROWS = 24

f32 = jnp.float32
bf16 = jnp.bfloat16
masked_score = -1e30
norm_eps = 1e-05
clip_limit = 1.0
beta_one = 0.9
beta_two = 0.999
adam_eps = 1e-08
matrix_rate = 0.02
vector_rate = 0.4
weight_decay = 0.01
gelu_scale = 0.7978845608028654
gelu_cubic = 0.044715

COST = 1e9

WHOLE = pl.BlockSpec(memory_space=pltpu.VMEM)
SCALARS = pl.BlockSpec(memory_space=pltpu.SMEM)
NN = ((1,), (0,))
NT = ((1,), (1,))
TN = ((0,), (0,))


def shape(*dims, kind=f32):
    return jax.ShapeDtypeStruct(dims, kind)


def run(
    kernel, scal, args, outs, scratch=(), sems=0, far_args=(), far_outs=(), room=8, work=1.0, name=None, after=()
):
    args, after = list(args), list(after)
    held = sum(math.prod(v.shape) * jnp.dtype(v.dtype).itemsize for v in scratch)
    anywhere, far = pl.BlockSpec(memory_space=pl.ANY), pl.BlockSpec(memory_space=pltpu.HBM)
    scratch = list(scratch) + ([pltpu.SemaphoreType.DMA((sems,))] if sems else [])

    def body(scal_ref, *refs):
        kernel(scal_ref, *refs[: len(args)], *refs[len(args) + len(after) :])

    return pl.pallas_call(
        body,
        out_shape=tuple(outs),
        in_specs=[SCALARS]
        + [far if i in far_args else WHOLE for i in range(len(args))]
        + [anywhere] * len(after),
        out_specs=tuple(far if i in far_outs else WHOLE for i in range(len(outs))),
        scratch_shapes=scratch,
        compiler_params=pltpu.CompilerParams(vmem_limit_bytes=held + (room << 20)),
        cost_estimate=pl.CostEstimate(
            flops=int(work * COST), bytes_accessed=1, transcendentals=0
        ),
        name=name,
    )(scal, *args, *after)


def gate(value, after):
    anywhere = pl.BlockSpec(memory_space=pl.ANY)
    return pl.pallas_call(
        lambda *refs: None,
        out_shape=shape(*value.shape, kind=value.dtype),
        in_specs=[anywhere] * (1 + len(after)),
        out_specs=anywhere,
        input_output_aliases={0: 0},
        compiler_params=pltpu.CompilerParams(vmem_limit_bytes=1 << 20),
        name="gate",
    )(value, *after)


def sums(groups, after=()):
    sizes = [len(group) for group in groups]

    def body(*refs):
        at = 0
        for number, size in enumerate(sizes):
            total = refs[at][...]
            for ref in refs[at + 1 : at + size]:
                total = total + ref[...]
            refs[sum(sizes) + len(after) + number][...] = total
            at += size

    return pl.pallas_call(
        body,
        out_shape=tuple(shape(*group[0].shape) for group in groups),
        in_specs=[WHOLE] * sum(sizes) + [pl.BlockSpec(memory_space=pl.ANY)] * len(after),
        out_specs=tuple([WHOLE] * len(groups)),
        compiler_params=pltpu.CompilerParams(vmem_limit_bytes=4 << 20),
        cost_estimate=pl.CostEstimate(flops=int(COST), bytes_accessed=1, transcendentals=0),
        name="plus",
    )(*(term for group in groups for term in group), *after)


def plus(*terms, after=()):
    return sums([terms], after)[0]


def split_rows(one, two, cut):
    def body(one_ref, two_ref, top, rest):
        top[...] = one_ref[:cut, :]
        rest[...] = two_ref[cut:, :]

    return pl.pallas_call(
        body,
        out_shape=(shape(cut, one.shape[1]), shape(two.shape[0] - cut, two.shape[1])),
        in_specs=[WHOLE] * 2,
        out_specs=(WHOLE, WHOLE),
        compiler_params=pltpu.CompilerParams(vmem_limit_bytes=4 << 20),
        cost_estimate=pl.CostEstimate(flops=int(COST), bytes_accessed=1, transcendentals=0),
        name="split_rows",
    )(one, two)


def owner(scal, k):
    spot = jnp.bitwise_and(scal[1] + k, GROUPS - 1)
    return jnp.where(scal[2] > 0, jnp.where(spot < HALF, 2 * spot, 2 * GROUPS - 1 - 2 * spot), k)


def halves(value):
    top = value.astype(bf16)
    return top, (value - top.astype(f32)).astype(bf16)


def dot(left, right, dims):
    return lax.dot_general(left, right, (dims, ((), ())), preferred_element_type=f32)


def dot3(lh, ll, rh, rl, dims):
    return dot(lh, rh, dims) + (dot(lh, rl, dims) + dot(ll, rh, dims))


def rows_at(index, size):
    return pl.ds(pl.multiple_of(index * size, size), size)


def piece(vec, number):
    a, b = 2 * number, 2 * number + 1
    return jnp.concatenate(
        [vec[a // 3, a % 3 : a % 3 + 1, :], vec[b // 3, b % 3 : b % 3 + 1, :]], axis=1
    )


def norm_stats(inputs):
    center = inputs - jnp.mean(inputs, axis=-1, keepdims=True)
    spread = jnp.mean(center * center, axis=-1, keepdims=True)
    scale = lax.rsqrt(spread + norm_eps)
    return center * scale, scale


def norm_back(hat, scale, gain, grad):
    inner = grad * gain
    return scale * (
        inner
        - jnp.mean(inner, axis=-1, keepdims=True)
        - hat * jnp.mean(inner * hat, axis=-1, keepdims=True)
    )


def low_lanes(dims):
    return lax.broadcasted_iota(jnp.int32, dims, 1) < HEAD


def lane_pairs(pair, last):
    low = low_lanes(pair.shape)
    roll = lambda v: pltpu.roll(v, HEAD, 1)
    ph = pair.astype(bf16).astype(f32)
    pl_ = pair - ph
    lh = last.astype(bf16).astype(f32)
    ll = last - lh
    return [
        jnp.where(low, ph, roll(pl_)).astype(bf16),
        jnp.where(low, roll(ph), pl_).astype(bf16),
        jnp.where(low, lh, roll(ll)).astype(bf16),
    ]


def row_halves(turned, head):
    part = turned[HEAD * head : HEAD * (head + 1)]
    return halves(part)


def pack_first_kernel(scal, wqkv, wproj, vec, seg, valid, tokens, first, packed, *refs):
    bands, proj, lines, marks, sems = refs
    mine = scal[0]
    aligned = pl.multiple_of(jnp.bitwise_and(mine * QUARTER, -128), 128)
    copies = [
        pltpu.make_async_copy(wqkv.at[:, pl.ds(part * D + aligned, CH)], bands.at[part], sems.at[part])
        for part in range(3)
    ]
    sub = pl.ds(pl.multiple_of(mine * SUB, 8), SUB)
    copies.append(pltpu.make_async_copy(wproj.at[sub, :], proj, sems.at[3]))
    copies.append(pltpu.make_async_copy(vec, lines, sems.at[4]))
    copies.append(pltpu.make_async_copy(seg, marks.at[0], sems.at[5]))
    copies.append(pltpu.make_async_copy(valid, marks.at[1], sems.at[6]))
    copies.append(pltpu.make_async_copy(tokens, packed.at[:CH, :], sems.at[7]))
    for copy in copies:
        copy.start()
    first[ROWS:, :] = jnp.zeros((8, D), f32)
    packed[CH:, :] = jnp.zeros((8, D), f32)
    for copy in copies[:5]:
        copy.wait()
    turn = jnp.where(jnp.bitwise_and(mine, 1) > 0, CH - HEAD, 0)
    for part in range(3):
        turned = pltpu.roll(bands[part], turn, 1)
        first[:ROWS, part * CH : part * CH + QUARTER] = turned[:, :QUARTER]
        for group in range(SEQ):
            lane = HEAD * (3 * group + part)
            first[group * SUB : (group + 1) * SUB, part * CH + QUARTER : (part + 1) * CH] = proj[
                :, lane : lane + HEAD
            ]
        first[ROWS + part : ROWS + part + 1, :HALF_VEC] = jnp.concatenate(
            [lines[3 * part + i : 3 * part + i + 1, :] for i in range(3)], axis=1
        )
    for copy in copies[5:]:
        copy.wait()
    packed[CH : CH + 1, :CH] = jnp.where(marks[1] > 0, marks[0], -1).astype(f32)


def pack_second_kernel(scal, win, wout, second):
    mine = scal[0]
    turn = lax.rem(HALF_VEC - mine * ROWS, HALF_VEC)
    for part in range(GROUPS):
        turned = pltpu.roll(win[:, part * HALF_VEC : (part + 1) * HALF_VEC], turn, 1)
        second[:ROWS, part * ROWS : (part + 1) * ROWS] = turned[:, :ROWS]
    second[ROWS:, :] = wout[pl.ds(pl.multiple_of(mine * ROWS, 8), ROWS), :]


def mask_kernel(scal, cotangent, valid, result):
    keep = jnp.where(valid[...] > 0, 1.0, 0.0).astype(f32)
    column = jnp.broadcast_to(keep, (128, CH)).T[:, :1]
    result[...] = cotangent[...] * column


def weights_kernel(scal, *refs):
    blocks, (wh, wl, vec, proj) = refs[:GROUPS], refs[GROUPS:]
    for k in range(GROUPS):
        at = owner(scal, k)
        block = blocks[k][:ROWS, :]
        here = rows_at(at, ROWS)
        wh[here, :], wl[here, :] = halves(block)
        vec[at] = blocks[k][ROWS:, :HALF_VEC]
        for group in range(SEQ):
            for part in range(3):
                lane = HEAD * (3 * group + part)
                proj[pl.ds(pl.multiple_of(at * SUB, 8), SUB), lane : lane + HEAD] = block[
                    group * SUB : (group + 1) * SUB, part * CH + QUARTER : (part + 1) * CH
                ]


def front_kernel(scal, *refs):
    toks, refs = refs[:4], refs[4:]
    wh, wl, vec = refs[:3]
    xh, xl, kcat, qturn, vcat, qpair, kturn, low_row, outs_turn, lse, vturn, label = refs[3:]
    mine = scal[0]

    gain, shift = piece(vec, 0), piece(vec, 1)
    turn = lax.rem(D - mine * QUARTER, D)
    own = lambda number: pltpu.roll(jnp.broadcast_to(piece(vec, number), (8, D)), turn, 1)[:1, :CH]
    query_bias, value_bias = own(2), own(3)

    for r in range(SEQ):
        nat = jnp.bitwise_xor(mine, r)
        at = rows_at(nat, CH)
        label[nat] = toks[r][CH:, :CH]
        hat, _ = norm_stats(toks[r][:CH, :])
        xh[at, :], xl[at, :] = halves(hat)
        nh, nl = halves(hat * gain + shift)
        joined = dot3(nh, nl, wh[...], wl[...], NN)
        query = (joined[:, :CH] + query_bias) * HEAD ** (-0.5)
        key = joined[:, CH : 2 * CH]
        value = joined[:, 2 * CH :] + value_bias
        keys = lane_pairs(key[:, :128], key[:, 128:])
        values = lane_pairs(value[:, :128], value[:, 128:])
        queries = lane_pairs(query[:, :128], query[:, 128:])
        key_t, value_t, query_t = key.T, value.T, query.T
        for h in range(OWN):
            kcat[h, at, :] = jnp.concatenate([keys[h], keys[h]], axis=1)
            vcat[h, at, :] = jnp.concatenate([values[h], values[h]], axis=1)
            qpair[h, at, :] = queries[h]
            a, b = row_halves(query_t, h)
            qturn[h, :, at] = jnp.concatenate([a, a, b, b], axis=0)
            a, b = row_halves(key_t, h)
            kturn[h, :, at] = jnp.concatenate([a, b], axis=0)
            a, b = row_halves(value_t, h)
            vturn[h, :, at] = jnp.concatenate([a, b], axis=0)

    labels = jnp.concatenate([label[c][:1, :] for c in range(SEQ)], axis=1)
    spot = lax.broadcasted_iota(jnp.int32, (1, LEN), 1).astype(f32)
    begin = jnp.zeros((1, LEN), f32)
    for segment in range(3):
        held = jnp.sum(jnp.where(labels == float(segment), 1.0, 0.0), axis=1, keepdims=True)
        begin = begin + jnp.where(labels > float(segment), held, 0.0)
    begin = jnp.where(labels < 0.0, spot, begin)
    low_row[...] = jnp.broadcast_to(begin, (8, LEN))

    def one_head(h, carry):
        for c in range(SEQ):
            size = CH * (c + 1)
            lanes = slice(c * CH, (c + 1) * CH)
            score = dot(kcat[h, :size, :], qturn[h, :, lanes], NN)
            mask = allowed(low_row, c, size)
            score = jnp.where(mask, score, masked_score)
            peak = jnp.max(score, axis=0, keepdims=True)
            weight = jnp.exp(score - peak)
            total = jnp.sum(weight, axis=0, keepdims=True)
            top, rest = halves(weight)
            both = dot(vturn[h, :, :size], top, NN)
            extra = dot(vturn[h, :HEAD, :size], rest, NN)
            result = (both[:HEAD] + both[HEAD:] + extra) / total
            outs_turn[pl.ds(pl.multiple_of(h * HEAD, HEAD), HEAD), lanes] = result
            lse[h, :, lanes] = jnp.broadcast_to(peak + jnp.log(total), (8, CH))
        return carry

    lax.fori_loop(0, OWN, one_head, 0)


def allowed(low_row, c, size):
    key_at = lax.broadcasted_iota(jnp.int32, (size, CH), 0).astype(f32)
    query_at = (lax.broadcasted_iota(jnp.int32, (1, CH), 1) + c * CH).astype(f32)
    begin = low_row[:1, c * CH : (c + 1) * CH]
    return (key_at >= begin) & (key_at <= query_at)


def proj_kernel(scal, *refs):
    toks, heads, parts, refs = refs[:4], refs[4:8], refs[8:12], refs[12:]
    vec, wh, wl, heads_h, heads_l, norm_h, norm_l, mixed, hat, scale, weight, joined = refs
    mine = scal[0]
    for r in range(SEQ):
        at = jnp.bitwise_xor(mine, r)
        for d in range(GROUPS):
            weight[pl.ds(pl.multiple_of(d * ROWS + at * SUB, 8), SUB), :] = parts[r][
                d * SUB : (d + 1) * SUB, :
            ]
        joined[rows_at(at, QUARTER), :] = heads[r][...]
    wh[...], wl[...] = halves(weight[...])
    heads_h[...], heads_l[...] = halves(joined[:, rows_at(mine, CH)])
    gain, shift = piece(vec, 5), piece(vec, 6)
    for r in range(SEQ):
        at = rows_at(jnp.bitwise_xor(mine, r), CH)
        a, b = halves(joined[:, at].T)
        total = toks[r][:CH, :] + dot3(a, b, wh[...], wl[...], NN)
        total = total + piece(vec, 4)
        normed, size = norm_stats(total)
        norm_h[r], norm_l[r] = halves(normed * gain + shift)
        if r == 0:
            mixed[...] = total
            hat[...] = normed
            scale[...] = jnp.broadcast_to(size, (CH, 128))


def hidden_kernel(scal, norm_h, norm_l, *refs):
    blocks, vec, acts_h, acts_l, slope, winh, winl = refs[:GROUPS], *refs[GROUPS:]
    mine = scal[0]
    for k in range(GROUPS):
        at = rows_at(owner(scal, k), ROWS)
        winh[at, :], winl[at, :] = halves(blocks[k][:ROWS, :])
    marks = [16 + d for d in range(GROUPS)]
    table = jnp.concatenate([vec[m // 3, m % 3 : m % 3 + 1, :] for m in marks], axis=0)
    table = pltpu.roll(table, lax.rem(HALF_VEC - mine * ROWS, HALF_VEC), 1)[:, :ROWS]
    bias = jnp.concatenate([table[d : d + 1] for d in range(GROUPS)], axis=1)
    for r in range(SEQ):
        at = slice(r * CH, (r + 1) * CH)
        hidden = dot3(norm_h[r], norm_l[r], winh[...], winl[...], NN) + bias
        inner = jnp.tanh(gelu_scale * (hidden + gelu_cubic * hidden * hidden * hidden))
        acts_h[at, :], acts_l[at, :] = halves(0.5 * hidden * (1.0 + inner))
        slope[at, :] = 0.5 * (1.0 + inner) + 0.5 * hidden * (1.0 - inner * inner) * gelu_scale * (
            1.0 + 3.0 * gelu_cubic * hidden * hidden
        )


def emit_blocks(scal, outs, whole):
    for k in range(GROUPS):
        outs[k][...] = whole[rows_at(owner(scal, k), ROWS), :]


def out_grad_kernel(scal, acts_h, acts_l, *refs):
    grads, (out_h, out_l), outs, whole = refs[:4], refs[4:6], refs[6 : 6 + GROUPS], refs[6 + GROUPS]
    for r in range(SEQ):
        at = slice(r * CH, (r + 1) * CH)
        out_h[at, :], out_l[at, :] = halves(grads[r][...])
    whole[...] = dot3(acts_h[...], acts_l[...], out_h[...], out_l[...], TN)
    emit_blocks(scal, outs, whole)


def hidden_back_kernel(scal, out_h, out_l, slope, winh, winl, *refs):
    blocks, rest, refs = refs[:GROUPS], refs[GROUPS], refs[GROUPS + 1 :]
    hid_h, hid_l, wouth, woutl, bias_sum = refs[:5]
    parts = refs[5:]
    for k in range(GROUPS):
        at = rows_at(owner(scal, k), ROWS)
        block = rest[...] if k == HALF else blocks[k][ROWS:, :]
        wouth[at, :], woutl[at, :] = halves(block)
    sums = jnp.zeros((1, D), f32)
    for r in (1, 3, 2, 0):
        at = slice(r * CH, (r + 1) * CH)
        back = dot3(out_h[at, :], out_l[at, :], wouth[...], woutl[...], NT) * slope[at, :]
        sums = sums + jnp.sum(back, axis=0, keepdims=True)
        bh, bl = halves(back)
        hid_h[at, :], hid_l[at, :] = bh, bl
        parts[r][...] = dot3(bh, bl, winh[...], winl[...], NT)
    bias_sum[...] = jnp.broadcast_to(sums, (8, D))


def in_grad_kernel(scal, norm_h, norm_l, hid_h, hid_l, *refs):
    outs, whole = refs[:GROUPS], refs[GROUPS]
    flat = lambda ref: ref[...].reshape(LEN, D)
    whole[...] = dot3(flat(norm_h), flat(norm_l), hid_h[...], hid_l[...], TN)
    emit_blocks(scal, outs, whole)


def ffn_out_kernel(scal, acts_h, acts_l, wouth, woutl, *parts):
    for r in (1, 3, 2, 0):
        at = slice(r * CH, (r + 1) * CH)
        parts[r][...] = dot3(acts_h[at, :], acts_l[at, :], wouth[...], woutl[...], NN)


def output_kernel(scal, mixed, one, two, three, vec, output):
    output[...] = mixed[...] + (one[...] + two[...] + three[...]) + piece(vec, 7)


def proj_back_kernel(scal, one, two, three, hat, scale, vec, grad_out, wh, wl, mixed_grad, sums, *parts):
    mine = scal[0]
    normed = one[...] + two[...] + three[...]
    back = norm_back(hat[...], scale[:, :1], piece(vec, 5), normed)
    total = grad_out[...] + back
    mixed_grad[...] = total
    a, b = halves(total)
    for r in range(SEQ):
        at = rows_at(jnp.bitwise_xor(mine, r), QUARTER)
        parts[r][...] = dot3(wh[at, :], wl[at, :], a, b, NT)
    add = lambda v: jnp.sum(v, axis=0, keepdims=True)
    sums[...] = jnp.concatenate(
        [add(total), add(normed * hat[...]), add(normed), add(grad_out[...]), jnp.zeros((4, D), f32)],
        axis=0,
    )


def proj_grad_kernel(scal, heads_h, heads_l, mixed_grad, *refs):
    outs, whole = refs[:-1], refs[-1]
    mine = scal[0]
    gh, gl = halves(mixed_grad[...])
    whole[...] = dot3(heads_h[...], heads_l[...], gh, gl, NN)
    for r in range(SEQ):
        at = jnp.bitwise_xor(mine, r)
        for d in range(GROUPS):
            outs[r][d * SUB : (d + 1) * SUB, :] = whole[
                pl.ds(pl.multiple_of(d * ROWS + at * SUB, 8), SUB), :
            ]


def back_kernel(scal, *refs):
    grads, refs = refs[:4], refs[4:]
    kcat, qturn, vcat, qpair, kturn, outs_turn, lse, low_row = refs[:8]
    joined_h, joined_l, joined_sums = refs[8:11]
    gturn, gpair, dots, key_sum, value_sum, query_turn = refs[11:]
    mine = scal[0]

    for r in range(SEQ):
        at = rows_at(jnp.bitwise_xor(mine, r), CH)
        turned = grads[r][...]
        grad = jnp.concatenate([turned, jnp.zeros((HEAD, CH), f32)], axis=0).T
        pairs = lane_pairs(grad[:, :128], grad[:, 128:])
        for h in range(OWN):
            gpair[h, at, :] = pairs[h]
            part = turned[HEAD * h : HEAD * (h + 1)]
            dots[h, :, at] = jnp.broadcast_to(
                jnp.sum(part * outs_turn[HEAD * h : HEAD * (h + 1), at], axis=0, keepdims=True), (8, CH)
            )
            a, b = halves(part)
            gturn[h, :, at] = jnp.concatenate([a, a, b, b], axis=0)

    key_sum[...] = jnp.zeros_like(key_sum)
    value_sum[...] = jnp.zeros_like(value_sum)

    def one_head(h, carry):
        for c in range(SEQ):
            size = CH * (c + 1)
            lanes = slice(c * CH, (c + 1) * CH)
            score = dot(kcat[h, :size, :], qturn[h, :, lanes], NN)
            weight = jnp.where(allowed(low_row, c, size), jnp.exp(score - lse[h, :1, lanes]), 0.0)
            back = dot(vcat[h, :size, :], gturn[h, :, lanes], NN)
            score_back = weight * (back - dots[h, :1, lanes])
            a, b = halves(weight)
            pair = gpair[h, lanes, :]
            value_sum[h, :size, :] += dot(a, pair, NN) + dot(b, pair, NN)
            a, b = halves(score_back)
            pair = qpair[h, lanes, :]
            key_sum[h, :size, :] += dot(a, pair, NN) + dot(b, pair, NN)
            turned = dot(kturn[h, :, :size], a, NN) + dot(kturn[h, :, :size], b, NN)
            query_turn[h, :, lanes] = (turned[:HEAD] + turned[HEAD:]) * HEAD ** (-0.5)
        return carry

    lax.fori_loop(0, OWN, one_head, 0)

    column_sums = jnp.zeros((1, D), f32)
    low = low_lanes((CH, 128))
    for c in range(SEQ):
        at = slice(c * CH, (c + 1) * CH)
        blank = jnp.zeros((HEAD, CH), f32)
        query = jnp.concatenate([query_turn[h, :, at] for h in range(OWN)] + [blank], axis=0).T
        done = [query]
        for kept in (key_sum, value_sum):
            full = [kept[h, at, :] for h in range(OWN)]
            full = [v + pltpu.roll(v, HEAD, 1) for v in full]
            done.append(jnp.where(low, full[0], full[1]))
            done.append(jnp.where(low, full[2], 0.0))
        joined = jnp.concatenate(done, axis=1)
        column_sums = column_sums + jnp.sum(joined, axis=0, keepdims=True)
        joined_h[at, :], joined_l[at, :] = halves(joined)

    joined_sums[...] = jnp.broadcast_to(column_sums, (8, D))


def qkv_grad_kernel(scal, xh, xl, joined_h, joined_l, joined_sums, wh, wl, vec, *refs):
    proj_one, proj_two, vector_sums, bias_sum = refs[:4]
    outs, (whole, rows) = refs[4 : 4 + GROUPS], refs[4 + GROUPS :]
    mine = scal[0]
    column_sums = joined_sums[:1, :]
    core = dot3(xh[...], xl[...], joined_h[...], joined_l[...], TN)
    gain, shift = piece(vec, 0), piece(vec, 1)
    as_column = lambda v: jnp.broadcast_to(v, (128, D)).T[:, :1]
    whole[...] = as_column(gain) * core + as_column(shift) * column_sums
    weights = wh[...].astype(f32) + wl[...].astype(f32)
    gain_grad = jnp.sum(weights * core, axis=1, keepdims=True)
    shift_grad = jnp.sum(weights * column_sums, axis=1, keepdims=True)
    lane = lax.broadcasted_iota(jnp.int32, (D, 128), 1)
    norm_grads = jnp.where(lane == 0, gain_grad, shift_grad).T

    def place(part, scale):
        wide = jnp.concatenate([part[:, :QUARTER], jnp.zeros((1, D - QUARTER), f32)], axis=1)
        wide = jnp.broadcast_to(wide, (8, D))
        return pltpu.roll(wide, mine * QUARTER, 1)[:1]

    entries = [
        norm_grads[0:1],
        norm_grads[1:2],
        place(column_sums[:, :CH], 1.0),
        place(column_sums[:, 2 * CH :], 1.0),
        vector_sums[0:1],
        vector_sums[1:2],
        vector_sums[2:3],
        vector_sums[3:4],
    ]
    lines = [e[:, i * HALF_VEC : (i + 1) * HALF_VEC] for e in entries for i in range(2)]
    bias = jnp.concatenate(
        [bias_sum[:1, d * ROWS : (d + 1) * ROWS] for d in range(GROUPS)], axis=0
    )
    bias = jnp.concatenate([bias, jnp.zeros((GROUPS, HALF_VEC - ROWS), f32)], axis=1)
    bias = pltpu.roll(bias, mine * ROWS, 1)
    lines = lines + [bias[d : d + 1] for d in range(GROUPS)]
    filler = jnp.zeros((5, HALF_VEC), f32)
    for d in range(GROUPS):
        rows[d] = jnp.concatenate(lines[3 * d : 3 * d + 3] + [filler], axis=0)

    for k in range(GROUPS):
        at = owner(scal, k)
        outs[k][:ROWS, :] = whole[rows_at(at, ROWS), :]
        here = pl.ds(pl.multiple_of(at * SUB, 8), SUB)
        proj = proj_one[here, :] + proj_two[here, :]
        for group in range(SEQ):
            for part in range(3):
                lane_at = HEAD * (3 * group + part)
                outs[k][
                    group * SUB : (group + 1) * SUB, part * CH + QUARTER : (part + 1) * CH
                ] = proj[:, lane_at : lane_at + HEAD]
        outs[k][ROWS:, :HALF_VEC] = rows[at]
        outs[k][ROWS:, HALF_VEC:] = jnp.zeros((8, HALF_VEC), f32)


def pre_back_kernel(scal, joined_h, joined_l, wh, wl, *parts):
    mine = scal[0]
    for r in (1, 3, 2, 0):
        at = rows_at(jnp.bitwise_xor(mine, r), CH)
        parts[r][...] = dot3(joined_h[at, :], joined_l[at, :], wh[...], wl[...], NT)


def input_grad_kernel(scal, tokens, one, two, three, vec, mixed_grad, result):
    hat, scale = norm_stats(tokens[...])
    grad = one[...] + two[...] + three[...]
    result[...] = mixed_grad[...] + norm_back(hat, scale, piece(vec, 0), grad)


def total_square(value):
    return jnp.sum(jnp.sum(value * value, axis=0, keepdims=True), axis=1, keepdims=True)


def second_squares_kernel(scal, *refs):
    parts, squares = refs[:8], refs[8]
    total = sum(total_square(part[...]) for part in parts)
    squares[...] = jnp.broadcast_to(total, (8, 128))


def first_squares_kernel(scal, one, two, three, four, before, squares):
    parts = (one, two, three, four)
    total = sum(total_square(part[:ROWS, :]) for part in parts)
    line = sum(part[ROWS:, :HALF_VEC] for part in parts)
    squares[...] = before[...] + (total + total_square(line))


def stage_kernel(scal, *refs):
    sources, targets, sems = refs[:15], refs[15:30], refs[30]
    copies = [
        pltpu.make_async_copy(source, target, sems.at[i])
        for i, (source, target) in enumerate(zip(sources, targets))
    ]
    for copy in copies:
        copy.start()
    for copy in copies:
        copy.wait()


def adamw_kernel(scal, squares, *refs):
    firsts, ins, outs, refs = refs[:4], refs[4:8], refs[8:12], refs[12:]
    states, clip, finals, news = refs[:15], refs[15], refs[16:31], refs[31:46]
    first, second, sems = refs[46:]
    send = lambda number: [
        pltpu.make_async_copy(news[i], finals[i], sems.at[i]) for i in range(3 * number, 3 * number + 3)
    ]
    mine = scal[0]
    norm = jnp.sqrt(squares[...])
    clip[...] = norm
    factor = (clip_limit / jnp.maximum(norm, clip_limit))[:1, :1]
    for r in range(SEQ):
        at = jnp.bitwise_xor(mine, r)
        first[at] = firsts[r][:ROWS, :]
        second[at, :ROWS] = ins[r][...]
        second[at, ROWS:] = outs[r][...]

    def update(number, spot, grad, rate, decay):
        held = [states[3 * number + i][spot] for i in range(3)]
        fresh = adamw_update(*held, factor * grad, rate, decay)
        for i in range(3):
            news[3 * number + i][spot] = fresh[i]

    def finish(number):
        for copy in send(number):
            copy.start()

    line = sum(firsts[r][ROWS:, :HALF_VEC] for r in range(SEQ))
    for i in range(3):
        for j in range(3):
            spot = (slice(3 * i + j, 3 * i + j + 1), slice(None))
            update(0, spot, line[i : i + 1, 128 * j : 128 * (j + 1)], vector_rate, 0.0)
    finish(0)
    every = slice(None)
    for part in range(3):
        grad = jnp.concatenate(
            [first[j][:, part * CH : part * CH + QUARTER] for j in range(SEQ)], axis=1
        )
        update(1, (every, slice(part * D, (part + 1) * D)), grad, matrix_rate, weight_decay)
    finish(1)
    for j in range(SEQ):
        grad = jnp.concatenate(
            [
                first[j][group * SUB : (group + 1) * SUB, part * CH + QUARTER : (part + 1) * CH]
                for group in range(SEQ)
                for part in range(3)
            ],
            axis=1,
        )
        update(2, (slice(j * SUB, (j + 1) * SUB), every), grad, matrix_rate, weight_decay)
    finish(2)
    for d in range(GROUPS):
        grad = jnp.concatenate(
            [second[j][:ROWS, d * ROWS : (d + 1) * ROWS] for j in range(SEQ)], axis=1
        )
        update(3, (every, slice(d * HALF_VEC, (d + 1) * HALF_VEC)), grad, matrix_rate, weight_decay)
    finish(3)
    for j in range(SEQ):
        update(
            4, (slice(j * ROWS, (j + 1) * ROWS), every), second[j][ROWS:, :], matrix_rate, weight_decay
        )
    finish(4)
    for number in range(5):
        for copy in send(number):
            copy.wait()


def adamw_update(weight, first, second, grad, rate, decay):
    new_first = beta_one * first + (1.0 - beta_one) * grad
    new_second = beta_two * second + (1.0 - beta_two) * grad * grad
    first_hat = new_first / (1.0 - beta_one**STEP)
    second_hat = new_second / (1.0 - beta_two**STEP)
    new_weight = weight - rate * (first_hat / (jnp.sqrt(second_hat) + adam_eps) + decay * weight)
    return (new_first, new_second, new_weight)


def ring_tables(count):
    evens = [2 * i for i in range(count // 2)]
    order = evens + [i + 1 for i in reversed(evens)]
    place = [0] * count
    for position, device in enumerate(order):
        place[device] = position
    right = [(order[i], order[(i + 1) % count]) for i in range(count)]
    left = [(b, a) for a, b in right]
    return order, place, right, left


class RingGather:
    def __init__(self, block, name):
        _, _, self.right, self.left = ring_tables(GROUPS)
        self.got, self.name, self.at = {0: block}, name, 0

    def step(self, after=()):
        places = (-self.at % GROUPS, self.at)
        if after:
            for place in set(places):
                self.got[place] = gate(self.got[place], after)
        forth, back = (self.got[place] for place in places)
        self.at += 1
        self.got[GROUPS - self.at] = move(forth, "dp", self.right, f"{self.name}_right_{self.at}")
        self.got[self.at] = move(back, "dp", self.left, f"{self.name}_left_{self.at}")
        return [forth, back]

    def last(self, cut=0):
        forth, back = self.got[GROUPS - self.at], self.got[self.at]
        if not cut:
            self.got[HALF] = move(forth, "dp", self.right, f"{self.name}_right_{HALF}")
            return None
        top, rest = split_rows(forth, back, cut)
        self.got[HALF] = move(top, "dp", self.right, f"{self.name}_right_{HALF}")
        return move(rest, "dp", self.left, f"{self.name}_left_{HALF}")

    def blocks(self):
        return [self.got[k] for k in range(GROUPS)]


class RingScatter:
    def __init__(self, blocks, name, flip=False):
        _, _, self.right, self.left = ring_tables(GROUPS)
        self.blocks = blocks
        if flip:
            self.right, self.left = self.left, self.right
            self.blocks = [blocks[-k % GROUPS] for k in range(GROUPS)]
        self.name, self.back, self.at = name, None, HALF
        self.forth = move(self.blocks[HALF], "dp", self.right, f"{name}_right_1")

    def step(self, after=()):
        self.at -= 1
        ahead, back = self.blocks[self.at], self.blocks[GROUPS - self.at]
        if self.back is None:
            forth = plus(self.forth, ahead, after=after)
        else:
            forth, back = sums([(self.forth, ahead), (self.back, back)], after)
        number = HALF + 1 - self.at
        self.forth = move(forth, "dp", self.right, f"{self.name}_right_{number}")
        self.back = move(back, "dp", self.left, f"{self.name}_left_{number}")
        return [forth, back]

    def result(self, after=()):
        return plus(self.forth, self.back, self.blocks[0], after=after)


def move(block, axis, pairs, name):
    with jax.named_scope(name):
        return lax.ppermute(block, axis, pairs)


def swap(block, bits, name):
    return move(block, "seq", [(i, i ^ bits) for i in range(SEQ)], f"{name}_{bits}")


def gather_seq(block, name):
    across = swap(block, 2, name)
    core = swap(block, 1, name)
    return [block, core, across, swap(across, 1, f"{name}_2")]


def exchange_seq(parts, name):
    return [parts[0]] + [swap(parts[r], r, name) for r in range(1, SEQ)]


def scatter_core(parts, name):
    return parts[0], swap(parts[1], 1, f"{name}_own"), parts[2], swap(parts[3], 1, f"{name}_across")


def ordered(blocks, mine):
    stack = jnp.stack(blocks, axis=0)
    return [lax.dynamic_index_in_dim(stack, mine ^ j, 0, keepdims=False) for j in range(len(blocks))]


def local(
    tokens,
    cotangent,
    segment_ids,
    valid,
    vectors,
    vec_first,
    vec_second,
    w_qkv,
    qkv_first,
    qkv_second,
    w_proj,
    proj_first,
    proj_second,
    w_in,
    in_first,
    in_second,
    w_out,
    out_first,
    out_second,
):
    dp_parts = lax.axis_size("dp")
    ring = dp_parts == GROUPS
    mine = lax.axis_index("seq")
    home = lax.axis_index("dp")
    rows = w_qkv.shape[0]
    units = w_out.shape[0] // SEQ
    far, near = home // 2, home % 2
    position = jnp.where(near > 0, GROUPS - 1 - far, far)
    scal = jnp.stack([mine, position, jnp.full_like(mine, 1 if ring else 0)]).astype(jnp.int32)
    flat_in = tokens.reshape(CH, D)
    chunk, tall, square = shape(CH, D), shape(LEN, D, kind=bf16), shape(D, D, kind=bf16)

    if ring:
        first, packed = run(
            pack_first_kernel,
            scal,
            [w_qkv, w_proj, vectors.reshape(9, 128), segment_ids, valid, flat_in],
            [shape(ROWS + 8, D), shape(CH + 8, D)],
            scratch=[
                pltpu.VMEM((3, ROWS, CH), f32),
                pltpu.VMEM((SUB, D), f32),
                pltpu.VMEM((9, 128), f32),
                pltpu.VMEM((2, 1, CH), jnp.int32),
            ],
            sems=8,
            far_args=range(6),
            room=54,
            name="pack_first", work=3.0,
        )
        ring_first = RingGather(first, "first")
        for _ in range(HALF - 1):
            ring_first.step()
        ring_first.last()
        firsts = ring_first.blocks()
        (second,) = run(
            pack_second_kernel,
            scal,
            [w_in, w_out],
            [shape(2 * ROWS, D)],
            name="pack_second", work=3.0,
            after=[firsts[GROUPS - 1]],
        )
        ring_second = RingGather(second, "second")
        ring_second.step([firsts[HALF]])
    else:
        padded = jnp.pad(w_qkv, ((0, 0), (0, CH)))
        own = lambda part: lax.dynamic_slice_in_dim(padded, part * D + mine * QUARTER, CH, 1)
        first = jnp.concatenate([own(0), own(1), own(2)], axis=1)
        first = lax.all_gather(first, "dp", axis=0, tiled=True).reshape(GROUPS, ROWS, D)
        all_vec = lax.all_gather(vectors, "dp", axis=0, tiled=True).reshape(GROUPS, 3, HALF_VEC)
        first = jnp.concatenate([first, jnp.pad(all_vec, ((0, 0), (0, 5), (0, D - HALF_VEC)))], axis=1)
        firsts = [first[k] for k in range(GROUPS)]
        in_part = lax.dynamic_index_in_dim(
            w_in.reshape(rows, dp_parts, SEQ, units), mine, 2, keepdims=False
        ).reshape(rows, D)
        out_part = lax.dynamic_slice_in_dim(w_out, mine * units, units, 0)
        second = jnp.concatenate(
            [
                lax.all_gather(part, "dp", axis=0, tiled=True).reshape(GROUPS, ROWS, D)
                for part in (in_part, out_part)
            ],
            axis=1,
        )
        seconds = [second[k] for k in range(GROUPS)]
        seconds[HALF], second_rest = second[HALF, :ROWS], second[HALF, ROWS:]
        marks = jnp.where(valid > 0, segment_ids, -1).astype(f32)
        packed = jnp.concatenate([flat_in, jnp.pad(marks, ((0, 7), (0, D - CH)))], axis=0)
    toks = gather_seq(packed, "tokens")
    (grad_out,) = run(
        mask_kernel, scal, [cotangent.reshape(CH, D), valid], [chunk], name="mask", work=2.0, after=[toks[2]]
    )
    grads_row = gather_seq(grad_out, "cotangent")

    qkv_h, qkv_l, vec, proj = run(
        weights_kernel,
        scal,
        firsts,
        [square, square, shape(GROUPS, 8, HALF_VEC), shape(GROUPS * SUB, D)],
        name="weights", work=3.0,
    )
    if ring:
        proj_parts = gather_seq(proj, "w_proj")
    else:
        full = lax.all_gather(w_proj, "dp", axis=0, tiled=True).reshape(GROUPS, SEQ, SUB, D)
        proj_parts = [
            lax.dynamic_index_in_dim(full, mine ^ r, 1, keepdims=False).reshape(GROUPS * SUB, D)
            for r in range(SEQ)
        ]
    hat_h, hat_l, kcat, qturn, vcat, qpair, kturn, low_row, heads, lse = run(
        front_kernel,
        scal,
        toks + [qkv_h, qkv_l, vec],
        [
            tall,
            tall,
            shape(OWN, LEN, 256, kind=bf16),
            shape(OWN, 256, LEN, kind=bf16),
            shape(OWN, LEN, 256, kind=bf16),
            shape(OWN, LEN, 128, kind=bf16),
            shape(OWN, 128, LEN, kind=bf16),
            shape(8, LEN),
            shape(QUARTER, LEN),
            shape(OWN, 8, LEN),
        ],
        scratch=[pltpu.VMEM((OWN, 128, LEN), bf16), pltpu.VMEM((SEQ, 8, CH), f32)],
        name="front", work=14.0,
        after=[grads_row[2]],
    )
    if ring:
        ring_second.step([lse])
        ring_second.step()
        second_rest = ring_second.last(ROWS)
        seconds = ring_second.blocks()
        heads = gate(heads, [proj_parts[2]])
    wide = shape(D, CH, kind=bf16)
    split = shape(SEQ, CH, D, kind=bf16)
    proj_h, proj_l, heads_h, heads_l, norm_h, norm_l, mixed, hat_two, scale_two = run(
        proj_kernel,
        scal,
        toks + gather_seq(heads, "heads") + proj_parts + [vec],
        [square, square, wide, wide, split, split, chunk, chunk, shape(CH, 128)],
        scratch=[pltpu.VMEM((D, D), f32), pltpu.VMEM((D, LEN), f32)],
        name="proj", work=8.0,
    )

    block = shape(ROWS, D)
    acts_h, acts_l, slope, in_wh, in_wl = run(
        hidden_kernel,
        scal,
        [norm_h, norm_l] + seconds + [vec],
        [tall, tall, shape(LEN, D), square, square],
        name="hidden", work=8.0,
    )
    done = run(
        out_grad_kernel,
        scal,
        [acts_h, acts_l] + grads_row,
        [tall, tall] + [block] * GROUPS,
        scratch=[pltpu.VMEM((D, D), f32)],
        name="out_grad", work=5.0,
    )
    out_h, out_l = done[:2]
    out_grads = list(done[2:])
    if ring:
        ring_out = RingScatter(out_grads, "out_grad")
    done = run(
        hidden_back_kernel,
        scal,
        [out_h, out_l, slope, in_wh, in_wl] + seconds + [second_rest],
        [tall, tall, square, square, shape(8, D)] + [chunk] * SEQ,
        name="hidden_back", work=11.0,
        after=out_grads[:1],
    )
    hid_h, hid_l, out_wh, out_wl, bias_sum = done[:5]
    parts = list(done[5:])
    if ring:
        parts[3] = gate(parts[3], ring_out.step())
    norm_own, norm_near, norm_across, norm_far = scatter_core(parts, "norm_grad")
    norm_pair = plus(norm_across, norm_far)
    norm_last = swap(norm_pair, 2, "norm_grad")
    in_grads = list(
        run(
            in_grad_kernel,
            scal,
            [norm_h, norm_l, hid_h, hid_l],
            [block] * GROUPS,
            scratch=[pltpu.VMEM((D, D), f32)],
            name="in_grad", work=5.0,
            after=[norm_pair],
        )
    )
    if ring:
        ring_in = RingScatter(in_grads, "in_grad", flip=True)
        out_sent = ring_out.step()
        in_sent = ring_in.step()
    done = run(
        proj_back_kernel,
        scal,
        [norm_own, norm_near, norm_last, hat_two, scale_two, vec, grad_out, proj_h, proj_l],
        [chunk, shape(8, D)] + [shape(QUARTER, CH)] * SEQ,
        name="proj_back", work=5.0,
        after=out_sent + in_sent if ring else [],
    )
    mixed_grad, vector_sums = done[:2]
    head_grads = exchange_seq(list(done[2:]), "head_grad")
    if ring:
        out_sent = ring_out.step([mixed_grad])
        in_sent = ring_in.step([mixed_grad])
    out_parts = run(
        ffn_out_kernel,
        scal,
        [acts_h, acts_l, out_wh, out_wl],
        [chunk] * SEQ,
        name="ffn_out", work=7.0,
        after=[mixed_grad],
    )
    proj_grads = run(
        proj_grad_kernel,
        scal,
        [heads_h, heads_l, mixed_grad],
        [shape(GROUPS * SUB, D)] * SEQ,
        scratch=[pltpu.VMEM((D, D), f32)],
        name="proj_grad", work=4.0,
        after=[*head_grads[1:], *out_sent, *in_sent, out_parts[0]] if ring else [],
    )
    wait = [head_grads[3], head_grads[2]]
    out_own, out_near, out_across, out_far = scatter_core(out_parts, "output")
    if ring:
        proj_own, proj_near, proj_across, proj_far = scatter_core(proj_grads, "proj_grad")
        proj_pair, proj_base = sums([(proj_across, proj_far), (proj_own, proj_near)], wait)
        proj_last = swap(proj_pair, 2, "proj_grad")
    else:
        proj_base = proj_last = proj_grads[0]
    joined_h, joined_l, joined_sums = run(
        back_kernel,
        scal,
        head_grads + [kcat, qturn, vcat, qpair, kturn, heads, lse, low_row],
        [tall, tall, shape(8, D)],
        scratch=[
            pltpu.VMEM((OWN, 256, LEN), bf16),
            pltpu.VMEM((OWN, LEN, 128), bf16),
            pltpu.VMEM((OWN, 8, LEN), f32),
            pltpu.VMEM((OWN, LEN, 128), f32),
            pltpu.VMEM((OWN, LEN, 128), f32),
            pltpu.VMEM((OWN, HEAD, LEN), f32),
        ],
        name="back", work=16.0,
        after=[proj_grads[0]],
    )
    if ring:
        shard_out = ring_out.result([joined_sums])
        in_sent = ring_in.step([joined_sums])
    done = run(
        qkv_grad_kernel,
        scal,
        [hat_h, hat_l, joined_h, joined_l, joined_sums, qkv_h, qkv_l, vec]
        + [proj_base, proj_last, vector_sums, bias_sum],
        [shape(ROWS + 8, D)] * GROUPS,
        scratch=[pltpu.VMEM((D, D), f32), pltpu.VMEM((GROUPS, 8, HALF_VEC), f32)],
        name="qkv_grad", work=1.0,
        after=[*in_sent, shard_out] if ring else [],
    )
    first_grads = list(done)
    if ring:
        shard_in = ring_in.result([first_grads[0]])
        first_grads[HALF] = gate(first_grads[HALF], [shard_in])
        ring_first = RingScatter(first_grads, "first_grad")
        out_all = gather_seq(shard_out, "out_shard")
        in_all = gather_seq(shard_in, "in_shard")
        first_sent = ring_first.step()
    pre_parts = run(
        pre_back_kernel,
        scal,
        [joined_h, joined_l, qkv_h, qkv_l],
        [chunk] * SEQ,
        name="pre_back", work=1.0,
        after=[shard_in, *first_sent] if ring else [],
    )
    pre_parts = list(pre_parts)
    if ring:
        first_sent = ring_first.step()
        pre_parts[3] = gate(pre_parts[3], [*first_sent, out_all[2]])
    pre_own, pre_near, pre_across, pre_far = scatter_core(pre_parts, "pre_grad")
    pre_pair = plus(pre_across, pre_far)
    pre_last = swap(pre_pair, 2, "pre_grad")
    states = [vectors, vec_first, vec_second, w_qkv, qkv_first, qkv_second, w_proj, proj_first, proj_second]
    states = states + [w_in, in_first, in_second, w_out, out_first, out_second]
    if ring:
        ring_first.step([in_all[2]])
        shard_first = ring_first.result()
        held = [v.reshape(9, 128) for v in states[:3]] + states[3:]
        held = run(
            stage_kernel,
            scal,
            held,
            [shape(*v.shape) for v in held],
            sems=15,
            far_args=range(15),
            name="stage", work=4.0,
            after=[pre_pair],
        )
    (input_grad,) = run(
        input_grad_kernel,
        scal,
        [flat_in, pre_own, pre_near, pre_last, vec, mixed_grad],
        [chunk],
        name="input_grad", work=3.0,
    )

    if ring:
        (squares,) = run(
            second_squares_kernel, scal, in_all + out_all, [shape(8, 128)], name="second_squares", work=2.0
        )
        shard_first = gate(shard_first, [pre_last, held[3]])
        across = gate(swap(shard_first, 2, "first_shard"), [input_grad, squares])
        core = swap(shard_first, 1, "first_shard")
        first_all = [shard_first, core, across, swap(across, 1, "first_shard_2")]
        out_pair = plus(out_across, out_far, after=[across])
        (squares,) = run(
            first_squares_kernel,
            scal,
            first_all + [squares],
            [shape(8, 128)],
            name="first_squares", work=2.0,
            after=[out_pair],
        )
        for bits in (1, 2, 4):
            pairs = [(i, i ^ bits) for i in range(GROUPS)]
            squares = plus(squares, move(squares, "dp", pairs, "squares"))
        done = run(
            adamw_kernel,
            scal,
            [squares] + first_all + in_all + out_all + list(held),
            [shape(8, 128)] + [shape(*v.shape) for v in held],
            scratch=[pltpu.VMEM(v.shape, f32) for v in held]
            + [pltpu.VMEM((SEQ, ROWS, D), f32), pltpu.VMEM((SEQ, 2 * ROWS, D), f32)],
            sems=15,
            far_outs=range(1, 16),
            name="adamw", work=0.1,
        )
        new = [v.reshape(-1) for v in done[1:4]] + list(done[4:])
        clip_norm = done[0][0, 0]
    else:
        out_pair = plus(out_across, out_far)
        by_group = jnp.stack(first_grads)
        shard_first = lax.psum_scatter(
            by_group[:, :ROWS].reshape(D, D), "dp", scatter_dimension=0, tiled=True
        )
        proj_full = jnp.stack([p.reshape(GROUPS, SUB, D) for p in ordered(proj_grads, mine)], axis=1)
        proj_grad = lax.psum(
            lax.psum_scatter(proj_full.reshape(D, D), "dp", scatter_dimension=0, tiled=True), "seq"
        )
        all_vec = lax.psum(by_group[:, ROWS : ROWS + 3, :HALF_VEC], ("dp", "seq")).reshape(-1)
        vec_grad = lax.dynamic_slice_in_dim(all_vec, home * vectors.shape[0], vectors.shape[0])
        joined = lax.all_gather(shard_first, "seq", axis=0, tiled=False)
        qkv_grad = jnp.concatenate(
            [joined[j, :, i * CH : i * CH + QUARTER] for i in range(3) for j in range(SEQ)], axis=1
        )
        shard_in, shard_out = (
            lax.psum_scatter(jnp.concatenate(parts, axis=0), "dp", scatter_dimension=0, tiled=True)
            for parts in (in_grads, out_grads)
        )
        in_all = lax.all_gather(shard_in, "seq", axis=0, tiled=False)
        in_grad = in_all.reshape(SEQ, rows, dp_parts, units).transpose(1, 2, 0, 3).reshape(rows, -1)
        out_grad = lax.all_gather(shard_out, "seq", axis=0, tiled=True)
        total = sum(jnp.sum(g * g) for g in (qkv_grad, proj_grad, in_grad, out_grad, vec_grad))
        total = lax.psum(total, "dp")
        clip_norm = jnp.sqrt(total)
        factor = clip_limit / jnp.maximum(clip_norm, clip_limit)
        grads = (vec_grad, qkv_grad, proj_grad, in_grad, out_grad)
        new = []
        for number, grad in enumerate(grads):
            rate, decay = (matrix_rate, weight_decay) if number else (vector_rate, 0.0)
            new.extend(adamw_update(*states[3 * number : 3 * number + 3], factor * grad, rate, decay))
    out_last = swap(out_pair, 2, "output")
    (output,) = run(
        output_kernel, scal, [mixed, out_own, out_near, out_last, vec], [chunk], name="output", work=2.0
    )
    return (output.reshape(tokens.shape), input_grad.reshape(tokens.shape), clip_norm, *new)


def solution(mesh):
    row = P("dp", "seq", None)
    mark = P("dp", "seq")
    vec = P("dp")
    mat = P("dp", None)
    return jax.shard_map(
        local,
        mesh=mesh,
        in_specs=(row, row, mark, mark) + (vec,) * 3 + (mat,) * 12,
        out_specs=(row, row, P()) + (vec,) * 3 + (mat,) * 12,
        check_vma=False,
    )
```

```python
import functools
import math

import jax
import jax.numpy as jnp
from jax import lax
from jax.experimental import pallas as pl
from jax.experimental.pallas import tpu as pltpu
from jax.sharding import PartitionSpec as P

D = 768
HEADS = 12
HEAD = 64
STEP = 10
CH = 256
LEN = 1024
SEQ = 4
QUARTER = D // SEQ
OWN = HEADS // SEQ
GROUPS = 8
ROWS = D // GROUPS
SUB = ROWS // SEQ
HALF = GROUPS // 2
HALF_VEC = D // 2
VEC_ROWS = 24

f32 = jnp.float32
bf16 = jnp.bfloat16
masked_score = -1e30
norm_eps = 1e-05
clip_limit = 1.0
beta_one = 0.9
beta_two = 0.999
adam_eps = 1e-08
matrix_rate = 0.02
vector_rate = 0.4
weight_decay = 0.01
gelu_scale = 0.7978845608028654
gelu_cubic = 0.044715

COST = 1e9

WHOLE = pl.BlockSpec(memory_space=pltpu.VMEM)
SCALARS = pl.BlockSpec(memory_space=pltpu.SMEM)
NN = ((1,), (0,))
NT = ((1,), (1,))
TN = ((0,), (0,))


def shape(*dims, kind=f32):
    return jax.ShapeDtypeStruct(dims, kind)


def run(
    kernel, scal, args, outs, scratch=(), sems=0, far_args=(), far_outs=(), room=8, work=1.0, name=None, after=()
):
    args, after = list(args), list(after)
    held = sum(math.prod(v.shape) * jnp.dtype(v.dtype).itemsize for v in scratch)
    anywhere, far = pl.BlockSpec(memory_space=pl.ANY), pl.BlockSpec(memory_space=pltpu.HBM)
    scratch = list(scratch) + ([pltpu.SemaphoreType.DMA((sems,))] if sems else [])

    def body(scal_ref, *refs):
        kernel(scal_ref, *refs[: len(args)], *refs[len(args) + len(after) :])

    return pl.pallas_call(
        body,
        out_shape=tuple(outs),
        in_specs=[SCALARS]
        + [far if i in far_args else WHOLE for i in range(len(args))]
        + [anywhere] * len(after),
        out_specs=tuple(far if i in far_outs else WHOLE for i in range(len(outs))),
        scratch_shapes=scratch,
        compiler_params=pltpu.CompilerParams(vmem_limit_bytes=held + (room << 20)),
        cost_estimate=pl.CostEstimate(
            flops=int(work * COST), bytes_accessed=1, transcendentals=0
        ),
        name=name,
    )(scal, *args, *after)


def gate(value, after):
    anywhere = pl.BlockSpec(memory_space=pl.ANY)
    return pl.pallas_call(
        lambda *refs: None,
        out_shape=shape(*value.shape, kind=value.dtype),
        in_specs=[anywhere] * (1 + len(after)),
        out_specs=anywhere,
        input_output_aliases={0: 0},
        compiler_params=pltpu.CompilerParams(vmem_limit_bytes=1 << 20),
        name="gate",
    )(value, *after)


def sums(groups, after=()):
    sizes = [len(group) for group in groups]

    def body(*refs):
        at = 0
        for number, size in enumerate(sizes):
            total = refs[at][...]
            for ref in refs[at + 1 : at + size]:
                total = total + ref[...]
            refs[sum(sizes) + len(after) + number][...] = total
            at += size

    return pl.pallas_call(
        body,
        out_shape=tuple(shape(*group[0].shape) for group in groups),
        in_specs=[WHOLE] * sum(sizes) + [pl.BlockSpec(memory_space=pl.ANY)] * len(after),
        out_specs=tuple([WHOLE] * len(groups)),
        compiler_params=pltpu.CompilerParams(vmem_limit_bytes=4 << 20),
        cost_estimate=pl.CostEstimate(flops=int(COST), bytes_accessed=1, transcendentals=0),
        name="plus",
    )(*(term for group in groups for term in group), *after)


def plus(*terms, after=()):
    return sums([terms], after)[0]


def sum_pairs(one, two, three, four):
    def body(a, b, c, d, result):
        result[...] = (a[...] + b[...]) + (c[...] + d[...])

    return pl.pallas_call(
        body,
        out_shape=shape(*one.shape),
        in_specs=[WHOLE] * 4,
        out_specs=WHOLE,
        compiler_params=pltpu.CompilerParams(vmem_limit_bytes=1 << 20),
        name="sum_pairs",
    )(one, two, three, four)


def owner(scal, k):
    spot = jnp.bitwise_and(scal[1] + k, GROUPS - 1)
    return jnp.where(scal[2] > 0, jnp.where(spot < HALF, 2 * spot, 2 * GROUPS - 1 - 2 * spot), k)


def halves(value):
    top = value.astype(bf16)
    return top, (value - top.astype(f32)).astype(bf16)


def dot(left, right, dims):
    return lax.dot_general(left, right, (dims, ((), ())), preferred_element_type=f32)


def dot3(lh, ll, rh, rl, dims):
    return dot(lh, rh, dims) + (dot(lh, rl, dims) + dot(ll, rh, dims))


def rows_at(index, size):
    return pl.ds(pl.multiple_of(index * size, size), size)


def piece(vec, number):
    a, b = 2 * number, 2 * number + 1
    return jnp.concatenate(
        [vec[a // 3, a % 3 : a % 3 + 1, :], vec[b // 3, b % 3 : b % 3 + 1, :]], axis=1
    )


def norm_stats(inputs):
    center = inputs - jnp.mean(inputs, axis=-1, keepdims=True)
    spread = jnp.mean(center * center, axis=-1, keepdims=True)
    scale = lax.rsqrt(spread + norm_eps)
    return center * scale, scale


def norm_back(hat, scale, gain, grad):
    inner = grad * gain
    return scale * (
        inner
        - jnp.mean(inner, axis=-1, keepdims=True)
        - hat * jnp.mean(inner * hat, axis=-1, keepdims=True)
    )


def low_lanes(dims):
    return lax.broadcasted_iota(jnp.int32, dims, 1) < HEAD


def lane_pairs(pair, last):
    low = low_lanes(pair.shape)
    roll = lambda v: pltpu.roll(v, HEAD, 1)
    ph = pair.astype(bf16).astype(f32)
    pl_ = pair - ph
    lh = last.astype(bf16).astype(f32)
    ll = last - lh
    return [
        jnp.where(low, ph, roll(pl_)).astype(bf16),
        jnp.where(low, roll(ph), pl_).astype(bf16),
        jnp.where(low, lh, roll(ll)).astype(bf16),
    ]


def row_halves(turned, head):
    part = turned[HEAD * head : HEAD * (head + 1)]
    return halves(part)


def pack_first_kernel(scal, wqkv, wproj, vec, seg, valid, tokens, first, packed, *refs):
    bands, proj, lines, marks, sems = refs
    mine = scal[0]
    aligned = pl.multiple_of(jnp.bitwise_and(mine * QUARTER, -128), 128)
    copies = [
        pltpu.make_async_copy(wqkv.at[:, pl.ds(part * D + aligned, CH)], bands.at[part], sems.at[part])
        for part in range(3)
    ]
    sub = pl.ds(pl.multiple_of(mine * SUB, 8), SUB)
    copies.append(pltpu.make_async_copy(wproj.at[sub, :], proj, sems.at[3]))
    copies.append(pltpu.make_async_copy(vec, lines, sems.at[4]))
    copies.append(pltpu.make_async_copy(seg, marks.at[0], sems.at[5]))
    copies.append(pltpu.make_async_copy(valid, marks.at[1], sems.at[6]))
    copies.append(pltpu.make_async_copy(tokens, packed.at[:CH, :], sems.at[7]))
    for copy in copies:
        copy.start()
    first[ROWS:, :] = jnp.zeros((8, D), f32)
    packed[CH:, :] = jnp.zeros((8, D), f32)
    for copy in copies[:5]:
        copy.wait()
    turn = jnp.where(jnp.bitwise_and(mine, 1) > 0, CH - HEAD, 0)
    for part in range(3):
        turned = pltpu.roll(bands[part], turn, 1)
        first[:ROWS, part * CH : part * CH + QUARTER] = turned[:, :QUARTER]
        for group in range(SEQ):
            lane = HEAD * (3 * group + part)
            first[group * SUB : (group + 1) * SUB, part * CH + QUARTER : (part + 1) * CH] = proj[
                :, lane : lane + HEAD
            ]
        first[ROWS + part : ROWS + part + 1, :HALF_VEC] = jnp.concatenate(
            [lines[3 * part + i : 3 * part + i + 1, :] for i in range(3)], axis=1
        )
    for copy in copies[5:]:
        copy.wait()
    packed[CH : CH + 1, :CH] = jnp.where(marks[1] > 0, marks[0], -1).astype(f32)


def pack_second_kernel(scal, win, wout, in_block, out_block):
    mine = scal[0]
    turn = lax.rem(HALF_VEC - mine * ROWS, HALF_VEC)
    for part in range(GROUPS):
        turned = pltpu.roll(win[:, part * HALF_VEC : (part + 1) * HALF_VEC], turn, 1)
        in_block[:, part * ROWS : (part + 1) * ROWS] = turned[:, :ROWS]
    out_block[...] = wout[pl.ds(pl.multiple_of(mine * ROWS, 8), ROWS), :]


def mask_kernel(scal, cotangent, valid, result):
    keep = jnp.where(valid[...] > 0, 1.0, 0.0).astype(f32)
    column = jnp.broadcast_to(keep, (128, CH)).T[:, :1]
    result[...] = cotangent[...] * column


def weights_kernel(scal, *refs):
    blocks, (wh, wl, vec, proj) = refs[:GROUPS], refs[GROUPS:]
    for k in range(GROUPS):
        at = owner(scal, k)
        block = blocks[k][:ROWS, :]
        here = rows_at(at, ROWS)
        wh[here, :], wl[here, :] = halves(block)
        vec[at] = blocks[k][ROWS:, :HALF_VEC]
        for group in range(SEQ):
            for part in range(3):
                lane = HEAD * (3 * group + part)
                proj[pl.ds(pl.multiple_of(at * SUB, 8), SUB), lane : lane + HEAD] = block[
                    group * SUB : (group + 1) * SUB, part * CH + QUARTER : (part + 1) * CH
                ]


def front_kernel(scal, *refs):
    toks, refs = refs[:4], refs[4:]
    wh, wl, vec = refs[:3]
    xh, xl, kcat, qturn, vcat, qpair, kturn, low_row, outs_turn, lse, vturn, label = refs[3:]
    mine = scal[0]

    gain, shift = piece(vec, 0), piece(vec, 1)
    turn = lax.rem(D - mine * QUARTER, D)
    own = lambda number: pltpu.roll(jnp.broadcast_to(piece(vec, number), (8, D)), turn, 1)[:1, :CH]
    query_bias, value_bias = own(2), own(3)

    for r in range(SEQ):
        nat = jnp.bitwise_xor(mine, r)
        at = rows_at(nat, CH)
        label[nat] = toks[r][CH:, :CH]
        hat, _ = norm_stats(toks[r][:CH, :])
        xh[at, :], xl[at, :] = halves(hat)
        nh, nl = halves(hat * gain + shift)
        joined = dot3(nh, nl, wh[...], wl[...], NN)
        query = (joined[:, :CH] + query_bias) * HEAD ** (-0.5)
        key = joined[:, CH : 2 * CH]
        value = joined[:, 2 * CH :] + value_bias
        keys = lane_pairs(key[:, :128], key[:, 128:])
        values = lane_pairs(value[:, :128], value[:, 128:])
        queries = lane_pairs(query[:, :128], query[:, 128:])
        key_t, value_t, query_t = key.T, value.T, query.T
        for h in range(OWN):
            kcat[h, at, :] = jnp.concatenate([keys[h], keys[h]], axis=1)
            vcat[h, at, :] = jnp.concatenate([values[h], values[h]], axis=1)
            qpair[h, at, :] = queries[h]
            a, b = row_halves(query_t, h)
            qturn[h, :, at] = jnp.concatenate([a, a, b, b], axis=0)
            a, b = row_halves(key_t, h)
            kturn[h, :, at] = jnp.concatenate([a, b], axis=0)
            a, b = row_halves(value_t, h)
            vturn[h, :, at] = jnp.concatenate([a, b], axis=0)

    labels = jnp.concatenate([label[c][:1, :] for c in range(SEQ)], axis=1)
    spot = lax.broadcasted_iota(jnp.int32, (1, LEN), 1).astype(f32)
    begin = jnp.zeros((1, LEN), f32)
    for segment in range(3):
        held = jnp.sum(jnp.where(labels == float(segment), 1.0, 0.0), axis=1, keepdims=True)
        begin = begin + jnp.where(labels > float(segment), held, 0.0)
    begin = jnp.where(labels < 0.0, spot, begin)
    low_row[...] = jnp.broadcast_to(begin, (8, LEN))

    def one_head(h, carry):
        for c in range(SEQ):
            size = CH * (c + 1)
            lanes = slice(c * CH, (c + 1) * CH)
            score = dot(kcat[h, :size, :], qturn[h, :, lanes], NN)
            mask = allowed(low_row, c, size)
            score = jnp.where(mask, score, masked_score)
            peak = jnp.max(score, axis=0, keepdims=True)
            weight = jnp.exp(score - peak)
            total = jnp.sum(weight, axis=0, keepdims=True)
            top, rest = halves(weight)
            both = dot(vturn[h, :, :size], top, NN)
            extra = dot(vturn[h, :HEAD, :size], rest, NN)
            result = (both[:HEAD] + both[HEAD:] + extra) / total
            outs_turn[pl.ds(pl.multiple_of(h * HEAD, HEAD), HEAD), lanes] = result
            lse[h, :, lanes] = jnp.broadcast_to(peak + jnp.log(total), (8, CH))
        return carry

    lax.fori_loop(0, OWN, one_head, 0)


def allowed(low_row, c, size):
    key_at = lax.broadcasted_iota(jnp.int32, (size, CH), 0).astype(f32)
    query_at = (lax.broadcasted_iota(jnp.int32, (1, CH), 1) + c * CH).astype(f32)
    begin = low_row[:1, c * CH : (c + 1) * CH]
    return (key_at >= begin) & (key_at <= query_at)


def proj_kernel(scal, *refs):
    toks, heads, parts, refs = refs[:4], refs[4:8], refs[8:12], refs[12:]
    vec, wh, wl, heads_h, heads_l, norm_h, norm_l, mixed, hat, scale, weight, joined = refs
    mine = scal[0]
    for r in range(SEQ):
        at = jnp.bitwise_xor(mine, r)
        for d in range(GROUPS):
            weight[pl.ds(pl.multiple_of(d * ROWS + at * SUB, 8), SUB), :] = parts[r][
                d * SUB : (d + 1) * SUB, :
            ]
        joined[rows_at(at, QUARTER), :] = heads[r][...]
    wh[...], wl[...] = halves(weight[...])
    heads_h[...], heads_l[...] = halves(joined[:, rows_at(mine, CH)])
    gain, shift = piece(vec, 5), piece(vec, 6)
    for r in range(SEQ):
        at = rows_at(jnp.bitwise_xor(mine, r), CH)
        a, b = halves(joined[:, at].T)
        total = toks[r][:CH, :] + dot3(a, b, wh[...], wl[...], NN)
        total = total + piece(vec, 4)
        normed, size = norm_stats(total)
        norm_h[r], norm_l[r] = halves(normed * gain + shift)
        if r == 0:
            mixed[...] = total
            hat[...] = normed
            scale[...] = jnp.broadcast_to(size, (CH, 128))


def hidden_kernel(scal, norm_h, norm_l, *refs):
    blocks, vec, acts_h, acts_l, slope, winh, winl = refs[:GROUPS], *refs[GROUPS:]
    mine = scal[0]
    for k in range(GROUPS):
        at = rows_at(owner(scal, k), ROWS)
        winh[at, :], winl[at, :] = halves(blocks[k][...])
    marks = [16 + d for d in range(GROUPS)]
    table = jnp.concatenate([vec[m // 3, m % 3 : m % 3 + 1, :] for m in marks], axis=0)
    table = pltpu.roll(table, lax.rem(HALF_VEC - mine * ROWS, HALF_VEC), 1)[:, :ROWS]
    bias = jnp.concatenate([table[d : d + 1] for d in range(GROUPS)], axis=1)
    for r in range(SEQ):
        at = slice(r * CH, (r + 1) * CH)
        hidden = dot3(norm_h[r], norm_l[r], winh[...], winl[...], NN) + bias
        inner = jnp.tanh(gelu_scale * (hidden + gelu_cubic * hidden * hidden * hidden))
        acts_h[at, :], acts_l[at, :] = halves(0.5 * hidden * (1.0 + inner))
        slope[at, :] = 0.5 * (1.0 + inner) + 0.5 * hidden * (1.0 - inner * inner) * gelu_scale * (
            1.0 + 3.0 * gelu_cubic * hidden * hidden
        )


def emit_blocks(scal, outs, whole):
    for k in range(GROUPS):
        outs[k][...] = whole[rows_at(owner(scal, k), ROWS), :]


def out_grad_kernel(scal, acts_h, acts_l, *refs):
    grads, (out_h, out_l), outs, whole = refs[:4], refs[4:6], refs[6 : 6 + GROUPS], refs[6 + GROUPS]
    for r in range(SEQ):
        at = slice(r * CH, (r + 1) * CH)
        out_h[at, :], out_l[at, :] = halves(grads[r][...])
    whole[...] = dot3(acts_h[...], acts_l[...], out_h[...], out_l[...], TN)
    emit_blocks(scal, outs, whole)


def hidden_back_kernel(scal, out_h, out_l, slope, winh, winl, *refs):
    blocks, refs = refs[:GROUPS], refs[GROUPS:]
    hid_h, hid_l, wouth, woutl, bias_sum = refs[:5]
    parts = refs[5:]
    for k in range(GROUPS):
        at = rows_at(owner(scal, k), ROWS)
        wouth[at, :], woutl[at, :] = halves(blocks[k][...])
    sums = jnp.zeros((1, D), f32)
    for r in (1, 3, 2, 0):
        at = slice(r * CH, (r + 1) * CH)
        back = dot3(out_h[at, :], out_l[at, :], wouth[...], woutl[...], NT) * slope[at, :]
        sums = sums + jnp.sum(back, axis=0, keepdims=True)
        bh, bl = halves(back)
        hid_h[at, :], hid_l[at, :] = bh, bl
        parts[r][...] = dot3(bh, bl, winh[...], winl[...], NT)
    bias_sum[...] = jnp.broadcast_to(sums, (8, D))


def in_grad_kernel(scal, norm_h, norm_l, hid_h, hid_l, *refs):
    outs, whole = refs[:GROUPS], refs[GROUPS]
    flat = lambda ref: ref[...].reshape(LEN, D)
    whole[...] = dot3(flat(norm_h), flat(norm_l), hid_h[...], hid_l[...], TN)
    emit_blocks(scal, outs, whole)


def ffn_out_kernel(scal, acts_h, acts_l, wouth, woutl, *parts):
    for r in (1, 3, 2, 0):
        at = slice(r * CH, (r + 1) * CH)
        parts[r][...] = dot3(acts_h[at, :], acts_l[at, :], wouth[...], woutl[...], NN)


def output_kernel(scal, mixed, one, two, three, vec, output):
    output[...] = mixed[...] + (one[...] + two[...] + three[...]) + piece(vec, 7)


def proj_back_kernel(scal, one, two, three, hat, scale, vec, grad_out, wh, wl, mixed_grad, sums, *parts):
    mine = scal[0]
    normed = one[...] + two[...] + three[...]
    back = norm_back(hat[...], scale[:, :1], piece(vec, 5), normed)
    total = grad_out[...] + back
    mixed_grad[...] = total
    a, b = halves(total)
    for r in range(SEQ):
        at = rows_at(jnp.bitwise_xor(mine, r), QUARTER)
        parts[r][...] = dot3(wh[at, :], wl[at, :], a, b, NT)
    add = lambda v: jnp.sum(v, axis=0, keepdims=True)
    sums[...] = jnp.concatenate(
        [add(total), add(normed * hat[...]), add(normed), add(grad_out[...]), jnp.zeros((4, D), f32)],
        axis=0,
    )


def proj_grad_kernel(scal, heads_h, heads_l, mixed_grad, *refs):
    outs, whole = refs[:-1], refs[-1]
    mine = scal[0]
    gh, gl = halves(mixed_grad[...])
    whole[...] = dot3(heads_h[...], heads_l[...], gh, gl, NN)
    for r in range(SEQ):
        at = jnp.bitwise_xor(mine, r)
        for d in range(GROUPS):
            outs[r][d * SUB : (d + 1) * SUB, :] = whole[
                pl.ds(pl.multiple_of(d * ROWS + at * SUB, 8), SUB), :
            ]


def back_kernel(scal, *refs):
    grads, refs = refs[:4], refs[4:]
    kcat, qturn, vcat, qpair, kturn, outs_turn, lse, low_row = refs[:8]
    joined_h, joined_l, joined_sums = refs[8:11]
    gturn, gpair, dots, key_sum, value_sum, query_turn = refs[11:]
    mine = scal[0]

    for r in range(SEQ):
        at = rows_at(jnp.bitwise_xor(mine, r), CH)
        turned = grads[r][...]
        grad = jnp.concatenate([turned, jnp.zeros((HEAD, CH), f32)], axis=0).T
        pairs = lane_pairs(grad[:, :128], grad[:, 128:])
        for h in range(OWN):
            gpair[h, at, :] = pairs[h]
            part = turned[HEAD * h : HEAD * (h + 1)]
            dots[h, :, at] = jnp.broadcast_to(
                jnp.sum(part * outs_turn[HEAD * h : HEAD * (h + 1), at], axis=0, keepdims=True), (8, CH)
            )
            a, b = halves(part)
            gturn[h, :, at] = jnp.concatenate([a, a, b, b], axis=0)

    key_sum[...] = jnp.zeros_like(key_sum)
    value_sum[...] = jnp.zeros_like(value_sum)

    def one_head(h, carry):
        for c in range(SEQ):
            size = CH * (c + 1)
            lanes = slice(c * CH, (c + 1) * CH)
            score = dot(kcat[h, :size, :], qturn[h, :, lanes], NN)
            weight = jnp.where(allowed(low_row, c, size), jnp.exp(score - lse[h, :1, lanes]), 0.0)
            back = dot(vcat[h, :size, :], gturn[h, :, lanes], NN)
            score_back = weight * (back - dots[h, :1, lanes])
            a, b = halves(weight)
            pair = gpair[h, lanes, :]
            value_sum[h, :size, :] += dot(a, pair, NN) + dot(b, pair, NN)
            a, b = halves(score_back)
            pair = qpair[h, lanes, :]
            key_sum[h, :size, :] += dot(a, pair, NN) + dot(b, pair, NN)
            turned = dot(kturn[h, :, :size], a, NN) + dot(kturn[h, :, :size], b, NN)
            query_turn[h, :, lanes] = (turned[:HEAD] + turned[HEAD:]) * HEAD ** (-0.5)
        return carry

    lax.fori_loop(0, OWN, one_head, 0)

    column_sums = jnp.zeros((1, D), f32)
    low = low_lanes((CH, 128))
    for c in range(SEQ):
        at = slice(c * CH, (c + 1) * CH)
        blank = jnp.zeros((HEAD, CH), f32)
        query = jnp.concatenate([query_turn[h, :, at] for h in range(OWN)] + [blank], axis=0).T
        done = [query]
        for kept in (key_sum, value_sum):
            full = [kept[h, at, :] for h in range(OWN)]
            full = [v + pltpu.roll(v, HEAD, 1) for v in full]
            done.append(jnp.where(low, full[0], full[1]))
            done.append(jnp.where(low, full[2], 0.0))
        joined = jnp.concatenate(done, axis=1)
        column_sums = column_sums + jnp.sum(joined, axis=0, keepdims=True)
        joined_h[at, :], joined_l[at, :] = halves(joined)

    joined_sums[...] = jnp.broadcast_to(column_sums, (8, D))


def qkv_grad_kernel(scal, xh, xl, joined_h, joined_l, joined_sums, wh, wl, vec, *refs):
    proj_one, proj_two, vector_sums, bias_sum = refs[:4]
    outs, (whole, rows) = refs[4 : 4 + GROUPS], refs[4 + GROUPS :]
    mine = scal[0]
    column_sums = joined_sums[:1, :]
    core = dot3(xh[...], xl[...], joined_h[...], joined_l[...], TN)
    gain, shift = piece(vec, 0), piece(vec, 1)
    as_column = lambda v: jnp.broadcast_to(v, (128, D)).T[:, :1]
    whole[...] = as_column(gain) * core + as_column(shift) * column_sums
    weights = wh[...].astype(f32) + wl[...].astype(f32)
    gain_grad = jnp.sum(weights * core, axis=1, keepdims=True)
    shift_grad = jnp.sum(weights * column_sums, axis=1, keepdims=True)
    lane = lax.broadcasted_iota(jnp.int32, (D, 128), 1)
    norm_grads = jnp.where(lane == 0, gain_grad, shift_grad).T

    def place(part, scale):
        wide = jnp.concatenate([part[:, :QUARTER], jnp.zeros((1, D - QUARTER), f32)], axis=1)
        wide = jnp.broadcast_to(wide, (8, D))
        return pltpu.roll(wide, mine * QUARTER, 1)[:1]

    entries = [
        norm_grads[0:1],
        norm_grads[1:2],
        place(column_sums[:, :CH], 1.0),
        place(column_sums[:, 2 * CH :], 1.0),
        vector_sums[0:1],
        vector_sums[1:2],
        vector_sums[2:3],
        vector_sums[3:4],
    ]
    lines = [e[:, i * HALF_VEC : (i + 1) * HALF_VEC] for e in entries for i in range(2)]
    bias = jnp.concatenate(
        [bias_sum[:1, d * ROWS : (d + 1) * ROWS] for d in range(GROUPS)], axis=0
    )
    bias = jnp.concatenate([bias, jnp.zeros((GROUPS, HALF_VEC - ROWS), f32)], axis=1)
    bias = pltpu.roll(bias, mine * ROWS, 1)
    lines = lines + [bias[d : d + 1] for d in range(GROUPS)]
    filler = jnp.zeros((5, HALF_VEC), f32)
    for d in range(GROUPS):
        rows[d] = jnp.concatenate(lines[3 * d : 3 * d + 3] + [filler], axis=0)

    for k in range(GROUPS):
        at = owner(scal, k)
        outs[k][:ROWS, :] = whole[rows_at(at, ROWS), :]
        here = pl.ds(pl.multiple_of(at * SUB, 8), SUB)
        proj = proj_one[here, :] + proj_two[here, :]
        for group in range(SEQ):
            for part in range(3):
                lane_at = HEAD * (3 * group + part)
                outs[k][
                    group * SUB : (group + 1) * SUB, part * CH + QUARTER : (part + 1) * CH
                ] = proj[:, lane_at : lane_at + HEAD]
        outs[k][ROWS:, :HALF_VEC] = rows[at]
        outs[k][ROWS:, HALF_VEC:] = jnp.zeros((8, HALF_VEC), f32)


def pre_back_kernel(scal, joined_h, joined_l, wh, wl, *parts):
    mine = scal[0]
    for r in (1, 3, 2, 0):
        at = rows_at(jnp.bitwise_xor(mine, r), CH)
        parts[r][...] = dot3(joined_h[at, :], joined_l[at, :], wh[...], wl[...], NT)


def input_grad_kernel(scal, tokens, one, two, three, vec, mixed_grad, result):
    hat, scale = norm_stats(tokens[...])
    grad = one[...] + two[...] + three[...]
    result[...] = mixed_grad[...] + norm_back(hat, scale, piece(vec, 0), grad)


def total_square(value):
    return jnp.sum(jnp.sum(value * value, axis=0, keepdims=True), axis=1, keepdims=True)


def second_squares_kernel(scal, *refs):
    parts, squares = refs[:8], refs[8]
    total = sum(total_square(part[...]) for part in parts)
    squares[...] = jnp.broadcast_to(total, (8, 128))


def first_squares_kernel(scal, one, two, three, four, before, squares):
    parts = (one, two, three, four)
    total = sum(total_square(part[:ROWS, :]) for part in parts)
    line = sum(part[ROWS:, :HALF_VEC] for part in parts)
    squares[...] = before[...] + (total + total_square(line))


def stage_kernel(scal, *refs):
    sources, targets, sems = refs[:15], refs[15:30], refs[30]
    copies = [
        pltpu.make_async_copy(source, target, sems.at[i])
        for i, (source, target) in enumerate(zip(sources, targets))
    ]
    for copy in copies:
        copy.start()
    for copy in copies:
        copy.wait()


def adamw_kernel(scal, squares, *refs):
    firsts, ins, outs, refs = refs[:4], refs[4:8], refs[8:12], refs[12:]
    states, clip, finals, news = refs[:15], refs[15], refs[16:31], refs[31:46]
    first, second, sems = refs[46:]
    send = lambda number: [
        pltpu.make_async_copy(news[i], finals[i], sems.at[i]) for i in range(3 * number, 3 * number + 3)
    ]
    mine = scal[0]
    norm = jnp.sqrt(squares[...])
    clip[...] = norm
    factor = (clip_limit / jnp.maximum(norm, clip_limit))[:1, :1]
    for r in range(SEQ):
        at = jnp.bitwise_xor(mine, r)
        first[at] = firsts[r][:ROWS, :]
        second[at, :ROWS] = ins[r][...]
        second[at, ROWS:] = outs[r][...]

    def update(number, spot, grad, rate, decay):
        held = [states[3 * number + i][spot] for i in range(3)]
        fresh = adamw_update(*held, factor * grad, rate, decay)
        for i in range(3):
            news[3 * number + i][spot] = fresh[i]

    def finish(number):
        for copy in send(number):
            copy.start()

    line = sum(firsts[r][ROWS:, :HALF_VEC] for r in range(SEQ))
    for i in range(3):
        for j in range(3):
            spot = (slice(3 * i + j, 3 * i + j + 1), slice(None))
            update(0, spot, line[i : i + 1, 128 * j : 128 * (j + 1)], vector_rate, 0.0)
    finish(0)
    every = slice(None)
    for part in range(3):
        grad = jnp.concatenate(
            [first[j][:, part * CH : part * CH + QUARTER] for j in range(SEQ)], axis=1
        )
        update(1, (every, slice(part * D, (part + 1) * D)), grad, matrix_rate, weight_decay)
    finish(1)
    for j in range(SEQ):
        grad = jnp.concatenate(
            [
                first[j][group * SUB : (group + 1) * SUB, part * CH + QUARTER : (part + 1) * CH]
                for group in range(SEQ)
                for part in range(3)
            ],
            axis=1,
        )
        update(2, (slice(j * SUB, (j + 1) * SUB), every), grad, matrix_rate, weight_decay)
    finish(2)
    for d in range(GROUPS):
        grad = jnp.concatenate(
            [second[j][:ROWS, d * ROWS : (d + 1) * ROWS] for j in range(SEQ)], axis=1
        )
        update(3, (every, slice(d * HALF_VEC, (d + 1) * HALF_VEC)), grad, matrix_rate, weight_decay)
    finish(3)
    for j in range(SEQ):
        update(
            4, (slice(j * ROWS, (j + 1) * ROWS), every), second[j][ROWS:, :], matrix_rate, weight_decay
        )
    finish(4)
    for number in range(5):
        for copy in send(number):
            copy.wait()


def adamw_update(weight, first, second, grad, rate, decay):
    new_first = beta_one * first + (1.0 - beta_one) * grad
    new_second = beta_two * second + (1.0 - beta_two) * grad * grad
    first_hat = new_first / (1.0 - beta_one**STEP)
    second_hat = new_second / (1.0 - beta_two**STEP)
    new_weight = weight - rate * (first_hat / (jnp.sqrt(second_hat) + adam_eps) + decay * weight)
    return (new_first, new_second, new_weight)


def ring_tables(count):
    evens = [2 * i for i in range(count // 2)]
    order = evens + [i + 1 for i in reversed(evens)]
    place = [0] * count
    for position, device in enumerate(order):
        place[device] = position
    right = [(order[i], order[(i + 1) % count]) for i in range(count)]
    left = [(b, a) for a, b in right]
    return order, place, right, left


class RingGather:
    def __init__(self, block, name, flip=False):
        _, _, self.right, self.left = ring_tables(GROUPS)
        if flip:
            self.right, self.left = self.left, self.right
        self.got, self.name, self.at, self.flip = {0: block}, name, 0, flip

    def step(self, after=()):
        places = (-self.at % GROUPS, self.at)
        if after:
            for place in set(places):
                self.got[place] = gate(self.got[place], after)
        forth, back = (self.got[place] for place in places)
        self.at += 1
        self.got[GROUPS - self.at] = move(forth, "dp", self.right, f"{self.name}_right_{self.at}")
        if self.at < HALF:
            self.got[self.at] = move(back, "dp", self.left, f"{self.name}_left_{self.at}")
        return [self.got[place] for place in {GROUPS - self.at, min(self.at, HALF)}]

    def blocks(self):
        return [self.got[-k % GROUPS if self.flip else k] for k in range(GROUPS)]


class RingScatter:
    def __init__(self, blocks, name, flip=False):
        _, _, self.right, self.left = ring_tables(GROUPS)
        self.blocks = blocks
        if flip:
            self.right, self.left = self.left, self.right
            self.blocks = [blocks[-k % GROUPS] for k in range(GROUPS)]
        self.name, self.back, self.at = name, None, HALF
        self.forth = move(self.blocks[HALF], "dp", self.right, f"{name}_right_1")

    def step(self, after=()):
        self.at -= 1
        ahead, back = self.blocks[self.at], self.blocks[GROUPS - self.at]
        if self.back is None:
            forth = plus(self.forth, ahead, after=after)
        else:
            forth, back = sums([(self.forth, ahead), (self.back, back)], after)
        number = HALF + 1 - self.at
        self.forth = move(forth, "dp", self.right, f"{self.name}_right_{number}")
        self.back = move(back, "dp", self.left, f"{self.name}_left_{number}")
        return [forth, back]

    def result(self, after=()):
        return plus(self.forth, self.back, self.blocks[0], after=after)


def move(block, axis, pairs, name):
    with jax.named_scope(name):
        return lax.ppermute(block, axis, pairs)


def swap(block, bits, name):
    return move(block, "seq", [(i, i ^ bits) for i in range(SEQ)], f"{name}_{bits}")


def gather_seq(block, name):
    across = swap(block, 2, name)
    core = swap(block, 1, name)
    return [block, core, across, swap(across, 1, f"{name}_2")]


def exchange_seq(parts, name):
    return [parts[0]] + [swap(parts[r], r, name) for r in range(1, SEQ)]


def scatter_core(parts, name):
    return parts[0], swap(parts[1], 1, f"{name}_own"), parts[2], swap(parts[3], 1, f"{name}_across")


def ordered(blocks, mine):
    stack = jnp.stack(blocks, axis=0)
    return [lax.dynamic_index_in_dim(stack, mine ^ j, 0, keepdims=False) for j in range(len(blocks))]


def local(
    tokens,
    cotangent,
    segment_ids,
    valid,
    vectors,
    vec_first,
    vec_second,
    w_qkv,
    qkv_first,
    qkv_second,
    w_proj,
    proj_first,
    proj_second,
    w_in,
    in_first,
    in_second,
    w_out,
    out_first,
    out_second,
):
    dp_parts = lax.axis_size("dp")
    ring = dp_parts == GROUPS
    mine = lax.axis_index("seq")
    home = lax.axis_index("dp")
    rows = w_qkv.shape[0]
    units = w_out.shape[0] // SEQ
    far, near = home // 2, home % 2
    position = jnp.where(near > 0, GROUPS - 1 - far, far)
    scal = jnp.stack([mine, position, jnp.full_like(mine, 1 if ring else 0)]).astype(jnp.int32)
    flat_in = tokens.reshape(CH, D)
    chunk, tall, square = shape(CH, D), shape(LEN, D, kind=bf16), shape(D, D, kind=bf16)

    if ring:
        first, packed = run(
            pack_first_kernel,
            scal,
            [w_qkv, w_proj, vectors.reshape(9, 128), segment_ids, valid, flat_in],
            [shape(ROWS + 8, D), shape(CH + 8, D)],
            scratch=[
                pltpu.VMEM((3, ROWS, CH), f32),
                pltpu.VMEM((SUB, D), f32),
                pltpu.VMEM((9, 128), f32),
                pltpu.VMEM((2, 1, CH), jnp.int32),
            ],
            sems=8,
            far_args=range(6),
            room=54,
            name="pack_first", work=3.0,
        )
        ring_first = RingGather(first, "first")
        for _ in range(HALF):
            ring_first.step()
        firsts = ring_first.blocks()
        in_block, out_block = run(
            pack_second_kernel,
            scal,
            [w_in, w_out],
            [shape(ROWS, D)] * 2,
            name="pack_second", work=3.0,
            after=[firsts[GROUPS - 1]],
        )
        ring_in = RingGather(in_block, "w_in")
        ring_out = RingGather(out_block, "w_out", flip=True)
        came = ring_in.step([firsts[HALF]])
        came = came + ring_out.step([firsts[HALF]])
    else:
        padded = jnp.pad(w_qkv, ((0, 0), (0, CH)))
        own = lambda part: lax.dynamic_slice_in_dim(padded, part * D + mine * QUARTER, CH, 1)
        first = jnp.concatenate([own(0), own(1), own(2)], axis=1)
        first = lax.all_gather(first, "dp", axis=0, tiled=True).reshape(GROUPS, ROWS, D)
        all_vec = lax.all_gather(vectors, "dp", axis=0, tiled=True).reshape(GROUPS, 3, HALF_VEC)
        first = jnp.concatenate([first, jnp.pad(all_vec, ((0, 0), (0, 5), (0, D - HALF_VEC)))], axis=1)
        firsts = [first[k] for k in range(GROUPS)]
        in_part = lax.dynamic_index_in_dim(
            w_in.reshape(rows, dp_parts, SEQ, units), mine, 2, keepdims=False
        ).reshape(rows, D)
        out_part = lax.dynamic_slice_in_dim(w_out, mine * units, units, 0)
        in_blocks, out_blocks = (
            list(lax.all_gather(part, "dp", axis=0, tiled=True).reshape(GROUPS, ROWS, D))
            for part in (in_part, out_part)
        )
        marks = jnp.where(valid > 0, segment_ids, -1).astype(f32)
        packed = jnp.concatenate([flat_in, jnp.pad(marks, ((0, 7), (0, D - CH)))], axis=0)
    toks = gather_seq(packed, "tokens")
    (grad_out,) = run(
        mask_kernel, scal, [cotangent.reshape(CH, D), valid], [chunk], name="mask", work=2.0, after=[toks[2]]
    )
    grads_row = gather_seq(grad_out, "cotangent")

    qkv_h, qkv_l, vec, proj = run(
        weights_kernel,
        scal,
        firsts,
        [square, square, shape(GROUPS, 8, HALF_VEC), shape(GROUPS * SUB, D)],
        name="weights", work=3.0,
    )
    if ring:
        proj_parts = gather_seq(proj, "w_proj")
    else:
        full = lax.all_gather(w_proj, "dp", axis=0, tiled=True).reshape(GROUPS, SEQ, SUB, D)
        proj_parts = [
            lax.dynamic_index_in_dim(full, mine ^ r, 1, keepdims=False).reshape(GROUPS * SUB, D)
            for r in range(SEQ)
        ]
    hat_h, hat_l, kcat, qturn, vcat, qpair, kturn, low_row, heads, lse = run(
        front_kernel,
        scal,
        toks + [qkv_h, qkv_l, vec],
        [
            tall,
            tall,
            shape(OWN, LEN, 256, kind=bf16),
            shape(OWN, 256, LEN, kind=bf16),
            shape(OWN, LEN, 256, kind=bf16),
            shape(OWN, LEN, 128, kind=bf16),
            shape(OWN, 128, LEN, kind=bf16),
            shape(8, LEN),
            shape(QUARTER, LEN),
            shape(OWN, 8, LEN),
        ],
        scratch=[pltpu.VMEM((OWN, 128, LEN), bf16), pltpu.VMEM((SEQ, 8, CH), f32)],
        name="front", work=14.0,
        after=[grads_row[2]],
    )
    if ring:
        heads = gate(heads, [proj_parts[2], *came])
        came = ring_in.step([lse])
        ring_out.step(came)
        came = ring_in.step()
        ring_out.step(came)
        ring_in.step()
        ring_out.step()
        in_blocks, out_blocks = ring_in.blocks(), ring_out.blocks()
    wide = shape(D, CH, kind=bf16)
    split = shape(SEQ, CH, D, kind=bf16)
    proj_h, proj_l, heads_h, heads_l, norm_h, norm_l, mixed, hat_two, scale_two = run(
        proj_kernel,
        scal,
        toks + gather_seq(heads, "heads") + proj_parts + [vec],
        [square, square, wide, wide, split, split, chunk, chunk, shape(CH, 128)],
        scratch=[pltpu.VMEM((D, D), f32), pltpu.VMEM((D, LEN), f32)],
        name="proj", work=8.0,
    )

    block = shape(ROWS, D)
    acts_h, acts_l, slope, in_wh, in_wl = run(
        hidden_kernel,
        scal,
        [norm_h, norm_l] + in_blocks + [vec],
        [tall, tall, shape(LEN, D), square, square],
        name="hidden", work=8.0,
    )
    done = run(
        out_grad_kernel,
        scal,
        [acts_h, acts_l] + grads_row,
        [tall, tall] + [block] * GROUPS,
        scratch=[pltpu.VMEM((D, D), f32)],
        name="out_grad", work=5.0,
    )
    out_h, out_l = done[:2]
    out_grads = list(done[2:])
    if ring:
        ring_out = RingScatter(out_grads, "out_grad")
    done = run(
        hidden_back_kernel,
        scal,
        [out_h, out_l, slope, in_wh, in_wl] + out_blocks,
        [tall, tall, square, square, shape(8, D)] + [chunk] * SEQ,
        name="hidden_back", work=11.0,
        after=out_grads[:1],
    )
    hid_h, hid_l, out_wh, out_wl, bias_sum = done[:5]
    parts = list(done[5:])
    if ring:
        parts[3] = gate(parts[3], ring_out.step())
    norm_own, norm_near, norm_across, norm_far = scatter_core(parts, "norm_grad")
    norm_pair = plus(norm_across, norm_far)
    norm_last = swap(norm_pair, 2, "norm_grad")
    in_grads = list(
        run(
            in_grad_kernel,
            scal,
            [norm_h, norm_l, hid_h, hid_l],
            [block] * GROUPS,
            scratch=[pltpu.VMEM((D, D), f32)],
            name="in_grad", work=5.0,
            after=[norm_pair],
        )
    )
    if ring:
        ring_in = RingScatter(in_grads, "in_grad", flip=True)
        out_sent = ring_out.step()
        in_sent = ring_in.step()
    done = run(
        proj_back_kernel,
        scal,
        [norm_own, norm_near, norm_last, hat_two, scale_two, vec, grad_out, proj_h, proj_l],
        [chunk, shape(8, D)] + [shape(QUARTER, CH)] * SEQ,
        name="proj_back", work=5.0,
        after=out_sent + in_sent if ring else [],
    )
    mixed_grad, vector_sums = done[:2]
    head_grads = exchange_seq(list(done[2:]), "head_grad")
    if ring:
        out_sent = ring_out.step([mixed_grad])
        in_sent = ring_in.step([mixed_grad])
    out_parts = run(
        ffn_out_kernel,
        scal,
        [acts_h, acts_l, out_wh, out_wl],
        [chunk] * SEQ,
        name="ffn_out", work=7.0,
        after=[mixed_grad],
    )
    proj_grads = run(
        proj_grad_kernel,
        scal,
        [heads_h, heads_l, mixed_grad],
        [shape(GROUPS * SUB, D)] * SEQ,
        scratch=[pltpu.VMEM((D, D), f32)],
        name="proj_grad", work=4.0,
        after=[*head_grads[1:], *out_sent, *in_sent, out_parts[0]] if ring else [],
    )
    wait = [head_grads[3], head_grads[2]]
    out_own, out_near, out_across, out_far = scatter_core(out_parts, "output")
    if ring:
        proj_own, proj_near, proj_across, proj_far = scatter_core(proj_grads, "proj_grad")
        proj_pair, proj_base = sums([(proj_across, proj_far), (proj_own, proj_near)], wait)
        proj_last = swap(proj_pair, 2, "proj_grad")
    else:
        proj_base = proj_last = proj_grads[0]
    joined_h, joined_l, joined_sums = run(
        back_kernel,
        scal,
        head_grads + [kcat, qturn, vcat, qpair, kturn, heads, lse, low_row],
        [tall, tall, shape(8, D)],
        scratch=[
            pltpu.VMEM((OWN, 256, LEN), bf16),
            pltpu.VMEM((OWN, LEN, 128), bf16),
            pltpu.VMEM((OWN, 8, LEN), f32),
            pltpu.VMEM((OWN, LEN, 128), f32),
            pltpu.VMEM((OWN, LEN, 128), f32),
            pltpu.VMEM((OWN, HEAD, LEN), f32),
        ],
        name="back", work=16.0,
        after=[proj_grads[0]],
    )
    if ring:
        shard_out = ring_out.result([joined_sums])
        in_sent = ring_in.step([joined_sums])
    done = run(
        qkv_grad_kernel,
        scal,
        [hat_h, hat_l, joined_h, joined_l, joined_sums, qkv_h, qkv_l, vec]
        + [proj_base, proj_last, vector_sums, bias_sum],
        [shape(ROWS + 8, D)] * GROUPS,
        scratch=[pltpu.VMEM((D, D), f32), pltpu.VMEM((GROUPS, 8, HALF_VEC), f32)],
        name="qkv_grad", work=1.0,
        after=[*in_sent, shard_out] if ring else [],
    )
    first_grads = list(done)
    if ring:
        shard_in = ring_in.result([first_grads[0]])
        out_all = gather_seq(shard_out, "out_shard")
        in_all = gather_seq(shard_in, "in_shard")
        first_grads[HALF] = gate(first_grads[HALF], [shard_in, out_all[2]])
        ring_first = RingScatter(first_grads, "first_grad")
        first_sent = ring_first.step([in_all[2]])
    pre_parts = run(
        pre_back_kernel,
        scal,
        [joined_h, joined_l, qkv_h, qkv_l],
        [chunk] * SEQ,
        name="pre_back", work=1.0,
        after=[shard_in, *first_sent] if ring else [],
    )
    pre_parts = list(pre_parts)
    if ring:
        first_sent = ring_first.step()
        pre_parts[3] = gate(pre_parts[3], first_sent)
    pre_own, pre_near, pre_across, pre_far = scatter_core(pre_parts, "pre_grad")
    pre_pair = plus(pre_across, pre_far)
    pre_last = swap(pre_pair, 2, "pre_grad")
    states = [vectors, vec_first, vec_second, w_qkv, qkv_first, qkv_second, w_proj, proj_first, proj_second]
    states = states + [w_in, in_first, in_second, w_out, out_first, out_second]
    if ring:
        held = [v.reshape(9, 128) for v in states[:3]] + states[3:]
        held = run(
            stage_kernel,
            scal,
            held,
            [shape(*v.shape) for v in held],
            sems=15,
            far_args=range(15),
            name="stage", work=4.0,
            after=[pre_parts[0]],
        )
        ring_first.step([held[3]])
        shard_first = ring_first.result()
    (input_grad,) = run(
        input_grad_kernel,
        scal,
        [flat_in, pre_own, pre_near, pre_last, vec, mixed_grad],
        [chunk],
        name="input_grad", work=3.0,
    )

    if ring:
        (squares,) = run(
            second_squares_kernel, scal, in_all + out_all, [shape(8, 128)], name="second_squares", work=2.0
        )
        shard_first = gate(shard_first, [pre_last])
        across = gate(swap(shard_first, 2, "first_shard"), [input_grad, squares])
        core = swap(shard_first, 1, "first_shard")
        first_all = [shard_first, core, across, swap(across, 1, "first_shard_2")]
        out_pair = plus(out_across, out_far, after=[across])
        (squares,) = run(
            first_squares_kernel,
            scal,
            first_all + [squares],
            [shape(8, 128)],
            name="first_squares", work=2.0,
            after=[out_pair],
        )
        flipped = lambda bits: [(i, i ^ bits) for i in range(GROUPS)]
        one, two, three = (move(squares, "dp", flipped(bits), "squares") for bits in (1, 2, 3))
        squares = sum_pairs(squares, one, two, three)
        squares = plus(squares, move(squares, "dp", flipped(4), "squares"))
        done = run(
            adamw_kernel,
            scal,
            [squares] + first_all + in_all + out_all + list(held),
            [shape(8, 128)] + [shape(*v.shape) for v in held],
            scratch=[pltpu.VMEM(v.shape, f32) for v in held]
            + [pltpu.VMEM((SEQ, ROWS, D), f32), pltpu.VMEM((SEQ, 2 * ROWS, D), f32)],
            sems=15,
            far_outs=range(1, 16),
            name="adamw", work=0.1,
        )
        new = [v.reshape(-1) for v in done[1:4]] + list(done[4:])
        clip_norm = done[0][0, 0]
    else:
        out_pair = plus(out_across, out_far)
        by_group = jnp.stack(first_grads)
        shard_first = lax.psum_scatter(
            by_group[:, :ROWS].reshape(D, D), "dp", scatter_dimension=0, tiled=True
        )
        proj_full = jnp.stack([p.reshape(GROUPS, SUB, D) for p in ordered(proj_grads, mine)], axis=1)
        proj_grad = lax.psum(
            lax.psum_scatter(proj_full.reshape(D, D), "dp", scatter_dimension=0, tiled=True), "seq"
        )
        all_vec = lax.psum(by_group[:, ROWS : ROWS + 3, :HALF_VEC], ("dp", "seq")).reshape(-1)
        vec_grad = lax.dynamic_slice_in_dim(all_vec, home * vectors.shape[0], vectors.shape[0])
        joined = lax.all_gather(shard_first, "seq", axis=0, tiled=False)
        qkv_grad = jnp.concatenate(
            [joined[j, :, i * CH : i * CH + QUARTER] for i in range(3) for j in range(SEQ)], axis=1
        )
        shard_in, shard_out = (
            lax.psum_scatter(jnp.concatenate(parts, axis=0), "dp", scatter_dimension=0, tiled=True)
            for parts in (in_grads, out_grads)
        )
        in_all = lax.all_gather(shard_in, "seq", axis=0, tiled=False)
        in_grad = in_all.reshape(SEQ, rows, dp_parts, units).transpose(1, 2, 0, 3).reshape(rows, -1)
        out_grad = lax.all_gather(shard_out, "seq", axis=0, tiled=True)
        total = sum(jnp.sum(g * g) for g in (qkv_grad, proj_grad, in_grad, out_grad, vec_grad))
        total = lax.psum(total, "dp")
        clip_norm = jnp.sqrt(total)
        factor = clip_limit / jnp.maximum(clip_norm, clip_limit)
        grads = (vec_grad, qkv_grad, proj_grad, in_grad, out_grad)
        new = []
        for number, grad in enumerate(grads):
            rate, decay = (matrix_rate, weight_decay) if number else (vector_rate, 0.0)
            new.extend(adamw_update(*states[3 * number : 3 * number + 3], factor * grad, rate, decay))
    out_last = swap(out_pair, 2, "output")
    (output,) = run(
        output_kernel, scal, [mixed, out_own, out_near, out_last, vec], [chunk], name="output", work=2.0
    )
    return (output.reshape(tokens.shape), input_grad.reshape(tokens.shape), clip_norm, *new)


def solution(mesh):
    row = P("dp", "seq", None)
    mark = P("dp", "seq")
    vec = P("dp")
    mat = P("dp", None)
    return jax.shard_map(
        local,
        mesh=mesh,
        in_specs=(row, row, mark, mark) + (vec,) * 3 + (mat,) * 12,
        out_specs=(row, row, P()) + (vec,) * 3 + (mat,) * 12,
        check_vma=False,
    )
```

```python
import functools
import math

import jax
import jax.numpy as jnp
from jax import lax
from jax.experimental import pallas as pl
from jax.experimental.pallas import tpu as pltpu
from jax.sharding import PartitionSpec as P

D = 768
HEADS = 12
HEAD = 64
STEP = 10
CH = 256
LEN = 1024
SEQ = 4
QUARTER = D // SEQ
OWN = HEADS // SEQ
GROUPS = 8
ROWS = D // GROUPS
SUB = ROWS // SEQ
HALF = GROUPS // 2
HALF_VEC = D // 2
VEC_ROWS = 24

f32 = jnp.float32
bf16 = jnp.bfloat16
masked_score = -1e30
norm_eps = 1e-05
clip_limit = 1.0
beta_one = 0.9
beta_two = 0.999
adam_eps = 1e-08
matrix_rate = 0.02
vector_rate = 0.4
weight_decay = 0.01
gelu_scale = 0.7978845608028654
gelu_cubic = 0.044715

COST = 1e9

WHOLE = pl.BlockSpec(memory_space=pltpu.VMEM)
SCALARS = pl.BlockSpec(memory_space=pltpu.SMEM)
NN = ((1,), (0,))
NT = ((1,), (1,))
TN = ((0,), (0,))


def shape(*dims, kind=f32):
    return jax.ShapeDtypeStruct(dims, kind)


def run(
    kernel, scal, args, outs, scratch=(), sems=0, far_args=(), far_outs=(), room=8, work=1.0, name=None, after=()
):
    args, after = list(args), list(after)
    held = sum(math.prod(v.shape) * jnp.dtype(v.dtype).itemsize for v in scratch)
    anywhere, far = pl.BlockSpec(memory_space=pl.ANY), pl.BlockSpec(memory_space=pltpu.HBM)
    scratch = list(scratch) + ([pltpu.SemaphoreType.DMA((sems,))] if sems else [])

    def body(scal_ref, *refs):
        kernel(scal_ref, *refs[: len(args)], *refs[len(args) + len(after) :])

    return pl.pallas_call(
        body,
        out_shape=tuple(outs),
        in_specs=[SCALARS]
        + [far if i in far_args else WHOLE for i in range(len(args))]
        + [anywhere] * len(after),
        out_specs=tuple(far if i in far_outs else WHOLE for i in range(len(outs))),
        scratch_shapes=scratch,
        compiler_params=pltpu.CompilerParams(vmem_limit_bytes=held + (room << 20)),
        cost_estimate=pl.CostEstimate(
            flops=int(work * COST), bytes_accessed=1, transcendentals=0
        ),
        name=name,
    )(scal, *args, *after)


def gate(value, after):
    anywhere = pl.BlockSpec(memory_space=pl.ANY)
    return pl.pallas_call(
        lambda *refs: None,
        out_shape=shape(*value.shape, kind=value.dtype),
        in_specs=[anywhere] * (1 + len(after)),
        out_specs=anywhere,
        input_output_aliases={0: 0},
        compiler_params=pltpu.CompilerParams(vmem_limit_bytes=1 << 20),
        name="gate",
    )(value, *after)


def sums(groups, after=()):
    sizes = [len(group) for group in groups]

    def body(*refs):
        at = 0
        for number, size in enumerate(sizes):
            total = refs[at][...]
            for ref in refs[at + 1 : at + size]:
                total = total + ref[...]
            refs[sum(sizes) + len(after) + number][...] = total
            at += size

    return pl.pallas_call(
        body,
        out_shape=tuple(shape(*group[0].shape) for group in groups),
        in_specs=[WHOLE] * sum(sizes) + [pl.BlockSpec(memory_space=pl.ANY)] * len(after),
        out_specs=tuple([WHOLE] * len(groups)),
        compiler_params=pltpu.CompilerParams(vmem_limit_bytes=4 << 20),
        cost_estimate=pl.CostEstimate(flops=int(COST), bytes_accessed=1, transcendentals=0),
        name="plus",
    )(*(term for group in groups for term in group), *after)


def plus(*terms, after=()):
    return sums([terms], after)[0]


def sum_pairs(one, two, three, four):
    def body(a, b, c, d, result):
        result[...] = (a[...] + b[...]) + (c[...] + d[...])

    return pl.pallas_call(
        body,
        out_shape=shape(*one.shape),
        in_specs=[WHOLE] * 4,
        out_specs=WHOLE,
        compiler_params=pltpu.CompilerParams(vmem_limit_bytes=1 << 20),
        name="sum_pairs",
    )(one, two, three, four)


def owner(scal, k):
    spot = jnp.bitwise_and(scal[1] + k, GROUPS - 1)
    return jnp.where(scal[2] > 0, jnp.where(spot < HALF, 2 * spot, 2 * GROUPS - 1 - 2 * spot), k)


def halves(value):
    top = value.astype(bf16)
    return top, (value - top.astype(f32)).astype(bf16)


def dot(left, right, dims):
    return lax.dot_general(left, right, (dims, ((), ())), preferred_element_type=f32)


def dot3(lh, ll, rh, rl, dims):
    return dot(lh, rh, dims) + (dot(lh, rl, dims) + dot(ll, rh, dims))


def rows_at(index, size):
    return pl.ds(pl.multiple_of(index * size, size), size)


def piece(vec, number):
    a, b = 2 * number, 2 * number + 1
    return jnp.concatenate(
        [vec[a // 3, a % 3 : a % 3 + 1, :], vec[b // 3, b % 3 : b % 3 + 1, :]], axis=1
    )


def norm_stats(inputs):
    center = inputs - jnp.mean(inputs, axis=-1, keepdims=True)
    spread = jnp.mean(center * center, axis=-1, keepdims=True)
    scale = lax.rsqrt(spread + norm_eps)
    return center * scale, scale


def norm_back(hat, scale, gain, grad):
    inner = grad * gain
    return scale * (
        inner
        - jnp.mean(inner, axis=-1, keepdims=True)
        - hat * jnp.mean(inner * hat, axis=-1, keepdims=True)
    )


def low_lanes(dims):
    return lax.broadcasted_iota(jnp.int32, dims, 1) < HEAD


def lane_pairs(pair, last):
    low = low_lanes(pair.shape)
    roll = lambda v: pltpu.roll(v, HEAD, 1)
    ph = pair.astype(bf16).astype(f32)
    pl_ = pair - ph
    lh = last.astype(bf16).astype(f32)
    ll = last - lh
    return [
        jnp.where(low, ph, roll(pl_)).astype(bf16),
        jnp.where(low, roll(ph), pl_).astype(bf16),
        jnp.where(low, lh, roll(ll)).astype(bf16),
    ]


def row_halves(turned, head):
    part = turned[HEAD * head : HEAD * (head + 1)]
    return halves(part)


def pack_first_kernel(scal, wqkv, wproj, vec, seg, valid, tokens, first, packed, *refs):
    bands, proj, lines, marks, sems = refs
    mine = scal[0]
    aligned = pl.multiple_of(jnp.bitwise_and(mine * QUARTER, -128), 128)
    copies = [
        pltpu.make_async_copy(wqkv.at[:, pl.ds(part * D + aligned, CH)], bands.at[part], sems.at[part])
        for part in range(3)
    ]
    sub = pl.ds(pl.multiple_of(mine * SUB, 8), SUB)
    copies.append(pltpu.make_async_copy(wproj.at[sub, :], proj, sems.at[3]))
    copies.append(pltpu.make_async_copy(vec, lines, sems.at[4]))
    copies.append(pltpu.make_async_copy(seg, marks.at[0], sems.at[5]))
    copies.append(pltpu.make_async_copy(valid, marks.at[1], sems.at[6]))
    copies.append(pltpu.make_async_copy(tokens, packed.at[:CH, :], sems.at[7]))
    for copy in copies:
        copy.start()
    first[ROWS:, :] = jnp.zeros((8, D), f32)
    packed[CH:, :] = jnp.zeros((8, D), f32)
    for copy in copies[:5]:
        copy.wait()
    turn = jnp.where(jnp.bitwise_and(mine, 1) > 0, CH - HEAD, 0)
    for part in range(3):
        turned = pltpu.roll(bands[part], turn, 1)
        first[:ROWS, part * CH : part * CH + QUARTER] = turned[:, :QUARTER]
        for group in range(SEQ):
            lane = HEAD * (3 * group + part)
            first[group * SUB : (group + 1) * SUB, part * CH + QUARTER : (part + 1) * CH] = proj[
                :, lane : lane + HEAD
            ]
        first[ROWS + part : ROWS + part + 1, :HALF_VEC] = jnp.concatenate(
            [lines[3 * part + i : 3 * part + i + 1, :] for i in range(3)], axis=1
        )
    for copy in copies[5:]:
        copy.wait()
    packed[CH : CH + 1, :CH] = jnp.where(marks[1] > 0, marks[0], -1).astype(f32)


def pack_second_kernel(scal, win, wout, in_block, out_block):
    mine = scal[0]
    turn = lax.rem(HALF_VEC - mine * ROWS, HALF_VEC)
    for part in range(GROUPS):
        turned = pltpu.roll(win[:, part * HALF_VEC : (part + 1) * HALF_VEC], turn, 1)
        in_block[:, part * ROWS : (part + 1) * ROWS] = turned[:, :ROWS]
    out_block[...] = wout[pl.ds(pl.multiple_of(mine * ROWS, 8), ROWS), :]


def mask_kernel(scal, cotangent, valid, result):
    keep = jnp.where(valid[...] > 0, 1.0, 0.0).astype(f32)
    column = jnp.broadcast_to(keep, (128, CH)).T[:, :1]
    result[...] = cotangent[...] * column


def weights_kernel(scal, *refs):
    blocks, (wh, wl, vec, proj) = refs[:GROUPS], refs[GROUPS:]
    for k in range(GROUPS):
        at = owner(scal, k)
        block = blocks[k][:ROWS, :]
        here = rows_at(at, ROWS)
        wh[here, :], wl[here, :] = halves(block)
        vec[at] = blocks[k][ROWS:, :HALF_VEC]
        for group in range(SEQ):
            for part in range(3):
                lane = HEAD * (3 * group + part)
                proj[pl.ds(pl.multiple_of(at * SUB, 8), SUB), lane : lane + HEAD] = block[
                    group * SUB : (group + 1) * SUB, part * CH + QUARTER : (part + 1) * CH
                ]


def front_kernel(scal, *refs):
    toks, refs = refs[:4], refs[4:]
    wh, wl, vec = refs[:3]
    xh, xl, kcat, qturn, vcat, qpair, kturn, low_row, outs_turn, lse, vturn, label = refs[3:]
    mine = scal[0]

    gain, shift = piece(vec, 0), piece(vec, 1)
    turn = lax.rem(D - mine * QUARTER, D)
    own = lambda number: pltpu.roll(jnp.broadcast_to(piece(vec, number), (8, D)), turn, 1)[:1, :CH]
    query_bias, value_bias = own(2), own(3)

    for r in range(SEQ):
        nat = jnp.bitwise_xor(mine, r)
        at = rows_at(nat, CH)
        label[nat] = toks[r][CH:, :CH]
        hat, _ = norm_stats(toks[r][:CH, :])
        xh[at, :], xl[at, :] = halves(hat)
        nh, nl = halves(hat * gain + shift)
        joined = dot3(nh, nl, wh[...], wl[...], NN)
        query = (joined[:, :CH] + query_bias) * HEAD ** (-0.5)
        key = joined[:, CH : 2 * CH]
        value = joined[:, 2 * CH :] + value_bias
        keys = lane_pairs(key[:, :128], key[:, 128:])
        values = lane_pairs(value[:, :128], value[:, 128:])
        queries = lane_pairs(query[:, :128], query[:, 128:])
        key_t, value_t, query_t = key.T, value.T, query.T
        for h in range(OWN):
            kcat[h, at, :] = jnp.concatenate([keys[h], keys[h]], axis=1)
            vcat[h, at, :] = jnp.concatenate([values[h], values[h]], axis=1)
            qpair[h, at, :] = queries[h]
            a, b = row_halves(query_t, h)
            qturn[h, :, at] = jnp.concatenate([a, a, b, b], axis=0)
            a, b = row_halves(key_t, h)
            kturn[h, :, at] = jnp.concatenate([a, b], axis=0)
            a, b = row_halves(value_t, h)
            vturn[h, :, at] = jnp.concatenate([a, b], axis=0)

    labels = jnp.concatenate([label[c][:1, :] for c in range(SEQ)], axis=1)
    spot = lax.broadcasted_iota(jnp.int32, (1, LEN), 1).astype(f32)
    begin = jnp.zeros((1, LEN), f32)
    for segment in range(3):
        held = jnp.sum(jnp.where(labels == float(segment), 1.0, 0.0), axis=1, keepdims=True)
        begin = begin + jnp.where(labels > float(segment), held, 0.0)
    begin = jnp.where(labels < 0.0, spot, begin)
    low_row[...] = jnp.broadcast_to(begin, (8, LEN))

    def one_head(h, carry):
        for c in range(SEQ):
            size = CH * (c + 1)
            lanes = slice(c * CH, (c + 1) * CH)
            score = dot(kcat[h, :size, :], qturn[h, :, lanes], NN)
            mask = allowed(low_row, c, size)
            score = jnp.where(mask, score, masked_score)
            peak = jnp.max(score, axis=0, keepdims=True)
            weight = jnp.exp(score - peak)
            total = jnp.sum(weight, axis=0, keepdims=True)
            top, rest = halves(weight)
            both = dot(vturn[h, :, :size], top, NN)
            extra = dot(vturn[h, :HEAD, :size], rest, NN)
            result = (both[:HEAD] + both[HEAD:] + extra) / total
            outs_turn[pl.ds(pl.multiple_of(h * HEAD, HEAD), HEAD), lanes] = result
            lse[h, :, lanes] = jnp.broadcast_to(peak + jnp.log(total), (8, CH))
        return carry

    lax.fori_loop(0, OWN, one_head, 0)


def allowed(low_row, c, size):
    key_at = lax.broadcasted_iota(jnp.int32, (size, CH), 0).astype(f32)
    query_at = (lax.broadcasted_iota(jnp.int32, (1, CH), 1) + c * CH).astype(f32)
    begin = low_row[:1, c * CH : (c + 1) * CH]
    return (key_at >= begin) & (key_at <= query_at)


def proj_kernel(scal, *refs):
    toks, heads, parts, refs = refs[:4], refs[4:8], refs[8:12], refs[12:]
    vec, wh, wl, heads_h, heads_l, norm_h, norm_l, mixed, hat, scale, weight, joined = refs
    mine = scal[0]
    for r in range(SEQ):
        at = jnp.bitwise_xor(mine, r)
        for d in range(GROUPS):
            weight[pl.ds(pl.multiple_of(d * ROWS + at * SUB, 8), SUB), :] = parts[r][
                d * SUB : (d + 1) * SUB, :
            ]
        joined[rows_at(at, QUARTER), :] = heads[r][...]
    wh[...], wl[...] = halves(weight[...])
    heads_h[...], heads_l[...] = halves(joined[:, rows_at(mine, CH)])
    gain, shift = piece(vec, 5), piece(vec, 6)
    for r in range(SEQ):
        at = rows_at(jnp.bitwise_xor(mine, r), CH)
        a, b = halves(joined[:, at].T)
        total = toks[r][:CH, :] + dot3(a, b, wh[...], wl[...], NN)
        total = total + piece(vec, 4)
        normed, size = norm_stats(total)
        norm_h[r], norm_l[r] = halves(normed * gain + shift)
        if r == 0:
            mixed[...] = total
            hat[...] = normed
            scale[...] = jnp.broadcast_to(size, (CH, 128))


def hidden_kernel(scal, norm_h, norm_l, *refs):
    blocks, vec, acts_h, acts_l, slope, winh, winl = refs[:GROUPS], *refs[GROUPS:]
    mine = scal[0]
    for k in range(GROUPS):
        at = rows_at(owner(scal, k), ROWS)
        winh[at, :], winl[at, :] = halves(blocks[k][...])
    marks = [16 + d for d in range(GROUPS)]
    table = jnp.concatenate([vec[m // 3, m % 3 : m % 3 + 1, :] for m in marks], axis=0)
    table = pltpu.roll(table, lax.rem(HALF_VEC - mine * ROWS, HALF_VEC), 1)[:, :ROWS]
    bias = jnp.concatenate([table[d : d + 1] for d in range(GROUPS)], axis=1)
    for r in range(SEQ):
        at = slice(r * CH, (r + 1) * CH)
        hidden = dot3(norm_h[r], norm_l[r], winh[...], winl[...], NN) + bias
        inner = jnp.tanh(gelu_scale * (hidden + gelu_cubic * hidden * hidden * hidden))
        acts_h[at, :], acts_l[at, :] = halves(0.5 * hidden * (1.0 + inner))
        slope[at, :] = 0.5 * (1.0 + inner) + 0.5 * hidden * (1.0 - inner * inner) * gelu_scale * (
            1.0 + 3.0 * gelu_cubic * hidden * hidden
        )


def emit_blocks(scal, outs, whole):
    for k in range(GROUPS):
        outs[k][...] = whole[rows_at(owner(scal, k), ROWS), :]


def out_grad_kernel(scal, acts_h, acts_l, *refs):
    grads, (out_h, out_l), outs, whole = refs[:4], refs[4:6], refs[6 : 6 + GROUPS], refs[6 + GROUPS]
    for r in range(SEQ):
        at = slice(r * CH, (r + 1) * CH)
        out_h[at, :], out_l[at, :] = halves(grads[r][...])
    whole[...] = dot3(acts_h[...], acts_l[...], out_h[...], out_l[...], TN)
    emit_blocks(scal, outs, whole)


def hidden_back_kernel(scal, out_h, out_l, slope, winh, winl, *refs):
    blocks, refs = refs[:GROUPS], refs[GROUPS:]
    hid_h, hid_l, wouth, woutl, bias_sum = refs[:5]
    parts = refs[5:]
    for k in range(GROUPS):
        at = rows_at(owner(scal, k), ROWS)
        wouth[at, :], woutl[at, :] = halves(blocks[k][...])
    sums = jnp.zeros((1, D), f32)
    for r in (1, 3, 2, 0):
        at = slice(r * CH, (r + 1) * CH)
        back = dot3(out_h[at, :], out_l[at, :], wouth[...], woutl[...], NT) * slope[at, :]
        sums = sums + jnp.sum(back, axis=0, keepdims=True)
        bh, bl = halves(back)
        hid_h[at, :], hid_l[at, :] = bh, bl
        parts[r][...] = dot3(bh, bl, winh[...], winl[...], NT)
    bias_sum[...] = jnp.broadcast_to(sums, (8, D))


def in_grad_kernel(scal, norm_h, norm_l, hid_h, hid_l, *refs):
    outs, whole = refs[:GROUPS], refs[GROUPS]
    flat = lambda ref: ref[...].reshape(LEN, D)
    whole[...] = dot3(flat(norm_h), flat(norm_l), hid_h[...], hid_l[...], TN)
    emit_blocks(scal, outs, whole)


def ffn_out_kernel(scal, acts_h, acts_l, wouth, woutl, *parts):
    for r in (1, 3, 2, 0):
        at = slice(r * CH, (r + 1) * CH)
        parts[r][...] = dot3(acts_h[at, :], acts_l[at, :], wouth[...], woutl[...], NN)


def output_kernel(scal, mixed, one, two, three, vec, output):
    output[...] = mixed[...] + (one[...] + two[...] + three[...]) + piece(vec, 7)


def proj_back_kernel(scal, one, two, three, hat, scale, vec, grad_out, wh, wl, mixed_grad, sums, *parts):
    mine = scal[0]
    normed = one[...] + two[...] + three[...]
    back = norm_back(hat[...], scale[:, :1], piece(vec, 5), normed)
    total = grad_out[...] + back
    mixed_grad[...] = total
    a, b = halves(total)
    for r in range(SEQ):
        at = rows_at(jnp.bitwise_xor(mine, r), QUARTER)
        parts[r][...] = dot3(wh[at, :], wl[at, :], a, b, NT)
    add = lambda v: jnp.sum(v, axis=0, keepdims=True)
    sums[...] = jnp.concatenate(
        [add(total), add(normed * hat[...]), add(normed), add(grad_out[...]), jnp.zeros((4, D), f32)],
        axis=0,
    )


def proj_grad_kernel(scal, heads_h, heads_l, mixed_grad, *refs):
    outs, whole = refs[:-1], refs[-1]
    mine = scal[0]
    gh, gl = halves(mixed_grad[...])
    whole[...] = dot3(heads_h[...], heads_l[...], gh, gl, NN)
    for r in range(SEQ):
        at = jnp.bitwise_xor(mine, r)
        for d in range(GROUPS):
            outs[r][d * SUB : (d + 1) * SUB, :] = whole[
                pl.ds(pl.multiple_of(d * ROWS + at * SUB, 8), SUB), :
            ]


def back_kernel(scal, *refs):
    grads, refs = refs[:4], refs[4:]
    kcat, qturn, vcat, qpair, kturn, outs_turn, lse, low_row = refs[:8]
    joined_h, joined_l, joined_sums = refs[8:11]
    gturn, gpair, dots, key_sum, value_sum, query_turn = refs[11:]
    mine = scal[0]

    for r in range(SEQ):
        at = rows_at(jnp.bitwise_xor(mine, r), CH)
        turned = grads[r][...]
        grad = jnp.concatenate([turned, jnp.zeros((HEAD, CH), f32)], axis=0).T
        pairs = lane_pairs(grad[:, :128], grad[:, 128:])
        for h in range(OWN):
            gpair[h, at, :] = pairs[h]
            part = turned[HEAD * h : HEAD * (h + 1)]
            dots[h, :, at] = jnp.broadcast_to(
                jnp.sum(part * outs_turn[HEAD * h : HEAD * (h + 1), at], axis=0, keepdims=True), (8, CH)
            )
            a, b = halves(part)
            gturn[h, :, at] = jnp.concatenate([a, a, b, b], axis=0)

    key_sum[...] = jnp.zeros_like(key_sum)
    value_sum[...] = jnp.zeros_like(value_sum)

    def one_head(h, carry):
        for c in range(SEQ):
            size = CH * (c + 1)
            lanes = slice(c * CH, (c + 1) * CH)
            score = dot(kcat[h, :size, :], qturn[h, :, lanes], NN)
            weight = jnp.where(allowed(low_row, c, size), jnp.exp(score - lse[h, :1, lanes]), 0.0)
            back = dot(vcat[h, :size, :], gturn[h, :, lanes], NN)
            score_back = weight * (back - dots[h, :1, lanes])
            a, b = halves(weight)
            pair = gpair[h, lanes, :]
            value_sum[h, :size, :] += dot(a, pair, NN) + dot(b, pair, NN)
            a, b = halves(score_back)
            pair = qpair[h, lanes, :]
            key_sum[h, :size, :] += dot(a, pair, NN) + dot(b, pair, NN)
            turned = dot(kturn[h, :, :size], a, NN) + dot(kturn[h, :, :size], b, NN)
            query_turn[h, :, lanes] = (turned[:HEAD] + turned[HEAD:]) * HEAD ** (-0.5)
        return carry

    lax.fori_loop(0, OWN, one_head, 0)

    column_sums = jnp.zeros((1, D), f32)
    low = low_lanes((CH, 128))
    for c in range(SEQ):
        at = slice(c * CH, (c + 1) * CH)
        blank = jnp.zeros((HEAD, CH), f32)
        query = jnp.concatenate([query_turn[h, :, at] for h in range(OWN)] + [blank], axis=0).T
        done = [query]
        for kept in (key_sum, value_sum):
            full = [kept[h, at, :] for h in range(OWN)]
            full = [v + pltpu.roll(v, HEAD, 1) for v in full]
            done.append(jnp.where(low, full[0], full[1]))
            done.append(jnp.where(low, full[2], 0.0))
        joined = jnp.concatenate(done, axis=1)
        column_sums = column_sums + jnp.sum(joined, axis=0, keepdims=True)
        joined_h[at, :], joined_l[at, :] = halves(joined)

    joined_sums[...] = jnp.broadcast_to(column_sums, (8, D))


def qkv_grad_kernel(scal, xh, xl, joined_h, joined_l, joined_sums, wh, wl, vec, *refs):
    proj_one, proj_two, vector_sums, bias_sum = refs[:4]
    outs, (whole, rows) = refs[4 : 4 + GROUPS], refs[4 + GROUPS :]
    mine = scal[0]
    column_sums = joined_sums[:1, :]
    core = dot3(xh[...], xl[...], joined_h[...], joined_l[...], TN)
    gain, shift = piece(vec, 0), piece(vec, 1)
    as_column = lambda v: jnp.broadcast_to(v, (128, D)).T[:, :1]
    whole[...] = as_column(gain) * core + as_column(shift) * column_sums
    weights = wh[...].astype(f32) + wl[...].astype(f32)
    gain_grad = jnp.sum(weights * core, axis=1, keepdims=True)
    shift_grad = jnp.sum(weights * column_sums, axis=1, keepdims=True)
    lane = lax.broadcasted_iota(jnp.int32, (D, 128), 1)
    norm_grads = jnp.where(lane == 0, gain_grad, shift_grad).T

    def place(part, scale):
        wide = jnp.concatenate([part[:, :QUARTER], jnp.zeros((1, D - QUARTER), f32)], axis=1)
        wide = jnp.broadcast_to(wide, (8, D))
        return pltpu.roll(wide, mine * QUARTER, 1)[:1]

    entries = [
        norm_grads[0:1],
        norm_grads[1:2],
        place(column_sums[:, :CH], 1.0),
        place(column_sums[:, 2 * CH :], 1.0),
        vector_sums[0:1],
        vector_sums[1:2],
        vector_sums[2:3],
        vector_sums[3:4],
    ]
    lines = [e[:, i * HALF_VEC : (i + 1) * HALF_VEC] for e in entries for i in range(2)]
    bias = jnp.concatenate(
        [bias_sum[:1, d * ROWS : (d + 1) * ROWS] for d in range(GROUPS)], axis=0
    )
    bias = jnp.concatenate([bias, jnp.zeros((GROUPS, HALF_VEC - ROWS), f32)], axis=1)
    bias = pltpu.roll(bias, mine * ROWS, 1)
    lines = lines + [bias[d : d + 1] for d in range(GROUPS)]
    filler = jnp.zeros((5, HALF_VEC), f32)
    for d in range(GROUPS):
        rows[d] = jnp.concatenate(lines[3 * d : 3 * d + 3] + [filler], axis=0)

    for k in range(GROUPS):
        at = owner(scal, k)
        outs[k][:ROWS, :] = whole[rows_at(at, ROWS), :]
        here = pl.ds(pl.multiple_of(at * SUB, 8), SUB)
        proj = proj_one[here, :] + proj_two[here, :]
        for group in range(SEQ):
            for part in range(3):
                lane_at = HEAD * (3 * group + part)
                outs[k][
                    group * SUB : (group + 1) * SUB, part * CH + QUARTER : (part + 1) * CH
                ] = proj[:, lane_at : lane_at + HEAD]
        outs[k][ROWS:, :HALF_VEC] = rows[at]
        outs[k][ROWS:, HALF_VEC:] = jnp.zeros((8, HALF_VEC), f32)


def pre_back_kernel(scal, joined_h, joined_l, wh, wl, *parts):
    mine = scal[0]
    for r in (1, 3, 2, 0):
        at = rows_at(jnp.bitwise_xor(mine, r), CH)
        parts[r][...] = dot3(joined_h[at, :], joined_l[at, :], wh[...], wl[...], NT)


def input_grad_kernel(scal, tokens, one, two, three, vec, mixed_grad, result):
    hat, scale = norm_stats(tokens[...])
    grad = one[...] + two[...] + three[...]
    result[...] = mixed_grad[...] + norm_back(hat, scale, piece(vec, 0), grad)


def total_square(value):
    return jnp.sum(jnp.sum(value * value, axis=0, keepdims=True), axis=1, keepdims=True)


def second_squares_kernel(scal, *refs):
    parts, squares = refs[:8], refs[8]
    total = sum(total_square(part[...]) for part in parts)
    squares[...] = jnp.broadcast_to(total, (8, 128))


def first_squares_kernel(scal, one, two, three, four, before, squares):
    parts = (one, two, three, four)
    total = sum(total_square(part[:ROWS, :]) for part in parts)
    line = sum(part[ROWS:, :HALF_VEC] for part in parts)
    squares[...] = before[...] + (total + total_square(line))


def stage_kernel(scal, *refs):
    sources, targets, sems = refs[:15], refs[15:30], refs[30]
    copies = [
        pltpu.make_async_copy(source, target, sems.at[i])
        for i, (source, target) in enumerate(zip(sources, targets))
    ]
    for copy in copies:
        copy.start()
    for copy in copies:
        copy.wait()


def adamw_kernel(scal, squares, *refs):
    firsts, ins, outs, refs = refs[:4], refs[4:8], refs[8:12], refs[12:]
    states, clip, finals, news = refs[:15], refs[15], refs[16:31], refs[31:46]
    first, second, sems = refs[46:]
    send = lambda number: [
        pltpu.make_async_copy(news[i], finals[i], sems.at[i]) for i in range(3 * number, 3 * number + 3)
    ]
    mine = scal[0]
    norm = jnp.sqrt(squares[...])
    clip[...] = norm
    factor = (clip_limit / jnp.maximum(norm, clip_limit))[:1, :1]
    for r in range(SEQ):
        at = jnp.bitwise_xor(mine, r)
        first[at] = firsts[r][:ROWS, :]
        second[at, :ROWS] = ins[r][...]
        second[at, ROWS:] = outs[r][...]

    def update(number, spot, grad, rate, decay):
        held = [states[3 * number + i][spot] for i in range(3)]
        fresh = adamw_update(*held, factor * grad, rate, decay)
        for i in range(3):
            news[3 * number + i][spot] = fresh[i]

    def finish(number):
        for copy in send(number):
            copy.start()

    line = sum(firsts[r][ROWS:, :HALF_VEC] for r in range(SEQ))
    for i in range(3):
        for j in range(3):
            spot = (slice(3 * i + j, 3 * i + j + 1), slice(None))
            update(0, spot, line[i : i + 1, 128 * j : 128 * (j + 1)], vector_rate, 0.0)
    finish(0)
    every = slice(None)
    for part in range(3):
        grad = jnp.concatenate(
            [first[j][:, part * CH : part * CH + QUARTER] for j in range(SEQ)], axis=1
        )
        update(1, (every, slice(part * D, (part + 1) * D)), grad, matrix_rate, weight_decay)
    finish(1)
    for j in range(SEQ):
        grad = jnp.concatenate(
            [
                first[j][group * SUB : (group + 1) * SUB, part * CH + QUARTER : (part + 1) * CH]
                for group in range(SEQ)
                for part in range(3)
            ],
            axis=1,
        )
        update(2, (slice(j * SUB, (j + 1) * SUB), every), grad, matrix_rate, weight_decay)
    finish(2)
    for d in range(GROUPS):
        grad = jnp.concatenate(
            [second[j][:ROWS, d * ROWS : (d + 1) * ROWS] for j in range(SEQ)], axis=1
        )
        update(3, (every, slice(d * HALF_VEC, (d + 1) * HALF_VEC)), grad, matrix_rate, weight_decay)
    finish(3)
    for j in range(SEQ):
        update(
            4, (slice(j * ROWS, (j + 1) * ROWS), every), second[j][ROWS:, :], matrix_rate, weight_decay
        )
    finish(4)
    for number in range(5):
        for copy in send(number):
            copy.wait()


def adamw_update(weight, first, second, grad, rate, decay):
    new_first = beta_one * first + (1.0 - beta_one) * grad
    new_second = beta_two * second + (1.0 - beta_two) * grad * grad
    first_hat = new_first / (1.0 - beta_one**STEP)
    second_hat = new_second / (1.0 - beta_two**STEP)
    new_weight = weight - rate * (first_hat / (jnp.sqrt(second_hat) + adam_eps) + decay * weight)
    return (new_first, new_second, new_weight)


def ring_tables(count):
    evens = [2 * i for i in range(count // 2)]
    order = evens + [i + 1 for i in reversed(evens)]
    place = [0] * count
    for position, device in enumerate(order):
        place[device] = position
    right = [(order[i], order[(i + 1) % count]) for i in range(count)]
    left = [(b, a) for a, b in right]
    return order, place, right, left


class RingGather:
    def __init__(self, block, name, flip=False):
        _, _, self.right, self.left = ring_tables(GROUPS)
        if flip:
            self.right, self.left = self.left, self.right
        self.got, self.name, self.at, self.flip = {0: block}, name, 0, flip

    def step(self, after=()):
        places = (-self.at % GROUPS, self.at)
        if after:
            for place in set(places):
                self.got[place] = gate(self.got[place], after)
        forth, back = (self.got[place] for place in places)
        self.at += 1
        self.got[GROUPS - self.at] = move(forth, "dp", self.right, f"{self.name}_right_{self.at}")
        if self.at < HALF:
            self.got[self.at] = move(back, "dp", self.left, f"{self.name}_left_{self.at}")
        return [self.got[place] for place in {GROUPS - self.at, min(self.at, HALF)}]

    def blocks(self):
        return [self.got[-k % GROUPS if self.flip else k] for k in range(GROUPS)]


class RingScatter:
    def __init__(self, blocks, name, flip=False):
        _, _, self.right, self.left = ring_tables(GROUPS)
        self.blocks = blocks
        if flip:
            self.right, self.left = self.left, self.right
            self.blocks = [blocks[-k % GROUPS] for k in range(GROUPS)]
        self.name, self.back, self.at = name, None, HALF
        self.forth = move(self.blocks[HALF], "dp", self.right, f"{name}_right_1")

    def step(self, after=()):
        self.at -= 1
        ahead, back = self.blocks[self.at], self.blocks[GROUPS - self.at]
        if self.back is None:
            forth = plus(self.forth, ahead, after=after)
        else:
            forth, back = sums([(self.forth, ahead), (self.back, back)], after)
        number = HALF + 1 - self.at
        self.forth = move(forth, "dp", self.right, f"{self.name}_right_{number}")
        self.back = move(back, "dp", self.left, f"{self.name}_left_{number}")
        return [forth, back]

    def result(self, after=()):
        return plus(self.forth, self.back, self.blocks[0], after=after)


def move(block, axis, pairs, name):
    with jax.named_scope(name):
        return lax.ppermute(block, axis, pairs)


def swap(block, bits, name):
    return move(block, "seq", [(i, i ^ bits) for i in range(SEQ)], f"{name}_{bits}")


def gather_seq(block, name):
    across = swap(block, 2, name)
    core = swap(block, 1, name)
    return [block, core, across, swap(across, 1, f"{name}_2")]


def exchange_seq(parts, name):
    return [parts[0]] + [swap(parts[r], r, name) for r in range(1, SEQ)]


def scatter_core(parts, name):
    return parts[0], swap(parts[1], 1, f"{name}_own"), parts[2], swap(parts[3], 1, f"{name}_across")


def ordered(blocks, mine):
    stack = jnp.stack(blocks, axis=0)
    return [lax.dynamic_index_in_dim(stack, mine ^ j, 0, keepdims=False) for j in range(len(blocks))]


def local(
    tokens,
    cotangent,
    segment_ids,
    valid,
    vectors,
    vec_first,
    vec_second,
    w_qkv,
    qkv_first,
    qkv_second,
    w_proj,
    proj_first,
    proj_second,
    w_in,
    in_first,
    in_second,
    w_out,
    out_first,
    out_second,
):
    dp_parts = lax.axis_size("dp")
    ring = dp_parts == GROUPS
    mine = lax.axis_index("seq")
    home = lax.axis_index("dp")
    rows = w_qkv.shape[0]
    units = w_out.shape[0] // SEQ
    far, near = home // 2, home % 2
    position = jnp.where(near > 0, GROUPS - 1 - far, far)
    scal = jnp.stack([mine, position, jnp.full_like(mine, 1 if ring else 0)]).astype(jnp.int32)
    flat_in = tokens.reshape(CH, D)
    chunk, tall, square = shape(CH, D), shape(LEN, D, kind=bf16), shape(D, D, kind=bf16)

    if ring:
        first, packed = run(
            pack_first_kernel,
            scal,
            [w_qkv, w_proj, vectors.reshape(9, 128), segment_ids, valid, flat_in],
            [shape(ROWS + 8, D), shape(CH + 8, D)],
            scratch=[
                pltpu.VMEM((3, ROWS, CH), f32),
                pltpu.VMEM((SUB, D), f32),
                pltpu.VMEM((9, 128), f32),
                pltpu.VMEM((2, 1, CH), jnp.int32),
            ],
            sems=8,
            far_args=range(6),
            room=54,
            name="pack_first", work=3.0,
        )
        ring_first = RingGather(first, "first")
        for _ in range(HALF):
            ring_first.step()
        firsts = ring_first.blocks()
        in_block, out_block = run(
            pack_second_kernel,
            scal,
            [w_in, w_out],
            [shape(ROWS, D)] * 2,
            name="pack_second", work=3.0,
            after=[firsts[GROUPS - 1]],
        )
        ring_in = RingGather(in_block, "w_in")
        ring_out = RingGather(out_block, "w_out", flip=True)
        came = ring_in.step([firsts[HALF]])
        came = came + ring_out.step([firsts[HALF]])
    else:
        padded = jnp.pad(w_qkv, ((0, 0), (0, CH)))
        own = lambda part: lax.dynamic_slice_in_dim(padded, part * D + mine * QUARTER, CH, 1)
        first = jnp.concatenate([own(0), own(1), own(2)], axis=1)
        first = lax.all_gather(first, "dp", axis=0, tiled=True).reshape(GROUPS, ROWS, D)
        all_vec = lax.all_gather(vectors, "dp", axis=0, tiled=True).reshape(GROUPS, 3, HALF_VEC)
        first = jnp.concatenate([first, jnp.pad(all_vec, ((0, 0), (0, 5), (0, D - HALF_VEC)))], axis=1)
        firsts = [first[k] for k in range(GROUPS)]
        in_part = lax.dynamic_index_in_dim(
            w_in.reshape(rows, dp_parts, SEQ, units), mine, 2, keepdims=False
        ).reshape(rows, D)
        out_part = lax.dynamic_slice_in_dim(w_out, mine * units, units, 0)
        in_blocks, out_blocks = (
            list(lax.all_gather(part, "dp", axis=0, tiled=True).reshape(GROUPS, ROWS, D))
            for part in (in_part, out_part)
        )
        marks = jnp.where(valid > 0, segment_ids, -1).astype(f32)
        packed = jnp.concatenate([flat_in, jnp.pad(marks, ((0, 7), (0, D - CH)))], axis=0)
    toks = gather_seq(packed, "tokens")
    (grad_out,) = run(
        mask_kernel, scal, [cotangent.reshape(CH, D), valid], [chunk], name="mask", work=2.0, after=[toks[2]]
    )
    grads_row = gather_seq(grad_out, "cotangent")

    qkv_h, qkv_l, vec, proj = run(
        weights_kernel,
        scal,
        firsts,
        [square, square, shape(GROUPS, 8, HALF_VEC), shape(GROUPS * SUB, D)],
        name="weights", work=3.0,
    )
    if ring:
        proj_parts = gather_seq(proj, "w_proj")
    else:
        full = lax.all_gather(w_proj, "dp", axis=0, tiled=True).reshape(GROUPS, SEQ, SUB, D)
        proj_parts = [
            lax.dynamic_index_in_dim(full, mine ^ r, 1, keepdims=False).reshape(GROUPS * SUB, D)
            for r in range(SEQ)
        ]
    hat_h, hat_l, kcat, qturn, vcat, qpair, kturn, low_row, heads, lse = run(
        front_kernel,
        scal,
        toks + [qkv_h, qkv_l, vec],
        [
            tall,
            tall,
            shape(OWN, LEN, 256, kind=bf16),
            shape(OWN, 256, LEN, kind=bf16),
            shape(OWN, LEN, 256, kind=bf16),
            shape(OWN, LEN, 128, kind=bf16),
            shape(OWN, 128, LEN, kind=bf16),
            shape(8, LEN),
            shape(QUARTER, LEN),
            shape(OWN, 8, LEN),
        ],
        scratch=[pltpu.VMEM((OWN, 128, LEN), bf16), pltpu.VMEM((SEQ, 8, CH), f32)],
        name="front", work=14.0,
        after=[grads_row[2]],
    )
    if ring:
        heads = gate(heads, [proj_parts[2], *came])
        ring_in.step([lse])
        came = ring_in.step()
        ring_out.step(came)
        ring_in.step()
        in_blocks = ring_in.blocks()
    across = swap(heads, 2, "heads")
    if ring:
        across = gate(across, came)
    all_heads = [heads, swap(heads, 1, "heads"), across, swap(across, 1, "heads_2")]
    wide = shape(D, CH, kind=bf16)
    split = shape(SEQ, CH, D, kind=bf16)
    proj_h, proj_l, heads_h, heads_l, norm_h, norm_l, mixed, hat_two, scale_two = run(
        proj_kernel,
        scal,
        toks + all_heads + proj_parts + [vec],
        [square, square, wide, wide, split, split, chunk, chunk, shape(CH, 128)],
        scratch=[pltpu.VMEM((D, D), f32), pltpu.VMEM((D, LEN), f32)],
        name="proj", work=8.0,
    )

    if ring:
        ring_out.step([norm_h])
        ring_out.step()
        out_blocks = ring_out.blocks()
    block = shape(ROWS, D)
    acts_h, acts_l, slope, in_wh, in_wl = run(
        hidden_kernel,
        scal,
        [norm_h, norm_l] + in_blocks + [vec],
        [tall, tall, shape(LEN, D), square, square],
        name="hidden", work=8.0,
    )
    done = run(
        out_grad_kernel,
        scal,
        [acts_h, acts_l] + grads_row,
        [tall, tall] + [block] * GROUPS,
        scratch=[pltpu.VMEM((D, D), f32)],
        name="out_grad", work=5.0,
    )
    out_h, out_l = done[:2]
    out_grads = list(done[2:])
    if ring:
        ring_out = RingScatter(out_grads, "out_grad")
    done = run(
        hidden_back_kernel,
        scal,
        [out_h, out_l, slope, in_wh, in_wl] + out_blocks,
        [tall, tall, square, square, shape(8, D)] + [chunk] * SEQ,
        name="hidden_back", work=11.0,
        after=out_grads[:1],
    )
    hid_h, hid_l, out_wh, out_wl, bias_sum = done[:5]
    parts = list(done[5:])
    if ring:
        parts[3] = gate(parts[3], ring_out.step([bias_sum]))
    norm_own, norm_near, norm_across, norm_far = scatter_core(parts, "norm_grad")
    norm_pair = plus(norm_across, norm_far)
    norm_last = swap(norm_pair, 2, "norm_grad")
    in_grads = list(
        run(
            in_grad_kernel,
            scal,
            [norm_h, norm_l, hid_h, hid_l],
            [block] * GROUPS,
            scratch=[pltpu.VMEM((D, D), f32)],
            name="in_grad", work=5.0,
            after=[norm_pair],
        )
    )
    if ring:
        ring_in = RingScatter(in_grads, "in_grad", flip=True)
        out_sent = ring_out.step()
        in_sent = ring_in.step()
    done = run(
        proj_back_kernel,
        scal,
        [norm_own, norm_near, norm_last, hat_two, scale_two, vec, grad_out, proj_h, proj_l],
        [chunk, shape(8, D)] + [shape(QUARTER, CH)] * SEQ,
        name="proj_back", work=5.0,
        after=out_sent + in_sent if ring else [],
    )
    mixed_grad, vector_sums = done[:2]
    head_grads = exchange_seq(list(done[2:]), "head_grad")
    if ring:
        out_sent = ring_out.step([mixed_grad])
        in_sent = ring_in.step([mixed_grad])
    out_parts = run(
        ffn_out_kernel,
        scal,
        [acts_h, acts_l, out_wh, out_wl],
        [chunk] * SEQ,
        name="ffn_out", work=7.0,
        after=[mixed_grad],
    )
    proj_grads = run(
        proj_grad_kernel,
        scal,
        [heads_h, heads_l, mixed_grad],
        [shape(GROUPS * SUB, D)] * SEQ,
        scratch=[pltpu.VMEM((D, D), f32)],
        name="proj_grad", work=4.0,
        after=[*head_grads[1:], *out_sent, *in_sent, out_parts[0]] if ring else [],
    )
    wait = [head_grads[3], head_grads[2]]
    out_own, out_near, out_across, out_far = scatter_core(out_parts, "output")
    if ring:
        proj_own, proj_near, proj_across, proj_far = scatter_core(proj_grads, "proj_grad")
        proj_pair, proj_base = sums([(proj_across, proj_far), (proj_own, proj_near)], wait)
        proj_last = swap(proj_pair, 2, "proj_grad")
    else:
        proj_base = proj_last = proj_grads[0]
    joined_h, joined_l, joined_sums = run(
        back_kernel,
        scal,
        head_grads + [kcat, qturn, vcat, qpair, kturn, heads, lse, low_row],
        [tall, tall, shape(8, D)],
        scratch=[
            pltpu.VMEM((OWN, 256, LEN), bf16),
            pltpu.VMEM((OWN, LEN, 128), bf16),
            pltpu.VMEM((OWN, 8, LEN), f32),
            pltpu.VMEM((OWN, LEN, 128), f32),
            pltpu.VMEM((OWN, LEN, 128), f32),
            pltpu.VMEM((OWN, HEAD, LEN), f32),
        ],
        name="back", work=16.0,
        after=[proj_grads[0]],
    )
    if ring:
        shard_out = ring_out.result([joined_sums])
        in_sent = ring_in.step([joined_sums])
    done = run(
        qkv_grad_kernel,
        scal,
        [hat_h, hat_l, joined_h, joined_l, joined_sums, qkv_h, qkv_l, vec]
        + [proj_base, proj_last, vector_sums, bias_sum],
        [shape(ROWS + 8, D)] * GROUPS,
        scratch=[pltpu.VMEM((D, D), f32), pltpu.VMEM((GROUPS, 8, HALF_VEC), f32)],
        name="qkv_grad", work=1.0,
        after=[*in_sent, shard_out] if ring else [],
    )
    first_grads = list(done)
    if ring:
        shard_in = ring_in.result([first_grads[0]])
        out_all = gather_seq(shard_out, "out_shard")
        in_all = gather_seq(shard_in, "in_shard")
        first_grads[HALF] = gate(first_grads[HALF], [shard_in, out_all[2]])
        ring_first = RingScatter(first_grads, "first_grad")
        first_sent = ring_first.step([in_all[2]])
    pre_parts = run(
        pre_back_kernel,
        scal,
        [joined_h, joined_l, qkv_h, qkv_l],
        [chunk] * SEQ,
        name="pre_back", work=1.0,
        after=[shard_in, *first_sent] if ring else [],
    )
    pre_parts = list(pre_parts)
    if ring:
        first_sent = ring_first.step()
        pre_parts[3] = gate(pre_parts[3], first_sent)
    pre_own, pre_near, pre_across, pre_far = scatter_core(pre_parts, "pre_grad")
    pre_pair = plus(pre_across, pre_far)
    pre_last = swap(pre_pair, 2, "pre_grad")
    states = [vectors, vec_first, vec_second, w_qkv, qkv_first, qkv_second, w_proj, proj_first, proj_second]
    states = states + [w_in, in_first, in_second, w_out, out_first, out_second]
    if ring:
        held = [v.reshape(9, 128) for v in states[:3]] + states[3:]
        held = run(
            stage_kernel,
            scal,
            held,
            [shape(*v.shape) for v in held],
            sems=15,
            far_args=range(15),
            name="stage", work=4.0,
            after=[pre_parts[0]],
        )
        ring_first.step([held[3]])
        shard_first = ring_first.result()
    (input_grad,) = run(
        input_grad_kernel,
        scal,
        [flat_in, pre_own, pre_near, pre_last, vec, mixed_grad],
        [chunk],
        name="input_grad", work=3.0,
    )

    if ring:
        (squares,) = run(
            second_squares_kernel, scal, in_all + out_all, [shape(8, 128)], name="second_squares", work=2.0
        )
        shard_first = gate(shard_first, [pre_last])
        across = gate(swap(shard_first, 2, "first_shard"), [input_grad, squares])
        core = swap(shard_first, 1, "first_shard")
        first_all = [shard_first, core, across, swap(across, 1, "first_shard_2")]
        out_pair = plus(out_across, out_far, after=[across])
        (squares,) = run(
            first_squares_kernel,
            scal,
            first_all + [squares],
            [shape(8, 128)],
            name="first_squares", work=2.0,
            after=[out_pair],
        )
        flipped = lambda bits: [(i, i ^ bits) for i in range(GROUPS)]
        one, two, three = (move(squares, "dp", flipped(bits), "squares") for bits in (1, 2, 3))
        squares = sum_pairs(squares, one, two, three)
        squares = plus(squares, move(squares, "dp", flipped(4), "squares"))
        done = run(
            adamw_kernel,
            scal,
            [squares] + first_all + in_all + out_all + list(held),
            [shape(8, 128)] + [shape(*v.shape) for v in held],
            scratch=[pltpu.VMEM(v.shape, f32) for v in held]
            + [pltpu.VMEM((SEQ, ROWS, D), f32), pltpu.VMEM((SEQ, 2 * ROWS, D), f32)],
            sems=15,
            far_outs=range(1, 16),
            name="adamw", work=0.1,
        )
        new = [v.reshape(-1) for v in done[1:4]] + list(done[4:])
        clip_norm = done[0][0, 0]
    else:
        out_pair = plus(out_across, out_far)
        by_group = jnp.stack(first_grads)
        shard_first = lax.psum_scatter(
            by_group[:, :ROWS].reshape(D, D), "dp", scatter_dimension=0, tiled=True
        )
        proj_full = jnp.stack([p.reshape(GROUPS, SUB, D) for p in ordered(proj_grads, mine)], axis=1)
        proj_grad = lax.psum(
            lax.psum_scatter(proj_full.reshape(D, D), "dp", scatter_dimension=0, tiled=True), "seq"
        )
        all_vec = lax.psum(by_group[:, ROWS : ROWS + 3, :HALF_VEC], ("dp", "seq")).reshape(-1)
        vec_grad = lax.dynamic_slice_in_dim(all_vec, home * vectors.shape[0], vectors.shape[0])
        joined = lax.all_gather(shard_first, "seq", axis=0, tiled=False)
        qkv_grad = jnp.concatenate(
            [joined[j, :, i * CH : i * CH + QUARTER] for i in range(3) for j in range(SEQ)], axis=1
        )
        shard_in, shard_out = (
            lax.psum_scatter(jnp.concatenate(parts, axis=0), "dp", scatter_dimension=0, tiled=True)
            for parts in (in_grads, out_grads)
        )
        in_all = lax.all_gather(shard_in, "seq", axis=0, tiled=False)
        in_grad = in_all.reshape(SEQ, rows, dp_parts, units).transpose(1, 2, 0, 3).reshape(rows, -1)
        out_grad = lax.all_gather(shard_out, "seq", axis=0, tiled=True)
        total = sum(jnp.sum(g * g) for g in (qkv_grad, proj_grad, in_grad, out_grad, vec_grad))
        total = lax.psum(total, "dp")
        clip_norm = jnp.sqrt(total)
        factor = clip_limit / jnp.maximum(clip_norm, clip_limit)
        grads = (vec_grad, qkv_grad, proj_grad, in_grad, out_grad)
        new = []
        for number, grad in enumerate(grads):
            rate, decay = (matrix_rate, weight_decay) if number else (vector_rate, 0.0)
            new.extend(adamw_update(*states[3 * number : 3 * number + 3], factor * grad, rate, decay))
    out_last = swap(out_pair, 2, "output")
    (output,) = run(
        output_kernel, scal, [mixed, out_own, out_near, out_last, vec], [chunk], name="output", work=2.0
    )
    return (output.reshape(tokens.shape), input_grad.reshape(tokens.shape), clip_norm, *new)


def solution(mesh):
    row = P("dp", "seq", None)
    mark = P("dp", "seq")
    vec = P("dp")
    mat = P("dp", None)
    return jax.shard_map(
        local,
        mesh=mesh,
        in_specs=(row, row, mark, mark) + (vec,) * 3 + (mat,) * 12,
        out_specs=(row, row, P()) + (vec,) * 3 + (mat,) * 12,
        check_vma=False,
    )
```

```python
import functools
import math

import jax
import jax.numpy as jnp
from jax import lax
from jax.experimental import pallas as pl
from jax.experimental.pallas import tpu as pltpu
from jax.sharding import PartitionSpec as P

D = 768
HEADS = 12
HEAD = 64
STEP = 10
CH = 256
LEN = 1024
SEQ = 4
QUARTER = D // SEQ
OWN = HEADS // SEQ
GROUPS = 8
ROWS = D // GROUPS
SUB = ROWS // SEQ
HALF = GROUPS // 2
HALF_VEC = D // 2
VEC_ROWS = 24

f32 = jnp.float32
bf16 = jnp.bfloat16
masked_score = -1e30
norm_eps = 1e-05
clip_limit = 1.0
beta_one = 0.9
beta_two = 0.999
adam_eps = 1e-08
matrix_rate = 0.02
vector_rate = 0.4
weight_decay = 0.01
gelu_scale = 0.7978845608028654
gelu_cubic = 0.044715

COST = 1e9

WHOLE = pl.BlockSpec(memory_space=pltpu.VMEM)
SCALARS = pl.BlockSpec(memory_space=pltpu.SMEM)
NN = ((1,), (0,))
NT = ((1,), (1,))
TN = ((0,), (0,))


def shape(*dims, kind=f32):
    return jax.ShapeDtypeStruct(dims, kind)


def run(
    kernel, scal, args, outs, scratch=(), sems=0, far_args=(), far_outs=(), room=8, work=1.0, name=None, after=()
):
    args, after = list(args), list(after)
    held = sum(math.prod(v.shape) * jnp.dtype(v.dtype).itemsize for v in scratch)
    anywhere, far = pl.BlockSpec(memory_space=pl.ANY), pl.BlockSpec(memory_space=pltpu.HBM)
    scratch = list(scratch) + ([pltpu.SemaphoreType.DMA((sems,))] if sems else [])

    def body(scal_ref, *refs):
        kernel(scal_ref, *refs[: len(args)], *refs[len(args) + len(after) :])

    return pl.pallas_call(
        body,
        out_shape=tuple(outs),
        in_specs=[SCALARS]
        + [far if i in far_args else WHOLE for i in range(len(args))]
        + [anywhere] * len(after),
        out_specs=tuple(far if i in far_outs else WHOLE for i in range(len(outs))),
        scratch_shapes=scratch,
        compiler_params=pltpu.CompilerParams(vmem_limit_bytes=held + (room << 20)),
        cost_estimate=pl.CostEstimate(
            flops=int(work * COST), bytes_accessed=1, transcendentals=0
        ),
        name=name,
    )(scal, *args, *after)


def gate(value, after):
    anywhere = pl.BlockSpec(memory_space=pl.ANY)
    return pl.pallas_call(
        lambda *refs: None,
        out_shape=shape(*value.shape, kind=value.dtype),
        in_specs=[anywhere] * (1 + len(after)),
        out_specs=anywhere,
        input_output_aliases={0: 0},
        compiler_params=pltpu.CompilerParams(vmem_limit_bytes=1 << 20),
        name="gate",
    )(value, *after)


def sums(groups, after=()):
    sizes = [len(group) for group in groups]

    def body(*refs):
        at = 0
        for number, size in enumerate(sizes):
            total = refs[at][...]
            for ref in refs[at + 1 : at + size]:
                total = total + ref[...]
            refs[sum(sizes) + len(after) + number][...] = total
            at += size

    return pl.pallas_call(
        body,
        out_shape=tuple(shape(*group[0].shape) for group in groups),
        in_specs=[WHOLE] * sum(sizes) + [pl.BlockSpec(memory_space=pl.ANY)] * len(after),
        out_specs=tuple([WHOLE] * len(groups)),
        compiler_params=pltpu.CompilerParams(vmem_limit_bytes=4 << 20),
        cost_estimate=pl.CostEstimate(flops=int(COST), bytes_accessed=1, transcendentals=0),
        name="plus",
    )(*(term for group in groups for term in group), *after)


def plus(*terms, after=()):
    return sums([terms], after)[0]


def sum_pairs(one, two, three, four):
    def body(a, b, c, d, result):
        result[...] = (a[...] + b[...]) + (c[...] + d[...])

    return pl.pallas_call(
        body,
        out_shape=shape(*one.shape),
        in_specs=[WHOLE] * 4,
        out_specs=WHOLE,
        compiler_params=pltpu.CompilerParams(vmem_limit_bytes=1 << 20),
        name="sum_pairs",
    )(one, two, three, four)


def owner(scal, k):
    spot = jnp.bitwise_and(scal[1] + k, GROUPS - 1)
    return jnp.where(scal[2] > 0, jnp.where(spot < HALF, 2 * spot, 2 * GROUPS - 1 - 2 * spot), k)


def halves(value):
    top = value.astype(bf16)
    return top, (value - top.astype(f32)).astype(bf16)


def dot(left, right, dims):
    return lax.dot_general(left, right, (dims, ((), ())), preferred_element_type=f32)


def dot3(lh, ll, rh, rl, dims):
    (left,), (right,) = dims
    join = lambda parts, axis: jnp.concatenate([part[...] for part in parts], axis=axis)
    return dot(join([lh, lh, ll], left), join([rh, rl, rh], right), dims)


def rows_at(index, size):
    return pl.ds(pl.multiple_of(index * size, size), size)


def piece(vec, number):
    a, b = 2 * number, 2 * number + 1
    return jnp.concatenate(
        [vec[a // 3, a % 3 : a % 3 + 1, :], vec[b // 3, b % 3 : b % 3 + 1, :]], axis=1
    )


def norm_stats(inputs):
    center = inputs - jnp.mean(inputs, axis=-1, keepdims=True)
    spread = jnp.mean(center * center, axis=-1, keepdims=True)
    scale = lax.rsqrt(spread + norm_eps)
    return center * scale, scale


def norm_back(hat, scale, gain, grad):
    inner = grad * gain
    return scale * (
        inner
        - jnp.mean(inner, axis=-1, keepdims=True)
        - hat * jnp.mean(inner * hat, axis=-1, keepdims=True)
    )


def low_lanes(dims):
    return lax.broadcasted_iota(jnp.int32, dims, 1) < HEAD


def lane_pairs(pair, last):
    low = low_lanes(pair.shape)
    roll = lambda v: pltpu.roll(v, HEAD, 1)
    ph = pair.astype(bf16).astype(f32)
    pl_ = pair - ph
    lh = last.astype(bf16).astype(f32)
    ll = last - lh
    return [
        jnp.where(low, ph, roll(pl_)).astype(bf16),
        jnp.where(low, roll(ph), pl_).astype(bf16),
        jnp.where(low, lh, roll(ll)).astype(bf16),
    ]


def row_halves(turned, head):
    part = turned[HEAD * head : HEAD * (head + 1)]
    return halves(part)


def pack_first_kernel(scal, wqkv, wproj, vec, seg, valid, tokens, first, packed, *refs):
    bands, proj, lines, marks, sems = refs
    mine = scal[0]
    aligned = pl.multiple_of(jnp.bitwise_and(mine * QUARTER, -128), 128)
    copies = [
        pltpu.make_async_copy(wqkv.at[:, pl.ds(part * D + aligned, CH)], bands.at[part], sems.at[part])
        for part in range(3)
    ]
    sub = pl.ds(pl.multiple_of(mine * SUB, 8), SUB)
    copies.append(pltpu.make_async_copy(wproj.at[sub, :], proj, sems.at[3]))
    copies.append(pltpu.make_async_copy(vec, lines, sems.at[4]))
    copies.append(pltpu.make_async_copy(seg, marks.at[0], sems.at[5]))
    copies.append(pltpu.make_async_copy(valid, marks.at[1], sems.at[6]))
    copies.append(pltpu.make_async_copy(tokens, packed.at[:CH, :], sems.at[7]))
    for copy in copies:
        copy.start()
    first[ROWS:, :] = jnp.zeros((8, D), f32)
    packed[CH:, :] = jnp.zeros((8, D), f32)
    for copy in copies[:5]:
        copy.wait()
    turn = jnp.where(jnp.bitwise_and(mine, 1) > 0, CH - HEAD, 0)
    for part in range(3):
        turned = pltpu.roll(bands[part], turn, 1)
        first[:ROWS, part * CH : part * CH + QUARTER] = turned[:, :QUARTER]
        for group in range(SEQ):
            lane = HEAD * (3 * group + part)
            first[group * SUB : (group + 1) * SUB, part * CH + QUARTER : (part + 1) * CH] = proj[
                :, lane : lane + HEAD
            ]
        first[ROWS + part : ROWS + part + 1, :HALF_VEC] = jnp.concatenate(
            [lines[3 * part + i : 3 * part + i + 1, :] for i in range(3)], axis=1
        )
    for copy in copies[5:]:
        copy.wait()
    packed[CH : CH + 1, :CH] = jnp.where(marks[1] > 0, marks[0], -1).astype(f32)


def pack_second_kernel(scal, win, wout, in_block, out_block):
    mine = scal[0]
    turn = lax.rem(HALF_VEC - mine * ROWS, HALF_VEC)
    for part in range(GROUPS):
        turned = pltpu.roll(win[:, part * HALF_VEC : (part + 1) * HALF_VEC], turn, 1)
        in_block[:, part * ROWS : (part + 1) * ROWS] = turned[:, :ROWS]
    out_block[...] = wout[pl.ds(pl.multiple_of(mine * ROWS, 8), ROWS), :]


def mask_kernel(scal, cotangent, valid, result):
    keep = jnp.where(valid[...] > 0, 1.0, 0.0).astype(f32)
    column = jnp.broadcast_to(keep, (128, CH)).T[:, :1]
    result[...] = cotangent[...] * column


def weights_kernel(scal, *refs):
    blocks, (wh, wl, vec, proj) = refs[:GROUPS], refs[GROUPS:]
    for k in range(GROUPS):
        at = owner(scal, k)
        block = blocks[k][:ROWS, :]
        here = rows_at(at, ROWS)
        wh[here, :], wl[here, :] = halves(block)
        vec[at] = blocks[k][ROWS:, :HALF_VEC]
        for group in range(SEQ):
            for part in range(3):
                lane = HEAD * (3 * group + part)
                proj[pl.ds(pl.multiple_of(at * SUB, 8), SUB), lane : lane + HEAD] = block[
                    group * SUB : (group + 1) * SUB, part * CH + QUARTER : (part + 1) * CH
                ]


def front_kernel(scal, *refs):
    toks, refs = refs[:4], refs[4:]
    wh, wl, vec = refs[:3]
    xh, xl, kcat, qturn, vcat, qpair, kturn, low_row, outs_turn, lse, vturn, label = refs[3:]
    mine = scal[0]

    gain, shift = piece(vec, 0), piece(vec, 1)
    turn = lax.rem(D - mine * QUARTER, D)
    own = lambda number: pltpu.roll(jnp.broadcast_to(piece(vec, number), (8, D)), turn, 1)[:1, :CH]
    query_bias, value_bias = own(2), own(3)

    for r in range(SEQ):
        nat = jnp.bitwise_xor(mine, r)
        at = rows_at(nat, CH)
        label[nat] = toks[r][CH:, :CH]
        hat, _ = norm_stats(toks[r][:CH, :])
        xh[at, :], xl[at, :] = halves(hat)
        nh, nl = halves(hat * gain + shift)
        joined = dot3(nh, nl, wh[...], wl[...], NN)
        query = (joined[:, :CH] + query_bias) * HEAD ** (-0.5)
        key = joined[:, CH : 2 * CH]
        value = joined[:, 2 * CH :] + value_bias
        keys = lane_pairs(key[:, :128], key[:, 128:])
        values = lane_pairs(value[:, :128], value[:, 128:])
        queries = lane_pairs(query[:, :128], query[:, 128:])
        key_t, value_t, query_t = key.T, value.T, query.T
        for h in range(OWN):
            kcat[h, at, :] = jnp.concatenate([keys[h], keys[h]], axis=1)
            vcat[h, at, :] = jnp.concatenate([values[h], values[h]], axis=1)
            qpair[h, at, :] = queries[h]
            a, b = row_halves(query_t, h)
            qturn[h, :, at] = jnp.concatenate([a, a, b, b], axis=0)
            a, b = row_halves(key_t, h)
            kturn[h, :, at] = jnp.concatenate([a, b], axis=0)
            a, b = row_halves(value_t, h)
            vturn[h, :, at] = jnp.concatenate([a, b], axis=0)

    labels = jnp.concatenate([label[c][:1, :] for c in range(SEQ)], axis=1)
    spot = lax.broadcasted_iota(jnp.int32, (1, LEN), 1).astype(f32)
    begin = jnp.zeros((1, LEN), f32)
    for segment in range(3):
        held = jnp.sum(jnp.where(labels == float(segment), 1.0, 0.0), axis=1, keepdims=True)
        begin = begin + jnp.where(labels > float(segment), held, 0.0)
    begin = jnp.where(labels < 0.0, spot, begin)
    low_row[...] = jnp.broadcast_to(begin, (8, LEN))

    def one_head(h, carry):
        for c in range(SEQ):
            size = CH * (c + 1)
            lanes = slice(c * CH, (c + 1) * CH)
            score = dot(kcat[h, :size, :], qturn[h, :, lanes], NN)
            mask = allowed(low_row, c, size)
            score = jnp.where(mask, score, masked_score)
            peak = jnp.max(score, axis=0, keepdims=True)
            weight = jnp.exp(score - peak)
            total = jnp.sum(weight, axis=0, keepdims=True)
            top, rest = halves(weight)
            both = dot(vturn[h, :, :size], top, NN)
            extra = dot(vturn[h, :HEAD, :size], rest, NN)
            result = (both[:HEAD] + both[HEAD:] + extra) / total
            outs_turn[pl.ds(pl.multiple_of(h * HEAD, HEAD), HEAD), lanes] = result
            lse[h, :, lanes] = jnp.broadcast_to(peak + jnp.log(total), (8, CH))
        return carry

    lax.fori_loop(0, OWN, one_head, 0)


def allowed(low_row, c, size):
    key_at = lax.broadcasted_iota(jnp.int32, (size, CH), 0).astype(f32)
    query_at = (lax.broadcasted_iota(jnp.int32, (1, CH), 1) + c * CH).astype(f32)
    begin = low_row[:1, c * CH : (c + 1) * CH]
    return (key_at >= begin) & (key_at <= query_at)


def proj_kernel(scal, *refs):
    toks, heads, parts, refs = refs[:4], refs[4:8], refs[8:12], refs[12:]
    vec, wh, wl, heads_h, heads_l, norm_h, norm_l, mixed, hat, scale, weight, joined = refs
    mine = scal[0]
    for r in range(SEQ):
        at = jnp.bitwise_xor(mine, r)
        for d in range(GROUPS):
            weight[pl.ds(pl.multiple_of(d * ROWS + at * SUB, 8), SUB), :] = parts[r][
                d * SUB : (d + 1) * SUB, :
            ]
        joined[rows_at(at, QUARTER), :] = heads[r][...]
    wh[...], wl[...] = halves(weight[...])
    heads_h[...], heads_l[...] = halves(joined[:, rows_at(mine, CH)])
    gain, shift = piece(vec, 5), piece(vec, 6)
    for r in range(SEQ):
        at = rows_at(jnp.bitwise_xor(mine, r), CH)
        a, b = halves(joined[:, at].T)
        total = toks[r][:CH, :] + dot3(a, b, wh[...], wl[...], NN)
        total = total + piece(vec, 4)
        normed, size = norm_stats(total)
        norm_h[r], norm_l[r] = halves(normed * gain + shift)
        if r == 0:
            mixed[...] = total
            hat[...] = normed
            scale[...] = jnp.broadcast_to(size, (CH, 128))


def hidden_kernel(scal, norm_h, norm_l, *refs):
    blocks, vec, acts_h, acts_l, slope, winh, winl = refs[:GROUPS], *refs[GROUPS:]
    mine = scal[0]
    for k in range(GROUPS):
        at = rows_at(owner(scal, k), ROWS)
        winh[at, :], winl[at, :] = halves(blocks[k][...])
    marks = [16 + d for d in range(GROUPS)]
    table = jnp.concatenate([vec[m // 3, m % 3 : m % 3 + 1, :] for m in marks], axis=0)
    table = pltpu.roll(table, lax.rem(HALF_VEC - mine * ROWS, HALF_VEC), 1)[:, :ROWS]
    bias = jnp.concatenate([table[d : d + 1] for d in range(GROUPS)], axis=1)
    for r in range(SEQ):
        at = slice(r * CH, (r + 1) * CH)
        hidden = dot3(norm_h[r], norm_l[r], winh[...], winl[...], NN) + bias
        inner = jnp.tanh(gelu_scale * (hidden + gelu_cubic * hidden * hidden * hidden))
        acts_h[at, :], acts_l[at, :] = halves(0.5 * hidden * (1.0 + inner))
        slope[at, :] = 0.5 * (1.0 + inner) + 0.5 * hidden * (1.0 - inner * inner) * gelu_scale * (
            1.0 + 3.0 * gelu_cubic * hidden * hidden
        )


def emit_blocks(scal, outs, whole):
    for k in range(GROUPS):
        outs[k][...] = whole[rows_at(owner(scal, k), ROWS), :]


def out_grad_kernel(scal, acts_h, acts_l, *refs):
    grads, (out_h, out_l), outs, whole = refs[:4], refs[4:6], refs[6 : 6 + GROUPS], refs[6 + GROUPS]
    for r in range(SEQ):
        at = slice(r * CH, (r + 1) * CH)
        out_h[at, :], out_l[at, :] = halves(grads[r][...])
    whole[...] = dot3(acts_h[...], acts_l[...], out_h[...], out_l[...], TN)
    emit_blocks(scal, outs, whole)


def hidden_back_kernel(scal, out_h, out_l, slope, winh, winl, *refs):
    blocks, refs = refs[:GROUPS], refs[GROUPS:]
    hid_h, hid_l, wouth, woutl, bias_sum = refs[:5]
    parts = refs[5:]
    for k in range(GROUPS):
        at = rows_at(owner(scal, k), ROWS)
        wouth[at, :], woutl[at, :] = halves(blocks[k][...])
    sums = jnp.zeros((1, D), f32)
    for r in (1, 3, 2, 0):
        at = slice(r * CH, (r + 1) * CH)
        back = dot3(out_h[at, :], out_l[at, :], wouth[...], woutl[...], NT) * slope[at, :]
        sums = sums + jnp.sum(back, axis=0, keepdims=True)
        bh, bl = halves(back)
        hid_h[at, :], hid_l[at, :] = bh, bl
        parts[r][...] = dot3(bh, bl, winh[...], winl[...], NT)
    bias_sum[...] = jnp.broadcast_to(sums, (8, D))


def in_grad_kernel(scal, norm_h, norm_l, hid_h, hid_l, *refs):
    outs, whole = refs[:GROUPS], refs[GROUPS]
    flat = lambda ref: ref[...].reshape(LEN, D)
    whole[...] = dot3(flat(norm_h), flat(norm_l), hid_h[...], hid_l[...], TN)
    emit_blocks(scal, outs, whole)


def ffn_out_kernel(scal, acts_h, acts_l, wouth, woutl, *parts):
    for r in (1, 3, 2, 0):
        at = slice(r * CH, (r + 1) * CH)
        parts[r][...] = dot3(acts_h[at, :], acts_l[at, :], wouth[...], woutl[...], NN)


def output_kernel(scal, mixed, one, two, three, vec, output):
    output[...] = mixed[...] + (one[...] + two[...] + three[...]) + piece(vec, 7)


def proj_back_kernel(scal, one, two, three, hat, scale, vec, grad_out, wh, wl, mixed_grad, sums, *parts):
    mine = scal[0]
    normed = one[...] + two[...] + three[...]
    back = norm_back(hat[...], scale[:, :1], piece(vec, 5), normed)
    total = grad_out[...] + back
    mixed_grad[...] = total
    a, b = halves(total)
    for r in range(SEQ):
        at = rows_at(jnp.bitwise_xor(mine, r), QUARTER)
        parts[r][...] = dot3(wh[at, :], wl[at, :], a, b, NT)
    add = lambda v: jnp.sum(v, axis=0, keepdims=True)
    sums[...] = jnp.concatenate(
        [add(total), add(normed * hat[...]), add(normed), add(grad_out[...]), jnp.zeros((4, D), f32)],
        axis=0,
    )


def proj_grad_kernel(scal, heads_h, heads_l, mixed_grad, *refs):
    outs, whole = refs[:-1], refs[-1]
    mine = scal[0]
    gh, gl = halves(mixed_grad[...])
    whole[...] = dot3(heads_h[...], heads_l[...], gh, gl, NN)
    for r in range(SEQ):
        at = jnp.bitwise_xor(mine, r)
        for d in range(GROUPS):
            outs[r][d * SUB : (d + 1) * SUB, :] = whole[
                pl.ds(pl.multiple_of(d * ROWS + at * SUB, 8), SUB), :
            ]


def back_kernel(scal, *refs):
    grads, refs = refs[:4], refs[4:]
    kcat, qturn, vcat, qpair, kturn, outs_turn, lse, low_row = refs[:8]
    joined_h, joined_l, joined_sums = refs[8:11]
    gturn, gpair, dots, key_sum, value_sum, query_turn = refs[11:]
    mine = scal[0]

    for r in range(SEQ):
        at = rows_at(jnp.bitwise_xor(mine, r), CH)
        turned = grads[r][...]
        grad = jnp.concatenate([turned, jnp.zeros((HEAD, CH), f32)], axis=0).T
        pairs = lane_pairs(grad[:, :128], grad[:, 128:])
        for h in range(OWN):
            gpair[h, at, :] = pairs[h]
            part = turned[HEAD * h : HEAD * (h + 1)]
            dots[h, :, at] = jnp.broadcast_to(
                jnp.sum(part * outs_turn[HEAD * h : HEAD * (h + 1), at], axis=0, keepdims=True), (8, CH)
            )
            a, b = halves(part)
            gturn[h, :, at] = jnp.concatenate([a, a, b, b], axis=0)

    key_sum[...] = jnp.zeros_like(key_sum)
    value_sum[...] = jnp.zeros_like(value_sum)

    def one_head(h, carry):
        for c in range(SEQ):
            size = CH * (c + 1)
            lanes = slice(c * CH, (c + 1) * CH)
            score = dot(kcat[h, :size, :], qturn[h, :, lanes], NN)
            weight = jnp.where(allowed(low_row, c, size), jnp.exp(score - lse[h, :1, lanes]), 0.0)
            back = dot(vcat[h, :size, :], gturn[h, :, lanes], NN)
            score_back = weight * (back - dots[h, :1, lanes])
            a, b = halves(weight)
            pair = gpair[h, lanes, :]
            value_sum[h, :size, :] += dot(a, pair, NN) + dot(b, pair, NN)
            a, b = halves(score_back)
            pair = qpair[h, lanes, :]
            key_sum[h, :size, :] += dot(a, pair, NN) + dot(b, pair, NN)
            turned = dot(kturn[h, :, :size], a, NN) + dot(kturn[h, :, :size], b, NN)
            query_turn[h, :, lanes] = (turned[:HEAD] + turned[HEAD:]) * HEAD ** (-0.5)
        return carry

    lax.fori_loop(0, OWN, one_head, 0)

    column_sums = jnp.zeros((1, D), f32)
    low = low_lanes((CH, 128))
    for c in range(SEQ):
        at = slice(c * CH, (c + 1) * CH)
        blank = jnp.zeros((HEAD, CH), f32)
        query = jnp.concatenate([query_turn[h, :, at] for h in range(OWN)] + [blank], axis=0).T
        done = [query]
        for kept in (key_sum, value_sum):
            full = [kept[h, at, :] for h in range(OWN)]
            full = [v + pltpu.roll(v, HEAD, 1) for v in full]
            done.append(jnp.where(low, full[0], full[1]))
            done.append(jnp.where(low, full[2], 0.0))
        joined = jnp.concatenate(done, axis=1)
        column_sums = column_sums + jnp.sum(joined, axis=0, keepdims=True)
        joined_h[at, :], joined_l[at, :] = halves(joined)

    joined_sums[...] = jnp.broadcast_to(column_sums, (8, D))


def qkv_grad_kernel(scal, xh, xl, joined_h, joined_l, joined_sums, wh, wl, vec, *refs):
    proj_one, proj_two, vector_sums, bias_sum = refs[:4]
    outs, (whole, rows) = refs[4 : 4 + GROUPS], refs[4 + GROUPS :]
    mine = scal[0]
    column_sums = joined_sums[:1, :]
    core = dot3(xh[...], xl[...], joined_h[...], joined_l[...], TN)
    gain, shift = piece(vec, 0), piece(vec, 1)
    as_column = lambda v: jnp.broadcast_to(v, (128, D)).T[:, :1]
    whole[...] = as_column(gain) * core + as_column(shift) * column_sums
    weights = wh[...].astype(f32) + wl[...].astype(f32)
    gain_grad = jnp.sum(weights * core, axis=1, keepdims=True)
    shift_grad = jnp.sum(weights * column_sums, axis=1, keepdims=True)
    lane = lax.broadcasted_iota(jnp.int32, (D, 128), 1)
    norm_grads = jnp.where(lane == 0, gain_grad, shift_grad).T

    def place(part, scale):
        wide = jnp.concatenate([part[:, :QUARTER], jnp.zeros((1, D - QUARTER), f32)], axis=1)
        wide = jnp.broadcast_to(wide, (8, D))
        return pltpu.roll(wide, mine * QUARTER, 1)[:1]

    entries = [
        norm_grads[0:1],
        norm_grads[1:2],
        place(column_sums[:, :CH], 1.0),
        place(column_sums[:, 2 * CH :], 1.0),
        vector_sums[0:1],
        vector_sums[1:2],
        vector_sums[2:3],
        vector_sums[3:4],
    ]
    lines = [e[:, i * HALF_VEC : (i + 1) * HALF_VEC] for e in entries for i in range(2)]
    bias = jnp.concatenate(
        [bias_sum[:1, d * ROWS : (d + 1) * ROWS] for d in range(GROUPS)], axis=0
    )
    bias = jnp.concatenate([bias, jnp.zeros((GROUPS, HALF_VEC - ROWS), f32)], axis=1)
    bias = pltpu.roll(bias, mine * ROWS, 1)
    lines = lines + [bias[d : d + 1] for d in range(GROUPS)]
    filler = jnp.zeros((5, HALF_VEC), f32)
    for d in range(GROUPS):
        rows[d] = jnp.concatenate(lines[3 * d : 3 * d + 3] + [filler], axis=0)

    for k in range(GROUPS):
        at = owner(scal, k)
        outs[k][:ROWS, :] = whole[rows_at(at, ROWS), :]
        here = pl.ds(pl.multiple_of(at * SUB, 8), SUB)
        proj = proj_one[here, :] + proj_two[here, :]
        for group in range(SEQ):
            for part in range(3):
                lane_at = HEAD * (3 * group + part)
                outs[k][
                    group * SUB : (group + 1) * SUB, part * CH + QUARTER : (part + 1) * CH
                ] = proj[:, lane_at : lane_at + HEAD]
        outs[k][ROWS:, :HALF_VEC] = rows[at]
        outs[k][ROWS:, HALF_VEC:] = jnp.zeros((8, HALF_VEC), f32)


def pre_back_kernel(scal, joined_h, joined_l, wh, wl, *parts):
    mine = scal[0]
    for r in (1, 3, 2, 0):
        at = rows_at(jnp.bitwise_xor(mine, r), CH)
        parts[r][...] = dot3(joined_h[at, :], joined_l[at, :], wh[...], wl[...], NT)


def input_grad_kernel(scal, tokens, one, two, three, vec, mixed_grad, result):
    hat, scale = norm_stats(tokens[...])
    grad = one[...] + two[...] + three[...]
    result[...] = mixed_grad[...] + norm_back(hat, scale, piece(vec, 0), grad)


def total_square(value):
    return jnp.sum(jnp.sum(value * value, axis=0, keepdims=True), axis=1, keepdims=True)


def second_squares_kernel(scal, *refs):
    parts, squares = refs[:8], refs[8]
    total = sum(total_square(part[...]) for part in parts)
    squares[...] = jnp.broadcast_to(total, (8, 128))


def first_squares_kernel(scal, one, two, three, four, before, squares):
    parts = (one, two, three, four)
    total = sum(total_square(part[:ROWS, :]) for part in parts)
    line = sum(part[ROWS:, :HALF_VEC] for part in parts)
    squares[...] = before[...] + (total + total_square(line))


def stage_kernel(scal, *refs):
    sources, targets, sems = refs[:15], refs[15:30], refs[30]
    copies = [
        pltpu.make_async_copy(source, target, sems.at[i])
        for i, (source, target) in enumerate(zip(sources, targets))
    ]
    for copy in copies:
        copy.start()
    for copy in copies:
        copy.wait()


def adamw_kernel(scal, squares, *refs):
    firsts, ins, outs, refs = refs[:4], refs[4:8], refs[8:12], refs[12:]
    states, clip, finals, news = refs[:15], refs[15], refs[16:31], refs[31:46]
    first, second, sems = refs[46:]
    send = lambda number: [
        pltpu.make_async_copy(news[i], finals[i], sems.at[i]) for i in range(3 * number, 3 * number + 3)
    ]
    mine = scal[0]
    norm = jnp.sqrt(squares[...])
    clip[...] = norm
    factor = (clip_limit / jnp.maximum(norm, clip_limit))[:1, :1]
    for r in range(SEQ):
        at = jnp.bitwise_xor(mine, r)
        first[at] = firsts[r][:ROWS, :]
        second[at, :ROWS] = ins[r][...]
        second[at, ROWS:] = outs[r][...]

    def update(number, spot, grad, rate, decay):
        held = [states[3 * number + i][spot] for i in range(3)]
        fresh = adamw_update(*held, factor * grad, rate, decay)
        for i in range(3):
            news[3 * number + i][spot] = fresh[i]

    def finish(number):
        for copy in send(number):
            copy.start()

    line = sum(firsts[r][ROWS:, :HALF_VEC] for r in range(SEQ))
    for i in range(3):
        for j in range(3):
            spot = (slice(3 * i + j, 3 * i + j + 1), slice(None))
            update(0, spot, line[i : i + 1, 128 * j : 128 * (j + 1)], vector_rate, 0.0)
    finish(0)
    every = slice(None)
    for part in range(3):
        grad = jnp.concatenate(
            [first[j][:, part * CH : part * CH + QUARTER] for j in range(SEQ)], axis=1
        )
        update(1, (every, slice(part * D, (part + 1) * D)), grad, matrix_rate, weight_decay)
    finish(1)
    for j in range(SEQ):
        grad = jnp.concatenate(
            [
                first[j][group * SUB : (group + 1) * SUB, part * CH + QUARTER : (part + 1) * CH]
                for group in range(SEQ)
                for part in range(3)
            ],
            axis=1,
        )
        update(2, (slice(j * SUB, (j + 1) * SUB), every), grad, matrix_rate, weight_decay)
    finish(2)
    for d in range(GROUPS):
        grad = jnp.concatenate(
            [second[j][:ROWS, d * ROWS : (d + 1) * ROWS] for j in range(SEQ)], axis=1
        )
        update(3, (every, slice(d * HALF_VEC, (d + 1) * HALF_VEC)), grad, matrix_rate, weight_decay)
    finish(3)
    for j in range(SEQ):
        update(
            4, (slice(j * ROWS, (j + 1) * ROWS), every), second[j][ROWS:, :], matrix_rate, weight_decay
        )
    finish(4)
    for number in range(5):
        for copy in send(number):
            copy.wait()


def adamw_update(weight, first, second, grad, rate, decay):
    new_first = beta_one * first + (1.0 - beta_one) * grad
    new_second = beta_two * second + (1.0 - beta_two) * grad * grad
    first_hat = new_first / (1.0 - beta_one**STEP)
    second_hat = new_second / (1.0 - beta_two**STEP)
    new_weight = weight - rate * (first_hat / (jnp.sqrt(second_hat) + adam_eps) + decay * weight)
    return (new_first, new_second, new_weight)


def ring_tables(count):
    evens = [2 * i for i in range(count // 2)]
    order = evens + [i + 1 for i in reversed(evens)]
    place = [0] * count
    for position, device in enumerate(order):
        place[device] = position
    right = [(order[i], order[(i + 1) % count]) for i in range(count)]
    left = [(b, a) for a, b in right]
    return order, place, right, left


class RingGather:
    def __init__(self, block, name, flip=False):
        _, _, self.right, self.left = ring_tables(GROUPS)
        if flip:
            self.right, self.left = self.left, self.right
        self.got, self.name, self.at, self.flip = {0: block}, name, 0, flip

    def step(self, after=()):
        places = (-self.at % GROUPS, self.at)
        if after:
            for place in set(places):
                self.got[place] = gate(self.got[place], after)
        forth, back = (self.got[place] for place in places)
        self.at += 1
        self.got[GROUPS - self.at] = move(forth, "dp", self.right, f"{self.name}_right_{self.at}")
        if self.at < HALF:
            self.got[self.at] = move(back, "dp", self.left, f"{self.name}_left_{self.at}")
        return [self.got[GROUPS - self.at]] + ([self.got[self.at]] if self.at < HALF else [])

    def blocks(self):
        return [self.got[-k % GROUPS if self.flip else k] for k in range(GROUPS)]


class RingScatter:
    def __init__(self, blocks, name, flip=False):
        _, _, self.right, self.left = ring_tables(GROUPS)
        self.blocks = blocks
        if flip:
            self.right, self.left = self.left, self.right
            self.blocks = [blocks[-k % GROUPS] for k in range(GROUPS)]
        self.name, self.back, self.at = name, None, HALF
        self.forth = move(self.blocks[HALF], "dp", self.right, f"{name}_right_1")

    def step(self, after=()):
        self.at -= 1
        ahead, back = self.blocks[self.at], self.blocks[GROUPS - self.at]
        if self.back is None:
            forth = plus(self.forth, ahead, after=after)
        else:
            forth, back = sums([(self.forth, ahead), (self.back, back)], after)
        number = HALF + 1 - self.at
        self.forth = move(forth, "dp", self.right, f"{self.name}_right_{number}")
        self.back = move(back, "dp", self.left, f"{self.name}_left_{number}")
        return [forth, back]

    def result(self, after=()):
        return plus(self.forth, self.back, self.blocks[0], after=after)


def move(block, axis, pairs, name):
    with jax.named_scope(name):
        return lax.ppermute(block, axis, pairs)


def swap(block, bits, name):
    return move(block, "seq", [(i, i ^ bits) for i in range(SEQ)], f"{name}_{bits}")


def gather_seq(block, name):
    across = swap(block, 2, name)
    core = swap(block, 1, name)
    return [block, core, across, swap(across, 1, f"{name}_2")]


def exchange_seq(parts, name):
    return [parts[0]] + [swap(parts[r], r, name) for r in range(1, SEQ)]


def scatter_core(parts, name):
    return parts[0], swap(parts[1], 1, f"{name}_own"), parts[2], swap(parts[3], 1, f"{name}_across")


def ordered(blocks, mine):
    stack = jnp.stack(blocks, axis=0)
    return [lax.dynamic_index_in_dim(stack, mine ^ j, 0, keepdims=False) for j in range(len(blocks))]


def local(
    tokens,
    cotangent,
    segment_ids,
    valid,
    vectors,
    vec_first,
    vec_second,
    w_qkv,
    qkv_first,
    qkv_second,
    w_proj,
    proj_first,
    proj_second,
    w_in,
    in_first,
    in_second,
    w_out,
    out_first,
    out_second,
):
    dp_parts = lax.axis_size("dp")
    ring = dp_parts == GROUPS
    mine = lax.axis_index("seq")
    home = lax.axis_index("dp")
    rows = w_qkv.shape[0]
    units = w_out.shape[0] // SEQ
    far, near = home // 2, home % 2
    position = jnp.where(near > 0, GROUPS - 1 - far, far)
    scal = jnp.stack([mine, position, jnp.full_like(mine, 1 if ring else 0)]).astype(jnp.int32)
    flat_in = tokens.reshape(CH, D)
    chunk, tall, square = shape(CH, D), shape(LEN, D, kind=bf16), shape(D, D, kind=bf16)

    if ring:
        first, packed = run(
            pack_first_kernel,
            scal,
            [w_qkv, w_proj, vectors.reshape(9, 128), segment_ids, valid, flat_in],
            [shape(ROWS + 8, D), shape(CH + 8, D)],
            scratch=[
                pltpu.VMEM((3, ROWS, CH), f32),
                pltpu.VMEM((SUB, D), f32),
                pltpu.VMEM((9, 128), f32),
                pltpu.VMEM((2, 1, CH), jnp.int32),
            ],
            sems=8,
            far_args=range(6),
            room=54,
            name="pack_first", work=3.0,
        )
        ring_first = RingGather(first, "first")
        for _ in range(HALF):
            ring_first.step()
        firsts = ring_first.blocks()
        in_block, out_block = run(
            pack_second_kernel,
            scal,
            [w_in, w_out],
            [shape(ROWS, D)] * 2,
            name="pack_second", work=3.0,
            after=[firsts[GROUPS - 1]],
        )
        ring_in = RingGather(in_block, "w_in")
        ring_out = RingGather(out_block, "w_out", flip=True)
        came = ring_in.step([firsts[HALF]])
        came = came + ring_out.step([firsts[HALF]])
    else:
        padded = jnp.pad(w_qkv, ((0, 0), (0, CH)))
        own = lambda part: lax.dynamic_slice_in_dim(padded, part * D + mine * QUARTER, CH, 1)
        first = jnp.concatenate([own(0), own(1), own(2)], axis=1)
        first = lax.all_gather(first, "dp", axis=0, tiled=True).reshape(GROUPS, ROWS, D)
        all_vec = lax.all_gather(vectors, "dp", axis=0, tiled=True).reshape(GROUPS, 3, HALF_VEC)
        first = jnp.concatenate([first, jnp.pad(all_vec, ((0, 0), (0, 5), (0, D - HALF_VEC)))], axis=1)
        firsts = [first[k] for k in range(GROUPS)]
        in_part = lax.dynamic_index_in_dim(
            w_in.reshape(rows, dp_parts, SEQ, units), mine, 2, keepdims=False
        ).reshape(rows, D)
        out_part = lax.dynamic_slice_in_dim(w_out, mine * units, units, 0)
        in_blocks, out_blocks = (
            list(lax.all_gather(part, "dp", axis=0, tiled=True).reshape(GROUPS, ROWS, D))
            for part in (in_part, out_part)
        )
        marks = jnp.where(valid > 0, segment_ids, -1).astype(f32)
        packed = jnp.concatenate([flat_in, jnp.pad(marks, ((0, 7), (0, D - CH)))], axis=0)
    toks = gather_seq(packed, "tokens")
    (grad_out,) = run(
        mask_kernel, scal, [cotangent.reshape(CH, D), valid], [chunk], name="mask", work=2.0, after=[toks[2]]
    )
    grads_row = gather_seq(grad_out, "cotangent")

    qkv_h, qkv_l, vec, proj = run(
        weights_kernel,
        scal,
        firsts,
        [square, square, shape(GROUPS, 8, HALF_VEC), shape(GROUPS * SUB, D)],
        name="weights", work=3.0,
    )
    if ring:
        proj_parts = gather_seq(proj, "w_proj")
    else:
        full = lax.all_gather(w_proj, "dp", axis=0, tiled=True).reshape(GROUPS, SEQ, SUB, D)
        proj_parts = [
            lax.dynamic_index_in_dim(full, mine ^ r, 1, keepdims=False).reshape(GROUPS * SUB, D)
            for r in range(SEQ)
        ]
    hat_h, hat_l, kcat, qturn, vcat, qpair, kturn, low_row, heads, lse = run(
        front_kernel,
        scal,
        toks + [qkv_h, qkv_l, vec],
        [
            tall,
            tall,
            shape(OWN, LEN, 256, kind=bf16),
            shape(OWN, 256, LEN, kind=bf16),
            shape(OWN, LEN, 256, kind=bf16),
            shape(OWN, LEN, 128, kind=bf16),
            shape(OWN, 128, LEN, kind=bf16),
            shape(8, LEN),
            shape(QUARTER, LEN),
            shape(OWN, 8, LEN),
        ],
        scratch=[pltpu.VMEM((OWN, 128, LEN), bf16), pltpu.VMEM((SEQ, 8, CH), f32)],
        name="front", work=14.0,
        after=[grads_row[2]],
    )
    if ring:
        heads = gate(heads, [proj_parts[2], *came])
        ring_in.step([lse])
        came = ring_in.step()
        came = came + ring_in.step()
        ring_out.step(came)
        in_blocks = ring_in.blocks()
    across = swap(heads, 2, "heads")
    if ring:
        across = gate(across, came)
    all_heads = [heads, swap(heads, 1, "heads"), across, swap(across, 1, "heads_2")]
    wide = shape(D, CH, kind=bf16)
    split = shape(SEQ, CH, D, kind=bf16)
    proj_h, proj_l, heads_h, heads_l, norm_h, norm_l, mixed, hat_two, scale_two = run(
        proj_kernel,
        scal,
        toks + all_heads + proj_parts + [vec],
        [square, square, wide, wide, split, split, chunk, chunk, shape(CH, 128)],
        scratch=[pltpu.VMEM((D, D), f32), pltpu.VMEM((D, LEN), f32)],
        name="proj", work=8.0,
    )

    if ring:
        ring_out.step([norm_h])
        ring_out.step()
        out_blocks = ring_out.blocks()
    block = shape(ROWS, D)
    acts_h, acts_l, slope, in_wh, in_wl = run(
        hidden_kernel,
        scal,
        [norm_h, norm_l] + in_blocks + [vec],
        [tall, tall, shape(LEN, D), square, square],
        name="hidden", work=8.0,
    )
    done = run(
        out_grad_kernel,
        scal,
        [acts_h, acts_l] + grads_row,
        [tall, tall] + [block] * GROUPS,
        scratch=[pltpu.VMEM((D, D), f32)],
        name="out_grad", work=5.0,
    )
    out_h, out_l = done[:2]
    out_grads = list(done[2:])
    if ring:
        ring_out = RingScatter(out_grads, "out_grad")
    done = run(
        hidden_back_kernel,
        scal,
        [out_h, out_l, slope, in_wh, in_wl] + out_blocks,
        [tall, tall, square, square, shape(8, D)] + [chunk] * SEQ,
        name="hidden_back", work=11.0,
        after=out_grads[:1],
    )
    hid_h, hid_l, out_wh, out_wl, bias_sum = done[:5]
    parts = list(done[5:])
    if ring:
        parts[3] = gate(parts[3], ring_out.step([bias_sum]))
    norm_own, norm_near, norm_across, norm_far = scatter_core(parts, "norm_grad")
    norm_pair = plus(norm_across, norm_far)
    norm_last = swap(norm_pair, 2, "norm_grad")
    in_grads = list(
        run(
            in_grad_kernel,
            scal,
            [norm_h, norm_l, hid_h, hid_l],
            [block] * GROUPS,
            scratch=[pltpu.VMEM((D, D), f32)],
            name="in_grad", work=5.0,
            after=[norm_pair],
        )
    )
    if ring:
        ring_in = RingScatter(in_grads, "in_grad", flip=True)
        out_sent = ring_out.step()
        in_sent = ring_in.step()
    done = run(
        proj_back_kernel,
        scal,
        [norm_own, norm_near, norm_last, hat_two, scale_two, vec, grad_out, proj_h, proj_l],
        [chunk, shape(8, D)] + [shape(QUARTER, CH)] * SEQ,
        name="proj_back", work=5.0,
        after=out_sent + in_sent if ring else [],
    )
    mixed_grad, vector_sums = done[:2]
    head_grads = exchange_seq(list(done[2:]), "head_grad")
    if ring:
        out_sent = ring_out.step([mixed_grad])
        in_sent = ring_in.step([mixed_grad])
    out_parts = run(
        ffn_out_kernel,
        scal,
        [acts_h, acts_l, out_wh, out_wl],
        [chunk] * SEQ,
        name="ffn_out", work=7.0,
        after=[mixed_grad],
    )
    proj_grads = run(
        proj_grad_kernel,
        scal,
        [heads_h, heads_l, mixed_grad],
        [shape(GROUPS * SUB, D)] * SEQ,
        scratch=[pltpu.VMEM((D, D), f32)],
        name="proj_grad", work=4.0,
        after=[*head_grads[1:], *out_sent, *in_sent, out_parts[0]] if ring else [],
    )
    wait = [head_grads[3], head_grads[2]]
    out_own, out_near, out_across, out_far = scatter_core(out_parts, "output")
    out_sum = plus(out_across, out_far)
    if ring:
        proj_own, proj_near, proj_across, proj_far = scatter_core(proj_grads, "proj_grad")
        proj_pair, proj_base = sums([(proj_across, proj_far), (proj_own, proj_near)], wait)
        proj_last = swap(proj_pair, 2, "proj_grad")
    else:
        proj_base = proj_last = proj_grads[0]
    joined_h, joined_l, joined_sums = run(
        back_kernel,
        scal,
        head_grads + [kcat, qturn, vcat, qpair, kturn, heads, lse, low_row],
        [tall, tall, shape(8, D)],
        scratch=[
            pltpu.VMEM((OWN, 256, LEN), bf16),
            pltpu.VMEM((OWN, LEN, 128), bf16),
            pltpu.VMEM((OWN, 8, LEN), f32),
            pltpu.VMEM((OWN, LEN, 128), f32),
            pltpu.VMEM((OWN, LEN, 128), f32),
            pltpu.VMEM((OWN, HEAD, LEN), f32),
        ],
        name="back", work=16.0,
        after=[proj_grads[0]],
    )
    if ring:
        shard_out = ring_out.result([joined_sums])
        in_sent = ring_in.step([joined_sums])
    done = run(
        qkv_grad_kernel,
        scal,
        [hat_h, hat_l, joined_h, joined_l, joined_sums, qkv_h, qkv_l, vec]
        + [proj_base, proj_last, vector_sums, bias_sum],
        [shape(ROWS + 8, D)] * GROUPS,
        scratch=[pltpu.VMEM((D, D), f32), pltpu.VMEM((GROUPS, 8, HALF_VEC), f32)],
        name="qkv_grad", work=1.0,
        after=[*in_sent, shard_out] if ring else [],
    )
    first_grads = list(done)
    if ring:
        shard_in = ring_in.result([first_grads[0]])
        out_all = gather_seq(shard_out, "out_shard")
        in_all = gather_seq(shard_in, "in_shard")
        first_grads[HALF] = gate(first_grads[HALF], [shard_in, out_all[2]])
        ring_first = RingScatter(first_grads, "first_grad")
        first_sent = ring_first.step([in_all[2]])
    pre_parts = run(
        pre_back_kernel,
        scal,
        [joined_h, joined_l, qkv_h, qkv_l],
        [chunk] * SEQ,
        name="pre_back", work=1.0,
        after=[shard_in, *first_sent] if ring else [],
    )
    pre_parts = list(pre_parts)
    if ring:
        first_sent = ring_first.step()
        pre_parts[3] = gate(pre_parts[3], first_sent)
    pre_own, pre_near, pre_across, pre_far = scatter_core(pre_parts, "pre_grad")
    pre_pair = plus(pre_across, pre_far)
    pre_last = swap(pre_pair, 2, "pre_grad")
    states = [vectors, vec_first, vec_second, w_qkv, qkv_first, qkv_second, w_proj, proj_first, proj_second]
    states = states + [w_in, in_first, in_second, w_out, out_first, out_second]
    if ring:
        held = [v.reshape(9, 128) for v in states[:3]] + states[3:]
        held = run(
            stage_kernel,
            scal,
            held,
            [shape(*v.shape) for v in held],
            sems=15,
            far_args=range(15),
            name="stage", work=4.0,
            after=[pre_parts[0], out_sum],
        )
        ring_first.step([held[3]])
        shard_first = ring_first.result()
    (input_grad,) = run(
        input_grad_kernel,
        scal,
        [flat_in, pre_own, pre_near, pre_last, vec, mixed_grad],
        [chunk],
        name="input_grad", work=3.0,
    )

    if ring:
        (squares,) = run(
            second_squares_kernel, scal, in_all + out_all, [shape(8, 128)], name="second_squares", work=2.0
        )
        shard_first = gate(shard_first, [pre_last])
        across = gate(swap(shard_first, 2, "first_shard"), [input_grad, squares])
        core = swap(shard_first, 1, "first_shard")
        first_all = [shard_first, core, across, swap(across, 1, "first_shard_2")]
        out_pair = gate(out_sum, [across])
        (squares,) = run(
            first_squares_kernel,
            scal,
            first_all + [squares],
            [shape(8, 128)],
            name="first_squares", work=2.0,
            after=[out_pair],
        )
        flipped = lambda bits: [(i, i ^ bits) for i in range(GROUPS)]
        one, two, three = (move(squares, "dp", flipped(bits), "squares") for bits in (1, 2, 3))
        squares = sum_pairs(squares, one, two, three)
        squares = plus(squares, move(squares, "dp", flipped(4), "squares"))
        done = run(
            adamw_kernel,
            scal,
            [squares] + first_all + in_all + out_all + list(held),
            [shape(8, 128)] + [shape(*v.shape) for v in held],
            scratch=[pltpu.VMEM(v.shape, f32) for v in held]
            + [pltpu.VMEM((SEQ, ROWS, D), f32), pltpu.VMEM((SEQ, 2 * ROWS, D), f32)],
            sems=15,
            far_outs=range(1, 16),
            name="adamw", work=0.1,
        )
        new = [v.reshape(-1) for v in done[1:4]] + list(done[4:])
        clip_norm = done[0][0, 0]
    else:
        out_pair = out_sum
        by_group = jnp.stack(first_grads)
        shard_first = lax.psum_scatter(
            by_group[:, :ROWS].reshape(D, D), "dp", scatter_dimension=0, tiled=True
        )
        proj_full = jnp.stack([p.reshape(GROUPS, SUB, D) for p in ordered(proj_grads, mine)], axis=1)
        proj_grad = lax.psum(
            lax.psum_scatter(proj_full.reshape(D, D), "dp", scatter_dimension=0, tiled=True), "seq"
        )
        all_vec = lax.psum(by_group[:, ROWS : ROWS + 3, :HALF_VEC], ("dp", "seq")).reshape(-1)
        vec_grad = lax.dynamic_slice_in_dim(all_vec, home * vectors.shape[0], vectors.shape[0])
        joined = lax.all_gather(shard_first, "seq", axis=0, tiled=False)
        qkv_grad = jnp.concatenate(
            [joined[j, :, i * CH : i * CH + QUARTER] for i in range(3) for j in range(SEQ)], axis=1
        )
        shard_in, shard_out = (
            lax.psum_scatter(jnp.concatenate(parts, axis=0), "dp", scatter_dimension=0, tiled=True)
            for parts in (in_grads, out_grads)
        )
        in_all = lax.all_gather(shard_in, "seq", axis=0, tiled=False)
        in_grad = in_all.reshape(SEQ, rows, dp_parts, units).transpose(1, 2, 0, 3).reshape(rows, -1)
        out_grad = lax.all_gather(shard_out, "seq", axis=0, tiled=True)
        total = sum(jnp.sum(g * g) for g in (qkv_grad, proj_grad, in_grad, out_grad, vec_grad))
        total = lax.psum(total, "dp")
        clip_norm = jnp.sqrt(total)
        factor = clip_limit / jnp.maximum(clip_norm, clip_limit)
        grads = (vec_grad, qkv_grad, proj_grad, in_grad, out_grad)
        new = []
        for number, grad in enumerate(grads):
            rate, decay = (matrix_rate, weight_decay) if number else (vector_rate, 0.0)
            new.extend(adamw_update(*states[3 * number : 3 * number + 3], factor * grad, rate, decay))
    out_last = swap(out_pair, 2, "output")
    (output,) = run(
        output_kernel, scal, [mixed, out_own, out_near, out_last, vec], [chunk], name="output", work=2.0
    )
    return (output.reshape(tokens.shape), input_grad.reshape(tokens.shape), clip_norm, *new)


def solution(mesh):
    row = P("dp", "seq", None)
    mark = P("dp", "seq")
    vec = P("dp")
    mat = P("dp", None)
    return jax.shard_map(
        local,
        mesh=mesh,
        in_specs=(row, row, mark, mark) + (vec,) * 3 + (mat,) * 12,
        out_specs=(row, row, P()) + (vec,) * 3 + (mat,) * 12,
        check_vma=False,
    )
```

```python
import functools
import math

import jax
import jax.numpy as jnp
from jax import lax
from jax.experimental import pallas as pl
from jax.experimental.pallas import tpu as pltpu
from jax.sharding import PartitionSpec as P

D = 768
HEADS = 12
HEAD = 64
STEP = 10
CH = 256
LEN = 1024
SEQ = 4
QUARTER = D // SEQ
OWN = HEADS // SEQ
GROUPS = 8
ROWS = D // GROUPS
SUB = ROWS // SEQ
HALF = GROUPS // 2
HALF_VEC = D // 2
VEC_ROWS = 24

f32 = jnp.float32
bf16 = jnp.bfloat16
masked_score = -1e30
norm_eps = 1e-05
clip_limit = 1.0
beta_one = 0.9
beta_two = 0.999
adam_eps = 1e-08
matrix_rate = 0.02
vector_rate = 0.4
weight_decay = 0.01
gelu_scale = 0.7978845608028654
gelu_cubic = 0.044715

COST = 1e9

WHOLE = pl.BlockSpec(memory_space=pltpu.VMEM)
SCALARS = pl.BlockSpec(memory_space=pltpu.SMEM)
NN = ((1,), (0,))
NT = ((1,), (1,))
TN = ((0,), (0,))


def shape(*dims, kind=f32):
    return jax.ShapeDtypeStruct(dims, kind)


def run(
    kernel, scal, args, outs, scratch=(), sems=0, far_args=(), far_outs=(), room=8, work=1.0, name=None, after=()
):
    args, after = list(args), list(after)
    held = sum(math.prod(v.shape) * jnp.dtype(v.dtype).itemsize for v in scratch)
    anywhere, far = pl.BlockSpec(memory_space=pl.ANY), pl.BlockSpec(memory_space=pltpu.HBM)
    scratch = list(scratch) + ([pltpu.SemaphoreType.DMA((sems,))] if sems else [])

    def body(scal_ref, *refs):
        kernel(scal_ref, *refs[: len(args)], *refs[len(args) + len(after) :])

    return pl.pallas_call(
        body,
        out_shape=tuple(outs),
        in_specs=[SCALARS]
        + [far if i in far_args else WHOLE for i in range(len(args))]
        + [anywhere] * len(after),
        out_specs=tuple(far if i in far_outs else WHOLE for i in range(len(outs))),
        scratch_shapes=scratch,
        compiler_params=pltpu.CompilerParams(vmem_limit_bytes=held + (room << 20)),
        cost_estimate=pl.CostEstimate(
            flops=int(work * COST), bytes_accessed=1, transcendentals=0
        ),
        name=name,
    )(scal, *args, *after)


def gate(value, after):
    anywhere = pl.BlockSpec(memory_space=pl.ANY)
    return pl.pallas_call(
        lambda *refs: None,
        out_shape=shape(*value.shape, kind=value.dtype),
        in_specs=[anywhere] * (1 + len(after)),
        out_specs=anywhere,
        input_output_aliases={0: 0},
        compiler_params=pltpu.CompilerParams(vmem_limit_bytes=1 << 20),
        name="gate",
    )(value, *after)


def sums(groups, after=()):
    sizes = [len(group) for group in groups]

    def body(*refs):
        at = 0
        for number, size in enumerate(sizes):
            total = refs[at][...]
            for ref in refs[at + 1 : at + size]:
                total = total + ref[...]
            refs[sum(sizes) + len(after) + number][...] = total
            at += size

    return pl.pallas_call(
        body,
        out_shape=tuple(shape(*group[0].shape) for group in groups),
        in_specs=[WHOLE] * sum(sizes) + [pl.BlockSpec(memory_space=pl.ANY)] * len(after),
        out_specs=tuple([WHOLE] * len(groups)),
        compiler_params=pltpu.CompilerParams(vmem_limit_bytes=4 << 20),
        cost_estimate=pl.CostEstimate(flops=int(COST), bytes_accessed=1, transcendentals=0),
        name="plus",
    )(*(term for group in groups for term in group), *after)


def plus(*terms, after=()):
    return sums([terms], after)[0]


def sum_pairs(one, two, three, four):
    def body(a, b, c, d, result):
        result[...] = (a[...] + b[...]) + (c[...] + d[...])

    return pl.pallas_call(
        body,
        out_shape=shape(*one.shape),
        in_specs=[WHOLE] * 4,
        out_specs=WHOLE,
        compiler_params=pltpu.CompilerParams(vmem_limit_bytes=1 << 20),
        name="sum_pairs",
    )(one, two, three, four)


def owner(scal, k):
    spot = jnp.bitwise_and(scal[1] + k, GROUPS - 1)
    return jnp.where(scal[2] > 0, jnp.where(spot < HALF, 2 * spot, 2 * GROUPS - 1 - 2 * spot), k)


def halves(value):
    top = value.astype(bf16)
    return top, (value - top.astype(f32)).astype(bf16)


def dot(left, right, dims):
    return lax.dot_general(left, right, (dims, ((), ())), preferred_element_type=f32)


def dot3(lh, ll, rh, rl, dims):
    (left,), (right,) = dims
    join = lambda parts, axis: jnp.concatenate([part[...] for part in parts], axis=axis)
    return dot(join([lh, lh, ll], left), join([rh, rl, rh], right), dims)


def rows_at(index, size):
    return pl.ds(pl.multiple_of(index * size, size), size)


def piece(vec, number):
    a, b = 2 * number, 2 * number + 1
    return jnp.concatenate(
        [vec[a // 3, a % 3 : a % 3 + 1, :], vec[b // 3, b % 3 : b % 3 + 1, :]], axis=1
    )


def norm_stats(inputs):
    center = inputs - jnp.mean(inputs, axis=-1, keepdims=True)
    spread = jnp.mean(center * center, axis=-1, keepdims=True)
    scale = lax.rsqrt(spread + norm_eps)
    return center * scale, scale


def norm_back(hat, scale, gain, grad):
    inner = grad * gain
    return scale * (
        inner
        - jnp.mean(inner, axis=-1, keepdims=True)
        - hat * jnp.mean(inner * hat, axis=-1, keepdims=True)
    )


def low_lanes(dims):
    return lax.broadcasted_iota(jnp.int32, dims, 1) < HEAD


def lane_pairs(pair, last):
    low = low_lanes(pair.shape)
    roll = lambda v: pltpu.roll(v, HEAD, 1)
    ph = pair.astype(bf16).astype(f32)
    pl_ = pair - ph
    lh = last.astype(bf16).astype(f32)
    ll = last - lh
    return [
        jnp.where(low, ph, roll(pl_)).astype(bf16),
        jnp.where(low, roll(ph), pl_).astype(bf16),
        jnp.where(low, lh, roll(ll)).astype(bf16),
    ]


def row_halves(turned, head):
    part = turned[HEAD * head : HEAD * (head + 1)]
    return halves(part)


def pack_first_kernel(scal, wqkv, wproj, vec, seg, valid, tokens, first, packed, *refs):
    bands, proj, lines, marks, sems = refs
    mine = scal[0]
    aligned = pl.multiple_of(jnp.bitwise_and(mine * QUARTER, -128), 128)
    copies = [
        pltpu.make_async_copy(wqkv.at[:, pl.ds(part * D + aligned, CH)], bands.at[part], sems.at[part])
        for part in range(3)
    ]
    sub = pl.ds(pl.multiple_of(mine * SUB, 8), SUB)
    copies.append(pltpu.make_async_copy(wproj.at[sub, :], proj, sems.at[3]))
    copies.append(pltpu.make_async_copy(vec, lines, sems.at[4]))
    copies.append(pltpu.make_async_copy(seg, marks.at[0], sems.at[5]))
    copies.append(pltpu.make_async_copy(valid, marks.at[1], sems.at[6]))
    copies.append(pltpu.make_async_copy(tokens, packed.at[:CH, :], sems.at[7]))
    for copy in copies:
        copy.start()
    first[ROWS:, :] = jnp.zeros((8, D), f32)
    packed[CH:, :] = jnp.zeros((8, D), f32)
    for copy in copies[:5]:
        copy.wait()
    turn = jnp.where(jnp.bitwise_and(mine, 1) > 0, CH - HEAD, 0)
    for part in range(3):
        turned = pltpu.roll(bands[part], turn, 1)
        first[:ROWS, part * CH : part * CH + QUARTER] = turned[:, :QUARTER]
        for group in range(SEQ):
            lane = HEAD * (3 * group + part)
            first[group * SUB : (group + 1) * SUB, part * CH + QUARTER : (part + 1) * CH] = proj[
                :, lane : lane + HEAD
            ]
        first[ROWS + part : ROWS + part + 1, :HALF_VEC] = jnp.concatenate(
            [lines[3 * part + i : 3 * part + i + 1, :] for i in range(3)], axis=1
        )
    for copy in copies[5:]:
        copy.wait()
    packed[CH : CH + 1, :CH] = jnp.where(marks[1] > 0, marks[0], -1).astype(f32)


def pack_second_kernel(scal, win, wout, in_block, out_block):
    mine = scal[0]
    turn = lax.rem(HALF_VEC - mine * ROWS, HALF_VEC)
    for part in range(GROUPS):
        turned = pltpu.roll(win[:, part * HALF_VEC : (part + 1) * HALF_VEC], turn, 1)
        in_block[:, part * ROWS : (part + 1) * ROWS] = turned[:, :ROWS]
    out_block[...] = wout[pl.ds(pl.multiple_of(mine * ROWS, 8), ROWS), :]


def mask_kernel(scal, cotangent, valid, result):
    keep = jnp.where(valid[...] > 0, 1.0, 0.0).astype(f32)
    column = jnp.broadcast_to(keep, (128, CH)).T[:, :1]
    result[...] = cotangent[...] * column


def weights_kernel(scal, *refs):
    blocks, (wh, wl, vec, proj) = refs[:GROUPS], refs[GROUPS:]
    for k in range(GROUPS):
        at = owner(scal, k)
        block = blocks[k][:ROWS, :]
        here = rows_at(at, ROWS)
        wh[here, :], wl[here, :] = halves(block)
        vec[at] = blocks[k][ROWS:, :HALF_VEC]
        for group in range(SEQ):
            for part in range(3):
                lane = HEAD * (3 * group + part)
                proj[pl.ds(pl.multiple_of(at * SUB, 8), SUB), lane : lane + HEAD] = block[
                    group * SUB : (group + 1) * SUB, part * CH + QUARTER : (part + 1) * CH
                ]


def front_kernel(scal, *refs):
    toks, refs = refs[:4], refs[4:]
    wh, wl, vec = refs[:3]
    xh, xl, kcat, qturn, vcat, qpair, kturn, low_row, outs_turn, lse, vturn, label = refs[3:]
    mine = scal[0]

    gain, shift = piece(vec, 0), piece(vec, 1)
    turn = lax.rem(D - mine * QUARTER, D)
    own = lambda number: pltpu.roll(jnp.broadcast_to(piece(vec, number), (8, D)), turn, 1)[:1, :CH]
    query_bias, value_bias = own(2), own(3)

    for r in range(SEQ):
        nat = jnp.bitwise_xor(mine, r)
        at = rows_at(nat, CH)
        label[nat] = toks[r][CH:, :CH]
        hat, _ = norm_stats(toks[r][:CH, :])
        xh[at, :], xl[at, :] = halves(hat)
        nh, nl = halves(hat * gain + shift)
        joined = dot3(nh, nl, wh[...], wl[...], NN)
        query = (joined[:, :CH] + query_bias) * HEAD ** (-0.5)
        key = joined[:, CH : 2 * CH]
        value = joined[:, 2 * CH :] + value_bias
        keys = lane_pairs(key[:, :128], key[:, 128:])
        values = lane_pairs(value[:, :128], value[:, 128:])
        queries = lane_pairs(query[:, :128], query[:, 128:])
        key_t, value_t, query_t = key.T, value.T, query.T
        for h in range(OWN):
            kcat[h, at, :] = jnp.concatenate([keys[h], keys[h]], axis=1)
            vcat[h, at, :] = jnp.concatenate([values[h], values[h]], axis=1)
            qpair[h, at, :] = queries[h]
            a, b = row_halves(query_t, h)
            qturn[h, :, at] = jnp.concatenate([a, a, b, b], axis=0)
            a, b = row_halves(key_t, h)
            kturn[h, :, at] = jnp.concatenate([a, b], axis=0)
            a, b = row_halves(value_t, h)
            vturn[h, :, at] = jnp.concatenate([a, b], axis=0)

    labels = jnp.concatenate([label[c][:1, :] for c in range(SEQ)], axis=1)
    spot = lax.broadcasted_iota(jnp.int32, (1, LEN), 1).astype(f32)
    begin = jnp.zeros((1, LEN), f32)
    for segment in range(3):
        held = jnp.sum(jnp.where(labels == float(segment), 1.0, 0.0), axis=1, keepdims=True)
        begin = begin + jnp.where(labels > float(segment), held, 0.0)
    begin = jnp.where(labels < 0.0, spot, begin)
    low_row[...] = jnp.broadcast_to(begin, (8, LEN))

    def one_head(h, carry):
        for c in range(SEQ):
            size = CH * (c + 1)
            lanes = slice(c * CH, (c + 1) * CH)
            score = dot(kcat[h, :size, :], qturn[h, :, lanes], NN)
            mask = allowed(low_row, c, size)
            score = jnp.where(mask, score, masked_score)
            peak = jnp.max(score, axis=0, keepdims=True)
            weight = jnp.exp(score - peak)
            total = jnp.sum(weight, axis=0, keepdims=True)
            top, rest = halves(weight)
            both = dot(vturn[h, :, :size], top, NN)
            extra = dot(vturn[h, :HEAD, :size], rest, NN)
            result = (both[:HEAD] + both[HEAD:] + extra) / total
            outs_turn[pl.ds(pl.multiple_of(h * HEAD, HEAD), HEAD), lanes] = result
            lse[h, :, lanes] = jnp.broadcast_to(peak + jnp.log(total), (8, CH))
        return carry

    lax.fori_loop(0, OWN, one_head, 0)


def allowed(low_row, c, size):
    key_at = lax.broadcasted_iota(jnp.int32, (size, CH), 0).astype(f32)
    query_at = (lax.broadcasted_iota(jnp.int32, (1, CH), 1) + c * CH).astype(f32)
    begin = low_row[:1, c * CH : (c + 1) * CH]
    return (key_at >= begin) & (key_at <= query_at)


def proj_kernel(scal, *refs):
    toks, heads, parts, refs = refs[:4], refs[4:8], refs[8:12], refs[12:]
    vec, wh, wl, heads_h, heads_l, norm_h, norm_l, mixed, hat, scale, weight, joined = refs
    mine = scal[0]
    for r in range(SEQ):
        at = jnp.bitwise_xor(mine, r)
        for d in range(GROUPS):
            weight[pl.ds(pl.multiple_of(d * ROWS + at * SUB, 8), SUB), :] = parts[r][
                d * SUB : (d + 1) * SUB, :
            ]
        joined[rows_at(at, QUARTER), :] = heads[r][...]
    wh[...], wl[...] = halves(weight[...])
    heads_h[...], heads_l[...] = halves(joined[:, rows_at(mine, CH)])
    gain, shift = piece(vec, 5), piece(vec, 6)
    for r in range(SEQ):
        at = rows_at(jnp.bitwise_xor(mine, r), CH)
        a, b = halves(joined[:, at].T)
        total = toks[r][:CH, :] + dot3(a, b, wh[...], wl[...], NN)
        total = total + piece(vec, 4)
        normed, size = norm_stats(total)
        norm_h[r], norm_l[r] = halves(normed * gain + shift)
        if r == 0:
            mixed[...] = total
            hat[...] = normed
            scale[...] = jnp.broadcast_to(size, (CH, 128))


def hidden_kernel(scal, norm_h, norm_l, *refs):
    blocks, vec, acts_h, acts_l, slope, winh, winl = refs[:GROUPS], *refs[GROUPS:]
    mine = scal[0]
    for k in range(GROUPS):
        at = rows_at(owner(scal, k), ROWS)
        winh[at, :], winl[at, :] = halves(blocks[k][...])
    marks = [16 + d for d in range(GROUPS)]
    table = jnp.concatenate([vec[m // 3, m % 3 : m % 3 + 1, :] for m in marks], axis=0)
    table = pltpu.roll(table, lax.rem(HALF_VEC - mine * ROWS, HALF_VEC), 1)[:, :ROWS]
    bias = jnp.concatenate([table[d : d + 1] for d in range(GROUPS)], axis=1)
    for r in range(SEQ):
        at = slice(r * CH, (r + 1) * CH)
        hidden = dot3(norm_h[r], norm_l[r], winh[...], winl[...], NN) + bias
        inner = jnp.tanh(gelu_scale * (hidden + gelu_cubic * hidden * hidden * hidden))
        acts_h[at, :], acts_l[at, :] = halves(0.5 * hidden * (1.0 + inner))
        slope[at, :] = 0.5 * (1.0 + inner) + 0.5 * hidden * (1.0 - inner * inner) * gelu_scale * (
            1.0 + 3.0 * gelu_cubic * hidden * hidden
        )


def emit_blocks(scal, outs, whole):
    for k in range(GROUPS):
        outs[k][...] = whole[rows_at(owner(scal, k), ROWS), :]


def out_grad_kernel(scal, acts_h, acts_l, *refs):
    grads, (out_h, out_l), outs, whole = refs[:4], refs[4:6], refs[6 : 6 + GROUPS], refs[6 + GROUPS]
    for r in range(SEQ):
        at = slice(r * CH, (r + 1) * CH)
        out_h[at, :], out_l[at, :] = halves(grads[r][...])
    whole[...] = dot3(acts_h[...], acts_l[...], out_h[...], out_l[...], TN)
    emit_blocks(scal, outs, whole)


def hidden_back_kernel(scal, out_h, out_l, slope, winh, winl, *refs):
    blocks, refs = refs[:GROUPS], refs[GROUPS:]
    hid_h, hid_l, wouth, woutl, bias_sum = refs[:5]
    parts = refs[5:]
    for k in range(GROUPS):
        at = rows_at(owner(scal, k), ROWS)
        wouth[at, :], woutl[at, :] = halves(blocks[k][...])
    sums = jnp.zeros((1, D), f32)
    for r in (1, 3, 2, 0):
        at = slice(r * CH, (r + 1) * CH)
        back = dot3(out_h[at, :], out_l[at, :], wouth[...], woutl[...], NT) * slope[at, :]
        sums = sums + jnp.sum(back, axis=0, keepdims=True)
        bh, bl = halves(back)
        hid_h[at, :], hid_l[at, :] = bh, bl
        parts[r][...] = dot3(bh, bl, winh[...], winl[...], NT)
    bias_sum[...] = jnp.broadcast_to(sums, (8, D))


def in_grad_kernel(scal, norm_h, norm_l, hid_h, hid_l, *refs):
    outs, whole = refs[:GROUPS], refs[GROUPS]
    flat = lambda ref: ref[...].reshape(LEN, D)
    whole[...] = dot3(flat(norm_h), flat(norm_l), hid_h[...], hid_l[...], TN)
    emit_blocks(scal, outs, whole)


def ffn_out_kernel(scal, acts_h, acts_l, wouth, woutl, *parts):
    for r in (1, 3, 2, 0):
        at = slice(r * CH, (r + 1) * CH)
        parts[r][...] = dot3(acts_h[at, :], acts_l[at, :], wouth[...], woutl[...], NN)


def output_kernel(scal, mixed, one, two, three, vec, output):
    output[...] = mixed[...] + (one[...] + two[...] + three[...]) + piece(vec, 7)


def proj_back_kernel(scal, one, two, three, hat, scale, vec, grad_out, wh, wl, mixed_grad, sums, *parts):
    mine = scal[0]
    normed = one[...] + two[...] + three[...]
    back = norm_back(hat[...], scale[:, :1], piece(vec, 5), normed)
    total = grad_out[...] + back
    mixed_grad[...] = total
    a, b = halves(total)
    for r in range(SEQ):
        at = rows_at(jnp.bitwise_xor(mine, r), QUARTER)
        parts[r][...] = dot3(wh[at, :], wl[at, :], a, b, NT)
    add = lambda v: jnp.sum(v, axis=0, keepdims=True)
    sums[...] = jnp.concatenate(
        [add(total), add(normed * hat[...]), add(normed), add(grad_out[...]), jnp.zeros((4, D), f32)],
        axis=0,
    )


def proj_grad_kernel(scal, heads_h, heads_l, mixed_grad, *refs):
    outs, whole = refs[:-1], refs[-1]
    mine = scal[0]
    gh, gl = halves(mixed_grad[...])
    whole[...] = dot3(heads_h[...], heads_l[...], gh, gl, NN)
    for r in range(SEQ):
        at = jnp.bitwise_xor(mine, r)
        for d in range(GROUPS):
            outs[r][d * SUB : (d + 1) * SUB, :] = whole[
                pl.ds(pl.multiple_of(d * ROWS + at * SUB, 8), SUB), :
            ]


def back_kernel(scal, *refs):
    grads, refs = refs[:4], refs[4:]
    kcat, qturn, vcat, qpair, kturn, outs_turn, lse, low_row = refs[:8]
    joined_h, joined_l, joined_sums = refs[8:11]
    gturn, gpair, dots, key_sum, value_sum, query_turn = refs[11:]
    mine = scal[0]

    for r in range(SEQ):
        at = rows_at(jnp.bitwise_xor(mine, r), CH)
        turned = grads[r][...]
        grad = jnp.concatenate([turned, jnp.zeros((HEAD, CH), f32)], axis=0).T
        pairs = lane_pairs(grad[:, :128], grad[:, 128:])
        for h in range(OWN):
            gpair[h, at, :] = pairs[h]
            part = turned[HEAD * h : HEAD * (h + 1)]
            dots[h, :, at] = jnp.broadcast_to(
                jnp.sum(part * outs_turn[HEAD * h : HEAD * (h + 1), at], axis=0, keepdims=True), (8, CH)
            )
            a, b = halves(part)
            gturn[h, :, at] = jnp.concatenate([a, a, b, b], axis=0)

    key_sum[...] = jnp.zeros_like(key_sum)
    value_sum[...] = jnp.zeros_like(value_sum)

    def one_head(h, carry):
        for c in range(SEQ):
            size = CH * (c + 1)
            lanes = slice(c * CH, (c + 1) * CH)
            score = dot(kcat[h, :size, :], qturn[h, :, lanes], NN)
            weight = jnp.where(allowed(low_row, c, size), jnp.exp(score - lse[h, :1, lanes]), 0.0)
            back = dot(vcat[h, :size, :], gturn[h, :, lanes], NN)
            score_back = weight * (back - dots[h, :1, lanes])
            a, b = halves(weight)
            pair = gpair[h, lanes, :]
            value_sum[h, :size, :] += dot(a, pair, NN) + dot(b, pair, NN)
            a, b = halves(score_back)
            pair = qpair[h, lanes, :]
            key_sum[h, :size, :] += dot(a, pair, NN) + dot(b, pair, NN)
            turned = dot(kturn[h, :, :size], a, NN) + dot(kturn[h, :, :size], b, NN)
            query_turn[h, :, lanes] = (turned[:HEAD] + turned[HEAD:]) * HEAD ** (-0.5)
        return carry

    lax.fori_loop(0, OWN, one_head, 0)

    column_sums = jnp.zeros((1, D), f32)
    low = low_lanes((CH, 128))
    for c in range(SEQ):
        at = slice(c * CH, (c + 1) * CH)
        blank = jnp.zeros((HEAD, CH), f32)
        query = jnp.concatenate([query_turn[h, :, at] for h in range(OWN)] + [blank], axis=0).T
        done = [query]
        for kept in (key_sum, value_sum):
            full = [kept[h, at, :] for h in range(OWN)]
            full = [v + pltpu.roll(v, HEAD, 1) for v in full]
            done.append(jnp.where(low, full[0], full[1]))
            done.append(jnp.where(low, full[2], 0.0))
        joined = jnp.concatenate(done, axis=1)
        column_sums = column_sums + jnp.sum(joined, axis=0, keepdims=True)
        joined_h[at, :], joined_l[at, :] = halves(joined)

    joined_sums[...] = jnp.broadcast_to(column_sums, (8, D))


def qkv_grad_kernel(scal, xh, xl, joined_h, joined_l, joined_sums, wh, wl, vec, *refs):
    proj_one, proj_two, vector_sums, bias_sum = refs[:4]
    outs, (whole, rows) = refs[4 : 4 + GROUPS], refs[4 + GROUPS :]
    mine = scal[0]
    column_sums = joined_sums[:1, :]
    core = dot3(xh[...], xl[...], joined_h[...], joined_l[...], TN)
    gain, shift = piece(vec, 0), piece(vec, 1)
    as_column = lambda v: jnp.broadcast_to(v, (128, D)).T[:, :1]
    whole[...] = as_column(gain) * core + as_column(shift) * column_sums
    weights = wh[...].astype(f32) + wl[...].astype(f32)
    gain_grad = jnp.sum(weights * core, axis=1, keepdims=True)
    shift_grad = jnp.sum(weights * column_sums, axis=1, keepdims=True)
    lane = lax.broadcasted_iota(jnp.int32, (D, 128), 1)
    norm_grads = jnp.where(lane == 0, gain_grad, shift_grad).T

    def place(part, scale):
        wide = jnp.concatenate([part[:, :QUARTER], jnp.zeros((1, D - QUARTER), f32)], axis=1)
        wide = jnp.broadcast_to(wide, (8, D))
        return pltpu.roll(wide, mine * QUARTER, 1)[:1]

    entries = [
        norm_grads[0:1],
        norm_grads[1:2],
        place(column_sums[:, :CH], 1.0),
        place(column_sums[:, 2 * CH :], 1.0),
        vector_sums[0:1],
        vector_sums[1:2],
        vector_sums[2:3],
        vector_sums[3:4],
    ]
    lines = [e[:, i * HALF_VEC : (i + 1) * HALF_VEC] for e in entries for i in range(2)]
    bias = jnp.concatenate(
        [bias_sum[:1, d * ROWS : (d + 1) * ROWS] for d in range(GROUPS)], axis=0
    )
    bias = jnp.concatenate([bias, jnp.zeros((GROUPS, HALF_VEC - ROWS), f32)], axis=1)
    bias = pltpu.roll(bias, mine * ROWS, 1)
    lines = lines + [bias[d : d + 1] for d in range(GROUPS)]
    filler = jnp.zeros((5, HALF_VEC), f32)
    for d in range(GROUPS):
        rows[d] = jnp.concatenate(lines[3 * d : 3 * d + 3] + [filler], axis=0)

    for k in range(GROUPS):
        at = owner(scal, k)
        outs[k][:ROWS, :] = whole[rows_at(at, ROWS), :]
        here = pl.ds(pl.multiple_of(at * SUB, 8), SUB)
        proj = proj_one[here, :] + proj_two[here, :]
        for group in range(SEQ):
            for part in range(3):
                lane_at = HEAD * (3 * group + part)
                outs[k][
                    group * SUB : (group + 1) * SUB, part * CH + QUARTER : (part + 1) * CH
                ] = proj[:, lane_at : lane_at + HEAD]
        outs[k][ROWS:, :HALF_VEC] = rows[at]
        outs[k][ROWS:, HALF_VEC:] = jnp.zeros((8, HALF_VEC), f32)


def pre_back_kernel(scal, joined_h, joined_l, wh, wl, *parts):
    mine = scal[0]
    for r in (1, 3, 2, 0):
        at = rows_at(jnp.bitwise_xor(mine, r), CH)
        parts[r][...] = dot3(joined_h[at, :], joined_l[at, :], wh[...], wl[...], NT)


def input_grad_kernel(scal, tokens, one, two, three, vec, mixed_grad, result):
    hat, scale = norm_stats(tokens[...])
    grad = one[...] + two[...] + three[...]
    result[...] = mixed_grad[...] + norm_back(hat, scale, piece(vec, 0), grad)


def total_square(value):
    return jnp.sum(jnp.sum(value * value, axis=0, keepdims=True), axis=1, keepdims=True)


def shard_sums_kernel(scal, first, in_shard, out_shard, small):
    total = total_square(first[:ROWS, :]) + total_square(in_shard[...]) + total_square(out_shard[...])
    small[...] = first[ROWS:, :]
    small[7:8, :] = jnp.broadcast_to(total, (1, D))


def shard_squares_kernel(scal, one, two, three, four, squares):
    whole = (one[...] + two[...]) + (three[...] + four[...])
    squares[...] = jnp.broadcast_to(whole[7:8, :1] + total_square(whole[:3, :HALF_VEC]), (8, 128))


def stage_kernel(scal, *refs):
    sources, targets, sems = refs[:15], refs[15:30], refs[30]
    copies = [
        pltpu.make_async_copy(source, target, sems.at[i])
        for i, (source, target) in enumerate(zip(sources, targets))
    ]
    for copy in copies:
        copy.start()
    for copy in copies:
        copy.wait()


def adamw_kernel(scal, squares, *refs):
    firsts, ins, outs, refs = refs[:4], refs[4:8], refs[8:12], refs[12:]
    states, clip, finals, news = refs[:15], refs[15], refs[16:31], refs[31:46]
    first, second, sems = refs[46:]
    send = lambda number: [
        pltpu.make_async_copy(news[i], finals[i], sems.at[i]) for i in range(3 * number, 3 * number + 3)
    ]
    mine = scal[0]
    norm = jnp.sqrt(squares[...])
    clip[...] = norm
    factor = (clip_limit / jnp.maximum(norm, clip_limit))[:1, :1]
    for r in range(SEQ):
        at = jnp.bitwise_xor(mine, r)
        first[at] = firsts[r][:ROWS, :]
        second[at, :ROWS] = ins[r][...]
        second[at, ROWS:] = outs[r][...]

    def update(number, spot, grad, rate, decay):
        held = [states[3 * number + i][spot] for i in range(3)]
        fresh = adamw_update(*held, factor * grad, rate, decay)
        for i in range(3):
            news[3 * number + i][spot] = fresh[i]

    def finish(number):
        for copy in send(number):
            copy.start()

    every = slice(None)
    for j in range(SEQ):
        update(
            4, (slice(j * ROWS, (j + 1) * ROWS), every), second[j][ROWS:, :], matrix_rate, weight_decay
        )
    finish(4)
    for d in range(GROUPS):
        grad = jnp.concatenate(
            [second[j][:ROWS, d * ROWS : (d + 1) * ROWS] for j in range(SEQ)], axis=1
        )
        update(3, (every, slice(d * HALF_VEC, (d + 1) * HALF_VEC)), grad, matrix_rate, weight_decay)
    finish(3)
    for part in range(3):
        grad = jnp.concatenate(
            [first[j][:, part * CH : part * CH + QUARTER] for j in range(SEQ)], axis=1
        )
        update(1, (every, slice(part * D, (part + 1) * D)), grad, matrix_rate, weight_decay)
    finish(1)
    for j in range(SEQ):
        grad = jnp.concatenate(
            [
                first[j][group * SUB : (group + 1) * SUB, part * CH + QUARTER : (part + 1) * CH]
                for group in range(SEQ)
                for part in range(3)
            ],
            axis=1,
        )
        update(2, (slice(j * SUB, (j + 1) * SUB), every), grad, matrix_rate, weight_decay)
    finish(2)
    lines = [firsts[r][ROWS:, :HALF_VEC] for r in range(SEQ)]
    line = (lines[0] + lines[1]) + (lines[2] + lines[3])
    for i in range(3):
        for j in range(3):
            spot = (slice(3 * i + j, 3 * i + j + 1), slice(None))
            update(0, spot, line[i : i + 1, 128 * j : 128 * (j + 1)], vector_rate, 0.0)
    finish(0)
    for number in range(5):
        for copy in send(number):
            copy.wait()


def adamw_update(weight, first, second, grad, rate, decay):
    new_first = beta_one * first + (1.0 - beta_one) * grad
    new_second = beta_two * second + (1.0 - beta_two) * grad * grad
    first_hat = new_first / (1.0 - beta_one**STEP)
    second_hat = new_second / (1.0 - beta_two**STEP)
    new_weight = weight - rate * (first_hat / (jnp.sqrt(second_hat) + adam_eps) + decay * weight)
    return (new_first, new_second, new_weight)


def ring_tables(count):
    evens = [2 * i for i in range(count // 2)]
    order = evens + [i + 1 for i in reversed(evens)]
    place = [0] * count
    for position, device in enumerate(order):
        place[device] = position
    right = [(order[i], order[(i + 1) % count]) for i in range(count)]
    left = [(b, a) for a, b in right]
    return order, place, right, left


class RingGather:
    def __init__(self, block, name, flip=False):
        _, _, self.right, self.left = ring_tables(GROUPS)
        if flip:
            self.right, self.left = self.left, self.right
        self.got, self.name, self.at, self.flip = {0: block}, name, 0, flip

    def step(self, after=()):
        places = (-self.at % GROUPS, self.at)
        if after:
            for place in set(places):
                self.got[place] = gate(self.got[place], after)
        forth, back = (self.got[place] for place in places)
        self.at += 1
        self.got[GROUPS - self.at] = move(forth, "dp", self.right, f"{self.name}_right_{self.at}")
        if self.at < HALF:
            self.got[self.at] = move(back, "dp", self.left, f"{self.name}_left_{self.at}")
        return [self.got[GROUPS - self.at]] + ([self.got[self.at]] if self.at < HALF else [])

    def blocks(self):
        return [self.got[-k % GROUPS if self.flip else k] for k in range(GROUPS)]


class RingScatter:
    def __init__(self, blocks, name, flip=False):
        _, _, self.right, self.left = ring_tables(GROUPS)
        self.blocks = blocks
        if flip:
            self.right, self.left = self.left, self.right
            self.blocks = [blocks[-k % GROUPS] for k in range(GROUPS)]
        self.name, self.back, self.at = name, None, HALF
        self.forth = move(self.blocks[HALF], "dp", self.right, f"{name}_right_1")

    def step(self, after=()):
        self.at -= 1
        ahead, back = self.blocks[self.at], self.blocks[GROUPS - self.at]
        if self.back is None:
            forth = plus(self.forth, ahead, after=after)
        else:
            forth, back = sums([(self.forth, ahead), (self.back, back)], after)
        number = HALF + 1 - self.at
        self.forth = move(forth, "dp", self.right, f"{self.name}_right_{number}")
        self.back = move(back, "dp", self.left, f"{self.name}_left_{number}")
        return [forth, back]

    def result(self, after=()):
        return plus(self.forth, self.back, self.blocks[0], after=after)


def move(block, axis, pairs, name):
    with jax.named_scope(name):
        return lax.ppermute(block, axis, pairs)


def swap(block, bits, name):
    return move(block, "seq", [(i, i ^ bits) for i in range(SEQ)], f"{name}_{bits}")


def gather_seq(block, name):
    across = swap(block, 2, name)
    core = swap(block, 1, name)
    return [block, core, across, swap(across, 1, f"{name}_2")]


def exchange_seq(parts, name):
    return [parts[0]] + [swap(parts[r], r, name) for r in range(1, SEQ)]


def scatter_core(parts, name):
    return parts[0], swap(parts[1], 1, f"{name}_own"), parts[2], swap(parts[3], 1, f"{name}_across")


def ordered(blocks, mine):
    stack = jnp.stack(blocks, axis=0)
    return [lax.dynamic_index_in_dim(stack, mine ^ j, 0, keepdims=False) for j in range(len(blocks))]


def local(
    tokens,
    cotangent,
    segment_ids,
    valid,
    vectors,
    vec_first,
    vec_second,
    w_qkv,
    qkv_first,
    qkv_second,
    w_proj,
    proj_first,
    proj_second,
    w_in,
    in_first,
    in_second,
    w_out,
    out_first,
    out_second,
):
    dp_parts = lax.axis_size("dp")
    ring = dp_parts == GROUPS
    mine = lax.axis_index("seq")
    home = lax.axis_index("dp")
    rows = w_qkv.shape[0]
    units = w_out.shape[0] // SEQ
    far, near = home // 2, home % 2
    position = jnp.where(near > 0, GROUPS - 1 - far, far)
    scal = jnp.stack([mine, position, jnp.full_like(mine, 1 if ring else 0)]).astype(jnp.int32)
    flat_in = tokens.reshape(CH, D)
    chunk, tall, square = shape(CH, D), shape(LEN, D, kind=bf16), shape(D, D, kind=bf16)

    if ring:
        first, packed = run(
            pack_first_kernel,
            scal,
            [w_qkv, w_proj, vectors.reshape(9, 128), segment_ids, valid, flat_in],
            [shape(ROWS + 8, D), shape(CH + 8, D)],
            scratch=[
                pltpu.VMEM((3, ROWS, CH), f32),
                pltpu.VMEM((SUB, D), f32),
                pltpu.VMEM((9, 128), f32),
                pltpu.VMEM((2, 1, CH), jnp.int32),
            ],
            sems=8,
            far_args=range(6),
            room=54,
            name="pack_first", work=3.0,
        )
        ring_first = RingGather(first, "first")
        for _ in range(HALF):
            ring_first.step()
        firsts = ring_first.blocks()
        in_block, out_block = run(
            pack_second_kernel,
            scal,
            [w_in, w_out],
            [shape(ROWS, D)] * 2,
            name="pack_second", work=3.0,
            after=[firsts[GROUPS - 1]],
        )
        ring_in = RingGather(in_block, "w_in")
        ring_out = RingGather(out_block, "w_out", flip=True)
        came = ring_in.step([firsts[HALF]])
        came = came + ring_out.step([firsts[HALF]])
    else:
        padded = jnp.pad(w_qkv, ((0, 0), (0, CH)))
        own = lambda part: lax.dynamic_slice_in_dim(padded, part * D + mine * QUARTER, CH, 1)
        first = jnp.concatenate([own(0), own(1), own(2)], axis=1)
        first = lax.all_gather(first, "dp", axis=0, tiled=True).reshape(GROUPS, ROWS, D)
        all_vec = lax.all_gather(vectors, "dp", axis=0, tiled=True).reshape(GROUPS, 3, HALF_VEC)
        first = jnp.concatenate([first, jnp.pad(all_vec, ((0, 0), (0, 5), (0, D - HALF_VEC)))], axis=1)
        firsts = [first[k] for k in range(GROUPS)]
        in_part = lax.dynamic_index_in_dim(
            w_in.reshape(rows, dp_parts, SEQ, units), mine, 2, keepdims=False
        ).reshape(rows, D)
        out_part = lax.dynamic_slice_in_dim(w_out, mine * units, units, 0)
        in_blocks, out_blocks = (
            list(lax.all_gather(part, "dp", axis=0, tiled=True).reshape(GROUPS, ROWS, D))
            for part in (in_part, out_part)
        )
        marks = jnp.where(valid > 0, segment_ids, -1).astype(f32)
        packed = jnp.concatenate([flat_in, jnp.pad(marks, ((0, 7), (0, D - CH)))], axis=0)
    toks = gather_seq(packed, "tokens")
    (grad_out,) = run(
        mask_kernel, scal, [cotangent.reshape(CH, D), valid], [chunk], name="mask", work=2.0, after=[toks[2]]
    )
    grads_row = gather_seq(grad_out, "cotangent")

    qkv_h, qkv_l, vec, proj = run(
        weights_kernel,
        scal,
        firsts,
        [square, square, shape(GROUPS, 8, HALF_VEC), shape(GROUPS * SUB, D)],
        name="weights", work=3.0,
    )
    if ring:
        proj_parts = gather_seq(proj, "w_proj")
    else:
        full = lax.all_gather(w_proj, "dp", axis=0, tiled=True).reshape(GROUPS, SEQ, SUB, D)
        proj_parts = [
            lax.dynamic_index_in_dim(full, mine ^ r, 1, keepdims=False).reshape(GROUPS * SUB, D)
            for r in range(SEQ)
        ]
    hat_h, hat_l, kcat, qturn, vcat, qpair, kturn, low_row, heads, lse = run(
        front_kernel,
        scal,
        toks + [qkv_h, qkv_l, vec],
        [
            tall,
            tall,
            shape(OWN, LEN, 256, kind=bf16),
            shape(OWN, 256, LEN, kind=bf16),
            shape(OWN, LEN, 256, kind=bf16),
            shape(OWN, LEN, 128, kind=bf16),
            shape(OWN, 128, LEN, kind=bf16),
            shape(8, LEN),
            shape(QUARTER, LEN),
            shape(OWN, 8, LEN),
        ],
        scratch=[pltpu.VMEM((OWN, 128, LEN), bf16), pltpu.VMEM((SEQ, 8, CH), f32)],
        name="front", work=14.0,
        after=[grads_row[2]],
    )
    if ring:
        heads = gate(heads, [proj_parts[2], *came])
        ring_in.step([lse])
        came = ring_in.step()
        came = came + ring_in.step()
        ring_out.step(came)
        in_blocks = ring_in.blocks()
    across = swap(heads, 2, "heads")
    if ring:
        across = gate(across, came)
    all_heads = [heads, swap(heads, 1, "heads"), across, swap(across, 1, "heads_2")]
    wide = shape(D, CH, kind=bf16)
    split = shape(SEQ, CH, D, kind=bf16)
    proj_h, proj_l, heads_h, heads_l, norm_h, norm_l, mixed, hat_two, scale_two = run(
        proj_kernel,
        scal,
        toks + all_heads + proj_parts + [vec],
        [square, square, wide, wide, split, split, chunk, chunk, shape(CH, 128)],
        scratch=[pltpu.VMEM((D, D), f32), pltpu.VMEM((D, LEN), f32)],
        name="proj", work=8.0,
    )

    if ring:
        ring_out.step([norm_h])
        ring_out.step()
        out_blocks = ring_out.blocks()
    block = shape(ROWS, D)
    acts_h, acts_l, slope, in_wh, in_wl = run(
        hidden_kernel,
        scal,
        [norm_h, norm_l] + in_blocks + [vec],
        [tall, tall, shape(LEN, D), square, square],
        name="hidden", work=8.0,
    )
    done = run(
        out_grad_kernel,
        scal,
        [acts_h, acts_l] + grads_row,
        [tall, tall] + [block] * GROUPS,
        scratch=[pltpu.VMEM((D, D), f32)],
        name="out_grad", work=5.0,
    )
    out_h, out_l = done[:2]
    out_grads = list(done[2:])
    if ring:
        ring_out = RingScatter(out_grads, "out_grad")
    done = run(
        hidden_back_kernel,
        scal,
        [out_h, out_l, slope, in_wh, in_wl] + out_blocks,
        [tall, tall, square, square, shape(8, D)] + [chunk] * SEQ,
        name="hidden_back", work=11.0,
        after=out_grads[:1],
    )
    hid_h, hid_l, out_wh, out_wl, bias_sum = done[:5]
    parts = list(done[5:])
    if ring:
        parts[3] = gate(parts[3], ring_out.step([bias_sum]))
    norm_own, norm_near, norm_across, norm_far = scatter_core(parts, "norm_grad")
    norm_pair = plus(norm_across, norm_far)
    norm_last = swap(norm_pair, 2, "norm_grad")
    in_grads = list(
        run(
            in_grad_kernel,
            scal,
            [norm_h, norm_l, hid_h, hid_l],
            [block] * GROUPS,
            scratch=[pltpu.VMEM((D, D), f32)],
            name="in_grad", work=5.0,
            after=[norm_pair],
        )
    )
    if ring:
        ring_in = RingScatter(in_grads, "in_grad", flip=True)
        out_sent = ring_out.step()
        in_sent = ring_in.step()
    done = run(
        proj_back_kernel,
        scal,
        [norm_own, norm_near, norm_last, hat_two, scale_two, vec, grad_out, proj_h, proj_l],
        [chunk, shape(8, D)] + [shape(QUARTER, CH)] * SEQ,
        name="proj_back", work=5.0,
        after=out_sent + in_sent if ring else [],
    )
    mixed_grad, vector_sums = done[:2]
    head_grads = exchange_seq(list(done[2:]), "head_grad")
    if ring:
        out_sent = ring_out.step([mixed_grad])
        in_sent = ring_in.step([mixed_grad])
    out_parts = run(
        ffn_out_kernel,
        scal,
        [acts_h, acts_l, out_wh, out_wl],
        [chunk] * SEQ,
        name="ffn_out", work=7.0,
        after=[mixed_grad],
    )
    proj_grads = run(
        proj_grad_kernel,
        scal,
        [heads_h, heads_l, mixed_grad],
        [shape(GROUPS * SUB, D)] * SEQ,
        scratch=[pltpu.VMEM((D, D), f32)],
        name="proj_grad", work=4.0,
        after=[*head_grads[1:], *out_sent, *in_sent, out_parts[0]] if ring else [],
    )
    wait = [head_grads[3], head_grads[2]]
    out_own, out_near, out_across, out_far = scatter_core(out_parts, "output")
    if ring:
        proj_own, proj_near, proj_across, proj_far = scatter_core(proj_grads, "proj_grad")
        proj_pair, proj_base, out_pair = sums(
            [(proj_across, proj_far), (proj_own, proj_near), (out_across, out_far)], wait
        )
        proj_last = swap(proj_pair, 2, "proj_grad")
    else:
        proj_base = proj_last = proj_grads[0]
        out_pair = plus(out_across, out_far)
    joined_h, joined_l, joined_sums = run(
        back_kernel,
        scal,
        head_grads + [kcat, qturn, vcat, qpair, kturn, heads, lse, low_row],
        [tall, tall, shape(8, D)],
        scratch=[
            pltpu.VMEM((OWN, 256, LEN), bf16),
            pltpu.VMEM((OWN, LEN, 128), bf16),
            pltpu.VMEM((OWN, 8, LEN), f32),
            pltpu.VMEM((OWN, LEN, 128), f32),
            pltpu.VMEM((OWN, LEN, 128), f32),
            pltpu.VMEM((OWN, HEAD, LEN), f32),
        ],
        name="back", work=16.0,
        after=[proj_grads[0]],
    )
    out_last = swap(gate(out_pair, [joined_sums]), 2, "output")
    if ring:
        shard_out = ring_out.result([joined_sums])
        in_sent = ring_in.step([joined_sums])
    done = run(
        qkv_grad_kernel,
        scal,
        [hat_h, hat_l, joined_h, joined_l, joined_sums, qkv_h, qkv_l, vec]
        + [proj_base, proj_last, vector_sums, bias_sum],
        [shape(ROWS + 8, D)] * GROUPS,
        scratch=[pltpu.VMEM((D, D), f32), pltpu.VMEM((GROUPS, 8, HALF_VEC), f32)],
        name="qkv_grad", work=1.0,
        after=[*in_sent, shard_out] if ring else [],
    )
    first_grads = list(done)
    if ring:
        shard_in = ring_in.result([first_grads[0]])
        out_all = gather_seq(shard_out, "out_shard")
        in_all = gather_seq(shard_in, "in_shard")
        first_grads[HALF] = gate(first_grads[HALF], [shard_in])
        ring_first = RingScatter(first_grads, "first_grad")
        first_sent = ring_first.step([out_last])
    pre_parts = run(
        pre_back_kernel,
        scal,
        [joined_h, joined_l, qkv_h, qkv_l],
        [chunk] * SEQ,
        name="pre_back", work=1.0,
        after=[shard_in, *first_sent] if ring else [],
    )
    pre_parts = list(pre_parts)
    if ring:
        first_sent = ring_first.step()
        pre_parts[3] = gate(pre_parts[3], [*first_sent, out_all[2]])
    (output,) = run(
        output_kernel, scal, [mixed, out_own, out_near, out_last, vec], [chunk], name="output", work=2.0
    )
    pre_own, pre_near, pre_across, pre_far = scatter_core(pre_parts, "pre_grad")
    pre_pair = plus(pre_across, pre_far, after=[in_all[2]] if ring else [])
    pre_last = swap(pre_pair, 2, "pre_grad")
    states = [vectors, vec_first, vec_second, w_qkv, qkv_first, qkv_second, w_proj, proj_first, proj_second]
    states = states + [w_in, in_first, in_second, w_out, out_first, out_second]
    if ring:
        held = [v.reshape(9, 128) for v in states[:3]] + states[3:]
        held = run(
            stage_kernel,
            scal,
            held,
            [shape(*v.shape) for v in held],
            sems=15,
            far_args=range(15),
            name="stage", work=4.0,
            after=[pre_parts[0], output],
        )
        ring_first.step([held[3]])
        shard_first = ring_first.result()
    (input_grad,) = run(
        input_grad_kernel,
        scal,
        [flat_in, pre_own, pre_near, pre_last, vec, mixed_grad],
        [chunk],
        name="input_grad", work=3.0,
    )

    if ring:
        (small,) = run(
            shard_sums_kernel, scal, [shard_first, shard_in, shard_out], [shape(8, D)], name="shard_sums", work=1.0
        )
        shard_first = gate(shard_first, [pre_last])
        across = swap(shard_first, 2, "first_shard")
        core = swap(shard_first, 1, "first_shard")
        (squares,) = run(
            shard_squares_kernel,
            scal,
            [small] + [swap(small, bits, "small") for bits in (1, 2, 3)],
            [shape(8, 128)],
            name="shard_squares", work=1.0,
        )
        flipped = lambda bits: [(i, i ^ bits) for i in range(GROUPS)]
        one, two, three = (move(squares, "dp", flipped(bits), "squares") for bits in (1, 2, 3))
        squares = sum_pairs(squares, one, two, three)
        across = gate(across, [input_grad, squares])
        first_all = [shard_first, core, across, swap(across, 1, "first_shard_2")]
        squares = plus(squares, move(squares, "dp", flipped(4), "squares"))
        done = run(
            adamw_kernel,
            scal,
            [squares] + first_all + in_all + out_all + list(held),
            [shape(8, 128)] + [shape(*v.shape) for v in held],
            scratch=[pltpu.VMEM(v.shape, f32) for v in held]
            + [pltpu.VMEM((SEQ, ROWS, D), f32), pltpu.VMEM((SEQ, 2 * ROWS, D), f32)],
            sems=15,
            far_outs=range(1, 16),
            name="adamw", work=0.1,
        )
        new = [v.reshape(-1) for v in done[1:4]] + list(done[4:])
        clip_norm = done[0][0, 0]
    else:
        by_group = jnp.stack(first_grads)
        shard_first = lax.psum_scatter(
            by_group[:, :ROWS].reshape(D, D), "dp", scatter_dimension=0, tiled=True
        )
        proj_full = jnp.stack([p.reshape(GROUPS, SUB, D) for p in ordered(proj_grads, mine)], axis=1)
        proj_grad = lax.psum(
            lax.psum_scatter(proj_full.reshape(D, D), "dp", scatter_dimension=0, tiled=True), "seq"
        )
        all_vec = lax.psum(by_group[:, ROWS : ROWS + 3, :HALF_VEC], ("dp", "seq")).reshape(-1)
        vec_grad = lax.dynamic_slice_in_dim(all_vec, home * vectors.shape[0], vectors.shape[0])
        joined = lax.all_gather(shard_first, "seq", axis=0, tiled=False)
        qkv_grad = jnp.concatenate(
            [joined[j, :, i * CH : i * CH + QUARTER] for i in range(3) for j in range(SEQ)], axis=1
        )
        shard_in, shard_out = (
            lax.psum_scatter(jnp.concatenate(parts, axis=0), "dp", scatter_dimension=0, tiled=True)
            for parts in (in_grads, out_grads)
        )
        in_all = lax.all_gather(shard_in, "seq", axis=0, tiled=False)
        in_grad = in_all.reshape(SEQ, rows, dp_parts, units).transpose(1, 2, 0, 3).reshape(rows, -1)
        out_grad = lax.all_gather(shard_out, "seq", axis=0, tiled=True)
        total = sum(jnp.sum(g * g) for g in (qkv_grad, proj_grad, in_grad, out_grad, vec_grad))
        total = lax.psum(total, "dp")
        clip_norm = jnp.sqrt(total)
        factor = clip_limit / jnp.maximum(clip_norm, clip_limit)
        grads = (vec_grad, qkv_grad, proj_grad, in_grad, out_grad)
        new = []
        for number, grad in enumerate(grads):
            rate, decay = (matrix_rate, weight_decay) if number else (vector_rate, 0.0)
            new.extend(adamw_update(*states[3 * number : 3 * number + 3], factor * grad, rate, decay))
    return (output.reshape(tokens.shape), input_grad.reshape(tokens.shape), clip_norm, *new)


def solution(mesh):
    row = P("dp", "seq", None)
    mark = P("dp", "seq")
    vec = P("dp")
    mat = P("dp", None)
    return jax.shard_map(
        local,
        mesh=mesh,
        in_specs=(row, row, mark, mark) + (vec,) * 3 + (mat,) * 12,
        out_specs=(row, row, P()) + (vec,) * 3 + (mat,) * 12,
        check_vma=False,
    )
```

```python
import functools
import math

import jax
import jax.numpy as jnp
from jax import lax
from jax.experimental import pallas as pl
from jax.experimental.pallas import tpu as pltpu
from jax.sharding import PartitionSpec as P

D = 768
HEADS = 12
HEAD = 64
STEP = 10
CH = 256
LEN = 1024
SEQ = 4
QUARTER = D // SEQ
OWN = HEADS // SEQ
GROUPS = 8
ROWS = D // GROUPS
SUB = ROWS // SEQ
HALF = GROUPS // 2
HALF_VEC = D // 2
VEC_ROWS = 24

f32 = jnp.float32
bf16 = jnp.bfloat16
masked_score = -1e30
norm_eps = 1e-05
clip_limit = 1.0
beta_one = 0.9
beta_two = 0.999
adam_eps = 1e-08
matrix_rate = 0.02
vector_rate = 0.4
weight_decay = 0.01
gelu_scale = 0.7978845608028654
gelu_cubic = 0.044715

COST = 1e9

WHOLE = pl.BlockSpec(memory_space=pltpu.VMEM)
SCALARS = pl.BlockSpec(memory_space=pltpu.SMEM)
NN = ((1,), (0,))
NT = ((1,), (1,))
TN = ((0,), (0,))


def shape(*dims, kind=f32):
    return jax.ShapeDtypeStruct(dims, kind)


def run(
    kernel, scal, args, outs, scratch=(), sems=0, far_args=(), far_outs=(), room=8, work=1.0, name=None, after=()
):
    args, after = list(args), list(after)
    held = sum(math.prod(v.shape) * jnp.dtype(v.dtype).itemsize for v in scratch)
    anywhere, far = pl.BlockSpec(memory_space=pl.ANY), pl.BlockSpec(memory_space=pltpu.HBM)
    scratch = list(scratch) + ([pltpu.SemaphoreType.DMA((sems,))] if sems else [])

    def body(scal_ref, *refs):
        kernel(scal_ref, *refs[: len(args)], *refs[len(args) + len(after) :])

    return pl.pallas_call(
        body,
        out_shape=tuple(outs),
        in_specs=[SCALARS]
        + [far if i in far_args else WHOLE for i in range(len(args))]
        + [anywhere] * len(after),
        out_specs=tuple(far if i in far_outs else WHOLE for i in range(len(outs))),
        scratch_shapes=scratch,
        compiler_params=pltpu.CompilerParams(vmem_limit_bytes=held + (room << 20)),
        cost_estimate=pl.CostEstimate(
            flops=int(work * COST), bytes_accessed=1, transcendentals=0
        ),
        name=name,
    )(scal, *args, *after)


def gate(value, after):
    anywhere = pl.BlockSpec(memory_space=pl.ANY)
    return pl.pallas_call(
        lambda *refs: None,
        out_shape=shape(*value.shape, kind=value.dtype),
        in_specs=[anywhere] * (1 + len(after)),
        out_specs=anywhere,
        input_output_aliases={0: 0},
        compiler_params=pltpu.CompilerParams(vmem_limit_bytes=1 << 20),
        name="gate",
    )(value, *after)


def sums(groups, after=()):
    sizes = [len(group) for group in groups]

    def body(*refs):
        at = 0
        for number, size in enumerate(sizes):
            total = refs[at][...]
            for ref in refs[at + 1 : at + size]:
                total = total + ref[...]
            refs[sum(sizes) + len(after) + number][...] = total
            at += size

    return pl.pallas_call(
        body,
        out_shape=tuple(shape(*group[0].shape) for group in groups),
        in_specs=[WHOLE] * sum(sizes) + [pl.BlockSpec(memory_space=pl.ANY)] * len(after),
        out_specs=tuple([WHOLE] * len(groups)),
        compiler_params=pltpu.CompilerParams(vmem_limit_bytes=4 << 20),
        cost_estimate=pl.CostEstimate(flops=int(COST), bytes_accessed=1, transcendentals=0),
        name="plus",
    )(*(term for group in groups for term in group), *after)


def plus(*terms, after=()):
    return sums([terms], after)[0]


def sum_pairs(one, two, three, four):
    def body(a, b, c, d, result):
        result[...] = (a[...] + b[...]) + (c[...] + d[...])

    return pl.pallas_call(
        body,
        out_shape=shape(*one.shape),
        in_specs=[WHOLE] * 4,
        out_specs=WHOLE,
        compiler_params=pltpu.CompilerParams(vmem_limit_bytes=1 << 20),
        name="sum_pairs",
    )(one, two, three, four)


def owner(scal, k):
    spot = jnp.bitwise_and(scal[1] + k, GROUPS - 1)
    return jnp.where(scal[2] > 0, jnp.where(spot < HALF, 2 * spot, 2 * GROUPS - 1 - 2 * spot), k)


def halves(value):
    top = value.astype(bf16)
    return top, (value - top.astype(f32)).astype(bf16)


def dot(left, right, dims):
    return lax.dot_general(left, right, (dims, ((), ())), preferred_element_type=f32)


def dot3(lh, ll, rh, rl, dims):
    (left,), (right,) = dims
    join = lambda parts, axis: jnp.concatenate([part[...] for part in parts], axis=axis)
    return dot(join([lh, lh, ll], left), join([rh, rl, rh], right), dims)


def rows_at(index, size):
    return pl.ds(pl.multiple_of(index * size, size), size)


def piece(vec, number):
    a, b = 2 * number, 2 * number + 1
    return jnp.concatenate(
        [vec[a // 3, a % 3 : a % 3 + 1, :], vec[b // 3, b % 3 : b % 3 + 1, :]], axis=1
    )


def norm_stats(inputs):
    center = inputs - jnp.mean(inputs, axis=-1, keepdims=True)
    spread = jnp.mean(center * center, axis=-1, keepdims=True)
    scale = lax.rsqrt(spread + norm_eps)
    return center * scale, scale


def norm_back(hat, scale, gain, grad):
    inner = grad * gain
    return scale * (
        inner
        - jnp.mean(inner, axis=-1, keepdims=True)
        - hat * jnp.mean(inner * hat, axis=-1, keepdims=True)
    )


def low_lanes(dims):
    return lax.broadcasted_iota(jnp.int32, dims, 1) < HEAD


def lane_pairs(pair, last):
    low = low_lanes(pair.shape)
    roll = lambda v: pltpu.roll(v, HEAD, 1)
    ph = pair.astype(bf16).astype(f32)
    pl_ = pair - ph
    lh = last.astype(bf16).astype(f32)
    ll = last - lh
    return [
        jnp.where(low, ph, roll(pl_)).astype(bf16),
        jnp.where(low, roll(ph), pl_).astype(bf16),
        jnp.where(low, lh, roll(ll)).astype(bf16),
    ]


def row_halves(turned, head):
    part = turned[HEAD * head : HEAD * (head + 1)]
    return halves(part)


def pack_first_kernel(scal, wqkv, wproj, vec, seg, valid, tokens, first, packed, *refs):
    bands, proj, lines, marks, sems = refs
    mine = scal[0]
    aligned = pl.multiple_of(jnp.bitwise_and(mine * QUARTER, -128), 128)
    copies = [
        pltpu.make_async_copy(wqkv.at[:, pl.ds(part * D + aligned, CH)], bands.at[part], sems.at[part])
        for part in range(3)
    ]
    sub = pl.ds(pl.multiple_of(mine * SUB, 8), SUB)
    copies.append(pltpu.make_async_copy(wproj.at[sub, :], proj, sems.at[3]))
    copies.append(pltpu.make_async_copy(vec, lines, sems.at[4]))
    copies.append(pltpu.make_async_copy(seg, marks.at[0], sems.at[5]))
    copies.append(pltpu.make_async_copy(valid, marks.at[1], sems.at[6]))
    copies.append(pltpu.make_async_copy(tokens, packed.at[:CH, :], sems.at[7]))
    for copy in copies:
        copy.start()
    first[ROWS:, :] = jnp.zeros((8, D), f32)
    packed[CH:, :] = jnp.zeros((8, D), f32)
    for copy in copies[:5]:
        copy.wait()
    turn = jnp.where(jnp.bitwise_and(mine, 1) > 0, CH - HEAD, 0)
    for part in range(3):
        turned = pltpu.roll(bands[part], turn, 1)
        first[:ROWS, part * CH : part * CH + QUARTER] = turned[:, :QUARTER]
        for group in range(SEQ):
            lane = HEAD * (3 * group + part)
            first[group * SUB : (group + 1) * SUB, part * CH + QUARTER : (part + 1) * CH] = proj[
                :, lane : lane + HEAD
            ]
        first[ROWS + part : ROWS + part + 1, :HALF_VEC] = jnp.concatenate(
            [lines[3 * part + i : 3 * part + i + 1, :] for i in range(3)], axis=1
        )
    for copy in copies[5:]:
        copy.wait()
    packed[CH : CH + 1, :CH] = jnp.where(marks[1] > 0, marks[0], -1).astype(f32)


def pack_second_kernel(scal, win, wout, in_block, out_block):
    mine = scal[0]
    turn = lax.rem(HALF_VEC - mine * ROWS, HALF_VEC)
    for part in range(GROUPS):
        turned = pltpu.roll(win[:, part * HALF_VEC : (part + 1) * HALF_VEC], turn, 1)
        in_block[:, part * ROWS : (part + 1) * ROWS] = turned[:, :ROWS]
    out_block[...] = wout[pl.ds(pl.multiple_of(mine * ROWS, 8), ROWS), :]


def mask_kernel(scal, cotangent, valid, result):
    keep = jnp.where(valid[...] > 0, 1.0, 0.0).astype(f32)
    column = jnp.broadcast_to(keep, (128, CH)).T[:, :1]
    result[...] = cotangent[...] * column


def weights_kernel(scal, *refs):
    blocks, (wh, wl, vec, proj) = refs[:GROUPS], refs[GROUPS:]
    for k in range(GROUPS):
        at = owner(scal, k)
        block = blocks[k][:ROWS, :]
        here = rows_at(at, ROWS)
        wh[here, :], wl[here, :] = halves(block)
        vec[at] = blocks[k][ROWS:, :HALF_VEC]
        for group in range(SEQ):
            for part in range(3):
                lane = HEAD * (3 * group + part)
                proj[pl.ds(pl.multiple_of(at * SUB, 8), SUB), lane : lane + HEAD] = block[
                    group * SUB : (group + 1) * SUB, part * CH + QUARTER : (part + 1) * CH
                ]


def front_kernel(scal, *refs):
    toks, refs = refs[:4], refs[4:]
    wh, wl, vec = refs[:3]
    xh, xl, kcat, qturn, vcat, qpair, kturn, low_row, outs_turn, lse, vturn, label = refs[3:]
    mine = scal[0]

    gain, shift = piece(vec, 0), piece(vec, 1)
    turn = lax.rem(D - mine * QUARTER, D)
    own = lambda number: pltpu.roll(jnp.broadcast_to(piece(vec, number), (8, D)), turn, 1)[:1, :CH]
    query_bias, value_bias = own(2), own(3)

    for r in range(SEQ):
        nat = jnp.bitwise_xor(mine, r)
        at = rows_at(nat, CH)
        label[nat] = toks[r][CH:, :CH]
        hat, _ = norm_stats(toks[r][:CH, :])
        xh[at, :], xl[at, :] = halves(hat)
        nh, nl = halves(hat * gain + shift)
        joined = dot3(nh, nl, wh[...], wl[...], NN)
        query = (joined[:, :CH] + query_bias) * HEAD ** (-0.5)
        key = joined[:, CH : 2 * CH]
        value = joined[:, 2 * CH :] + value_bias
        keys = lane_pairs(key[:, :128], key[:, 128:])
        values = lane_pairs(value[:, :128], value[:, 128:])
        queries = lane_pairs(query[:, :128], query[:, 128:])
        key_t, value_t, query_t = key.T, value.T, query.T
        for h in range(OWN):
            kcat[h, at, :] = jnp.concatenate([keys[h], keys[h]], axis=1)
            vcat[h, at, :] = jnp.concatenate([values[h], values[h]], axis=1)
            qpair[h, at, :] = queries[h]
            a, b = row_halves(query_t, h)
            qturn[h, :, at] = jnp.concatenate([a, a, b, b], axis=0)
            a, b = row_halves(key_t, h)
            kturn[h, :, at] = jnp.concatenate([a, b], axis=0)
            a, b = row_halves(value_t, h)
            vturn[h, :, at] = jnp.concatenate([a, b], axis=0)

    labels = jnp.concatenate([label[c][:1, :] for c in range(SEQ)], axis=1)
    spot = lax.broadcasted_iota(jnp.int32, (1, LEN), 1).astype(f32)
    begin = jnp.zeros((1, LEN), f32)
    for segment in range(3):
        held = jnp.sum(jnp.where(labels == float(segment), 1.0, 0.0), axis=1, keepdims=True)
        begin = begin + jnp.where(labels > float(segment), held, 0.0)
    begin = jnp.where(labels < 0.0, spot, begin)
    low_row[...] = jnp.broadcast_to(begin, (8, LEN))

    def one_head(h, carry):
        for c in range(SEQ):
            size = CH * (c + 1)
            lanes = slice(c * CH, (c + 1) * CH)
            score = dot(kcat[h, :size, :], qturn[h, :, lanes], NN)
            mask = allowed(low_row, c, size)
            score = jnp.where(mask, score, masked_score)
            peak = jnp.max(score, axis=0, keepdims=True)
            weight = jnp.exp(score - peak)
            total = jnp.sum(weight, axis=0, keepdims=True)
            top, rest = halves(weight)
            both = dot(vturn[h, :, :size], top, NN)
            extra = dot(vturn[h, :HEAD, :size], rest, NN)
            result = (both[:HEAD] + both[HEAD:] + extra) / total
            outs_turn[pl.ds(pl.multiple_of(h * HEAD, HEAD), HEAD), lanes] = result
            lse[h, :, lanes] = jnp.broadcast_to(peak + jnp.log(total), (8, CH))
        return carry

    lax.fori_loop(0, OWN, one_head, 0)


def allowed(low_row, c, size):
    key_at = lax.broadcasted_iota(jnp.int32, (size, CH), 0).astype(f32)
    query_at = (lax.broadcasted_iota(jnp.int32, (1, CH), 1) + c * CH).astype(f32)
    begin = low_row[:1, c * CH : (c + 1) * CH]
    return (key_at >= begin) & (key_at <= query_at)


def proj_kernel(scal, *refs):
    toks, heads, parts, refs = refs[:4], refs[4:8], refs[8:12], refs[12:]
    vec, wh, wl, heads_h, heads_l, norm_h, norm_l, mixed, hat, scale, weight, joined = refs
    mine = scal[0]
    for r in range(SEQ):
        at = jnp.bitwise_xor(mine, r)
        for d in range(GROUPS):
            weight[pl.ds(pl.multiple_of(d * ROWS + at * SUB, 8), SUB), :] = parts[r][
                d * SUB : (d + 1) * SUB, :
            ]
        joined[rows_at(at, QUARTER), :] = heads[r][...]
    wh[...], wl[...] = halves(weight[...])
    heads_h[...], heads_l[...] = halves(joined[:, rows_at(mine, CH)])
    gain, shift = piece(vec, 5), piece(vec, 6)
    for r in range(SEQ):
        at = rows_at(jnp.bitwise_xor(mine, r), CH)
        a, b = halves(joined[:, at].T)
        total = toks[r][:CH, :] + dot3(a, b, wh[...], wl[...], NN)
        total = total + piece(vec, 4)
        normed, size = norm_stats(total)
        norm_h[r], norm_l[r] = halves(normed * gain + shift)
        if r == 0:
            mixed[...] = total
            hat[...] = normed
            scale[...] = jnp.broadcast_to(size, (CH, 128))


def hidden_kernel(scal, norm_h, norm_l, *refs):
    blocks, vec, acts_h, acts_l, slope, winh, winl = refs[:GROUPS], *refs[GROUPS:]
    mine = scal[0]
    for k in range(GROUPS):
        at = rows_at(owner(scal, k), ROWS)
        winh[at, :], winl[at, :] = halves(blocks[k][...])
    marks = [16 + d for d in range(GROUPS)]
    table = jnp.concatenate([vec[m // 3, m % 3 : m % 3 + 1, :] for m in marks], axis=0)
    table = pltpu.roll(table, lax.rem(HALF_VEC - mine * ROWS, HALF_VEC), 1)[:, :ROWS]
    bias = jnp.concatenate([table[d : d + 1] for d in range(GROUPS)], axis=1)
    for r in range(SEQ):
        at = slice(r * CH, (r + 1) * CH)
        hidden = dot3(norm_h[r], norm_l[r], winh[...], winl[...], NN) + bias
        inner = jnp.tanh(gelu_scale * (hidden + gelu_cubic * hidden * hidden * hidden))
        acts_h[at, :], acts_l[at, :] = halves(0.5 * hidden * (1.0 + inner))
        slope[at, :] = 0.5 * (1.0 + inner) + 0.5 * hidden * (1.0 - inner * inner) * gelu_scale * (
            1.0 + 3.0 * gelu_cubic * hidden * hidden
        )


def emit_blocks(scal, outs, whole):
    for k in range(GROUPS):
        outs[k][...] = whole[rows_at(owner(scal, k), ROWS), :]


def out_grad_kernel(scal, acts_h, acts_l, *refs):
    grads, (out_h, out_l), outs, whole = refs[:4], refs[4:6], refs[6 : 6 + GROUPS], refs[6 + GROUPS]
    for r in range(SEQ):
        at = slice(r * CH, (r + 1) * CH)
        out_h[at, :], out_l[at, :] = halves(grads[r][...])
    whole[...] = dot3(acts_h[...], acts_l[...], out_h[...], out_l[...], TN)
    emit_blocks(scal, outs, whole)


def hidden_back_kernel(scal, out_h, out_l, slope, winh, winl, *refs):
    blocks, refs = refs[:GROUPS], refs[GROUPS:]
    hid_h, hid_l, wouth, woutl, bias_sum = refs[:5]
    parts = refs[5:]
    for k in range(GROUPS):
        at = rows_at(owner(scal, k), ROWS)
        wouth[at, :], woutl[at, :] = halves(blocks[k][...])
    sums = jnp.zeros((1, D), f32)
    for r in (1, 3, 2, 0):
        at = slice(r * CH, (r + 1) * CH)
        back = dot3(out_h[at, :], out_l[at, :], wouth[...], woutl[...], NT) * slope[at, :]
        sums = sums + jnp.sum(back, axis=0, keepdims=True)
        bh, bl = halves(back)
        hid_h[at, :], hid_l[at, :] = bh, bl
        parts[r][...] = dot3(bh, bl, winh[...], winl[...], NT)
    bias_sum[...] = jnp.broadcast_to(sums, (8, D))


def in_grad_kernel(scal, norm_h, norm_l, hid_h, hid_l, *refs):
    outs, whole = refs[:GROUPS], refs[GROUPS]
    flat = lambda ref: ref[...].reshape(LEN, D)
    whole[...] = dot3(flat(norm_h), flat(norm_l), hid_h[...], hid_l[...], TN)
    emit_blocks(scal, outs, whole)


def ffn_out_kernel(scal, acts_h, acts_l, wouth, woutl, *parts):
    for r in (1, 3, 2, 0):
        at = slice(r * CH, (r + 1) * CH)
        parts[r][...] = dot3(acts_h[at, :], acts_l[at, :], wouth[...], woutl[...], NN)


def output_kernel(scal, mixed, one, two, three, vec, output):
    output[...] = mixed[...] + (one[...] + two[...] + three[...]) + piece(vec, 7)


def proj_back_kernel(scal, one, two, three, hat, scale, vec, grad_out, wh, wl, mixed_grad, sums, *parts):
    mine = scal[0]
    normed = one[...] + two[...] + three[...]
    back = norm_back(hat[...], scale[:, :1], piece(vec, 5), normed)
    total = grad_out[...] + back
    mixed_grad[...] = total
    a, b = halves(total)
    for r in range(SEQ):
        at = rows_at(jnp.bitwise_xor(mine, r), QUARTER)
        parts[r][...] = dot3(wh[at, :], wl[at, :], a, b, NT)
    add = lambda v: jnp.sum(v, axis=0, keepdims=True)
    sums[...] = jnp.concatenate(
        [add(total), add(normed * hat[...]), add(normed), add(grad_out[...]), jnp.zeros((4, D), f32)],
        axis=0,
    )


def proj_grad_kernel(scal, heads_h, heads_l, mixed_grad, *refs):
    outs, whole = refs[:-1], refs[-1]
    mine = scal[0]
    gh, gl = halves(mixed_grad[...])
    whole[...] = dot3(heads_h[...], heads_l[...], gh, gl, NN)
    for r in range(SEQ):
        at = jnp.bitwise_xor(mine, r)
        for d in range(GROUPS):
            outs[r][d * SUB : (d + 1) * SUB, :] = whole[
                pl.ds(pl.multiple_of(d * ROWS + at * SUB, 8), SUB), :
            ]


def back_kernel(scal, *refs):
    grads, refs = refs[:4], refs[4:]
    kcat, qturn, vcat, qpair, kturn, outs_turn, lse, low_row = refs[:8]
    joined_h, joined_l, joined_sums = refs[8:11]
    gturn, gpair, dots, key_sum, value_sum, query_turn = refs[11:]
    mine = scal[0]

    for r in range(SEQ):
        at = rows_at(jnp.bitwise_xor(mine, r), CH)
        turned = grads[r][...]
        grad = jnp.concatenate([turned, jnp.zeros((HEAD, CH), f32)], axis=0).T
        pairs = lane_pairs(grad[:, :128], grad[:, 128:])
        for h in range(OWN):
            gpair[h, at, :] = pairs[h]
            part = turned[HEAD * h : HEAD * (h + 1)]
            dots[h, :, at] = jnp.broadcast_to(
                jnp.sum(part * outs_turn[HEAD * h : HEAD * (h + 1), at], axis=0, keepdims=True), (8, CH)
            )
            a, b = halves(part)
            gturn[h, :, at] = jnp.concatenate([a, a, b, b], axis=0)

    key_sum[...] = jnp.zeros_like(key_sum)
    value_sum[...] = jnp.zeros_like(value_sum)

    def one_head(h, carry):
        for c in range(SEQ):
            size = CH * (c + 1)
            lanes = slice(c * CH, (c + 1) * CH)
            score = dot(kcat[h, :size, :], qturn[h, :, lanes], NN)
            weight = jnp.where(allowed(low_row, c, size), jnp.exp(score - lse[h, :1, lanes]), 0.0)
            back = dot(vcat[h, :size, :], gturn[h, :, lanes], NN)
            score_back = weight * (back - dots[h, :1, lanes])
            a, b = halves(weight)
            pair = gpair[h, lanes, :]
            value_sum[h, :size, :] += dot(a, pair, NN) + dot(b, pair, NN)
            a, b = halves(score_back)
            pair = qpair[h, lanes, :]
            key_sum[h, :size, :] += dot(a, pair, NN) + dot(b, pair, NN)
            turned = dot(kturn[h, :, :size], a, NN) + dot(kturn[h, :, :size], b, NN)
            query_turn[h, :, lanes] = (turned[:HEAD] + turned[HEAD:]) * HEAD ** (-0.5)
        return carry

    lax.fori_loop(0, OWN, one_head, 0)

    column_sums = jnp.zeros((1, D), f32)
    low = low_lanes((CH, 128))
    for c in range(SEQ):
        at = slice(c * CH, (c + 1) * CH)
        blank = jnp.zeros((HEAD, CH), f32)
        query = jnp.concatenate([query_turn[h, :, at] for h in range(OWN)] + [blank], axis=0).T
        done = [query]
        for kept in (key_sum, value_sum):
            full = [kept[h, at, :] for h in range(OWN)]
            full = [v + pltpu.roll(v, HEAD, 1) for v in full]
            done.append(jnp.where(low, full[0], full[1]))
            done.append(jnp.where(low, full[2], 0.0))
        joined = jnp.concatenate(done, axis=1)
        column_sums = column_sums + jnp.sum(joined, axis=0, keepdims=True)
        joined_h[at, :], joined_l[at, :] = halves(joined)

    joined_sums[...] = jnp.broadcast_to(column_sums, (8, D))


def qkv_grad_kernel(scal, xh, xl, joined_h, joined_l, joined_sums, wh, wl, vec, *refs):
    proj_one, proj_two, vector_sums, bias_sum = refs[:4]
    outs, (whole, rows) = refs[4 : 4 + GROUPS], refs[4 + GROUPS :]
    mine = scal[0]
    column_sums = joined_sums[:1, :]
    core = dot3(xh[...], xl[...], joined_h[...], joined_l[...], TN)
    gain, shift = piece(vec, 0), piece(vec, 1)
    as_column = lambda v: jnp.broadcast_to(v, (128, D)).T[:, :1]
    whole[...] = as_column(gain) * core + as_column(shift) * column_sums
    weights = wh[...].astype(f32) + wl[...].astype(f32)
    gain_grad = jnp.sum(weights * core, axis=1, keepdims=True)
    shift_grad = jnp.sum(weights * column_sums, axis=1, keepdims=True)
    lane = lax.broadcasted_iota(jnp.int32, (D, 128), 1)
    norm_grads = jnp.where(lane == 0, gain_grad, shift_grad).T

    def place(part, scale):
        wide = jnp.concatenate([part[:, :QUARTER], jnp.zeros((1, D - QUARTER), f32)], axis=1)
        wide = jnp.broadcast_to(wide, (8, D))
        return pltpu.roll(wide, mine * QUARTER, 1)[:1]

    entries = [
        norm_grads[0:1],
        norm_grads[1:2],
        place(column_sums[:, :CH], 1.0),
        place(column_sums[:, 2 * CH :], 1.0),
        vector_sums[0:1],
        vector_sums[1:2],
        vector_sums[2:3],
        vector_sums[3:4],
    ]
    lines = [e[:, i * HALF_VEC : (i + 1) * HALF_VEC] for e in entries for i in range(2)]
    bias = jnp.concatenate(
        [bias_sum[:1, d * ROWS : (d + 1) * ROWS] for d in range(GROUPS)], axis=0
    )
    bias = jnp.concatenate([bias, jnp.zeros((GROUPS, HALF_VEC - ROWS), f32)], axis=1)
    bias = pltpu.roll(bias, mine * ROWS, 1)
    lines = lines + [bias[d : d + 1] for d in range(GROUPS)]
    filler = jnp.zeros((5, HALF_VEC), f32)
    for d in range(GROUPS):
        rows[d] = jnp.concatenate(lines[3 * d : 3 * d + 3] + [filler], axis=0)

    for k in range(GROUPS):
        at = owner(scal, k)
        outs[k][:ROWS, :] = whole[rows_at(at, ROWS), :]
        here = pl.ds(pl.multiple_of(at * SUB, 8), SUB)
        proj = proj_one[here, :] + proj_two[here, :]
        for group in range(SEQ):
            for part in range(3):
                lane_at = HEAD * (3 * group + part)
                outs[k][
                    group * SUB : (group + 1) * SUB, part * CH + QUARTER : (part + 1) * CH
                ] = proj[:, lane_at : lane_at + HEAD]
        outs[k][ROWS:, :HALF_VEC] = rows[at]
        outs[k][ROWS:, HALF_VEC:] = jnp.zeros((8, HALF_VEC), f32)


def pre_back_kernel(scal, joined_h, joined_l, wh, wl, *parts):
    mine = scal[0]
    for r in (1, 3, 2, 0):
        at = rows_at(jnp.bitwise_xor(mine, r), CH)
        parts[r][...] = dot3(joined_h[at, :], joined_l[at, :], wh[...], wl[...], NT)


def input_grad_kernel(scal, tokens, one, two, three, vec, mixed_grad, result):
    hat, scale = norm_stats(tokens[...])
    grad = one[...] + two[...] + three[...]
    result[...] = mixed_grad[...] + norm_back(hat, scale, piece(vec, 0), grad)


def total_square(value):
    return jnp.sum(jnp.sum(value * value, axis=0, keepdims=True), axis=1, keepdims=True)


def shard_sums_kernel(scal, first, in_shard, out_shard, small):
    total = total_square(first[:ROWS, :]) + total_square(in_shard[...]) + total_square(out_shard[...])
    small[...] = first[ROWS:, :]
    small[7:8, :] = jnp.broadcast_to(total, (1, D))


def shard_squares_kernel(scal, one, two, three, four, squares):
    whole = (one[...] + two[...]) + (three[...] + four[...])
    squares[...] = jnp.broadcast_to(whole[7:8, :1] + total_square(whole[:3, :HALF_VEC]), (8, 128))


def stage_kernel(scal, *refs):
    sources, targets, sems = refs[:15], refs[15:30], refs[30]
    copies = [
        pltpu.make_async_copy(source, target, sems.at[i])
        for i, (source, target) in enumerate(zip(sources, targets))
    ]
    for copy in copies:
        copy.start()
    for copy in copies:
        copy.wait()


def adamw_kernel(scal, squares, *refs):
    firsts, ins, outs, refs = refs[:4], refs[4:8], refs[8:12], refs[12:]
    states, clip, finals, news = refs[:15], refs[15], refs[16:31], refs[31:46]
    first, second, sems = refs[46:]
    send = lambda number: [
        pltpu.make_async_copy(news[i], finals[i], sems.at[i]) for i in range(3 * number, 3 * number + 3)
    ]
    mine = scal[0]
    norm = jnp.sqrt(squares[...])
    clip[...] = norm
    factor = (clip_limit / jnp.maximum(norm, clip_limit))[:1, :1]
    for r in range(SEQ):
        at = jnp.bitwise_xor(mine, r)
        first[at] = firsts[r][:ROWS, :]
        second[at, :ROWS] = ins[r][...]
        second[at, ROWS:] = outs[r][...]

    def update(number, spot, grad, rate, decay):
        held = [states[3 * number + i][spot] for i in range(3)]
        fresh = adamw_update(*held, factor * grad, rate, decay)
        for i in range(3):
            news[3 * number + i][spot] = fresh[i]

    def finish(number):
        for copy in send(number):
            copy.start()

    lines = [firsts[r][ROWS:, :HALF_VEC] for r in range(SEQ)]
    line = (lines[0] + lines[1]) + (lines[2] + lines[3])
    for i in range(3):
        for j in range(3):
            spot = (slice(3 * i + j, 3 * i + j + 1), slice(None))
            update(0, spot, line[i : i + 1, 128 * j : 128 * (j + 1)], vector_rate, 0.0)
    finish(0)
    every = slice(None)
    for part in range(3):
        grad = jnp.concatenate(
            [first[j][:, part * CH : part * CH + QUARTER] for j in range(SEQ)], axis=1
        )
        update(1, (every, slice(part * D, (part + 1) * D)), grad, matrix_rate, weight_decay)
    finish(1)
    for j in range(SEQ):
        grad = jnp.concatenate(
            [
                first[j][group * SUB : (group + 1) * SUB, part * CH + QUARTER : (part + 1) * CH]
                for group in range(SEQ)
                for part in range(3)
            ],
            axis=1,
        )
        update(2, (slice(j * SUB, (j + 1) * SUB), every), grad, matrix_rate, weight_decay)
    finish(2)
    for d in range(GROUPS):
        grad = jnp.concatenate(
            [second[j][:ROWS, d * ROWS : (d + 1) * ROWS] for j in range(SEQ)], axis=1
        )
        update(3, (every, slice(d * HALF_VEC, (d + 1) * HALF_VEC)), grad, matrix_rate, weight_decay)
    finish(3)
    for j in range(SEQ):
        update(
            4, (slice(j * ROWS, (j + 1) * ROWS), every), second[j][ROWS:, :], matrix_rate, weight_decay
        )
    finish(4)
    for number in range(5):
        for copy in send(number):
            copy.wait()


def adamw_update(weight, first, second, grad, rate, decay):
    new_first = beta_one * first + (1.0 - beta_one) * grad
    new_second = beta_two * second + (1.0 - beta_two) * grad * grad
    first_hat = new_first / (1.0 - beta_one**STEP)
    second_hat = new_second / (1.0 - beta_two**STEP)
    new_weight = weight - rate * (first_hat / (jnp.sqrt(second_hat) + adam_eps) + decay * weight)
    return (new_first, new_second, new_weight)


def ring_tables(count):
    evens = [2 * i for i in range(count // 2)]
    order = evens + [i + 1 for i in reversed(evens)]
    place = [0] * count
    for position, device in enumerate(order):
        place[device] = position
    right = [(order[i], order[(i + 1) % count]) for i in range(count)]
    left = [(b, a) for a, b in right]
    return order, place, right, left


class RingGather:
    def __init__(self, block, name, flip=False):
        _, _, self.right, self.left = ring_tables(GROUPS)
        if flip:
            self.right, self.left = self.left, self.right
        self.got, self.name, self.at, self.flip = {0: block}, name, 0, flip

    def step(self, after=()):
        places = (-self.at % GROUPS, self.at)
        if after:
            for place in set(places):
                self.got[place] = gate(self.got[place], after)
        forth, back = (self.got[place] for place in places)
        self.at += 1
        self.got[GROUPS - self.at] = move(forth, "dp", self.right, f"{self.name}_right_{self.at}")
        if self.at < HALF:
            self.got[self.at] = move(back, "dp", self.left, f"{self.name}_left_{self.at}")
        return [self.got[GROUPS - self.at]] + ([self.got[self.at]] if self.at < HALF else [])

    def blocks(self):
        return [self.got[-k % GROUPS if self.flip else k] for k in range(GROUPS)]


class RingScatter:
    def __init__(self, blocks, name, flip=False):
        _, _, self.right, self.left = ring_tables(GROUPS)
        self.blocks = blocks
        if flip:
            self.right, self.left = self.left, self.right
            self.blocks = [blocks[-k % GROUPS] for k in range(GROUPS)]
        self.name, self.back, self.at = name, None, HALF
        self.forth = move(self.blocks[HALF], "dp", self.right, f"{name}_right_1")

    def step(self, after=()):
        self.at -= 1
        ahead, back = self.blocks[self.at], self.blocks[GROUPS - self.at]
        if self.back is None:
            forth = plus(self.forth, ahead, after=after)
        else:
            forth, back = sums([(self.forth, ahead), (self.back, back)], after)
        number = HALF + 1 - self.at
        self.forth = move(forth, "dp", self.right, f"{self.name}_right_{number}")
        self.back = move(back, "dp", self.left, f"{self.name}_left_{number}")
        return [forth, back]

    def result(self, after=()):
        return plus(self.forth, self.back, self.blocks[0], after=after)


def move(block, axis, pairs, name):
    with jax.named_scope(name):
        return lax.ppermute(block, axis, pairs)


def swap(block, bits, name):
    return move(block, "seq", [(i, i ^ bits) for i in range(SEQ)], f"{name}_{bits}")


def gather_seq(block, name):
    across = swap(block, 2, name)
    core = swap(block, 1, name)
    return [block, core, across, swap(across, 1, f"{name}_2")]


def exchange_seq(parts, name):
    return [parts[0]] + [swap(parts[r], r, name) for r in range(1, SEQ)]


def scatter_core(parts, name):
    return parts[0], swap(parts[1], 1, f"{name}_own"), parts[2], swap(parts[3], 1, f"{name}_across")


def ordered(blocks, mine):
    stack = jnp.stack(blocks, axis=0)
    return [lax.dynamic_index_in_dim(stack, mine ^ j, 0, keepdims=False) for j in range(len(blocks))]


def local(
    tokens,
    cotangent,
    segment_ids,
    valid,
    vectors,
    vec_first,
    vec_second,
    w_qkv,
    qkv_first,
    qkv_second,
    w_proj,
    proj_first,
    proj_second,
    w_in,
    in_first,
    in_second,
    w_out,
    out_first,
    out_second,
):
    dp_parts = lax.axis_size("dp")
    ring = dp_parts == GROUPS
    mine = lax.axis_index("seq")
    home = lax.axis_index("dp")
    rows = w_qkv.shape[0]
    units = w_out.shape[0] // SEQ
    far, near = home // 2, home % 2
    position = jnp.where(near > 0, GROUPS - 1 - far, far)
    scal = jnp.stack([mine, position, jnp.full_like(mine, 1 if ring else 0)]).astype(jnp.int32)
    flat_in = tokens.reshape(CH, D)
    chunk, tall, square = shape(CH, D), shape(LEN, D, kind=bf16), shape(D, D, kind=bf16)

    if ring:
        first, packed = run(
            pack_first_kernel,
            scal,
            [w_qkv, w_proj, vectors.reshape(9, 128), segment_ids, valid, flat_in],
            [shape(ROWS + 8, D), shape(CH + 8, D)],
            scratch=[
                pltpu.VMEM((3, ROWS, CH), f32),
                pltpu.VMEM((SUB, D), f32),
                pltpu.VMEM((9, 128), f32),
                pltpu.VMEM((2, 1, CH), jnp.int32),
            ],
            sems=8,
            far_args=range(6),
            room=54,
            name="pack_first", work=3.0,
        )
        ring_first = RingGather(first, "first")
        for _ in range(HALF):
            ring_first.step()
        firsts = ring_first.blocks()
        in_block, out_block = run(
            pack_second_kernel,
            scal,
            [w_in, w_out],
            [shape(ROWS, D)] * 2,
            name="pack_second", work=3.0,
            after=[firsts[GROUPS - 1]],
        )
        ring_in = RingGather(in_block, "w_in")
        ring_out = RingGather(out_block, "w_out", flip=True)
        came = ring_in.step([firsts[HALF]])
        came = came + ring_out.step([firsts[HALF]])
    else:
        padded = jnp.pad(w_qkv, ((0, 0), (0, CH)))
        own = lambda part: lax.dynamic_slice_in_dim(padded, part * D + mine * QUARTER, CH, 1)
        first = jnp.concatenate([own(0), own(1), own(2)], axis=1)
        first = lax.all_gather(first, "dp", axis=0, tiled=True).reshape(GROUPS, ROWS, D)
        all_vec = lax.all_gather(vectors, "dp", axis=0, tiled=True).reshape(GROUPS, 3, HALF_VEC)
        first = jnp.concatenate([first, jnp.pad(all_vec, ((0, 0), (0, 5), (0, D - HALF_VEC)))], axis=1)
        firsts = [first[k] for k in range(GROUPS)]
        in_part = lax.dynamic_index_in_dim(
            w_in.reshape(rows, dp_parts, SEQ, units), mine, 2, keepdims=False
        ).reshape(rows, D)
        out_part = lax.dynamic_slice_in_dim(w_out, mine * units, units, 0)
        in_blocks, out_blocks = (
            list(lax.all_gather(part, "dp", axis=0, tiled=True).reshape(GROUPS, ROWS, D))
            for part in (in_part, out_part)
        )
        marks = jnp.where(valid > 0, segment_ids, -1).astype(f32)
        packed = jnp.concatenate([flat_in, jnp.pad(marks, ((0, 7), (0, D - CH)))], axis=0)
    toks = gather_seq(packed, "tokens")
    (grad_out,) = run(
        mask_kernel, scal, [cotangent.reshape(CH, D), valid], [chunk], name="mask", work=2.0, after=[toks[2]]
    )
    grads_row = gather_seq(grad_out, "cotangent")

    qkv_h, qkv_l, vec, proj = run(
        weights_kernel,
        scal,
        firsts,
        [square, square, shape(GROUPS, 8, HALF_VEC), shape(GROUPS * SUB, D)],
        name="weights", work=3.0,
    )
    if ring:
        proj_parts = gather_seq(proj, "w_proj")
    else:
        full = lax.all_gather(w_proj, "dp", axis=0, tiled=True).reshape(GROUPS, SEQ, SUB, D)
        proj_parts = [
            lax.dynamic_index_in_dim(full, mine ^ r, 1, keepdims=False).reshape(GROUPS * SUB, D)
            for r in range(SEQ)
        ]
    hat_h, hat_l, kcat, qturn, vcat, qpair, kturn, low_row, heads, lse = run(
        front_kernel,
        scal,
        toks + [qkv_h, qkv_l, vec],
        [
            tall,
            tall,
            shape(OWN, LEN, 256, kind=bf16),
            shape(OWN, 256, LEN, kind=bf16),
            shape(OWN, LEN, 256, kind=bf16),
            shape(OWN, LEN, 128, kind=bf16),
            shape(OWN, 128, LEN, kind=bf16),
            shape(8, LEN),
            shape(QUARTER, LEN),
            shape(OWN, 8, LEN),
        ],
        scratch=[pltpu.VMEM((OWN, 128, LEN), bf16), pltpu.VMEM((SEQ, 8, CH), f32)],
        name="front", work=14.0,
        after=[grads_row[2]],
    )
    if ring:
        heads = gate(heads, [proj_parts[2], *came])
        ring_in.step([lse])
        came = ring_in.step()
        came = came + ring_in.step()
        ring_out.step(came)
        in_blocks = ring_in.blocks()
    across = swap(heads, 2, "heads")
    if ring:
        across = gate(across, came)
    all_heads = [heads, swap(heads, 1, "heads"), across, swap(across, 1, "heads_2")]
    wide = shape(D, CH, kind=bf16)
    split = shape(SEQ, CH, D, kind=bf16)
    proj_h, proj_l, heads_h, heads_l, norm_h, norm_l, mixed, hat_two, scale_two = run(
        proj_kernel,
        scal,
        toks + all_heads + proj_parts + [vec],
        [square, square, wide, wide, split, split, chunk, chunk, shape(CH, 128)],
        scratch=[pltpu.VMEM((D, D), f32), pltpu.VMEM((D, LEN), f32)],
        name="proj", work=8.0,
    )

    if ring:
        ring_out.step([norm_h])
        ring_out.step()
        out_blocks = ring_out.blocks()
    block = shape(ROWS, D)
    acts_h, acts_l, slope, in_wh, in_wl = run(
        hidden_kernel,
        scal,
        [norm_h, norm_l] + in_blocks + [vec],
        [tall, tall, shape(LEN, D), square, square],
        name="hidden", work=8.0,
    )
    done = run(
        out_grad_kernel,
        scal,
        [acts_h, acts_l] + grads_row,
        [tall, tall] + [block] * GROUPS,
        scratch=[pltpu.VMEM((D, D), f32)],
        name="out_grad", work=5.0,
    )
    out_h, out_l = done[:2]
    out_grads = list(done[2:])
    if ring:
        ring_out = RingScatter(out_grads, "out_grad")
    done = run(
        hidden_back_kernel,
        scal,
        [out_h, out_l, slope, in_wh, in_wl] + out_blocks,
        [tall, tall, square, square, shape(8, D)] + [chunk] * SEQ,
        name="hidden_back", work=11.0,
        after=out_grads[:1],
    )
    hid_h, hid_l, out_wh, out_wl, bias_sum = done[:5]
    parts = list(done[5:])
    if ring:
        parts[3] = gate(parts[3], ring_out.step([bias_sum]))
    norm_own, norm_near, norm_across, norm_far = scatter_core(parts, "norm_grad")
    norm_pair = plus(norm_across, norm_far)
    norm_last = swap(norm_pair, 2, "norm_grad")
    in_grads = list(
        run(
            in_grad_kernel,
            scal,
            [norm_h, norm_l, hid_h, hid_l],
            [block] * GROUPS,
            scratch=[pltpu.VMEM((D, D), f32)],
            name="in_grad", work=5.0,
            after=[norm_pair],
        )
    )
    if ring:
        ring_in = RingScatter(in_grads, "in_grad", flip=True)
        out_sent = ring_out.step()
        in_sent = ring_in.step()
    done = run(
        proj_back_kernel,
        scal,
        [norm_own, norm_near, norm_last, hat_two, scale_two, vec, grad_out, proj_h, proj_l],
        [chunk, shape(8, D)] + [shape(QUARTER, CH)] * SEQ,
        name="proj_back", work=5.0,
        after=out_sent + in_sent if ring else [],
    )
    mixed_grad, vector_sums = done[:2]
    head_grads = exchange_seq(list(done[2:]), "head_grad")
    if ring:
        out_sent = ring_out.step([mixed_grad])
        in_sent = ring_in.step([mixed_grad])
    out_parts = run(
        ffn_out_kernel,
        scal,
        [acts_h, acts_l, out_wh, out_wl],
        [chunk] * SEQ,
        name="ffn_out", work=7.0,
        after=[mixed_grad],
    )
    proj_grads = run(
        proj_grad_kernel,
        scal,
        [heads_h, heads_l, mixed_grad],
        [shape(GROUPS * SUB, D)] * SEQ,
        scratch=[pltpu.VMEM((D, D), f32)],
        name="proj_grad", work=4.0,
        after=[*head_grads[1:], *out_sent, *in_sent, out_parts[0]] if ring else [],
    )
    wait = [head_grads[3], head_grads[2]]
    out_own, out_near, out_across, out_far = scatter_core(out_parts, "output")
    if ring:
        proj_own, proj_near, proj_across, proj_far = scatter_core(proj_grads, "proj_grad")
        proj_pair, proj_base, out_pair = sums(
            [(proj_across, proj_far), (proj_own, proj_near), (out_across, out_far)], wait
        )
        proj_last = swap(proj_pair, 2, "proj_grad")
    else:
        proj_base = proj_last = proj_grads[0]
        out_pair = plus(out_across, out_far)
    joined_h, joined_l, joined_sums = run(
        back_kernel,
        scal,
        head_grads + [kcat, qturn, vcat, qpair, kturn, heads, lse, low_row],
        [tall, tall, shape(8, D)],
        scratch=[
            pltpu.VMEM((OWN, 256, LEN), bf16),
            pltpu.VMEM((OWN, LEN, 128), bf16),
            pltpu.VMEM((OWN, 8, LEN), f32),
            pltpu.VMEM((OWN, LEN, 128), f32),
            pltpu.VMEM((OWN, LEN, 128), f32),
            pltpu.VMEM((OWN, HEAD, LEN), f32),
        ],
        name="back", work=16.0,
        after=[proj_grads[0]],
    )
    out_last = swap(gate(out_pair, [joined_sums]), 2, "output")
    if ring:
        shard_out = ring_out.result([joined_sums])
        in_sent = ring_in.step([joined_sums])
    done = run(
        qkv_grad_kernel,
        scal,
        [hat_h, hat_l, joined_h, joined_l, joined_sums, qkv_h, qkv_l, vec]
        + [proj_base, proj_last, vector_sums, bias_sum],
        [shape(ROWS + 8, D)] * GROUPS,
        scratch=[pltpu.VMEM((D, D), f32), pltpu.VMEM((GROUPS, 8, HALF_VEC), f32)],
        name="qkv_grad", work=1.0,
        after=[*in_sent, shard_out] if ring else [],
    )
    first_grads = list(done)
    if ring:
        shard_in = ring_in.result([first_grads[0]])
        out_all = gather_seq(shard_out, "out_shard")
        first_grads[HALF] = gate(first_grads[HALF], [shard_in])
        ring_first = RingScatter(first_grads, "first_grad")
        first_sent = ring_first.step([out_last])
    pre_parts = run(
        pre_back_kernel,
        scal,
        [joined_h, joined_l, qkv_h, qkv_l],
        [chunk] * SEQ,
        name="pre_back", work=1.0,
        after=[shard_in, *first_sent] if ring else [],
    )
    pre_parts = list(pre_parts)
    if ring:
        first_sent = ring_first.step()
        pre_parts[3] = gate(pre_parts[3], [*first_sent, out_all[2]])
    pre_own, pre_near, pre_across, pre_far = scatter_core(pre_parts, "pre_grad")
    pre_pair = plus(pre_across, pre_far)
    pre_last = swap(pre_pair, 2, "pre_grad")
    states = [vectors, vec_first, vec_second, w_qkv, qkv_first, qkv_second, w_proj, proj_first, proj_second]
    states = states + [w_in, in_first, in_second, w_out, out_first, out_second]
    last_sent = ring_first.step() if ring else []
    (output,) = run(
        output_kernel,
        scal,
        [mixed, out_own, out_near, out_last, vec],
        [chunk],
        name="output", work=2.0,
        after=last_sent,
    )
    if ring:
        held = [v.reshape(9, 128) for v in states[:3]] + states[3:]
        held = run(
            stage_kernel,
            scal,
            held,
            [shape(*v.shape) for v in held],
            sems=15,
            far_args=range(15),
            name="stage", work=3.0,
            after=last_sent,
        )
        shard_first = ring_first.result([output, held[3]])
    (input_grad,) = run(
        input_grad_kernel,
        scal,
        [flat_in, pre_own, pre_near, pre_last, vec, mixed_grad],
        [chunk],
        name="input_grad", work=3.0,
    )

    if ring:
        (small,) = run(
            shard_sums_kernel, scal, [shard_first, shard_in, shard_out], [shape(8, D)], name="shard_sums", work=1.0
        )
        shard_first = gate(shard_first, [pre_last])
        in_all = gather_seq(gate(shard_in, [pre_last]), "in_shard")
        across = swap(shard_first, 2, "first_shard")
        core = swap(shard_first, 1, "first_shard")
        (squares,) = run(
            shard_squares_kernel,
            scal,
            [small] + [swap(small, bits, "small") for bits in (1, 2, 3)],
            [shape(8, 128)],
            name="shard_squares", work=1.0,
        )
        flipped = lambda bits: [(i, i ^ bits) for i in range(GROUPS)]
        one, two, three = (move(squares, "dp", flipped(bits), "squares") for bits in (1, 2, 3))
        squares = sum_pairs(squares, one, two, three)
        across = gate(across, [input_grad, squares, in_all[2]])
        first_all = [shard_first, core, across, swap(across, 1, "first_shard_2")]
        squares = plus(squares, move(squares, "dp", flipped(4), "squares"))
        done = run(
            adamw_kernel,
            scal,
            [squares] + first_all + in_all + out_all + list(held),
            [shape(8, 128)] + [shape(*v.shape) for v in held],
            scratch=[pltpu.VMEM(v.shape, f32) for v in held]
            + [pltpu.VMEM((SEQ, ROWS, D), f32), pltpu.VMEM((SEQ, 2 * ROWS, D), f32)],
            sems=15,
            far_outs=range(1, 16),
            name="adamw", work=0.1,
        )
        new = [v.reshape(-1) for v in done[1:4]] + list(done[4:])
        clip_norm = done[0][0, 0]
    else:
        by_group = jnp.stack(first_grads)
        shard_first = lax.psum_scatter(
            by_group[:, :ROWS].reshape(D, D), "dp", scatter_dimension=0, tiled=True
        )
        proj_full = jnp.stack([p.reshape(GROUPS, SUB, D) for p in ordered(proj_grads, mine)], axis=1)
        proj_grad = lax.psum(
            lax.psum_scatter(proj_full.reshape(D, D), "dp", scatter_dimension=0, tiled=True), "seq"
        )
        all_vec = lax.psum(by_group[:, ROWS : ROWS + 3, :HALF_VEC], ("dp", "seq")).reshape(-1)
        vec_grad = lax.dynamic_slice_in_dim(all_vec, home * vectors.shape[0], vectors.shape[0])
        joined = lax.all_gather(shard_first, "seq", axis=0, tiled=False)
        qkv_grad = jnp.concatenate(
            [joined[j, :, i * CH : i * CH + QUARTER] for i in range(3) for j in range(SEQ)], axis=1
        )
        shard_in, shard_out = (
            lax.psum_scatter(jnp.concatenate(parts, axis=0), "dp", scatter_dimension=0, tiled=True)
            for parts in (in_grads, out_grads)
        )
        in_all = lax.all_gather(shard_in, "seq", axis=0, tiled=False)
        in_grad = in_all.reshape(SEQ, rows, dp_parts, units).transpose(1, 2, 0, 3).reshape(rows, -1)
        out_grad = lax.all_gather(shard_out, "seq", axis=0, tiled=True)
        total = sum(jnp.sum(g * g) for g in (qkv_grad, proj_grad, in_grad, out_grad, vec_grad))
        total = lax.psum(total, "dp")
        clip_norm = jnp.sqrt(total)
        factor = clip_limit / jnp.maximum(clip_norm, clip_limit)
        grads = (vec_grad, qkv_grad, proj_grad, in_grad, out_grad)
        new = []
        for number, grad in enumerate(grads):
            rate, decay = (matrix_rate, weight_decay) if number else (vector_rate, 0.0)
            new.extend(adamw_update(*states[3 * number : 3 * number + 3], factor * grad, rate, decay))
    return (output.reshape(tokens.shape), input_grad.reshape(tokens.shape), clip_norm, *new)


def solution(mesh):
    row = P("dp", "seq", None)
    mark = P("dp", "seq")
    vec = P("dp")
    mat = P("dp", None)
    return jax.shard_map(
        local,
        mesh=mesh,
        in_specs=(row, row, mark, mark) + (vec,) * 3 + (mat,) * 12,
        out_specs=(row, row, P()) + (vec,) * 3 + (mat,) * 12,
        check_vma=False,
    )
```

```python
import functools
import math

import jax
import jax.numpy as jnp
from jax import lax
from jax.experimental import pallas as pl
from jax.experimental.pallas import tpu as pltpu
from jax.sharding import PartitionSpec as P

D = 768
HEADS = 12
HEAD = 64
STEP = 10
CH = 256
LEN = 1024
SEQ = 4
QUARTER = D // SEQ
OWN = HEADS // SEQ
GROUPS = 8
ROWS = D // GROUPS
SUB = ROWS // SEQ
HALF = GROUPS // 2
CUT = ROWS // 2
HALF_VEC = D // 2
VEC_ROWS = 24

f32 = jnp.float32
bf16 = jnp.bfloat16
masked_score = -1e30
norm_eps = 1e-05
clip_limit = 1.0
beta_one = 0.9
beta_two = 0.999
adam_eps = 1e-08
matrix_rate = 0.02
vector_rate = 0.4
weight_decay = 0.01
gelu_scale = 0.7978845608028654
gelu_cubic = 0.044715

COST = 1e9

WHOLE = pl.BlockSpec(memory_space=pltpu.VMEM)
SCALARS = pl.BlockSpec(memory_space=pltpu.SMEM)
NN = ((1,), (0,))
NT = ((1,), (1,))
TN = ((0,), (0,))


def shape(*dims, kind=f32):
    return jax.ShapeDtypeStruct(dims, kind)


def run(
    kernel, scal, args, outs, scratch=(), sems=0, far_args=(), far_outs=(), room=8, work=1.0, name=None, after=()
):
    args, after = list(args), list(after)
    held = sum(math.prod(v.shape) * jnp.dtype(v.dtype).itemsize for v in scratch)
    anywhere, far = pl.BlockSpec(memory_space=pl.ANY), pl.BlockSpec(memory_space=pltpu.HBM)
    scratch = list(scratch) + ([pltpu.SemaphoreType.DMA((sems,))] if sems else [])

    def body(scal_ref, *refs):
        kernel(scal_ref, *refs[: len(args)], *refs[len(args) + len(after) :])

    return pl.pallas_call(
        body,
        out_shape=tuple(outs),
        in_specs=[SCALARS]
        + [far if i in far_args else WHOLE for i in range(len(args))]
        + [anywhere] * len(after),
        out_specs=tuple(far if i in far_outs else WHOLE for i in range(len(outs))),
        scratch_shapes=scratch,
        compiler_params=pltpu.CompilerParams(vmem_limit_bytes=held + (room << 20)),
        cost_estimate=pl.CostEstimate(
            flops=int(work * COST), bytes_accessed=1, transcendentals=0
        ),
        name=name,
    )(scal, *args, *after)


def gate(value, after):
    anywhere = pl.BlockSpec(memory_space=pl.ANY)
    return pl.pallas_call(
        lambda *refs: None,
        out_shape=shape(*value.shape, kind=value.dtype),
        in_specs=[anywhere] * (1 + len(after)),
        out_specs=anywhere,
        input_output_aliases={0: 0},
        compiler_params=pltpu.CompilerParams(vmem_limit_bytes=1 << 20),
        name="gate",
    )(value, *after)


def sums(groups, after=()):
    sizes = [len(group) for group in groups]

    def body(*refs):
        at = 0
        for number, size in enumerate(sizes):
            total = refs[at][...]
            for ref in refs[at + 1 : at + size]:
                total = total + ref[...]
            refs[sum(sizes) + len(after) + number][...] = total
            at += size

    return pl.pallas_call(
        body,
        out_shape=tuple(shape(*group[0].shape) for group in groups),
        in_specs=[WHOLE] * sum(sizes) + [pl.BlockSpec(memory_space=pl.ANY)] * len(after),
        out_specs=tuple([WHOLE] * len(groups)),
        compiler_params=pltpu.CompilerParams(vmem_limit_bytes=4 << 20),
        cost_estimate=pl.CostEstimate(flops=int(COST), bytes_accessed=1, transcendentals=0),
        name="plus",
    )(*(term for group in groups for term in group), *after)


def plus(*terms, after=()):
    return sums([terms], after)[0]


def sum_pairs(one, two, three, four):
    def body(a, b, c, d, result):
        result[...] = (a[...] + b[...]) + (c[...] + d[...])

    return pl.pallas_call(
        body,
        out_shape=shape(*one.shape),
        in_specs=[WHOLE] * 4,
        out_specs=WHOLE,
        compiler_params=pltpu.CompilerParams(vmem_limit_bytes=1 << 20),
        name="sum_pairs",
    )(one, two, three, four)


def split_rows(one, two, cut):
    def body(one_ref, two_ref, top, rest):
        top[...] = one_ref[:cut, :]
        rest[...] = two_ref[cut:, :]

    return pl.pallas_call(
        body,
        out_shape=(shape(cut, one.shape[1]), shape(two.shape[0] - cut, two.shape[1])),
        in_specs=[WHOLE] * 2,
        out_specs=(WHOLE, WHOLE),
        compiler_params=pltpu.CompilerParams(vmem_limit_bytes=4 << 20),
        cost_estimate=pl.CostEstimate(flops=int(COST), bytes_accessed=1, transcendentals=0),
        name="split_rows",
    )(one, two)


def owner(scal, k):
    spot = jnp.bitwise_and(scal[1] + k, GROUPS - 1)
    return jnp.where(scal[2] > 0, jnp.where(spot < HALF, 2 * spot, 2 * GROUPS - 1 - 2 * spot), k)


def halves(value):
    top = value.astype(bf16)
    return top, (value - top.astype(f32)).astype(bf16)


def dot(left, right, dims):
    return lax.dot_general(left, right, (dims, ((), ())), preferred_element_type=f32)


def dot3(lh, ll, rh, rl, dims):
    (left,), (right,) = dims
    join = lambda parts, axis: jnp.concatenate([part[...] for part in parts], axis=axis)
    return dot(join([lh, lh, ll], left), join([rh, rl, rh], right), dims)


def rows_at(index, size):
    return pl.ds(pl.multiple_of(index * size, size), size)


def piece(vec, number):
    a, b = 2 * number, 2 * number + 1
    return jnp.concatenate(
        [vec[a // 3, a % 3 : a % 3 + 1, :], vec[b // 3, b % 3 : b % 3 + 1, :]], axis=1
    )


def norm_stats(inputs):
    center = inputs - jnp.mean(inputs, axis=-1, keepdims=True)
    spread = jnp.mean(center * center, axis=-1, keepdims=True)
    scale = lax.rsqrt(spread + norm_eps)
    return center * scale, scale


def norm_back(hat, scale, gain, grad):
    inner = grad * gain
    return scale * (
        inner
        - jnp.mean(inner, axis=-1, keepdims=True)
        - hat * jnp.mean(inner * hat, axis=-1, keepdims=True)
    )


def low_lanes(dims):
    return lax.broadcasted_iota(jnp.int32, dims, 1) < HEAD


def lane_pairs(pair, last):
    low = low_lanes(pair.shape)
    roll = lambda v: pltpu.roll(v, HEAD, 1)
    ph = pair.astype(bf16).astype(f32)
    pl_ = pair - ph
    lh = last.astype(bf16).astype(f32)
    ll = last - lh
    return [
        jnp.where(low, ph, roll(pl_)).astype(bf16),
        jnp.where(low, roll(ph), pl_).astype(bf16),
        jnp.where(low, lh, roll(ll)).astype(bf16),
    ]


def row_halves(turned, head):
    part = turned[HEAD * head : HEAD * (head + 1)]
    return halves(part)


def pack_first_kernel(scal, wqkv, wproj, vec, seg, valid, tokens, first, packed, *refs):
    bands, proj, lines, marks, sems = refs
    mine = scal[0]
    aligned = pl.multiple_of(jnp.bitwise_and(mine * QUARTER, -128), 128)
    copies = [
        pltpu.make_async_copy(wqkv.at[:, pl.ds(part * D + aligned, CH)], bands.at[part], sems.at[part])
        for part in range(3)
    ]
    sub = pl.ds(pl.multiple_of(mine * SUB, 8), SUB)
    copies.append(pltpu.make_async_copy(wproj.at[sub, :], proj, sems.at[3]))
    copies.append(pltpu.make_async_copy(vec, lines, sems.at[4]))
    copies.append(pltpu.make_async_copy(seg, marks.at[0], sems.at[5]))
    copies.append(pltpu.make_async_copy(valid, marks.at[1], sems.at[6]))
    copies.append(pltpu.make_async_copy(tokens, packed.at[:CH, :], sems.at[7]))
    for copy in copies:
        copy.start()
    first[ROWS:, :] = jnp.zeros((8, D), f32)
    packed[CH:, :] = jnp.zeros((8, D), f32)
    for copy in copies[:5]:
        copy.wait()
    turn = jnp.where(jnp.bitwise_and(mine, 1) > 0, CH - HEAD, 0)
    for part in range(3):
        turned = pltpu.roll(bands[part], turn, 1)
        first[:ROWS, part * CH : part * CH + QUARTER] = turned[:, :QUARTER]
        for group in range(SEQ):
            lane = HEAD * (3 * group + part)
            first[group * SUB : (group + 1) * SUB, part * CH + QUARTER : (part + 1) * CH] = proj[
                :, lane : lane + HEAD
            ]
        first[ROWS + part : ROWS + part + 1, :HALF_VEC] = jnp.concatenate(
            [lines[3 * part + i : 3 * part + i + 1, :] for i in range(3)], axis=1
        )
    for copy in copies[5:]:
        copy.wait()
    packed[CH : CH + 1, :CH] = jnp.where(marks[1] > 0, marks[0], -1).astype(f32)


def pack_second_kernel(scal, win, wout, in_block, out_block):
    mine = scal[0]
    turn = lax.rem(HALF_VEC - mine * ROWS, HALF_VEC)
    for part in range(GROUPS):
        turned = pltpu.roll(win[:, part * HALF_VEC : (part + 1) * HALF_VEC], turn, 1)
        in_block[:, part * ROWS : (part + 1) * ROWS] = turned[:, :ROWS]
    out_block[...] = wout[pl.ds(pl.multiple_of(mine * ROWS, 8), ROWS), :]


def mask_kernel(scal, cotangent, valid, result):
    keep = jnp.where(valid[...] > 0, 1.0, 0.0).astype(f32)
    column = jnp.broadcast_to(keep, (128, CH)).T[:, :1]
    result[...] = cotangent[...] * column


def weights_kernel(scal, *refs):
    blocks, (wh, wl, vec, proj) = refs[: GROUPS + 1], refs[GROUPS + 1 :]
    spans = [(k, 0, ROWS + 8) for k in range(GROUPS)]
    spans[HALF : HALF + 1] = [(HALF, 0, CUT), (HALF, CUT, ROWS + 8)]
    for ref, (k, first, last) in zip(blocks, spans):
        at = owner(scal, k)
        size = min(last, ROWS) - first
        block = ref[:size, :]
        here = pl.ds(pl.multiple_of(at * ROWS + first, CUT), size)
        wh[here, :], wl[here, :] = halves(block)
        if last > ROWS:
            vec[at] = ref[size:, :HALF_VEC]
        for group in range(SEQ):
            top, end = group * SUB - first, (group + 1) * SUB - first
            if top < 0 or end > size:
                continue
            for part in range(3):
                lane = HEAD * (3 * group + part)
                proj[pl.ds(pl.multiple_of(at * SUB, 8), SUB), lane : lane + HEAD] = block[
                    top:end, part * CH + QUARTER : (part + 1) * CH
                ]


def front_kernel(scal, *refs):
    toks, refs = refs[:4], refs[4:]
    wh, wl, vec = refs[:3]
    xh, xl, kcat, qturn, vcat, qpair, kturn, low_row, outs_turn, lse, vturn, label = refs[3:]
    mine = scal[0]

    gain, shift = piece(vec, 0), piece(vec, 1)
    turn = lax.rem(D - mine * QUARTER, D)
    own = lambda number: pltpu.roll(jnp.broadcast_to(piece(vec, number), (8, D)), turn, 1)[:1, :CH]
    query_bias, value_bias = own(2), own(3)

    for r in range(SEQ):
        nat = jnp.bitwise_xor(mine, r)
        at = rows_at(nat, CH)
        label[nat] = toks[r][CH:, :CH]
        hat, _ = norm_stats(toks[r][:CH, :])
        xh[at, :], xl[at, :] = halves(hat)
        nh, nl = halves(hat * gain + shift)
        joined = dot3(nh, nl, wh[...], wl[...], NN)
        query = (joined[:, :CH] + query_bias) * HEAD ** (-0.5)
        key = joined[:, CH : 2 * CH]
        value = joined[:, 2 * CH :] + value_bias
        keys = lane_pairs(key[:, :128], key[:, 128:])
        values = lane_pairs(value[:, :128], value[:, 128:])
        queries = lane_pairs(query[:, :128], query[:, 128:])
        key_t, value_t, query_t = key.T, value.T, query.T
        for h in range(OWN):
            kcat[h, at, :] = jnp.concatenate([keys[h], keys[h]], axis=1)
            vcat[h, at, :] = jnp.concatenate([values[h], values[h]], axis=1)
            qpair[h, at, :] = queries[h]
            a, b = row_halves(query_t, h)
            qturn[h, :, at] = jnp.concatenate([a, a, b, b], axis=0)
            a, b = row_halves(key_t, h)
            kturn[h, :, at] = jnp.concatenate([a, b], axis=0)
            a, b = row_halves(value_t, h)
            vturn[h, :, at] = jnp.concatenate([a, b], axis=0)

    labels = jnp.concatenate([label[c][:1, :] for c in range(SEQ)], axis=1)
    spot = lax.broadcasted_iota(jnp.int32, (1, LEN), 1).astype(f32)
    begin = jnp.zeros((1, LEN), f32)
    for segment in range(3):
        held = jnp.sum(jnp.where(labels == float(segment), 1.0, 0.0), axis=1, keepdims=True)
        begin = begin + jnp.where(labels > float(segment), held, 0.0)
    begin = jnp.where(labels < 0.0, spot, begin)
    low_row[...] = jnp.broadcast_to(begin, (8, LEN))

    def one_head(h, carry):
        for c in range(SEQ):
            size = CH * (c + 1)
            lanes = slice(c * CH, (c + 1) * CH)
            score = dot(kcat[h, :size, :], qturn[h, :, lanes], NN)
            mask = allowed(low_row, c, size)
            score = jnp.where(mask, score, masked_score)
            peak = jnp.max(score, axis=0, keepdims=True)
            weight = jnp.exp(score - peak)
            total = jnp.sum(weight, axis=0, keepdims=True)
            top, rest = halves(weight)
            both = dot(vturn[h, :, :size], top, NN)
            extra = dot(vturn[h, :HEAD, :size], rest, NN)
            result = (both[:HEAD] + both[HEAD:] + extra) / total
            outs_turn[pl.ds(pl.multiple_of(h * HEAD, HEAD), HEAD), lanes] = result
            lse[h, :, lanes] = jnp.broadcast_to(peak + jnp.log(total), (8, CH))
        return carry

    lax.fori_loop(0, OWN, one_head, 0)


def allowed(low_row, c, size):
    key_at = lax.broadcasted_iota(jnp.int32, (size, CH), 0).astype(f32)
    query_at = (lax.broadcasted_iota(jnp.int32, (1, CH), 1) + c * CH).astype(f32)
    begin = low_row[:1, c * CH : (c + 1) * CH]
    return (key_at >= begin) & (key_at <= query_at)


def proj_kernel(scal, *refs):
    toks, heads, parts, refs = refs[:4], refs[4:8], refs[8:12], refs[12:]
    vec, wh, wl, heads_h, heads_l, norm_h, norm_l, mixed, hat, scale, weight, joined = refs
    mine = scal[0]
    for r in range(SEQ):
        at = jnp.bitwise_xor(mine, r)
        for d in range(GROUPS):
            weight[pl.ds(pl.multiple_of(d * ROWS + at * SUB, 8), SUB), :] = parts[r][
                d * SUB : (d + 1) * SUB, :
            ]
        joined[rows_at(at, QUARTER), :] = heads[r][...]
    wh[...], wl[...] = halves(weight[...])
    heads_h[...], heads_l[...] = halves(joined[:, rows_at(mine, CH)])
    gain, shift = piece(vec, 5), piece(vec, 6)
    for r in range(SEQ):
        at = rows_at(jnp.bitwise_xor(mine, r), CH)
        a, b = halves(joined[:, at].T)
        total = toks[r][:CH, :] + dot3(a, b, wh[...], wl[...], NN)
        total = total + piece(vec, 4)
        normed, size = norm_stats(total)
        norm_h[r], norm_l[r] = halves(normed * gain + shift)
        if r == 0:
            mixed[...] = total
            hat[...] = normed
            scale[...] = jnp.broadcast_to(size, (CH, 128))


def hidden_kernel(scal, norm_h, norm_l, *refs):
    blocks, vec, acts_h, acts_l, slope, winh, winl = refs[: GROUPS + 1], *refs[GROUPS + 1 :]
    mine = scal[0]
    spans = [(k, 0) for k in range(GROUPS)]
    spans.insert(HALF + 1, (HALF, CUT))
    for ref, (k, first) in zip(blocks, spans):
        at = pl.ds(pl.multiple_of(owner(scal, k) * ROWS + first, CUT), ref.shape[0])
        winh[at, :], winl[at, :] = halves(ref[...])
    marks = [16 + d for d in range(GROUPS)]
    table = jnp.concatenate([vec[m // 3, m % 3 : m % 3 + 1, :] for m in marks], axis=0)
    table = pltpu.roll(table, lax.rem(HALF_VEC - mine * ROWS, HALF_VEC), 1)[:, :ROWS]
    bias = jnp.concatenate([table[d : d + 1] for d in range(GROUPS)], axis=1)
    for r in range(SEQ):
        at = slice(r * CH, (r + 1) * CH)
        hidden = dot3(norm_h[r], norm_l[r], winh[...], winl[...], NN) + bias
        inner = jnp.tanh(gelu_scale * (hidden + gelu_cubic * hidden * hidden * hidden))
        acts_h[at, :], acts_l[at, :] = halves(0.5 * hidden * (1.0 + inner))
        slope[at, :] = 0.5 * (1.0 + inner) + 0.5 * hidden * (1.0 - inner * inner) * gelu_scale * (
            1.0 + 3.0 * gelu_cubic * hidden * hidden
        )


def emit_blocks(scal, outs, whole):
    for k in range(GROUPS):
        outs[k][...] = whole[rows_at(owner(scal, k), ROWS), :]


def out_grad_kernel(scal, acts_h, acts_l, *refs):
    grads, (out_h, out_l), outs, whole = refs[:4], refs[4:6], refs[6 : 6 + GROUPS], refs[6 + GROUPS]
    for r in range(SEQ):
        at = slice(r * CH, (r + 1) * CH)
        out_h[at, :], out_l[at, :] = halves(grads[r][...])
    whole[...] = dot3(acts_h[...], acts_l[...], out_h[...], out_l[...], TN)
    emit_blocks(scal, outs, whole)


def hidden_back_kernel(scal, out_h, out_l, slope, winh, winl, *refs):
    blocks, refs = refs[:GROUPS], refs[GROUPS:]
    hid_h, hid_l, wouth, woutl, bias_sum = refs[:5]
    parts = refs[5:]
    for k in range(GROUPS):
        at = rows_at(owner(scal, k), ROWS)
        wouth[at, :], woutl[at, :] = halves(blocks[k][...])
    sums = jnp.zeros((1, D), f32)
    for r in (1, 3, 2, 0):
        at = slice(r * CH, (r + 1) * CH)
        back = dot3(out_h[at, :], out_l[at, :], wouth[...], woutl[...], NT) * slope[at, :]
        sums = sums + jnp.sum(back, axis=0, keepdims=True)
        bh, bl = halves(back)
        hid_h[at, :], hid_l[at, :] = bh, bl
        parts[r][...] = dot3(bh, bl, winh[...], winl[...], NT)
    bias_sum[...] = jnp.broadcast_to(sums, (8, D))


def in_grad_kernel(scal, norm_h, norm_l, hid_h, hid_l, *refs):
    outs, whole = refs[:GROUPS], refs[GROUPS]
    flat = lambda ref: ref[...].reshape(LEN, D)
    whole[...] = dot3(flat(norm_h), flat(norm_l), hid_h[...], hid_l[...], TN)
    emit_blocks(scal, outs, whole)


def ffn_out_kernel(scal, acts_h, acts_l, wouth, woutl, *parts):
    for r in (1, 3, 2, 0):
        at = slice(r * CH, (r + 1) * CH)
        parts[r][...] = dot3(acts_h[at, :], acts_l[at, :], wouth[...], woutl[...], NN)


def output_kernel(scal, mixed, one, two, three, vec, output):
    output[...] = mixed[...] + (one[...] + two[...] + three[...]) + piece(vec, 7)


def proj_back_kernel(scal, one, two, three, hat, scale, vec, grad_out, wh, wl, mixed_grad, sums, *parts):
    mine = scal[0]
    normed = one[...] + two[...] + three[...]
    back = norm_back(hat[...], scale[:, :1], piece(vec, 5), normed)
    total = grad_out[...] + back
    mixed_grad[...] = total
    a, b = halves(total)
    for r in range(SEQ):
        at = rows_at(jnp.bitwise_xor(mine, r), QUARTER)
        parts[r][...] = dot3(wh[at, :], wl[at, :], a, b, NT)
    add = lambda v: jnp.sum(v, axis=0, keepdims=True)
    sums[...] = jnp.concatenate(
        [add(total), add(normed * hat[...]), add(normed), add(grad_out[...]), jnp.zeros((4, D), f32)],
        axis=0,
    )


def proj_grad_kernel(scal, heads_h, heads_l, mixed_grad, *refs):
    outs, whole = refs[:-1], refs[-1]
    mine = scal[0]
    gh, gl = halves(mixed_grad[...])
    whole[...] = dot3(heads_h[...], heads_l[...], gh, gl, NN)
    for r in range(SEQ):
        at = jnp.bitwise_xor(mine, r)
        for d in range(GROUPS):
            outs[r][d * SUB : (d + 1) * SUB, :] = whole[
                pl.ds(pl.multiple_of(d * ROWS + at * SUB, 8), SUB), :
            ]


def back_kernel(scal, *refs):
    grads, refs = refs[:4], refs[4:]
    kcat, qturn, vcat, qpair, kturn, outs_turn, lse, low_row = refs[:8]
    joined_h, joined_l, joined_sums = refs[8:11]
    gturn, gpair, dots, key_sum, value_sum, query_turn = refs[11:]
    mine = scal[0]

    for r in range(SEQ):
        at = rows_at(jnp.bitwise_xor(mine, r), CH)
        turned = grads[r][...]
        grad = jnp.concatenate([turned, jnp.zeros((HEAD, CH), f32)], axis=0).T
        pairs = lane_pairs(grad[:, :128], grad[:, 128:])
        for h in range(OWN):
            gpair[h, at, :] = pairs[h]
            part = turned[HEAD * h : HEAD * (h + 1)]
            dots[h, :, at] = jnp.broadcast_to(
                jnp.sum(part * outs_turn[HEAD * h : HEAD * (h + 1), at], axis=0, keepdims=True), (8, CH)
            )
            a, b = halves(part)
            gturn[h, :, at] = jnp.concatenate([a, a, b, b], axis=0)

    key_sum[...] = jnp.zeros_like(key_sum)
    value_sum[...] = jnp.zeros_like(value_sum)

    def one_head(h, carry):
        for c in range(SEQ):
            size = CH * (c + 1)
            lanes = slice(c * CH, (c + 1) * CH)
            score = dot(kcat[h, :size, :], qturn[h, :, lanes], NN)
            weight = jnp.where(allowed(low_row, c, size), jnp.exp(score - lse[h, :1, lanes]), 0.0)
            back = dot(vcat[h, :size, :], gturn[h, :, lanes], NN)
            score_back = weight * (back - dots[h, :1, lanes])
            a, b = halves(weight)
            pair = gpair[h, lanes, :]
            value_sum[h, :size, :] += dot(a, pair, NN) + dot(b, pair, NN)
            a, b = halves(score_back)
            pair = qpair[h, lanes, :]
            key_sum[h, :size, :] += dot(a, pair, NN) + dot(b, pair, NN)
            turned = dot(kturn[h, :, :size], a, NN) + dot(kturn[h, :, :size], b, NN)
            query_turn[h, :, lanes] = (turned[:HEAD] + turned[HEAD:]) * HEAD ** (-0.5)
        return carry

    lax.fori_loop(0, OWN, one_head, 0)

    column_sums = jnp.zeros((1, D), f32)
    low = low_lanes((CH, 128))
    for c in range(SEQ):
        at = slice(c * CH, (c + 1) * CH)
        blank = jnp.zeros((HEAD, CH), f32)
        query = jnp.concatenate([query_turn[h, :, at] for h in range(OWN)] + [blank], axis=0).T
        done = [query]
        for kept in (key_sum, value_sum):
            full = [kept[h, at, :] for h in range(OWN)]
            full = [v + pltpu.roll(v, HEAD, 1) for v in full]
            done.append(jnp.where(low, full[0], full[1]))
            done.append(jnp.where(low, full[2], 0.0))
        joined = jnp.concatenate(done, axis=1)
        column_sums = column_sums + jnp.sum(joined, axis=0, keepdims=True)
        joined_h[at, :], joined_l[at, :] = halves(joined)

    joined_sums[...] = jnp.broadcast_to(column_sums, (8, D))


def qkv_grad_kernel(scal, xh, xl, joined_h, joined_l, joined_sums, wh, wl, vec, *refs):
    proj_one, proj_two, vector_sums, bias_sum = refs[:4]
    outs, (whole, rows) = refs[4 : 4 + GROUPS], refs[4 + GROUPS :]
    mine = scal[0]
    column_sums = joined_sums[:1, :]
    core = dot3(xh[...], xl[...], joined_h[...], joined_l[...], TN)
    gain, shift = piece(vec, 0), piece(vec, 1)
    as_column = lambda v: jnp.broadcast_to(v, (128, D)).T[:, :1]
    whole[...] = as_column(gain) * core + as_column(shift) * column_sums
    weights = wh[...].astype(f32) + wl[...].astype(f32)
    gain_grad = jnp.sum(weights * core, axis=1, keepdims=True)
    shift_grad = jnp.sum(weights * column_sums, axis=1, keepdims=True)
    lane = lax.broadcasted_iota(jnp.int32, (D, 128), 1)
    norm_grads = jnp.where(lane == 0, gain_grad, shift_grad).T

    def place(part, scale):
        wide = jnp.concatenate([part[:, :QUARTER], jnp.zeros((1, D - QUARTER), f32)], axis=1)
        wide = jnp.broadcast_to(wide, (8, D))
        return pltpu.roll(wide, mine * QUARTER, 1)[:1]

    entries = [
        norm_grads[0:1],
        norm_grads[1:2],
        place(column_sums[:, :CH], 1.0),
        place(column_sums[:, 2 * CH :], 1.0),
        vector_sums[0:1],
        vector_sums[1:2],
        vector_sums[2:3],
        vector_sums[3:4],
    ]
    lines = [e[:, i * HALF_VEC : (i + 1) * HALF_VEC] for e in entries for i in range(2)]
    bias = jnp.concatenate(
        [bias_sum[:1, d * ROWS : (d + 1) * ROWS] for d in range(GROUPS)], axis=0
    )
    bias = jnp.concatenate([bias, jnp.zeros((GROUPS, HALF_VEC - ROWS), f32)], axis=1)
    bias = pltpu.roll(bias, mine * ROWS, 1)
    lines = lines + [bias[d : d + 1] for d in range(GROUPS)]
    filler = jnp.zeros((5, HALF_VEC), f32)
    for d in range(GROUPS):
        rows[d] = jnp.concatenate(lines[3 * d : 3 * d + 3] + [filler], axis=0)

    for k in range(GROUPS):
        at = owner(scal, k)
        outs[k][:ROWS, :] = whole[rows_at(at, ROWS), :]
        here = pl.ds(pl.multiple_of(at * SUB, 8), SUB)
        proj = proj_one[here, :] + proj_two[here, :]
        for group in range(SEQ):
            for part in range(3):
                lane_at = HEAD * (3 * group + part)
                outs[k][
                    group * SUB : (group + 1) * SUB, part * CH + QUARTER : (part + 1) * CH
                ] = proj[:, lane_at : lane_at + HEAD]
        outs[k][ROWS:, :HALF_VEC] = rows[at]
        outs[k][ROWS:, HALF_VEC:] = jnp.zeros((8, HALF_VEC), f32)


def pre_back_kernel(scal, joined_h, joined_l, wh, wl, *parts):
    mine = scal[0]
    for r in (1, 3, 2, 0):
        at = rows_at(jnp.bitwise_xor(mine, r), CH)
        parts[r][...] = dot3(joined_h[at, :], joined_l[at, :], wh[...], wl[...], NT)


def input_grad_kernel(scal, tokens, one, two, three, vec, mixed_grad, result):
    hat, scale = norm_stats(tokens[...])
    grad = one[...] + two[...] + three[...]
    result[...] = mixed_grad[...] + norm_back(hat, scale, piece(vec, 0), grad)


def total_square(value):
    return jnp.sum(jnp.sum(value * value, axis=0, keepdims=True), axis=1, keepdims=True)


def shard_sums_kernel(scal, first, in_shard, out_shard, small):
    total = total_square(first[:ROWS, :]) + total_square(in_shard[...]) + total_square(out_shard[...])
    small[...] = first[ROWS:, :]
    small[7:8, :] = jnp.broadcast_to(total, (1, D))


def shard_squares_kernel(scal, one, two, three, four, squares):
    whole = (one[...] + two[...]) + (three[...] + four[...])
    squares[...] = jnp.broadcast_to(whole[7:8, :1] + total_square(whole[:3, :HALF_VEC]), (8, 128))


def stage_kernel(scal, *refs):
    sources, targets, sems = refs[:15], refs[15:30], refs[30]
    copies = [
        pltpu.make_async_copy(source, target, sems.at[i])
        for i, (source, target) in enumerate(zip(sources, targets))
    ]
    for copy in copies:
        copy.start()
    for copy in copies:
        copy.wait()


def adamw_kernel(scal, squares, *refs):
    firsts, ins, outs, refs = refs[:4], refs[4:8], refs[8:12], refs[12:]
    states, clip, finals, news = refs[:15], refs[15], refs[16:31], refs[31:46]
    first, second, sems = refs[46:]
    send = lambda number: [
        pltpu.make_async_copy(news[i], finals[i], sems.at[i]) for i in range(3 * number, 3 * number + 3)
    ]
    mine = scal[0]
    norm = jnp.sqrt(squares[...])
    clip[...] = norm
    factor = (clip_limit / jnp.maximum(norm, clip_limit))[:1, :1]
    for r in range(SEQ):
        at = jnp.bitwise_xor(mine, r)
        first[at] = firsts[r][:ROWS, :]
        second[at, :ROWS] = ins[r][...]
        second[at, ROWS:] = outs[r][...]

    def update(number, spot, grad, rate, decay):
        held = [states[3 * number + i][spot] for i in range(3)]
        fresh = adamw_update(*held, factor * grad, rate, decay)
        for i in range(3):
            news[3 * number + i][spot] = fresh[i]

    def finish(number):
        for copy in send(number):
            copy.start()

    lines = [firsts[r][ROWS:, :HALF_VEC] for r in range(SEQ)]
    line = (lines[0] + lines[1]) + (lines[2] + lines[3])
    for i in range(3):
        for j in range(3):
            spot = (slice(3 * i + j, 3 * i + j + 1), slice(None))
            update(0, spot, line[i : i + 1, 128 * j : 128 * (j + 1)], vector_rate, 0.0)
    finish(0)
    every = slice(None)
    for part in range(3):
        grad = jnp.concatenate(
            [first[j][:, part * CH : part * CH + QUARTER] for j in range(SEQ)], axis=1
        )
        update(1, (every, slice(part * D, (part + 1) * D)), grad, matrix_rate, weight_decay)
    finish(1)
    for j in range(SEQ):
        grad = jnp.concatenate(
            [
                first[j][group * SUB : (group + 1) * SUB, part * CH + QUARTER : (part + 1) * CH]
                for group in range(SEQ)
                for part in range(3)
            ],
            axis=1,
        )
        update(2, (slice(j * SUB, (j + 1) * SUB), every), grad, matrix_rate, weight_decay)
    finish(2)
    for d in range(GROUPS):
        grad = jnp.concatenate(
            [second[j][:ROWS, d * ROWS : (d + 1) * ROWS] for j in range(SEQ)], axis=1
        )
        update(3, (every, slice(d * HALF_VEC, (d + 1) * HALF_VEC)), grad, matrix_rate, weight_decay)
    finish(3)
    for j in range(SEQ):
        update(
            4, (slice(j * ROWS, (j + 1) * ROWS), every), second[j][ROWS:, :], matrix_rate, weight_decay
        )
    finish(4)
    for number in range(5):
        for copy in send(number):
            copy.wait()


def adamw_update(weight, first, second, grad, rate, decay):
    new_first = beta_one * first + (1.0 - beta_one) * grad
    new_second = beta_two * second + (1.0 - beta_two) * grad * grad
    first_hat = new_first / (1.0 - beta_one**STEP)
    second_hat = new_second / (1.0 - beta_two**STEP)
    new_weight = weight - rate * (first_hat / (jnp.sqrt(second_hat) + adam_eps) + decay * weight)
    return (new_first, new_second, new_weight)


def ring_tables(count):
    evens = [2 * i for i in range(count // 2)]
    order = evens + [i + 1 for i in reversed(evens)]
    place = [0] * count
    for position, device in enumerate(order):
        place[device] = position
    right = [(order[i], order[(i + 1) % count]) for i in range(count)]
    left = [(b, a) for a, b in right]
    return order, place, right, left


class RingGather:
    def __init__(self, block, name, flip=False):
        _, _, self.right, self.left = ring_tables(GROUPS)
        if flip:
            self.right, self.left = self.left, self.right
        self.got, self.name, self.at, self.flip = {0: block}, name, 0, flip

    def step(self, after=()):
        places = (-self.at % GROUPS, self.at)
        if after:
            for place in set(places):
                self.got[place] = gate(self.got[place], after)
        forth, back = (self.got[place] for place in places)
        self.at += 1
        self.got[GROUPS - self.at] = move(forth, "dp", self.right, f"{self.name}_right_{self.at}")
        if self.at < HALF:
            self.got[self.at] = move(back, "dp", self.left, f"{self.name}_left_{self.at}")
        return [self.got[GROUPS - self.at]] + ([self.got[self.at]] if self.at < HALF else [])

    def halved(self, cut):
        top, rest = split_rows(self.got[GROUPS - self.at], self.got[self.at], cut)
        self.at += 1
        self.got[HALF] = move(top, "dp", self.right, f"{self.name}_right_{self.at}")
        self.got[GROUPS] = move(rest, "dp", self.left, f"{self.name}_left_{self.at}")
        return [self.got[HALF], self.got[GROUPS]]

    def blocks(self):
        blocks = [self.got[-k % GROUPS if self.flip else k] for k in range(GROUPS)]
        if GROUPS in self.got:
            blocks.insert(HALF + 1, self.got[GROUPS])
        return blocks


class RingScatter:
    def __init__(self, blocks, name, flip=False):
        _, _, self.right, self.left = ring_tables(GROUPS)
        self.blocks = blocks
        if flip:
            self.right, self.left = self.left, self.right
            self.blocks = [blocks[-k % GROUPS] for k in range(GROUPS)]
        self.name, self.back, self.at = name, None, HALF
        self.forth = move(self.blocks[HALF], "dp", self.right, f"{name}_right_1")

    def step(self, after=()):
        self.at -= 1
        ahead, back = self.blocks[self.at], self.blocks[GROUPS - self.at]
        if self.back is None:
            forth = plus(self.forth, ahead, after=after)
        else:
            forth, back = sums([(self.forth, ahead), (self.back, back)], after)
        number = HALF + 1 - self.at
        self.forth = move(forth, "dp", self.right, f"{self.name}_right_{number}")
        self.back = move(back, "dp", self.left, f"{self.name}_left_{number}")
        return [forth, back]

    def result(self, after=()):
        return plus(self.forth, self.back, self.blocks[0], after=after)


def move(block, axis, pairs, name):
    with jax.named_scope(name):
        return lax.ppermute(block, axis, pairs)


def swap(block, bits, name):
    return move(block, "seq", [(i, i ^ bits) for i in range(SEQ)], f"{name}_{bits}")


def gather_seq(block, name):
    across = swap(block, 2, name)
    core = swap(block, 1, name)
    return [block, core, across, swap(across, 1, f"{name}_2")]


def exchange_seq(parts, name):
    return [parts[0]] + [swap(parts[r], r, name) for r in range(1, SEQ)]


def scatter_core(parts, name):
    return parts[0], swap(parts[1], 1, f"{name}_own"), parts[2], swap(parts[3], 1, f"{name}_across")


def ordered(blocks, mine):
    stack = jnp.stack(blocks, axis=0)
    return [lax.dynamic_index_in_dim(stack, mine ^ j, 0, keepdims=False) for j in range(len(blocks))]


def local(
    tokens,
    cotangent,
    segment_ids,
    valid,
    vectors,
    vec_first,
    vec_second,
    w_qkv,
    qkv_first,
    qkv_second,
    w_proj,
    proj_first,
    proj_second,
    w_in,
    in_first,
    in_second,
    w_out,
    out_first,
    out_second,
):
    dp_parts = lax.axis_size("dp")
    ring = dp_parts == GROUPS
    mine = lax.axis_index("seq")
    home = lax.axis_index("dp")
    rows = w_qkv.shape[0]
    units = w_out.shape[0] // SEQ
    far, near = home // 2, home % 2
    position = jnp.where(near > 0, GROUPS - 1 - far, far)
    scal = jnp.stack([mine, position, jnp.full_like(mine, 1 if ring else 0)]).astype(jnp.int32)
    flat_in = tokens.reshape(CH, D)
    chunk, tall, square = shape(CH, D), shape(LEN, D, kind=bf16), shape(D, D, kind=bf16)

    if ring:
        first, packed = run(
            pack_first_kernel,
            scal,
            [w_qkv, w_proj, vectors.reshape(9, 128), segment_ids, valid, flat_in],
            [shape(ROWS + 8, D), shape(CH + 8, D)],
            scratch=[
                pltpu.VMEM((3, ROWS, CH), f32),
                pltpu.VMEM((SUB, D), f32),
                pltpu.VMEM((9, 128), f32),
                pltpu.VMEM((2, 1, CH), jnp.int32),
            ],
            sems=8,
            far_args=range(6),
            room=54,
            name="pack_first", work=3.0,
        )
        ring_first = RingGather(first, "first")
        for _ in range(HALF - 1):
            ring_first.step()
        ring_first.halved(CUT)
        firsts = ring_first.blocks()
        in_block, out_block = run(
            pack_second_kernel,
            scal,
            [w_in, w_out],
            [shape(ROWS, D)] * 2,
            name="pack_second", work=3.0,
            after=[firsts[GROUPS]],
        )
        ring_in = RingGather(in_block, "w_in")
        ring_out = RingGather(out_block, "w_out", flip=True)
        came = ring_in.step([firsts[HALF], firsts[HALF + 1]])
        came = came + ring_out.step([firsts[HALF], firsts[HALF + 1]])
    else:
        padded = jnp.pad(w_qkv, ((0, 0), (0, CH)))
        own = lambda part: lax.dynamic_slice_in_dim(padded, part * D + mine * QUARTER, CH, 1)
        first = jnp.concatenate([own(0), own(1), own(2)], axis=1)
        first = lax.all_gather(first, "dp", axis=0, tiled=True).reshape(GROUPS, ROWS, D)
        all_vec = lax.all_gather(vectors, "dp", axis=0, tiled=True).reshape(GROUPS, 3, HALF_VEC)
        first = jnp.concatenate([first, jnp.pad(all_vec, ((0, 0), (0, 5), (0, D - HALF_VEC)))], axis=1)
        firsts = [first[k] for k in range(GROUPS)]
        firsts[HALF : HALF + 1] = [first[HALF, :CUT], first[HALF, CUT:]]
        in_part = lax.dynamic_index_in_dim(
            w_in.reshape(rows, dp_parts, SEQ, units), mine, 2, keepdims=False
        ).reshape(rows, D)
        out_part = lax.dynamic_slice_in_dim(w_out, mine * units, units, 0)
        in_blocks, out_blocks = (
            list(lax.all_gather(part, "dp", axis=0, tiled=True).reshape(GROUPS, ROWS, D))
            for part in (in_part, out_part)
        )
        in_blocks[HALF : HALF + 1] = [in_blocks[HALF][:CUT], in_blocks[HALF][CUT:]]
        marks = jnp.where(valid > 0, segment_ids, -1).astype(f32)
        packed = jnp.concatenate([flat_in, jnp.pad(marks, ((0, 7), (0, D - CH)))], axis=0)
    toks = gather_seq(packed, "tokens")
    (grad_out,) = run(
        mask_kernel, scal, [cotangent.reshape(CH, D), valid], [chunk], name="mask", work=2.0, after=[toks[2]]
    )
    grads_row = gather_seq(grad_out, "cotangent")

    qkv_h, qkv_l, vec, proj = run(
        weights_kernel,
        scal,
        firsts,
        [square, square, shape(GROUPS, 8, HALF_VEC), shape(GROUPS * SUB, D)],
        name="weights", work=3.0,
    )
    if ring:
        proj_parts = gather_seq(proj, "w_proj")
    else:
        full = lax.all_gather(w_proj, "dp", axis=0, tiled=True).reshape(GROUPS, SEQ, SUB, D)
        proj_parts = [
            lax.dynamic_index_in_dim(full, mine ^ r, 1, keepdims=False).reshape(GROUPS * SUB, D)
            for r in range(SEQ)
        ]
    hat_h, hat_l, kcat, qturn, vcat, qpair, kturn, low_row, heads, lse = run(
        front_kernel,
        scal,
        toks + [qkv_h, qkv_l, vec],
        [
            tall,
            tall,
            shape(OWN, LEN, 256, kind=bf16),
            shape(OWN, 256, LEN, kind=bf16),
            shape(OWN, LEN, 256, kind=bf16),
            shape(OWN, LEN, 128, kind=bf16),
            shape(OWN, 128, LEN, kind=bf16),
            shape(8, LEN),
            shape(QUARTER, LEN),
            shape(OWN, 8, LEN),
        ],
        scratch=[pltpu.VMEM((OWN, 128, LEN), bf16), pltpu.VMEM((SEQ, 8, CH), f32)],
        name="front", work=14.0,
        after=[grads_row[2]],
    )
    if ring:
        heads = gate(heads, [proj_parts[2], *came])
        ring_in.step([lse])
        came = ring_in.step()
        came = came + ring_in.halved(CUT)
        ring_out.step(came)
        in_blocks = ring_in.blocks()
    across = swap(heads, 2, "heads")
    if ring:
        across = gate(across, came)
    all_heads = [heads, swap(heads, 1, "heads"), across, swap(across, 1, "heads_2")]
    wide = shape(D, CH, kind=bf16)
    split = shape(SEQ, CH, D, kind=bf16)
    proj_h, proj_l, heads_h, heads_l, norm_h, norm_l, mixed, hat_two, scale_two = run(
        proj_kernel,
        scal,
        toks + all_heads + proj_parts + [vec],
        [square, square, wide, wide, split, split, chunk, chunk, shape(CH, 128)],
        scratch=[pltpu.VMEM((D, D), f32), pltpu.VMEM((D, LEN), f32)],
        name="proj", work=8.0,
    )

    if ring:
        ring_out.step([norm_h])
        ring_out.step()
        out_blocks = ring_out.blocks()
    block = shape(ROWS, D)
    acts_h, acts_l, slope, in_wh, in_wl = run(
        hidden_kernel,
        scal,
        [norm_h, norm_l] + in_blocks + [vec],
        [tall, tall, shape(LEN, D), square, square],
        name="hidden", work=8.0,
    )
    done = run(
        out_grad_kernel,
        scal,
        [acts_h, acts_l] + grads_row,
        [tall, tall] + [block] * GROUPS,
        scratch=[pltpu.VMEM((D, D), f32)],
        name="out_grad", work=5.0,
    )
    out_h, out_l = done[:2]
    out_grads = list(done[2:])
    if ring:
        ring_out = RingScatter(out_grads, "out_grad")
    done = run(
        hidden_back_kernel,
        scal,
        [out_h, out_l, slope, in_wh, in_wl] + out_blocks,
        [tall, tall, square, square, shape(8, D)] + [chunk] * SEQ,
        name="hidden_back", work=11.0,
        after=out_grads[:1],
    )
    hid_h, hid_l, out_wh, out_wl, bias_sum = done[:5]
    parts = list(done[5:])
    if ring:
        parts[3] = gate(parts[3], ring_out.step([bias_sum]))
    norm_own, norm_near, norm_across, norm_far = scatter_core(parts, "norm_grad")
    norm_pair = plus(norm_across, norm_far)
    norm_last = swap(norm_pair, 2, "norm_grad")
    in_grads = list(
        run(
            in_grad_kernel,
            scal,
            [norm_h, norm_l, hid_h, hid_l],
            [block] * GROUPS,
            scratch=[pltpu.VMEM((D, D), f32)],
            name="in_grad", work=5.0,
            after=[norm_pair],
        )
    )
    if ring:
        ring_in = RingScatter(in_grads, "in_grad", flip=True)
        out_sent = ring_out.step()
        in_sent = ring_in.step()
    done = run(
        proj_back_kernel,
        scal,
        [norm_own, norm_near, norm_last, hat_two, scale_two, vec, grad_out, proj_h, proj_l],
        [chunk, shape(8, D)] + [shape(QUARTER, CH)] * SEQ,
        name="proj_back", work=5.0,
        after=out_sent + in_sent if ring else [],
    )
    mixed_grad, vector_sums = done[:2]
    head_grads = exchange_seq(list(done[2:]), "head_grad")
    if ring:
        out_sent = ring_out.step([mixed_grad])
        in_sent = ring_in.step([mixed_grad])
    out_parts = run(
        ffn_out_kernel,
        scal,
        [acts_h, acts_l, out_wh, out_wl],
        [chunk] * SEQ,
        name="ffn_out", work=7.0,
        after=[mixed_grad],
    )
    proj_grads = run(
        proj_grad_kernel,
        scal,
        [heads_h, heads_l, mixed_grad],
        [shape(GROUPS * SUB, D)] * SEQ,
        scratch=[pltpu.VMEM((D, D), f32)],
        name="proj_grad", work=4.0,
        after=[*head_grads[1:], *out_sent, *in_sent, out_parts[0]] if ring else [],
    )
    wait = [head_grads[3], head_grads[2]]
    out_own, out_near, out_across, out_far = scatter_core(out_parts, "output")
    if ring:
        proj_own, proj_near, proj_across, proj_far = scatter_core(proj_grads, "proj_grad")
        proj_pair, proj_base, out_pair = sums(
            [(proj_across, proj_far), (proj_own, proj_near), (out_across, out_far)], wait
        )
        proj_last = swap(proj_pair, 2, "proj_grad")
    else:
        proj_base = proj_last = proj_grads[0]
        out_pair = plus(out_across, out_far)
    joined_h, joined_l, joined_sums = run(
        back_kernel,
        scal,
        head_grads + [kcat, qturn, vcat, qpair, kturn, heads, lse, low_row],
        [tall, tall, shape(8, D)],
        scratch=[
            pltpu.VMEM((OWN, 256, LEN), bf16),
            pltpu.VMEM((OWN, LEN, 128), bf16),
            pltpu.VMEM((OWN, 8, LEN), f32),
            pltpu.VMEM((OWN, LEN, 128), f32),
            pltpu.VMEM((OWN, LEN, 128), f32),
            pltpu.VMEM((OWN, HEAD, LEN), f32),
        ],
        name="back", work=16.0,
        after=[proj_grads[0]],
    )
    out_last = swap(gate(out_pair, [joined_sums]), 2, "output")
    if ring:
        shard_out = ring_out.result([joined_sums])
        in_sent = ring_in.step([joined_sums])
    done = run(
        qkv_grad_kernel,
        scal,
        [hat_h, hat_l, joined_h, joined_l, joined_sums, qkv_h, qkv_l, vec]
        + [proj_base, proj_last, vector_sums, bias_sum],
        [shape(ROWS + 8, D)] * GROUPS,
        scratch=[pltpu.VMEM((D, D), f32), pltpu.VMEM((GROUPS, 8, HALF_VEC), f32)],
        name="qkv_grad", work=1.0,
        after=[*in_sent, shard_out] if ring else [],
    )
    first_grads = list(done)
    if ring:
        shard_in = ring_in.result([first_grads[0]])
        out_all = gather_seq(shard_out, "out_shard")
        in_all = gather_seq(shard_in, "in_shard")
        first_grads[HALF] = gate(first_grads[HALF], [shard_in])
        ring_first = RingScatter(first_grads, "first_grad")
        first_sent = ring_first.step([out_last])
    pre_parts = run(
        pre_back_kernel,
        scal,
        [joined_h, joined_l, qkv_h, qkv_l],
        [chunk] * SEQ,
        name="pre_back", work=1.0,
        after=[shard_in, *first_sent] if ring else [],
    )
    pre_parts = list(pre_parts)
    if ring:
        first_sent = ring_first.step()
        pre_parts[3] = gate(pre_parts[3], [*first_sent, out_all[2]])
    pre_own, pre_near, pre_across, pre_far = scatter_core(pre_parts, "pre_grad")
    pre_pair = plus(pre_across, pre_far, after=[in_all[2]] if ring else [])
    pre_last = swap(pre_pair, 2, "pre_grad")
    states = [vectors, vec_first, vec_second, w_qkv, qkv_first, qkv_second, w_proj, proj_first, proj_second]
    states = states + [w_in, in_first, in_second, w_out, out_first, out_second]
    last_sent = ring_first.step() if ring else []
    (output,) = run(
        output_kernel,
        scal,
        [mixed, out_own, out_near, out_last, vec],
        [chunk],
        name="output", work=2.0,
        after=last_sent,
    )
    if ring:
        held = [v.reshape(9, 128) for v in states[:3]] + states[3:]
        held = run(
            stage_kernel,
            scal,
            held,
            [shape(*v.shape) for v in held],
            sems=15,
            far_args=range(15),
            name="stage", work=3.0,
            after=last_sent,
        )
        shard_first = ring_first.result([output, held[3]])
    (input_grad,) = run(
        input_grad_kernel,
        scal,
        [flat_in, pre_own, pre_near, pre_last, vec, mixed_grad],
        [chunk],
        name="input_grad", work=3.0,
    )

    if ring:
        (small,) = run(
            shard_sums_kernel, scal, [shard_first, shard_in, shard_out], [shape(8, D)], name="shard_sums", work=1.0
        )
        shard_first = gate(shard_first, [pre_last])
        across = swap(shard_first, 2, "first_shard")
        core = swap(shard_first, 1, "first_shard")
        (squares,) = run(
            shard_squares_kernel,
            scal,
            [small] + [swap(small, bits, "small") for bits in (1, 2, 3)],
            [shape(8, 128)],
            name="shard_squares", work=1.0,
        )
        flipped = lambda bits: [(i, i ^ bits) for i in range(GROUPS)]
        one, two, three = (move(squares, "dp", flipped(bits), "squares") for bits in (1, 2, 3))
        squares = sum_pairs(squares, one, two, three)
        across = gate(across, [input_grad, squares])
        first_all = [shard_first, core, across, swap(across, 1, "first_shard_2")]
        squares = plus(squares, move(squares, "dp", flipped(4), "squares"))
        done = run(
            adamw_kernel,
            scal,
            [squares] + first_all + in_all + out_all + list(held),
            [shape(8, 128)] + [shape(*v.shape) for v in held],
            scratch=[pltpu.VMEM(v.shape, f32) for v in held]
            + [pltpu.VMEM((SEQ, ROWS, D), f32), pltpu.VMEM((SEQ, 2 * ROWS, D), f32)],
            sems=15,
            far_outs=range(1, 16),
            name="adamw", work=0.1,
        )
        new = [v.reshape(-1) for v in done[1:4]] + list(done[4:])
        clip_norm = done[0][0, 0]
    else:
        by_group = jnp.stack(first_grads)
        shard_first = lax.psum_scatter(
            by_group[:, :ROWS].reshape(D, D), "dp", scatter_dimension=0, tiled=True
        )
        proj_full = jnp.stack([p.reshape(GROUPS, SUB, D) for p in ordered(proj_grads, mine)], axis=1)
        proj_grad = lax.psum(
            lax.psum_scatter(proj_full.reshape(D, D), "dp", scatter_dimension=0, tiled=True), "seq"
        )
        all_vec = lax.psum(by_group[:, ROWS : ROWS + 3, :HALF_VEC], ("dp", "seq")).reshape(-1)
        vec_grad = lax.dynamic_slice_in_dim(all_vec, home * vectors.shape[0], vectors.shape[0])
        joined = lax.all_gather(shard_first, "seq", axis=0, tiled=False)
        qkv_grad = jnp.concatenate(
            [joined[j, :, i * CH : i * CH + QUARTER] for i in range(3) for j in range(SEQ)], axis=1
        )
        shard_in, shard_out = (
            lax.psum_scatter(jnp.concatenate(parts, axis=0), "dp", scatter_dimension=0, tiled=True)
            for parts in (in_grads, out_grads)
        )
        in_all = lax.all_gather(shard_in, "seq", axis=0, tiled=False)
        in_grad = in_all.reshape(SEQ, rows, dp_parts, units).transpose(1, 2, 0, 3).reshape(rows, -1)
        out_grad = lax.all_gather(shard_out, "seq", axis=0, tiled=True)
        total = sum(jnp.sum(g * g) for g in (qkv_grad, proj_grad, in_grad, out_grad, vec_grad))
        total = lax.psum(total, "dp")
        clip_norm = jnp.sqrt(total)
        factor = clip_limit / jnp.maximum(clip_norm, clip_limit)
        grads = (vec_grad, qkv_grad, proj_grad, in_grad, out_grad)
        new = []
        for number, grad in enumerate(grads):
            rate, decay = (matrix_rate, weight_decay) if number else (vector_rate, 0.0)
            new.extend(adamw_update(*states[3 * number : 3 * number + 3], factor * grad, rate, decay))
    return (output.reshape(tokens.shape), input_grad.reshape(tokens.shape), clip_norm, *new)


def solution(mesh):
    row = P("dp", "seq", None)
    mark = P("dp", "seq")
    vec = P("dp")
    mat = P("dp", None)
    return jax.shard_map(
        local,
        mesh=mesh,
        in_specs=(row, row, mark, mark) + (vec,) * 3 + (mat,) * 12,
        out_specs=(row, row, P()) + (vec,) * 3 + (mat,) * 12,
        check_vma=False,
    )
```

```python
import functools
import math

import jax
import jax.numpy as jnp
from jax import lax
from jax.experimental import pallas as pl
from jax.experimental.pallas import tpu as pltpu
from jax.sharding import PartitionSpec as P

D = 768
HEADS = 12
HEAD = 64
STEP = 10
CH = 256
LEN = 1024
SEQ = 4
QUARTER = D // SEQ
OWN = HEADS // SEQ
GROUPS = 8
ROWS = D // GROUPS
SUB = ROWS // SEQ
HALF = GROUPS // 2
CUT = ROWS // 2
HALF_VEC = D // 2
VEC_ROWS = 24

f32 = jnp.float32
bf16 = jnp.bfloat16
masked_score = -1e30
norm_eps = 1e-05
clip_limit = 1.0
beta_one = 0.9
beta_two = 0.999
adam_eps = 1e-08
matrix_rate = 0.02
vector_rate = 0.4
weight_decay = 0.01
gelu_scale = 0.7978845608028654
gelu_cubic = 0.044715

COST = 1e9

WHOLE = pl.BlockSpec(memory_space=pltpu.VMEM)
SCALARS = pl.BlockSpec(memory_space=pltpu.SMEM)
NN = ((1,), (0,))
NT = ((1,), (1,))
TN = ((0,), (0,))


def shape(*dims, kind=f32):
    return jax.ShapeDtypeStruct(dims, kind)


def run(
    kernel, scal, args, outs, scratch=(), sems=0, far_args=(), far_outs=(), room=8, work=1.0, name=None, after=()
):
    args, after = list(args), list(after)
    held = sum(math.prod(v.shape) * jnp.dtype(v.dtype).itemsize for v in scratch)
    anywhere, far = pl.BlockSpec(memory_space=pl.ANY), pl.BlockSpec(memory_space=pltpu.HBM)
    scratch = list(scratch) + ([pltpu.SemaphoreType.DMA((sems,))] if sems else [])

    def body(scal_ref, *refs):
        kernel(scal_ref, *refs[: len(args)], *refs[len(args) + len(after) :])

    return pl.pallas_call(
        body,
        out_shape=tuple(outs),
        in_specs=[SCALARS]
        + [far if i in far_args else WHOLE for i in range(len(args))]
        + [anywhere] * len(after),
        out_specs=tuple(far if i in far_outs else WHOLE for i in range(len(outs))),
        scratch_shapes=scratch,
        compiler_params=pltpu.CompilerParams(vmem_limit_bytes=held + (room << 20)),
        cost_estimate=pl.CostEstimate(
            flops=int(work * COST), bytes_accessed=1, transcendentals=0
        ),
        name=name,
    )(scal, *args, *after)


def gate(value, after):
    anywhere = pl.BlockSpec(memory_space=pl.ANY)
    return pl.pallas_call(
        lambda *refs: None,
        out_shape=shape(*value.shape, kind=value.dtype),
        in_specs=[anywhere] * (1 + len(after)),
        out_specs=anywhere,
        input_output_aliases={0: 0},
        compiler_params=pltpu.CompilerParams(vmem_limit_bytes=1 << 20),
        name="gate",
    )(value, *after)


def sums(groups, after=()):
    sizes = [len(group) for group in groups]

    def body(*refs):
        at = 0
        for number, size in enumerate(sizes):
            total = refs[at][...]
            for ref in refs[at + 1 : at + size]:
                total = total + ref[...]
            refs[sum(sizes) + len(after) + number][...] = total
            at += size

    return pl.pallas_call(
        body,
        out_shape=tuple(shape(*group[0].shape) for group in groups),
        in_specs=[WHOLE] * sum(sizes) + [pl.BlockSpec(memory_space=pl.ANY)] * len(after),
        out_specs=tuple([WHOLE] * len(groups)),
        compiler_params=pltpu.CompilerParams(vmem_limit_bytes=4 << 20),
        cost_estimate=pl.CostEstimate(flops=int(COST), bytes_accessed=1, transcendentals=0),
        name="plus",
    )(*(term for group in groups for term in group), *after)


def plus(*terms, after=()):
    return sums([terms], after)[0]


def sum_pairs(one, two, three, four):
    def body(a, b, c, d, result):
        result[...] = (a[...] + b[...]) + (c[...] + d[...])

    return pl.pallas_call(
        body,
        out_shape=shape(*one.shape),
        in_specs=[WHOLE] * 4,
        out_specs=WHOLE,
        compiler_params=pltpu.CompilerParams(vmem_limit_bytes=1 << 20),
        name="sum_pairs",
    )(one, two, three, four)


def split_rows(one, two, cut):
    def body(one_ref, two_ref, top, rest):
        top[...] = one_ref[:cut, :]
        rest[...] = two_ref[cut:, :]

    return pl.pallas_call(
        body,
        out_shape=(shape(cut, one.shape[1]), shape(two.shape[0] - cut, two.shape[1])),
        in_specs=[WHOLE] * 2,
        out_specs=(WHOLE, WHOLE),
        compiler_params=pltpu.CompilerParams(vmem_limit_bytes=4 << 20),
        cost_estimate=pl.CostEstimate(flops=int(COST), bytes_accessed=1, transcendentals=0),
        name="split_rows",
    )(one, two)


def owner(scal, k):
    spot = jnp.bitwise_and(scal[1] + k, GROUPS - 1)
    return jnp.where(scal[2] > 0, jnp.where(spot < HALF, 2 * spot, 2 * GROUPS - 1 - 2 * spot), k)


def halves(value):
    top = value.astype(bf16)
    return top, (value - top.astype(f32)).astype(bf16)


def dot(left, right, dims):
    return lax.dot_general(left, right, (dims, ((), ())), preferred_element_type=f32)


def dot3(lh, ll, rh, rl, dims):
    (left,), (right,) = dims
    join = lambda parts, axis: jnp.concatenate([part[...] for part in parts], axis=axis)
    return dot(join([lh, lh, ll], left), join([rh, rl, rh], right), dims)


def rows_at(index, size):
    return pl.ds(pl.multiple_of(index * size, size), size)


def piece(vec, number):
    a, b = 2 * number, 2 * number + 1
    return jnp.concatenate(
        [vec[a // 3, a % 3 : a % 3 + 1, :], vec[b // 3, b % 3 : b % 3 + 1, :]], axis=1
    )


def norm_stats(inputs):
    center = inputs - jnp.mean(inputs, axis=-1, keepdims=True)
    spread = jnp.mean(center * center, axis=-1, keepdims=True)
    scale = lax.rsqrt(spread + norm_eps)
    return center * scale, scale


def norm_back(hat, scale, gain, grad):
    inner = grad * gain
    return scale * (
        inner
        - jnp.mean(inner, axis=-1, keepdims=True)
        - hat * jnp.mean(inner * hat, axis=-1, keepdims=True)
    )


def low_lanes(dims):
    return lax.broadcasted_iota(jnp.int32, dims, 1) < HEAD


def lane_pairs(pair, last):
    low = low_lanes(pair.shape)
    roll = lambda v: pltpu.roll(v, HEAD, 1)
    ph = pair.astype(bf16).astype(f32)
    pl_ = pair - ph
    lh = last.astype(bf16).astype(f32)
    ll = last - lh
    return [
        jnp.where(low, ph, roll(pl_)).astype(bf16),
        jnp.where(low, roll(ph), pl_).astype(bf16),
        jnp.where(low, lh, roll(ll)).astype(bf16),
    ]


def row_halves(turned, head):
    part = turned[HEAD * head : HEAD * (head + 1)]
    return halves(part)


def pack_first_kernel(scal, wqkv, wproj, vec, seg, valid, tokens, first, packed, *refs):
    bands, proj, lines, marks, sems = refs
    mine = scal[0]
    aligned = pl.multiple_of(jnp.bitwise_and(mine * QUARTER, -128), 128)
    copies = [
        pltpu.make_async_copy(wqkv.at[:, pl.ds(part * D + aligned, CH)], bands.at[part], sems.at[part])
        for part in range(3)
    ]
    sub = pl.ds(pl.multiple_of(mine * SUB, 8), SUB)
    copies.append(pltpu.make_async_copy(wproj.at[sub, :], proj, sems.at[3]))
    copies.append(pltpu.make_async_copy(vec, lines, sems.at[4]))
    copies.append(pltpu.make_async_copy(seg, marks.at[0], sems.at[5]))
    copies.append(pltpu.make_async_copy(valid, marks.at[1], sems.at[6]))
    copies.append(pltpu.make_async_copy(tokens, packed.at[:CH, :], sems.at[7]))
    for copy in copies:
        copy.start()
    first[ROWS:, :] = jnp.zeros((8, D), f32)
    packed[CH:, :] = jnp.zeros((8, D), f32)
    for copy in copies[:5]:
        copy.wait()
    turn = jnp.where(jnp.bitwise_and(mine, 1) > 0, CH - HEAD, 0)
    for part in range(3):
        turned = pltpu.roll(bands[part], turn, 1)
        first[:ROWS, part * CH : part * CH + QUARTER] = turned[:, :QUARTER]
        for group in range(SEQ):
            lane = HEAD * (3 * group + part)
            first[group * SUB : (group + 1) * SUB, part * CH + QUARTER : (part + 1) * CH] = proj[
                :, lane : lane + HEAD
            ]
        first[ROWS + part : ROWS + part + 1, :HALF_VEC] = jnp.concatenate(
            [lines[3 * part + i : 3 * part + i + 1, :] for i in range(3)], axis=1
        )
    for copy in copies[5:]:
        copy.wait()
    packed[CH : CH + 1, :CH] = jnp.where(marks[1] > 0, marks[0], -1).astype(f32)


def pack_second_kernel(scal, win, wout, in_block, out_block):
    mine = scal[0]
    turn = lax.rem(HALF_VEC - mine * ROWS, HALF_VEC)
    for part in range(GROUPS):
        turned = pltpu.roll(win[:, part * HALF_VEC : (part + 1) * HALF_VEC], turn, 1)
        in_block[:, part * ROWS : (part + 1) * ROWS] = turned[:, :ROWS]
    out_block[...] = wout[pl.ds(pl.multiple_of(mine * ROWS, 8), ROWS), :]


def mask_kernel(scal, cotangent, valid, result):
    keep = jnp.where(valid[...] > 0, 1.0, 0.0).astype(f32)
    column = jnp.broadcast_to(keep, (128, CH)).T[:, :1]
    result[...] = cotangent[...] * column


def weights_kernel(scal, *refs):
    blocks, (wh, wl, vec, proj) = refs[: GROUPS + 1], refs[GROUPS + 1 :]
    spans = [(k, 0, ROWS + 8) for k in range(GROUPS)]
    spans[HALF : HALF + 1] = [(HALF, 0, CUT), (HALF, CUT, ROWS + 8)]
    for ref, (k, first, last) in zip(blocks, spans):
        at = owner(scal, k)
        size = min(last, ROWS) - first
        block = ref[:size, :]
        here = pl.ds(pl.multiple_of(at * ROWS + first, CUT), size)
        wh[here, :], wl[here, :] = halves(block)
        if last > ROWS:
            vec[at] = ref[size:, :HALF_VEC]
        for group in range(SEQ):
            top, end = group * SUB - first, (group + 1) * SUB - first
            if top < 0 or end > size:
                continue
            for part in range(3):
                lane = HEAD * (3 * group + part)
                proj[pl.ds(pl.multiple_of(at * SUB, 8), SUB), lane : lane + HEAD] = block[
                    top:end, part * CH + QUARTER : (part + 1) * CH
                ]


def front_kernel(scal, *refs):
    toks, refs = refs[:4], refs[4:]
    wh, wl, vec = refs[:3]
    xh, xl, kcat, qturn, vcat, qpair, kturn, low_row, outs_turn, lse, vturn, label = refs[3:]
    mine = scal[0]

    gain, shift = piece(vec, 0), piece(vec, 1)
    turn = lax.rem(D - mine * QUARTER, D)
    own = lambda number: pltpu.roll(jnp.broadcast_to(piece(vec, number), (8, D)), turn, 1)[:1, :CH]
    query_bias, value_bias = own(2), own(3)

    for r in range(SEQ):
        nat = jnp.bitwise_xor(mine, r)
        at = rows_at(nat, CH)
        label[nat] = toks[r][CH:, :CH]
        hat, _ = norm_stats(toks[r][:CH, :])
        xh[at, :], xl[at, :] = halves(hat)
        nh, nl = halves(hat * gain + shift)
        joined = dot3(nh, nl, wh[...], wl[...], NN)
        query = (joined[:, :CH] + query_bias) * HEAD ** (-0.5)
        key = joined[:, CH : 2 * CH]
        value = joined[:, 2 * CH :] + value_bias
        keys = lane_pairs(key[:, :128], key[:, 128:])
        values = lane_pairs(value[:, :128], value[:, 128:])
        queries = lane_pairs(query[:, :128], query[:, 128:])
        key_t, value_t, query_t = key.T, value.T, query.T
        for h in range(OWN):
            kcat[h, at, :] = jnp.concatenate([keys[h], keys[h]], axis=1)
            vcat[h, at, :] = jnp.concatenate([values[h], values[h]], axis=1)
            qpair[h, at, :] = queries[h]
            a, b = row_halves(query_t, h)
            qturn[h, :, at] = jnp.concatenate([a, a, b, b], axis=0)
            a, b = row_halves(key_t, h)
            kturn[h, :, at] = jnp.concatenate([a, b], axis=0)
            a, b = row_halves(value_t, h)
            vturn[h, :, at] = jnp.concatenate([a, b], axis=0)

    labels = jnp.concatenate([label[c][:1, :] for c in range(SEQ)], axis=1)
    spot = lax.broadcasted_iota(jnp.int32, (1, LEN), 1).astype(f32)
    begin = jnp.zeros((1, LEN), f32)
    for segment in range(3):
        held = jnp.sum(jnp.where(labels == float(segment), 1.0, 0.0), axis=1, keepdims=True)
        begin = begin + jnp.where(labels > float(segment), held, 0.0)
    begin = jnp.where(labels < 0.0, spot, begin)
    low_row[...] = jnp.broadcast_to(begin, (8, LEN))

    def one_head(h, carry):
        for c in range(SEQ):
            size = CH * (c + 1)
            lanes = slice(c * CH, (c + 1) * CH)
            score = dot(kcat[h, :size, :], qturn[h, :, lanes], NN)
            mask = allowed(low_row, c, size)
            score = jnp.where(mask, score, masked_score)
            peak = jnp.max(score, axis=0, keepdims=True)
            weight = jnp.exp(score - peak)
            total = jnp.sum(weight, axis=0, keepdims=True)
            top, rest = halves(weight)
            both = dot(vturn[h, :, :size], top, NN)
            extra = dot(vturn[h, :HEAD, :size], rest, NN)
            result = (both[:HEAD] + both[HEAD:] + extra) / total
            outs_turn[pl.ds(pl.multiple_of(h * HEAD, HEAD), HEAD), lanes] = result
            lse[h, :, lanes] = jnp.broadcast_to(peak + jnp.log(total), (8, CH))
        return carry

    lax.fori_loop(0, OWN, one_head, 0)


def allowed(low_row, c, size):
    key_at = lax.broadcasted_iota(jnp.int32, (size, CH), 0).astype(f32)
    query_at = (lax.broadcasted_iota(jnp.int32, (1, CH), 1) + c * CH).astype(f32)
    begin = low_row[:1, c * CH : (c + 1) * CH]
    return (key_at >= begin) & (key_at <= query_at)


def proj_kernel(scal, *refs):
    toks, heads, parts, refs = refs[:4], refs[4:8], refs[8:12], refs[12:]
    vec, wh, wl, heads_h, heads_l, norm_h, norm_l, mixed, hat, scale, weight, joined = refs
    mine = scal[0]
    for r in range(SEQ):
        at = jnp.bitwise_xor(mine, r)
        for d in range(GROUPS):
            weight[pl.ds(pl.multiple_of(d * ROWS + at * SUB, 8), SUB), :] = parts[r][
                d * SUB : (d + 1) * SUB, :
            ]
        joined[rows_at(at, QUARTER), :] = heads[r][...]
    wh[...], wl[...] = halves(weight[...])
    heads_h[...], heads_l[...] = halves(joined[:, rows_at(mine, CH)])
    gain, shift = piece(vec, 5), piece(vec, 6)
    for r in range(SEQ):
        at = rows_at(jnp.bitwise_xor(mine, r), CH)
        a, b = halves(joined[:, at].T)
        total = toks[r][:CH, :] + dot3(a, b, wh[...], wl[...], NN)
        total = total + piece(vec, 4)
        normed, size = norm_stats(total)
        norm_h[r], norm_l[r] = halves(normed * gain + shift)
        if r == 0:
            mixed[...] = total
            hat[...] = normed
            scale[...] = jnp.broadcast_to(size, (CH, 128))


def hidden_kernel(scal, norm_h, norm_l, *refs):
    blocks, vec, acts_h, acts_l, slope, winh, winl = refs[: GROUPS + 1], *refs[GROUPS + 1 :]
    mine = scal[0]
    spans = [(k, 0) for k in range(GROUPS)]
    spans.insert(HALF + 1, (HALF, CUT))
    for ref, (k, first) in zip(blocks, spans):
        at = pl.ds(pl.multiple_of(owner(scal, k) * ROWS + first, CUT), ref.shape[0])
        winh[at, :], winl[at, :] = halves(ref[...])
    marks = [16 + d for d in range(GROUPS)]
    table = jnp.concatenate([vec[m // 3, m % 3 : m % 3 + 1, :] for m in marks], axis=0)
    table = pltpu.roll(table, lax.rem(HALF_VEC - mine * ROWS, HALF_VEC), 1)[:, :ROWS]
    bias = jnp.concatenate([table[d : d + 1] for d in range(GROUPS)], axis=1)
    for r in range(SEQ):
        at = slice(r * CH, (r + 1) * CH)
        hidden = dot3(norm_h[r], norm_l[r], winh[...], winl[...], NN) + bias
        inner = jnp.tanh(gelu_scale * (hidden + gelu_cubic * hidden * hidden * hidden))
        acts_h[at, :], acts_l[at, :] = halves(0.5 * hidden * (1.0 + inner))
        slope[at, :] = 0.5 * (1.0 + inner) + 0.5 * hidden * (1.0 - inner * inner) * gelu_scale * (
            1.0 + 3.0 * gelu_cubic * hidden * hidden
        )


def emit_blocks(scal, outs, whole):
    for k in range(GROUPS):
        outs[k][...] = whole[rows_at(owner(scal, k), ROWS), :]


def out_grad_kernel(scal, acts_h, acts_l, *refs):
    grads, (out_h, out_l), outs, whole = refs[:4], refs[4:6], refs[6 : 6 + GROUPS], refs[6 + GROUPS]
    for r in range(SEQ):
        at = slice(r * CH, (r + 1) * CH)
        out_h[at, :], out_l[at, :] = halves(grads[r][...])
    whole[...] = dot3(acts_h[...], acts_l[...], out_h[...], out_l[...], TN)
    emit_blocks(scal, outs, whole)


def hidden_back_kernel(scal, out_h, out_l, slope, winh, winl, *refs):
    blocks, refs = refs[:GROUPS], refs[GROUPS:]
    hid_h, hid_l, wouth, woutl, bias_sum = refs[:5]
    parts = refs[5:]
    for k in range(GROUPS):
        at = rows_at(owner(scal, k), ROWS)
        wouth[at, :], woutl[at, :] = halves(blocks[k][...])
    sums = jnp.zeros((1, D), f32)
    for r in (1, 3, 2, 0):
        at = slice(r * CH, (r + 1) * CH)
        back = dot3(out_h[at, :], out_l[at, :], wouth[...], woutl[...], NT) * slope[at, :]
        sums = sums + jnp.sum(back, axis=0, keepdims=True)
        bh, bl = halves(back)
        hid_h[at, :], hid_l[at, :] = bh, bl
        parts[r][...] = dot3(bh, bl, winh[...], winl[...], NT)
    bias_sum[...] = jnp.broadcast_to(sums, (8, D))


def in_grad_kernel(scal, norm_h, norm_l, hid_h, hid_l, *refs):
    outs, whole = refs[:GROUPS], refs[GROUPS]
    flat = lambda ref: ref[...].reshape(LEN, D)
    whole[...] = dot3(flat(norm_h), flat(norm_l), hid_h[...], hid_l[...], TN)
    emit_blocks(scal, outs, whole)


def ffn_out_kernel(scal, acts_h, acts_l, wouth, woutl, *parts):
    for r in (1, 3, 2, 0):
        at = slice(r * CH, (r + 1) * CH)
        parts[r][...] = dot3(acts_h[at, :], acts_l[at, :], wouth[...], woutl[...], NN)


def output_kernel(scal, base, top, bottom, vec, output):
    whole = base[...] + piece(vec, 7)
    half = top.shape[0]
    output[:half, :] = whole[:half] + top[...]
    output[half:, :] = whole[half:] + bottom[...]


def proj_back_kernel(scal, one, two, three, hat, scale, vec, grad_out, wh, wl, mixed_grad, sums, *parts):
    mine = scal[0]
    normed = one[...] + two[...] + three[...]
    back = norm_back(hat[...], scale[:, :1], piece(vec, 5), normed)
    total = grad_out[...] + back
    mixed_grad[...] = total
    a, b = halves(total)
    for r in range(SEQ):
        at = rows_at(jnp.bitwise_xor(mine, r), QUARTER)
        parts[r][...] = dot3(wh[at, :], wl[at, :], a, b, NT)
    add = lambda v: jnp.sum(v, axis=0, keepdims=True)
    sums[...] = jnp.concatenate(
        [add(total), add(normed * hat[...]), add(normed), add(grad_out[...]), jnp.zeros((4, D), f32)],
        axis=0,
    )


def proj_grad_kernel(scal, heads_h, heads_l, mixed_grad, *refs):
    outs, whole = refs[:-1], refs[-1]
    mine = scal[0]
    gh, gl = halves(mixed_grad[...])
    whole[...] = dot3(heads_h[...], heads_l[...], gh, gl, NN)
    for r in range(SEQ):
        at = jnp.bitwise_xor(mine, r)
        for d in range(GROUPS):
            outs[r][d * SUB : (d + 1) * SUB, :] = whole[
                pl.ds(pl.multiple_of(d * ROWS + at * SUB, 8), SUB), :
            ]


def back_kernel(scal, *refs):
    grads, refs = refs[:4], refs[4:]
    kcat, qturn, vcat, qpair, kturn, outs_turn, lse, low_row = refs[:8]
    joined_h, joined_l, joined_sums = refs[8:11]
    gturn, gpair, dots, key_sum, value_sum, query_turn = refs[11:]
    mine = scal[0]

    for r in range(SEQ):
        at = rows_at(jnp.bitwise_xor(mine, r), CH)
        turned = grads[r][...]
        grad = jnp.concatenate([turned, jnp.zeros((HEAD, CH), f32)], axis=0).T
        pairs = lane_pairs(grad[:, :128], grad[:, 128:])
        for h in range(OWN):
            gpair[h, at, :] = pairs[h]
            part = turned[HEAD * h : HEAD * (h + 1)]
            dots[h, :, at] = jnp.broadcast_to(
                jnp.sum(part * outs_turn[HEAD * h : HEAD * (h + 1), at], axis=0, keepdims=True), (8, CH)
            )
            a, b = halves(part)
            gturn[h, :, at] = jnp.concatenate([a, a, b, b], axis=0)

    key_sum[...] = jnp.zeros_like(key_sum)
    value_sum[...] = jnp.zeros_like(value_sum)

    def one_head(h, carry):
        for c in range(SEQ):
            size = CH * (c + 1)
            lanes = slice(c * CH, (c + 1) * CH)
            score = dot(kcat[h, :size, :], qturn[h, :, lanes], NN)
            weight = jnp.where(allowed(low_row, c, size), jnp.exp(score - lse[h, :1, lanes]), 0.0)
            back = dot(vcat[h, :size, :], gturn[h, :, lanes], NN)
            score_back = weight * (back - dots[h, :1, lanes])
            a, b = halves(weight)
            pair = gpair[h, lanes, :]
            value_sum[h, :size, :] += dot(a, pair, NN) + dot(b, pair, NN)
            a, b = halves(score_back)
            pair = qpair[h, lanes, :]
            key_sum[h, :size, :] += dot(a, pair, NN) + dot(b, pair, NN)
            turned = dot(kturn[h, :, :size], a, NN) + dot(kturn[h, :, :size], b, NN)
            query_turn[h, :, lanes] = (turned[:HEAD] + turned[HEAD:]) * HEAD ** (-0.5)
        return carry

    lax.fori_loop(0, OWN, one_head, 0)

    column_sums = jnp.zeros((1, D), f32)
    low = low_lanes((CH, 128))
    for c in range(SEQ):
        at = slice(c * CH, (c + 1) * CH)
        blank = jnp.zeros((HEAD, CH), f32)
        query = jnp.concatenate([query_turn[h, :, at] for h in range(OWN)] + [blank], axis=0).T
        done = [query]
        for kept in (key_sum, value_sum):
            full = [kept[h, at, :] for h in range(OWN)]
            full = [v + pltpu.roll(v, HEAD, 1) for v in full]
            done.append(jnp.where(low, full[0], full[1]))
            done.append(jnp.where(low, full[2], 0.0))
        joined = jnp.concatenate(done, axis=1)
        column_sums = column_sums + jnp.sum(joined, axis=0, keepdims=True)
        joined_h[at, :], joined_l[at, :] = halves(joined)

    joined_sums[...] = jnp.broadcast_to(column_sums, (8, D))


def qkv_grad_kernel(scal, xh, xl, joined_h, joined_l, joined_sums, wh, wl, vec, *refs):
    proj_one, proj_two, vector_sums, bias_sum = refs[:4]
    outs, (whole, rows) = refs[4 : 4 + GROUPS], refs[4 + GROUPS :]
    mine = scal[0]
    column_sums = joined_sums[:1, :]
    core = dot3(xh[...], xl[...], joined_h[...], joined_l[...], TN)
    gain, shift = piece(vec, 0), piece(vec, 1)
    as_column = lambda v: jnp.broadcast_to(v, (128, D)).T[:, :1]
    whole[...] = as_column(gain) * core + as_column(shift) * column_sums
    weights = wh[...].astype(f32) + wl[...].astype(f32)
    gain_grad = jnp.sum(weights * core, axis=1, keepdims=True)
    shift_grad = jnp.sum(weights * column_sums, axis=1, keepdims=True)
    lane = lax.broadcasted_iota(jnp.int32, (D, 128), 1)
    norm_grads = jnp.where(lane == 0, gain_grad, shift_grad).T

    def place(part, scale):
        wide = jnp.concatenate([part[:, :QUARTER], jnp.zeros((1, D - QUARTER), f32)], axis=1)
        wide = jnp.broadcast_to(wide, (8, D))
        return pltpu.roll(wide, mine * QUARTER, 1)[:1]

    entries = [
        norm_grads[0:1],
        norm_grads[1:2],
        place(column_sums[:, :CH], 1.0),
        place(column_sums[:, 2 * CH :], 1.0),
        vector_sums[0:1],
        vector_sums[1:2],
        vector_sums[2:3],
        vector_sums[3:4],
    ]
    lines = [e[:, i * HALF_VEC : (i + 1) * HALF_VEC] for e in entries for i in range(2)]
    bias = jnp.concatenate(
        [bias_sum[:1, d * ROWS : (d + 1) * ROWS] for d in range(GROUPS)], axis=0
    )
    bias = jnp.concatenate([bias, jnp.zeros((GROUPS, HALF_VEC - ROWS), f32)], axis=1)
    bias = pltpu.roll(bias, mine * ROWS, 1)
    lines = lines + [bias[d : d + 1] for d in range(GROUPS)]
    filler = jnp.zeros((5, HALF_VEC), f32)
    for d in range(GROUPS):
        rows[d] = jnp.concatenate(lines[3 * d : 3 * d + 3] + [filler], axis=0)

    for k in range(GROUPS):
        at = owner(scal, k)
        outs[k][:ROWS, :] = whole[rows_at(at, ROWS), :]
        here = pl.ds(pl.multiple_of(at * SUB, 8), SUB)
        proj = proj_one[here, :] + proj_two[here, :]
        for group in range(SEQ):
            for part in range(3):
                lane_at = HEAD * (3 * group + part)
                outs[k][
                    group * SUB : (group + 1) * SUB, part * CH + QUARTER : (part + 1) * CH
                ] = proj[:, lane_at : lane_at + HEAD]
        outs[k][ROWS:, :HALF_VEC] = rows[at]
        outs[k][ROWS:, HALF_VEC:] = jnp.zeros((8, HALF_VEC), f32)


def pre_back_kernel(scal, joined_h, joined_l, wh, wl, *parts):
    mine = scal[0]
    for r in (1, 3, 2, 0):
        at = rows_at(jnp.bitwise_xor(mine, r), CH)
        parts[r][...] = dot3(joined_h[at, :], joined_l[at, :], wh[...], wl[...], NT)


def input_grad_kernel(scal, tokens, one, two, vec, mixed_grad, result):
    hat, scale = norm_stats(tokens[...])
    grad = one[...] + two[...]
    result[...] = mixed_grad[...] + norm_back(hat, scale, piece(vec, 0), grad)


def total_square(value):
    return jnp.sum(jnp.sum(value * value, axis=0, keepdims=True), axis=1, keepdims=True)


def shard_sums_kernel(scal, first, in_shard, out_shard, small):
    total = total_square(first[:ROWS, :]) + total_square(in_shard[...]) + total_square(out_shard[...])
    small[...] = first[ROWS:, :]
    small[7:8, :] = jnp.broadcast_to(total, (1, D))


def shard_squares_kernel(scal, one, two, three, four, squares):
    whole = (one[...] + two[...]) + (three[...] + four[...])
    squares[...] = jnp.broadcast_to(whole[7:8, :1] + total_square(whole[:3, :HALF_VEC]), (8, 128))


def stage_kernel(scal, *refs):
    sources, targets, sems = refs[:15], refs[15:30], refs[30]
    copies = [
        pltpu.make_async_copy(source, target, sems.at[i])
        for i, (source, target) in enumerate(zip(sources, targets))
    ]
    for copy in copies:
        copy.start()
    for copy in copies:
        copy.wait()


def adamw_kernel(scal, squares, *refs):
    firsts, ins, outs, refs = refs[:4], refs[4:8], refs[8:12], refs[12:]
    states, clip, finals, news = refs[:15], refs[15], refs[16:31], refs[31:46]
    first, second, sems = refs[46:]
    send = lambda number: [
        pltpu.make_async_copy(news[i], finals[i], sems.at[i]) for i in range(3 * number, 3 * number + 3)
    ]
    mine = scal[0]
    norm = jnp.sqrt(squares[...])
    clip[...] = norm
    factor = (clip_limit / jnp.maximum(norm, clip_limit))[:1, :1]
    for r in range(SEQ):
        at = jnp.bitwise_xor(mine, r)
        first[at] = firsts[r][:ROWS, :]
        second[at, :ROWS] = ins[r][...]
        second[at, ROWS:] = outs[r][...]

    def update(number, spot, grad, rate, decay):
        held = [states[3 * number + i][spot] for i in range(3)]
        fresh = adamw_update(*held, factor * grad, rate, decay)
        for i in range(3):
            news[3 * number + i][spot] = fresh[i]

    def finish(number):
        for copy in send(number):
            copy.start()

    lines = [firsts[r][ROWS:, :HALF_VEC] for r in range(SEQ)]
    line = (lines[0] + lines[1]) + (lines[2] + lines[3])
    for i in range(3):
        for j in range(3):
            spot = (slice(3 * i + j, 3 * i + j + 1), slice(None))
            update(0, spot, line[i : i + 1, 128 * j : 128 * (j + 1)], vector_rate, 0.0)
    finish(0)
    every = slice(None)
    for part in range(3):
        grad = jnp.concatenate(
            [first[j][:, part * CH : part * CH + QUARTER] for j in range(SEQ)], axis=1
        )
        update(1, (every, slice(part * D, (part + 1) * D)), grad, matrix_rate, weight_decay)
    finish(1)
    for j in range(SEQ):
        grad = jnp.concatenate(
            [
                first[j][group * SUB : (group + 1) * SUB, part * CH + QUARTER : (part + 1) * CH]
                for group in range(SEQ)
                for part in range(3)
            ],
            axis=1,
        )
        update(2, (slice(j * SUB, (j + 1) * SUB), every), grad, matrix_rate, weight_decay)
    finish(2)
    for d in range(GROUPS):
        grad = jnp.concatenate(
            [second[j][:ROWS, d * ROWS : (d + 1) * ROWS] for j in range(SEQ)], axis=1
        )
        update(3, (every, slice(d * HALF_VEC, (d + 1) * HALF_VEC)), grad, matrix_rate, weight_decay)
    finish(3)
    for j in range(SEQ):
        update(
            4, (slice(j * ROWS, (j + 1) * ROWS), every), second[j][ROWS:, :], matrix_rate, weight_decay
        )
    finish(4)
    for number in range(5):
        for copy in send(number):
            copy.wait()


def adamw_update(weight, first, second, grad, rate, decay):
    new_first = beta_one * first + (1.0 - beta_one) * grad
    new_second = beta_two * second + (1.0 - beta_two) * grad * grad
    first_hat = new_first / (1.0 - beta_one**STEP)
    second_hat = new_second / (1.0 - beta_two**STEP)
    new_weight = weight - rate * (first_hat / (jnp.sqrt(second_hat) + adam_eps) + decay * weight)
    return (new_first, new_second, new_weight)


def ring_tables(count):
    evens = [2 * i for i in range(count // 2)]
    order = evens + [i + 1 for i in reversed(evens)]
    place = [0] * count
    for position, device in enumerate(order):
        place[device] = position
    right = [(order[i], order[(i + 1) % count]) for i in range(count)]
    left = [(b, a) for a, b in right]
    return order, place, right, left


class RingGather:
    def __init__(self, block, name, flip=False):
        _, _, self.right, self.left = ring_tables(GROUPS)
        if flip:
            self.right, self.left = self.left, self.right
        self.got, self.name, self.at, self.flip = {0: block}, name, 0, flip

    def step(self, after=()):
        places = (-self.at % GROUPS, self.at)
        if after:
            for place in set(places):
                self.got[place] = gate(self.got[place], after)
        forth, back = (self.got[place] for place in places)
        self.at += 1
        self.got[GROUPS - self.at] = move(forth, "dp", self.right, f"{self.name}_right_{self.at}")
        if self.at < HALF:
            self.got[self.at] = move(back, "dp", self.left, f"{self.name}_left_{self.at}")
        return [self.got[GROUPS - self.at]] + ([self.got[self.at]] if self.at < HALF else [])

    def halved(self, cut):
        top, rest = split_rows(self.got[GROUPS - self.at], self.got[self.at], cut)
        self.at += 1
        self.got[HALF] = move(top, "dp", self.right, f"{self.name}_right_{self.at}")
        self.got[GROUPS] = move(rest, "dp", self.left, f"{self.name}_left_{self.at}")
        return [self.got[HALF], self.got[GROUPS]]

    def blocks(self):
        blocks = [self.got[-k % GROUPS if self.flip else k] for k in range(GROUPS)]
        if GROUPS in self.got:
            blocks.insert(HALF + 1, self.got[GROUPS])
        return blocks


class RingScatter:
    def __init__(self, blocks, name, flip=False):
        _, _, self.right, self.left = ring_tables(GROUPS)
        self.blocks = blocks
        if flip:
            self.right, self.left = self.left, self.right
            self.blocks = [blocks[-k % GROUPS] for k in range(GROUPS)]
        self.name, self.back, self.at = name, None, HALF
        self.forth = move(self.blocks[HALF], "dp", self.right, f"{name}_right_1")

    def step(self, after=()):
        self.at -= 1
        ahead, back = self.blocks[self.at], self.blocks[GROUPS - self.at]
        if self.back is None:
            forth = plus(self.forth, ahead, after=after)
        else:
            forth, back = sums([(self.forth, ahead), (self.back, back)], after)
        number = HALF + 1 - self.at
        self.forth = move(forth, "dp", self.right, f"{self.name}_right_{number}")
        self.back = move(back, "dp", self.left, f"{self.name}_left_{number}")
        return [forth, back]

    def result(self, after=()):
        return plus(self.forth, self.back, self.blocks[0], after=after)


def move(block, axis, pairs, name):
    with jax.named_scope(name):
        return lax.ppermute(block, axis, pairs)


def swap(block, bits, name):
    return move(block, "seq", [(i, i ^ bits) for i in range(SEQ)], f"{name}_{bits}")


def gather_seq(block, name):
    across = swap(block, 2, name)
    core = swap(block, 1, name)
    return [block, core, across, swap(across, 1, f"{name}_2")]


def exchange_seq(parts, name):
    return [parts[0]] + [swap(parts[r], r, name) for r in range(1, SEQ)]


def scatter_core(parts, name):
    return parts[0], swap(parts[1], 1, f"{name}_own"), parts[2], swap(parts[3], 1, f"{name}_across")


def ordered(blocks, mine):
    stack = jnp.stack(blocks, axis=0)
    return [lax.dynamic_index_in_dim(stack, mine ^ j, 0, keepdims=False) for j in range(len(blocks))]


def local(
    tokens,
    cotangent,
    segment_ids,
    valid,
    vectors,
    vec_first,
    vec_second,
    w_qkv,
    qkv_first,
    qkv_second,
    w_proj,
    proj_first,
    proj_second,
    w_in,
    in_first,
    in_second,
    w_out,
    out_first,
    out_second,
):
    dp_parts = lax.axis_size("dp")
    ring = dp_parts == GROUPS
    mine = lax.axis_index("seq")
    home = lax.axis_index("dp")
    rows = w_qkv.shape[0]
    units = w_out.shape[0] // SEQ
    far, near = home // 2, home % 2
    position = jnp.where(near > 0, GROUPS - 1 - far, far)
    scal = jnp.stack([mine, position, jnp.full_like(mine, 1 if ring else 0)]).astype(jnp.int32)
    flat_in = tokens.reshape(CH, D)
    chunk, tall, square = shape(CH, D), shape(LEN, D, kind=bf16), shape(D, D, kind=bf16)

    if ring:
        first, packed = run(
            pack_first_kernel,
            scal,
            [w_qkv, w_proj, vectors.reshape(9, 128), segment_ids, valid, flat_in],
            [shape(ROWS + 8, D), shape(CH + 8, D)],
            scratch=[
                pltpu.VMEM((3, ROWS, CH), f32),
                pltpu.VMEM((SUB, D), f32),
                pltpu.VMEM((9, 128), f32),
                pltpu.VMEM((2, 1, CH), jnp.int32),
            ],
            sems=8,
            far_args=range(6),
            room=54,
            name="pack_first", work=3.0,
        )
        ring_first = RingGather(first, "first")
        for _ in range(HALF - 1):
            ring_first.step()
        ring_first.halved(CUT)
        firsts = ring_first.blocks()
        in_block, out_block = run(
            pack_second_kernel,
            scal,
            [w_in, w_out],
            [shape(ROWS, D)] * 2,
            name="pack_second", work=3.0,
            after=[firsts[GROUPS]],
        )
        ring_in = RingGather(in_block, "w_in")
        ring_out = RingGather(out_block, "w_out", flip=True)
        came = ring_in.step([firsts[HALF], firsts[HALF + 1]])
        came = came + ring_out.step([firsts[HALF], firsts[HALF + 1]])
    else:
        padded = jnp.pad(w_qkv, ((0, 0), (0, CH)))
        own = lambda part: lax.dynamic_slice_in_dim(padded, part * D + mine * QUARTER, CH, 1)
        first = jnp.concatenate([own(0), own(1), own(2)], axis=1)
        first = lax.all_gather(first, "dp", axis=0, tiled=True).reshape(GROUPS, ROWS, D)
        all_vec = lax.all_gather(vectors, "dp", axis=0, tiled=True).reshape(GROUPS, 3, HALF_VEC)
        first = jnp.concatenate([first, jnp.pad(all_vec, ((0, 0), (0, 5), (0, D - HALF_VEC)))], axis=1)
        firsts = [first[k] for k in range(GROUPS)]
        firsts[HALF : HALF + 1] = [first[HALF, :CUT], first[HALF, CUT:]]
        in_part = lax.dynamic_index_in_dim(
            w_in.reshape(rows, dp_parts, SEQ, units), mine, 2, keepdims=False
        ).reshape(rows, D)
        out_part = lax.dynamic_slice_in_dim(w_out, mine * units, units, 0)
        in_blocks, out_blocks = (
            list(lax.all_gather(part, "dp", axis=0, tiled=True).reshape(GROUPS, ROWS, D))
            for part in (in_part, out_part)
        )
        in_blocks[HALF : HALF + 1] = [in_blocks[HALF][:CUT], in_blocks[HALF][CUT:]]
        marks = jnp.where(valid > 0, segment_ids, -1).astype(f32)
        packed = jnp.concatenate([flat_in, jnp.pad(marks, ((0, 7), (0, D - CH)))], axis=0)
    toks = gather_seq(packed, "tokens")
    (grad_out,) = run(
        mask_kernel, scal, [cotangent.reshape(CH, D), valid], [chunk], name="mask", work=2.0, after=[toks[2]]
    )
    grads_row = gather_seq(grad_out, "cotangent")

    qkv_h, qkv_l, vec, proj = run(
        weights_kernel,
        scal,
        firsts,
        [square, square, shape(GROUPS, 8, HALF_VEC), shape(GROUPS * SUB, D)],
        name="weights", work=3.0,
    )
    if ring:
        proj_parts = gather_seq(proj, "w_proj")
    else:
        full = lax.all_gather(w_proj, "dp", axis=0, tiled=True).reshape(GROUPS, SEQ, SUB, D)
        proj_parts = [
            lax.dynamic_index_in_dim(full, mine ^ r, 1, keepdims=False).reshape(GROUPS * SUB, D)
            for r in range(SEQ)
        ]
    hat_h, hat_l, kcat, qturn, vcat, qpair, kturn, low_row, heads, lse = run(
        front_kernel,
        scal,
        toks + [qkv_h, qkv_l, vec],
        [
            tall,
            tall,
            shape(OWN, LEN, 256, kind=bf16),
            shape(OWN, 256, LEN, kind=bf16),
            shape(OWN, LEN, 256, kind=bf16),
            shape(OWN, LEN, 128, kind=bf16),
            shape(OWN, 128, LEN, kind=bf16),
            shape(8, LEN),
            shape(QUARTER, LEN),
            shape(OWN, 8, LEN),
        ],
        scratch=[pltpu.VMEM((OWN, 128, LEN), bf16), pltpu.VMEM((SEQ, 8, CH), f32)],
        name="front", work=14.0,
        after=[grads_row[2]],
    )
    if ring:
        heads = gate(heads, [proj_parts[2], *came])
        ring_in.step([lse])
        came = ring_in.step()
        came = came + ring_in.halved(CUT)
        ring_out.step(came)
        in_blocks = ring_in.blocks()
    across = swap(heads, 2, "heads")
    if ring:
        across = gate(across, came)
    all_heads = [heads, swap(heads, 1, "heads"), across, swap(across, 1, "heads_2")]
    wide = shape(D, CH, kind=bf16)
    split = shape(SEQ, CH, D, kind=bf16)
    proj_h, proj_l, heads_h, heads_l, norm_h, norm_l, mixed, hat_two, scale_two = run(
        proj_kernel,
        scal,
        toks + all_heads + proj_parts + [vec],
        [square, square, wide, wide, split, split, chunk, chunk, shape(CH, 128)],
        scratch=[pltpu.VMEM((D, D), f32), pltpu.VMEM((D, LEN), f32)],
        name="proj", work=8.0,
    )

    if ring:
        ring_out.step([norm_h])
        ring_out.step()
        out_blocks = ring_out.blocks()
    block = shape(ROWS, D)
    acts_h, acts_l, slope, in_wh, in_wl = run(
        hidden_kernel,
        scal,
        [norm_h, norm_l] + in_blocks + [vec],
        [tall, tall, shape(LEN, D), square, square],
        name="hidden", work=8.0,
    )
    done = run(
        out_grad_kernel,
        scal,
        [acts_h, acts_l] + grads_row,
        [tall, tall] + [block] * GROUPS,
        scratch=[pltpu.VMEM((D, D), f32)],
        name="out_grad", work=5.0,
    )
    out_h, out_l = done[:2]
    out_grads = list(done[2:])
    if ring:
        ring_out = RingScatter(out_grads, "out_grad")
    done = run(
        hidden_back_kernel,
        scal,
        [out_h, out_l, slope, in_wh, in_wl] + out_blocks,
        [tall, tall, square, square, shape(8, D)] + [chunk] * SEQ,
        name="hidden_back", work=11.0,
        after=out_grads[:1],
    )
    hid_h, hid_l, out_wh, out_wl, bias_sum = done[:5]
    parts = list(done[5:])
    if ring:
        parts[3] = gate(parts[3], ring_out.step([bias_sum]))
    norm_own, norm_near, norm_across, norm_far = scatter_core(parts, "norm_grad")
    norm_pair = plus(norm_across, norm_far)
    norm_last = swap(norm_pair, 2, "norm_grad")
    in_grads = list(
        run(
            in_grad_kernel,
            scal,
            [norm_h, norm_l, hid_h, hid_l],
            [block] * GROUPS,
            scratch=[pltpu.VMEM((D, D), f32)],
            name="in_grad", work=5.0,
            after=[norm_pair],
        )
    )
    if ring:
        ring_in = RingScatter(in_grads, "in_grad", flip=True)
        out_sent = ring_out.step()
        in_sent = ring_in.step()
    done = run(
        proj_back_kernel,
        scal,
        [norm_own, norm_near, norm_last, hat_two, scale_two, vec, grad_out, proj_h, proj_l],
        [chunk, shape(8, D)] + [shape(QUARTER, CH)] * SEQ,
        name="proj_back", work=5.0,
        after=out_sent + in_sent if ring else [],
    )
    mixed_grad, vector_sums = done[:2]
    head_grads = exchange_seq(list(done[2:]), "head_grad")
    if ring:
        out_sent = ring_out.step([mixed_grad])
        in_sent = ring_in.step([mixed_grad])
    out_parts = run(
        ffn_out_kernel,
        scal,
        [acts_h, acts_l, out_wh, out_wl],
        [chunk] * SEQ,
        name="ffn_out", work=7.0,
        after=[mixed_grad],
    )
    proj_grads = run(
        proj_grad_kernel,
        scal,
        [heads_h, heads_l, mixed_grad],
        [shape(GROUPS * SUB, D)] * SEQ,
        scratch=[pltpu.VMEM((D, D), f32)],
        name="proj_grad", work=4.0,
        after=[*head_grads[1:], *out_sent, *in_sent, out_parts[0]] if ring else [],
    )
    wait = [head_grads[3], head_grads[2]]
    out_own, out_near, out_across, out_far = scatter_core(out_parts, "output")
    if ring:
        proj_own, proj_near, proj_across, proj_far = scatter_core(proj_grads, "proj_grad")
        proj_pair, proj_base, out_pair, out_base = sums(
            [
                (proj_across, proj_far),
                (proj_own, proj_near),
                (out_across, out_far),
                (mixed, out_own, out_near),
            ],
            wait,
        )
        proj_last = swap(proj_pair, 2, "proj_grad")
    else:
        proj_base = proj_last = proj_grads[0]
        out_pair, out_base = plus(out_across, out_far), plus(mixed, out_own, out_near)
    joined_h, joined_l, joined_sums = run(
        back_kernel,
        scal,
        head_grads + [kcat, qturn, vcat, qpair, kturn, heads, lse, low_row],
        [tall, tall, shape(8, D)],
        scratch=[
            pltpu.VMEM((OWN, 256, LEN), bf16),
            pltpu.VMEM((OWN, LEN, 128), bf16),
            pltpu.VMEM((OWN, 8, LEN), f32),
            pltpu.VMEM((OWN, LEN, 128), f32),
            pltpu.VMEM((OWN, LEN, 128), f32),
            pltpu.VMEM((OWN, HEAD, LEN), f32),
        ],
        name="back", work=16.0,
        after=[proj_grads[0]],
    )
    if ring:
        shard_out = ring_out.result([joined_sums])
        in_sent = ring_in.step([joined_sums])
    done = run(
        qkv_grad_kernel,
        scal,
        [hat_h, hat_l, joined_h, joined_l, joined_sums, qkv_h, qkv_l, vec]
        + [proj_base, proj_last, vector_sums, bias_sum],
        [shape(ROWS + 8, D)] * GROUPS,
        scratch=[pltpu.VMEM((D, D), f32), pltpu.VMEM((GROUPS, 8, HALF_VEC), f32)],
        name="qkv_grad", work=1.0,
        after=[*in_sent, shard_out] if ring else [],
    )
    first_grads = list(done)
    if ring:
        shard_in = ring_in.result([first_grads[0]])
        out_all = gather_seq(shard_out, "out_shard")
        in_all = gather_seq(shard_in, "in_shard")
        first_grads[HALF] = gate(first_grads[HALF], [shard_in, out_all[2]])
        ring_first = RingScatter(first_grads, "first_grad")
        first_sent = ring_first.step([in_all[2]])
    pre_parts = run(
        pre_back_kernel,
        scal,
        [joined_h, joined_l, qkv_h, qkv_l],
        [chunk] * SEQ,
        name="pre_back", work=1.0,
        after=[shard_in, *first_sent] if ring else [],
    )
    pre_parts = list(pre_parts)
    out_top, out_bottom = split_rows(out_pair, out_pair, CH // 2)
    if ring:
        first_sent = ring_first.step()
        out_top = gate(out_top, [in_all[2]])
    top_last = swap(out_top, 2, "output_top")
    if ring:
        pre_parts[3] = gate(pre_parts[3], [*first_sent, top_last])
    pre_own, pre_near, pre_across, pre_far = scatter_core(pre_parts, "pre_grad")
    pre_pair, pre_base = sums([(pre_across, pre_far), (pre_own, pre_near)])
    pre_last = swap(pre_pair, 2, "pre_grad")
    states = [vectors, vec_first, vec_second, w_qkv, qkv_first, qkv_second, w_proj, proj_first, proj_second]
    states = states + [w_in, in_first, in_second, w_out, out_first, out_second]
    last_sent = ring_first.step([out_all[1], out_all[3]]) if ring else []
    if ring:
        held = [v.reshape(9, 128) for v in states[:3]] + states[3:]
        held = run(
            stage_kernel,
            scal,
            held,
            [shape(*v.shape) for v in held],
            sems=15,
            far_args=range(15),
            name="stage", work=3.0,
            after=[*last_sent, in_all[1], in_all[3]],
        )
        shard_first = ring_first.result([held[3]])
    (input_grad,) = run(
        input_grad_kernel,
        scal,
        [flat_in, pre_base, pre_last, vec, mixed_grad],
        [chunk],
        name="input_grad", work=3.0,
    )

    if ring:
        (small,) = run(
            shard_sums_kernel, scal, [shard_first, shard_in, shard_out], [shape(8, D)], name="shard_sums", work=1.0
        )
        shard_first = gate(shard_first, [pre_last])
        across = swap(shard_first, 2, "first_shard")
        core = swap(shard_first, 1, "first_shard")
        (squares,) = run(
            shard_squares_kernel,
            scal,
            [small] + [swap(small, bits, "small") for bits in (1, 2, 3)],
            [shape(8, 128)],
            name="shard_squares", work=1.0,
            after=[input_grad],
        )
        flipped = lambda bits: [(i, i ^ bits) for i in range(GROUPS)]
        one, two, three = (move(squares, "dp", flipped(bits), "squares") for bits in (1, 2, 3))
        squares = sum_pairs(squares, one, two, three)
        out_bottom = gate(out_bottom, [across])
        across = gate(across, [squares, out_bottom])
        first_all = [shard_first, core, across, swap(across, 1, "first_shard_2")]
        squares = plus(squares, move(squares, "dp", flipped(4), "squares"))
        done = run(
            adamw_kernel,
            scal,
            [squares] + first_all + in_all + out_all + list(held),
            [shape(8, 128)] + [shape(*v.shape) for v in held],
            scratch=[pltpu.VMEM(v.shape, f32) for v in held]
            + [pltpu.VMEM((SEQ, ROWS, D), f32), pltpu.VMEM((SEQ, 2 * ROWS, D), f32)],
            sems=15,
            far_outs=range(1, 16),
            name="adamw", work=0.1,
        )
        new = [v.reshape(-1) for v in done[1:4]] + list(done[4:])
        clip_norm = done[0][0, 0]
    else:
        by_group = jnp.stack(first_grads)
        shard_first = lax.psum_scatter(
            by_group[:, :ROWS].reshape(D, D), "dp", scatter_dimension=0, tiled=True
        )
        proj_full = jnp.stack([p.reshape(GROUPS, SUB, D) for p in ordered(proj_grads, mine)], axis=1)
        proj_grad = lax.psum(
            lax.psum_scatter(proj_full.reshape(D, D), "dp", scatter_dimension=0, tiled=True), "seq"
        )
        all_vec = lax.psum(by_group[:, ROWS : ROWS + 3, :HALF_VEC], ("dp", "seq")).reshape(-1)
        vec_grad = lax.dynamic_slice_in_dim(all_vec, home * vectors.shape[0], vectors.shape[0])
        joined = lax.all_gather(shard_first, "seq", axis=0, tiled=False)
        qkv_grad = jnp.concatenate(
            [joined[j, :, i * CH : i * CH + QUARTER] for i in range(3) for j in range(SEQ)], axis=1
        )
        shard_in, shard_out = (
            lax.psum_scatter(jnp.concatenate(parts, axis=0), "dp", scatter_dimension=0, tiled=True)
            for parts in (in_grads, out_grads)
        )
        in_all = lax.all_gather(shard_in, "seq", axis=0, tiled=False)
        in_grad = in_all.reshape(SEQ, rows, dp_parts, units).transpose(1, 2, 0, 3).reshape(rows, -1)
        out_grad = lax.all_gather(shard_out, "seq", axis=0, tiled=True)
        total = sum(jnp.sum(g * g) for g in (qkv_grad, proj_grad, in_grad, out_grad, vec_grad))
        total = lax.psum(total, "dp")
        clip_norm = jnp.sqrt(total)
        factor = clip_limit / jnp.maximum(clip_norm, clip_limit)
        grads = (vec_grad, qkv_grad, proj_grad, in_grad, out_grad)
        new = []
        for number, grad in enumerate(grads):
            rate, decay = (matrix_rate, weight_decay) if number else (vector_rate, 0.0)
            new.extend(adamw_update(*states[3 * number : 3 * number + 3], factor * grad, rate, decay))
    (output,) = run(
        output_kernel,
        scal,
        [out_base, top_last, swap(out_bottom, 2, "output_bottom"), vec],
        [chunk],
        name="output", work=2.0,
    )
    return (output.reshape(tokens.shape), input_grad.reshape(tokens.shape), clip_norm, *new)


def solution(mesh):
    row = P("dp", "seq", None)
    mark = P("dp", "seq")
    vec = P("dp")
    mat = P("dp", None)
    return jax.shard_map(
        local,
        mesh=mesh,
        in_specs=(row, row, mark, mark) + (vec,) * 3 + (mat,) * 12,
        out_specs=(row, row, P()) + (vec,) * 3 + (mat,) * 12,
        check_vma=False,
    )
```

```python
import functools
import math

import jax
import jax.numpy as jnp
from jax import lax
from jax.experimental import pallas as pl
from jax.experimental.pallas import tpu as pltpu
from jax.sharding import PartitionSpec as P

D = 768
HEADS = 12
HEAD = 64
STEP = 10
CH = 256
LEN = 1024
SEQ = 4
QUARTER = D // SEQ
OWN = HEADS // SEQ
GROUPS = 8
ROWS = D // GROUPS
SUB = ROWS // SEQ
HALF = GROUPS // 2
CUT = ROWS // 2
HALF_VEC = D // 2
VEC_ROWS = 24

f32 = jnp.float32
bf16 = jnp.bfloat16
masked_score = -1e30
norm_eps = 1e-05
clip_limit = 1.0
beta_one = 0.9
beta_two = 0.999
adam_eps = 1e-08
matrix_rate = 0.02
vector_rate = 0.4
weight_decay = 0.01
gelu_scale = 0.7978845608028654
gelu_cubic = 0.044715

COST = 1e9

WHOLE = pl.BlockSpec(memory_space=pltpu.VMEM)
SCALARS = pl.BlockSpec(memory_space=pltpu.SMEM)
NN = ((1,), (0,))
NT = ((1,), (1,))
TN = ((0,), (0,))


def shape(*dims, kind=f32):
    return jax.ShapeDtypeStruct(dims, kind)


def run(
    kernel, scal, args, outs, scratch=(), sems=0, far_args=(), far_outs=(), room=8, work=1.0, name=None, after=()
):
    args, after = list(args), list(after)
    held = sum(math.prod(v.shape) * jnp.dtype(v.dtype).itemsize for v in scratch)
    anywhere, far = pl.BlockSpec(memory_space=pl.ANY), pl.BlockSpec(memory_space=pltpu.HBM)
    scratch = list(scratch) + ([pltpu.SemaphoreType.DMA((sems,))] if sems else [])

    def body(scal_ref, *refs):
        kernel(scal_ref, *refs[: len(args)], *refs[len(args) + len(after) :])

    return pl.pallas_call(
        body,
        out_shape=tuple(outs),
        in_specs=[SCALARS]
        + [far if i in far_args else WHOLE for i in range(len(args))]
        + [anywhere] * len(after),
        out_specs=tuple(far if i in far_outs else WHOLE for i in range(len(outs))),
        scratch_shapes=scratch,
        compiler_params=pltpu.CompilerParams(vmem_limit_bytes=held + (room << 20)),
        cost_estimate=pl.CostEstimate(
            flops=int(work * COST), bytes_accessed=1, transcendentals=0
        ),
        name=name,
    )(scal, *args, *after)


def gate(value, after):
    anywhere = pl.BlockSpec(memory_space=pl.ANY)
    return pl.pallas_call(
        lambda *refs: None,
        out_shape=shape(*value.shape, kind=value.dtype),
        in_specs=[anywhere] * (1 + len(after)),
        out_specs=anywhere,
        input_output_aliases={0: 0},
        compiler_params=pltpu.CompilerParams(vmem_limit_bytes=1 << 20),
        name="gate",
    )(value, *after)


def sums(groups, after=()):
    sizes = [len(group) for group in groups]

    def body(*refs):
        at = 0
        for number, size in enumerate(sizes):
            total = refs[at][...]
            for ref in refs[at + 1 : at + size]:
                total = total + ref[...]
            refs[sum(sizes) + len(after) + number][...] = total
            at += size

    return pl.pallas_call(
        body,
        out_shape=tuple(shape(*group[0].shape) for group in groups),
        in_specs=[WHOLE] * sum(sizes) + [pl.BlockSpec(memory_space=pl.ANY)] * len(after),
        out_specs=tuple([WHOLE] * len(groups)),
        compiler_params=pltpu.CompilerParams(vmem_limit_bytes=4 << 20),
        cost_estimate=pl.CostEstimate(flops=int(COST), bytes_accessed=1, transcendentals=0),
        name="plus",
    )(*(term for group in groups for term in group), *after)


def plus(*terms, after=()):
    return sums([terms], after)[0]


def sum_pairs(one, two, three, four):
    def body(a, b, c, d, result):
        result[...] = (a[...] + b[...]) + (c[...] + d[...])

    return pl.pallas_call(
        body,
        out_shape=shape(*one.shape),
        in_specs=[WHOLE] * 4,
        out_specs=WHOLE,
        compiler_params=pltpu.CompilerParams(vmem_limit_bytes=1 << 20),
        name="sum_pairs",
    )(one, two, three, four)


def split_rows(one, two, cut):
    def body(one_ref, two_ref, top, rest):
        top[...] = one_ref[:cut, :]
        rest[...] = two_ref[cut:, :]

    return pl.pallas_call(
        body,
        out_shape=(shape(cut, one.shape[1]), shape(two.shape[0] - cut, two.shape[1])),
        in_specs=[WHOLE] * 2,
        out_specs=(WHOLE, WHOLE),
        compiler_params=pltpu.CompilerParams(vmem_limit_bytes=4 << 20),
        cost_estimate=pl.CostEstimate(flops=int(COST), bytes_accessed=1, transcendentals=0),
        name="split_rows",
    )(one, two)


def owner(scal, k):
    spot = jnp.bitwise_and(scal[1] + k, GROUPS - 1)
    return jnp.where(scal[2] > 0, jnp.where(spot < HALF, 2 * spot, 2 * GROUPS - 1 - 2 * spot), k)


def halves(value):
    top = value.astype(bf16)
    return top, (value - top.astype(f32)).astype(bf16)


def dot(left, right, dims):
    return lax.dot_general(left, right, (dims, ((), ())), preferred_element_type=f32)


def dot3(lh, ll, rh, rl, dims):
    (left,), (right,) = dims
    join = lambda parts, axis: jnp.concatenate([part[...] for part in parts], axis=axis)
    return dot(join([lh, lh, ll], left), join([rh, rl, rh], right), dims)


def rows_at(index, size):
    return pl.ds(pl.multiple_of(index * size, size), size)


def piece(vec, number):
    a, b = 2 * number, 2 * number + 1
    return jnp.concatenate(
        [vec[a // 3, a % 3 : a % 3 + 1, :], vec[b // 3, b % 3 : b % 3 + 1, :]], axis=1
    )


def norm_stats(inputs):
    center = inputs - jnp.mean(inputs, axis=-1, keepdims=True)
    spread = jnp.mean(center * center, axis=-1, keepdims=True)
    scale = lax.rsqrt(spread + norm_eps)
    return center * scale, scale


def norm_back(hat, scale, gain, grad):
    inner = grad * gain
    return scale * (
        inner
        - jnp.mean(inner, axis=-1, keepdims=True)
        - hat * jnp.mean(inner * hat, axis=-1, keepdims=True)
    )


def low_lanes(dims):
    return lax.broadcasted_iota(jnp.int32, dims, 1) < HEAD


def lane_pairs(pair, last):
    low = low_lanes(pair.shape)
    roll = lambda v: pltpu.roll(v, HEAD, 1)
    ph = pair.astype(bf16).astype(f32)
    pl_ = pair - ph
    lh = last.astype(bf16).astype(f32)
    ll = last - lh
    return [
        jnp.where(low, ph, roll(pl_)).astype(bf16),
        jnp.where(low, roll(ph), pl_).astype(bf16),
        jnp.where(low, lh, roll(ll)).astype(bf16),
    ]


def row_halves(turned, head):
    part = turned[HEAD * head : HEAD * (head + 1)]
    return halves(part)


def pack_first_kernel(scal, wqkv, wproj, vec, seg, valid, tokens, first, packed, *refs):
    bands, proj, lines, marks, sems = refs
    mine = scal[0]
    aligned = pl.multiple_of(jnp.bitwise_and(mine * QUARTER, -128), 128)
    copies = [
        pltpu.make_async_copy(wqkv.at[:, pl.ds(part * D + aligned, CH)], bands.at[part], sems.at[part])
        for part in range(3)
    ]
    sub = pl.ds(pl.multiple_of(mine * SUB, 8), SUB)
    copies.append(pltpu.make_async_copy(wproj.at[sub, :], proj, sems.at[3]))
    copies.append(pltpu.make_async_copy(vec, lines, sems.at[4]))
    copies.append(pltpu.make_async_copy(seg, marks.at[0], sems.at[5]))
    copies.append(pltpu.make_async_copy(valid, marks.at[1], sems.at[6]))
    copies.append(pltpu.make_async_copy(tokens, packed.at[:CH, :], sems.at[7]))
    for copy in copies:
        copy.start()
    first[ROWS:, :] = jnp.zeros((8, D), f32)
    packed[CH:, :] = jnp.zeros((8, D), f32)
    for copy in copies[:5]:
        copy.wait()
    turn = jnp.where(jnp.bitwise_and(mine, 1) > 0, CH - HEAD, 0)
    for part in range(3):
        turned = pltpu.roll(bands[part], turn, 1)
        first[:ROWS, part * CH : part * CH + QUARTER] = turned[:, :QUARTER]
        for group in range(SEQ):
            lane = HEAD * (3 * group + part)
            first[group * SUB : (group + 1) * SUB, part * CH + QUARTER : (part + 1) * CH] = proj[
                :, lane : lane + HEAD
            ]
        first[ROWS + part : ROWS + part + 1, :HALF_VEC] = jnp.concatenate(
            [lines[3 * part + i : 3 * part + i + 1, :] for i in range(3)], axis=1
        )
    for copy in copies[5:]:
        copy.wait()
    packed[CH : CH + 1, :CH] = jnp.where(marks[1] > 0, marks[0], -1).astype(f32)


def pack_second_kernel(scal, win, wout, in_block, out_block):
    mine = scal[0]
    turn = lax.rem(HALF_VEC - mine * ROWS, HALF_VEC)
    for part in range(GROUPS):
        turned = pltpu.roll(win[:, part * HALF_VEC : (part + 1) * HALF_VEC], turn, 1)
        in_block[:, part * ROWS : (part + 1) * ROWS] = turned[:, :ROWS]
    out_block[...] = wout[pl.ds(pl.multiple_of(mine * ROWS, 8), ROWS), :]


def mask_kernel(scal, cotangent, valid, result):
    keep = jnp.where(valid[...] > 0, 1.0, 0.0).astype(f32)
    column = jnp.broadcast_to(keep, (128, CH)).T[:, :1]
    result[...] = cotangent[...] * column


def weights_kernel(scal, *refs):
    blocks, (wh, wl, vec, proj) = refs[: GROUPS + 1], refs[GROUPS + 1 :]
    spans = [(k, 0, ROWS + 8) for k in range(GROUPS)]
    spans[HALF : HALF + 1] = [(HALF, 0, CUT), (HALF, CUT, ROWS + 8)]
    for ref, (k, first, last) in zip(blocks, spans):
        at = owner(scal, k)
        size = min(last, ROWS) - first
        block = ref[:size, :]
        here = pl.ds(pl.multiple_of(at * ROWS + first, CUT), size)
        wh[here, :], wl[here, :] = halves(block)
        if last > ROWS:
            vec[at] = ref[size:, :HALF_VEC]
        for group in range(SEQ):
            top, end = group * SUB - first, (group + 1) * SUB - first
            if top < 0 or end > size:
                continue
            for part in range(3):
                lane = HEAD * (3 * group + part)
                proj[pl.ds(pl.multiple_of(at * SUB, 8), SUB), lane : lane + HEAD] = block[
                    top:end, part * CH + QUARTER : (part + 1) * CH
                ]


def front_kernel(scal, *refs):
    toks, refs = refs[:4], refs[4:]
    wh, wl, vec = refs[:3]
    xh, xl, kcat, qturn, vcat, qpair, kturn, low_row, outs_turn, lse, vturn, label = refs[3:]
    mine = scal[0]

    gain, shift = piece(vec, 0), piece(vec, 1)
    turn = lax.rem(D - mine * QUARTER, D)
    own = lambda number: pltpu.roll(jnp.broadcast_to(piece(vec, number), (8, D)), turn, 1)[:1, :CH]
    query_bias, value_bias = own(2), own(3)

    for r in range(SEQ):
        nat = jnp.bitwise_xor(mine, r)
        at = rows_at(nat, CH)
        label[nat] = toks[r][CH:, :CH]
        hat, _ = norm_stats(toks[r][:CH, :])
        xh[at, :], xl[at, :] = halves(hat)
        nh, nl = halves(hat * gain + shift)
        joined = dot3(nh, nl, wh[...], wl[...], NN)
        query = (joined[:, :CH] + query_bias) * HEAD ** (-0.5)
        key = joined[:, CH : 2 * CH]
        value = joined[:, 2 * CH :] + value_bias
        keys = lane_pairs(key[:, :128], key[:, 128:])
        values = lane_pairs(value[:, :128], value[:, 128:])
        queries = lane_pairs(query[:, :128], query[:, 128:])
        key_t, value_t, query_t = key.T, value.T, query.T
        for h in range(OWN):
            kcat[h, at, :] = jnp.concatenate([keys[h], keys[h]], axis=1)
            vcat[h, at, :] = jnp.concatenate([values[h], values[h]], axis=1)
            qpair[h, at, :] = queries[h]
            a, b = row_halves(query_t, h)
            qturn[h, :, at] = jnp.concatenate([a, a, b, b], axis=0)
            a, b = row_halves(key_t, h)
            kturn[h, :, at] = jnp.concatenate([a, b], axis=0)
            a, b = row_halves(value_t, h)
            vturn[h, :, at] = jnp.concatenate([a, b], axis=0)

    labels = jnp.concatenate([label[c][:1, :] for c in range(SEQ)], axis=1)
    spot = lax.broadcasted_iota(jnp.int32, (1, LEN), 1).astype(f32)
    begin = jnp.zeros((1, LEN), f32)
    for segment in range(3):
        held = jnp.sum(jnp.where(labels == float(segment), 1.0, 0.0), axis=1, keepdims=True)
        begin = begin + jnp.where(labels > float(segment), held, 0.0)
    begin = jnp.where(labels < 0.0, spot, begin)
    low_row[...] = jnp.broadcast_to(begin, (8, LEN))

    def one_head(h, carry):
        for c in range(SEQ):
            size = CH * (c + 1)
            lanes = slice(c * CH, (c + 1) * CH)
            score = dot(kcat[h, :size, :], qturn[h, :, lanes], NN)
            mask = allowed(low_row, c, size)
            score = jnp.where(mask, score, masked_score)
            peak = jnp.max(score, axis=0, keepdims=True)
            weight = jnp.exp(score - peak)
            total = jnp.sum(weight, axis=0, keepdims=True)
            top, rest = halves(weight)
            both = dot(vturn[h, :, :size], top, NN)
            extra = dot(vturn[h, :HEAD, :size], rest, NN)
            result = (both[:HEAD] + both[HEAD:] + extra) / total
            outs_turn[pl.ds(pl.multiple_of(h * HEAD, HEAD), HEAD), lanes] = result
            lse[h, :, lanes] = jnp.broadcast_to(peak + jnp.log(total), (8, CH))
        return carry

    lax.fori_loop(0, OWN, one_head, 0)


def allowed(low_row, c, size):
    key_at = lax.broadcasted_iota(jnp.int32, (size, CH), 0).astype(f32)
    query_at = (lax.broadcasted_iota(jnp.int32, (1, CH), 1) + c * CH).astype(f32)
    begin = low_row[:1, c * CH : (c + 1) * CH]
    return (key_at >= begin) & (key_at <= query_at)


def proj_kernel(scal, *refs):
    toks, heads, parts, refs = refs[:4], refs[4:8], refs[8:12], refs[12:]
    vec, wh, wl, heads_h, heads_l, norm_h, norm_l, mixed, hat, scale, weight, joined = refs
    mine = scal[0]
    for r in range(SEQ):
        at = jnp.bitwise_xor(mine, r)
        for d in range(GROUPS):
            weight[pl.ds(pl.multiple_of(d * ROWS + at * SUB, 8), SUB), :] = parts[r][
                d * SUB : (d + 1) * SUB, :
            ]
        joined[rows_at(at, QUARTER), :] = heads[r][...]
    wh[...], wl[...] = halves(weight[...])
    heads_h[...], heads_l[...] = halves(joined[:, rows_at(mine, CH)])
    gain, shift = piece(vec, 5), piece(vec, 6)
    for r in range(SEQ):
        at = rows_at(jnp.bitwise_xor(mine, r), CH)
        a, b = halves(joined[:, at].T)
        total = toks[r][:CH, :] + dot3(a, b, wh[...], wl[...], NN)
        total = total + piece(vec, 4)
        normed, size = norm_stats(total)
        norm_h[r], norm_l[r] = halves(normed * gain + shift)
        if r == 0:
            mixed[...] = total
            hat[...] = normed
            scale[...] = jnp.broadcast_to(size, (CH, 128))


def hidden_kernel(scal, norm_h, norm_l, *refs):
    blocks, vec, acts_h, acts_l, slope, winh, winl = refs[: GROUPS + 1], *refs[GROUPS + 1 :]
    mine = scal[0]
    spans = [(k, 0) for k in range(GROUPS)]
    spans.insert(HALF + 1, (HALF, CUT))
    for ref, (k, first) in zip(blocks, spans):
        at = pl.ds(pl.multiple_of(owner(scal, k) * ROWS + first, CUT), ref.shape[0])
        winh[at, :], winl[at, :] = halves(ref[...])
    marks = [16 + d for d in range(GROUPS)]
    table = jnp.concatenate([vec[m // 3, m % 3 : m % 3 + 1, :] for m in marks], axis=0)
    table = pltpu.roll(table, lax.rem(HALF_VEC - mine * ROWS, HALF_VEC), 1)[:, :ROWS]
    bias = jnp.concatenate([table[d : d + 1] for d in range(GROUPS)], axis=1)
    for r in range(SEQ):
        at = slice(r * CH, (r + 1) * CH)
        hidden = dot3(norm_h[r], norm_l[r], winh[...], winl[...], NN) + bias
        inner = jnp.tanh(gelu_scale * (hidden + gelu_cubic * hidden * hidden * hidden))
        acts_h[at, :], acts_l[at, :] = halves(0.5 * hidden * (1.0 + inner))
        slope[at, :] = 0.5 * (1.0 + inner) + 0.5 * hidden * (1.0 - inner * inner) * gelu_scale * (
            1.0 + 3.0 * gelu_cubic * hidden * hidden
        )


def emit_blocks(scal, outs, whole):
    for k in range(GROUPS):
        outs[k][...] = whole[rows_at(owner(scal, k), ROWS), :]


def out_grad_kernel(scal, acts_h, acts_l, *refs):
    grads, (out_h, out_l), outs, whole = refs[:4], refs[4:6], refs[6 : 6 + GROUPS], refs[6 + GROUPS]
    for r in range(SEQ):
        at = slice(r * CH, (r + 1) * CH)
        out_h[at, :], out_l[at, :] = halves(grads[r][...])
    whole[...] = dot3(acts_h[...], acts_l[...], out_h[...], out_l[...], TN)
    emit_blocks(scal, outs, whole)


def hidden_back_kernel(scal, out_h, out_l, slope, winh, winl, *refs):
    blocks, refs = refs[:GROUPS], refs[GROUPS:]
    hid_h, hid_l, wouth, woutl, bias_sum = refs[:5]
    parts = refs[5:]
    for k in range(GROUPS):
        at = rows_at(owner(scal, k), ROWS)
        wouth[at, :], woutl[at, :] = halves(blocks[k][...])
    sums = jnp.zeros((1, D), f32)
    for r in (1, 3, 2, 0):
        at = slice(r * CH, (r + 1) * CH)
        back = dot3(out_h[at, :], out_l[at, :], wouth[...], woutl[...], NT) * slope[at, :]
        sums = sums + jnp.sum(back, axis=0, keepdims=True)
        bh, bl = halves(back)
        hid_h[at, :], hid_l[at, :] = bh, bl
        parts[r][...] = dot3(bh, bl, winh[...], winl[...], NT)
    bias_sum[...] = jnp.broadcast_to(sums, (8, D))


def in_grad_kernel(scal, norm_h, norm_l, hid_h, hid_l, *refs):
    outs, whole = refs[:GROUPS], refs[GROUPS]
    flat = lambda ref: ref[...].reshape(LEN, D)
    whole[...] = dot3(flat(norm_h), flat(norm_l), hid_h[...], hid_l[...], TN)
    emit_blocks(scal, outs, whole)


def ffn_out_kernel(scal, acts_h, acts_l, wouth, woutl, *parts):
    for r in (1, 3, 2, 0):
        at = slice(r * CH, (r + 1) * CH)
        parts[r][...] = dot3(acts_h[at, :], acts_l[at, :], wouth[...], woutl[...], NN)


def output_kernel(scal, base, top, bottom, vec, output):
    whole = base[...] + piece(vec, 7)
    half = top.shape[0]
    output[:half, :] = whole[:half] + top[...]
    output[half:, :] = whole[half:] + bottom[...]


def proj_back_kernel(scal, one, two, three, hat, scale, vec, grad_out, wh, wl, mixed_grad, sums, *parts):
    mine = scal[0]
    normed = one[...] + two[...] + three[...]
    back = norm_back(hat[...], scale[:, :1], piece(vec, 5), normed)
    total = grad_out[...] + back
    mixed_grad[...] = total
    a, b = halves(total)
    for r in range(SEQ):
        at = rows_at(jnp.bitwise_xor(mine, r), QUARTER)
        parts[r][...] = dot3(wh[at, :], wl[at, :], a, b, NT)
    add = lambda v: jnp.sum(v, axis=0, keepdims=True)
    sums[...] = jnp.concatenate(
        [add(total), add(normed * hat[...]), add(normed), add(grad_out[...]), jnp.zeros((4, D), f32)],
        axis=0,
    )


def proj_grad_kernel(scal, heads_h, heads_l, mixed_grad, *refs):
    outs, whole = refs[:-1], refs[-1]
    mine = scal[0]
    gh, gl = halves(mixed_grad[...])
    whole[...] = dot3(heads_h[...], heads_l[...], gh, gl, NN)
    for r in range(SEQ):
        at = jnp.bitwise_xor(mine, r)
        for d in range(GROUPS):
            outs[r][d * SUB : (d + 1) * SUB, :] = whole[
                pl.ds(pl.multiple_of(d * ROWS + at * SUB, 8), SUB), :
            ]


def back_kernel(scal, *refs):
    grads, refs = refs[:4], refs[4:]
    kcat, qturn, vcat, qpair, kturn, outs_turn, lse, low_row = refs[:8]
    joined_h, joined_l, joined_sums = refs[8:11]
    gturn, gpair, dots, key_sum, value_sum, query_turn = refs[11:]
    mine = scal[0]

    for r in range(SEQ):
        at = rows_at(jnp.bitwise_xor(mine, r), CH)
        turned = grads[r][...]
        grad = jnp.concatenate([turned, jnp.zeros((HEAD, CH), f32)], axis=0).T
        pairs = lane_pairs(grad[:, :128], grad[:, 128:])
        for h in range(OWN):
            gpair[h, at, :] = pairs[h]
            part = turned[HEAD * h : HEAD * (h + 1)]
            dots[h, :, at] = jnp.broadcast_to(
                jnp.sum(part * outs_turn[HEAD * h : HEAD * (h + 1), at], axis=0, keepdims=True), (8, CH)
            )
            a, b = halves(part)
            gturn[h, :, at] = jnp.concatenate([a, a, b, b], axis=0)

    key_sum[...] = jnp.zeros_like(key_sum)
    value_sum[...] = jnp.zeros_like(value_sum)

    def one_head(h, carry):
        for c in range(SEQ):
            size = CH * (c + 1)
            lanes = slice(c * CH, (c + 1) * CH)
            score = dot(kcat[h, :size, :], qturn[h, :, lanes], NN)
            weight = jnp.where(allowed(low_row, c, size), jnp.exp(score - lse[h, :1, lanes]), 0.0)
            back = dot(vcat[h, :size, :], gturn[h, :, lanes], NN)
            score_back = weight * (back - dots[h, :1, lanes])
            a, b = halves(weight)
            pair = gpair[h, lanes, :]
            value_sum[h, :size, :] += dot(a, pair, NN) + dot(b, pair, NN)
            a, b = halves(score_back)
            pair = qpair[h, lanes, :]
            key_sum[h, :size, :] += dot(a, pair, NN) + dot(b, pair, NN)
            turned = dot(kturn[h, :, :size], a, NN) + dot(kturn[h, :, :size], b, NN)
            query_turn[h, :, lanes] = (turned[:HEAD] + turned[HEAD:]) * HEAD ** (-0.5)
        return carry

    lax.fori_loop(0, OWN, one_head, 0)

    column_sums = jnp.zeros((1, D), f32)
    low = low_lanes((CH, 128))
    for c in range(SEQ):
        at = slice(c * CH, (c + 1) * CH)
        blank = jnp.zeros((HEAD, CH), f32)
        query = jnp.concatenate([query_turn[h, :, at] for h in range(OWN)] + [blank], axis=0).T
        done = [query]
        for kept in (key_sum, value_sum):
            full = [kept[h, at, :] for h in range(OWN)]
            full = [v + pltpu.roll(v, HEAD, 1) for v in full]
            done.append(jnp.where(low, full[0], full[1]))
            done.append(jnp.where(low, full[2], 0.0))
        joined = jnp.concatenate(done, axis=1)
        column_sums = column_sums + jnp.sum(joined, axis=0, keepdims=True)
        joined_h[at, :], joined_l[at, :] = halves(joined)

    joined_sums[...] = jnp.broadcast_to(column_sums, (8, D))


def qkv_grad_kernel(scal, xh, xl, joined_h, joined_l, joined_sums, wh, wl, vec, *refs):
    proj_one, proj_two, vector_sums, bias_sum = refs[:4]
    outs, (whole, rows) = refs[4 : 4 + GROUPS], refs[4 + GROUPS :]
    mine = scal[0]
    column_sums = joined_sums[:1, :]
    core = dot3(xh[...], xl[...], joined_h[...], joined_l[...], TN)
    gain, shift = piece(vec, 0), piece(vec, 1)
    as_column = lambda v: jnp.broadcast_to(v, (128, D)).T[:, :1]
    whole[...] = as_column(gain) * core + as_column(shift) * column_sums
    weights = wh[...].astype(f32) + wl[...].astype(f32)
    gain_grad = jnp.sum(weights * core, axis=1, keepdims=True)
    shift_grad = jnp.sum(weights * column_sums, axis=1, keepdims=True)
    lane = lax.broadcasted_iota(jnp.int32, (D, 128), 1)
    norm_grads = jnp.where(lane == 0, gain_grad, shift_grad).T

    def place(part, scale):
        wide = jnp.concatenate([part[:, :QUARTER], jnp.zeros((1, D - QUARTER), f32)], axis=1)
        wide = jnp.broadcast_to(wide, (8, D))
        return pltpu.roll(wide, mine * QUARTER, 1)[:1]

    entries = [
        norm_grads[0:1],
        norm_grads[1:2],
        place(column_sums[:, :CH], 1.0),
        place(column_sums[:, 2 * CH :], 1.0),
        vector_sums[0:1],
        vector_sums[1:2],
        vector_sums[2:3],
        vector_sums[3:4],
    ]
    lines = [e[:, i * HALF_VEC : (i + 1) * HALF_VEC] for e in entries for i in range(2)]
    bias = jnp.concatenate(
        [bias_sum[:1, d * ROWS : (d + 1) * ROWS] for d in range(GROUPS)], axis=0
    )
    bias = jnp.concatenate([bias, jnp.zeros((GROUPS, HALF_VEC - ROWS), f32)], axis=1)
    bias = pltpu.roll(bias, mine * ROWS, 1)
    lines = lines + [bias[d : d + 1] for d in range(GROUPS)]
    filler = jnp.zeros((5, HALF_VEC), f32)
    for d in range(GROUPS):
        rows[d] = jnp.concatenate(lines[3 * d : 3 * d + 3] + [filler], axis=0)

    for k in range(GROUPS):
        at = owner(scal, k)
        outs[k][:ROWS, :] = whole[rows_at(at, ROWS), :]
        here = pl.ds(pl.multiple_of(at * SUB, 8), SUB)
        proj = proj_one[here, :] + proj_two[here, :]
        for group in range(SEQ):
            for part in range(3):
                lane_at = HEAD * (3 * group + part)
                outs[k][
                    group * SUB : (group + 1) * SUB, part * CH + QUARTER : (part + 1) * CH
                ] = proj[:, lane_at : lane_at + HEAD]
        outs[k][ROWS:, :HALF_VEC] = rows[at]
        outs[k][ROWS:, HALF_VEC:] = jnp.zeros((8, HALF_VEC), f32)


def pre_back_kernel(scal, joined_h, joined_l, wh, wl, *parts):
    mine = scal[0]
    for r in (1, 3, 2, 0):
        at = rows_at(jnp.bitwise_xor(mine, r), CH)
        parts[r][...] = dot3(joined_h[at, :], joined_l[at, :], wh[...], wl[...], NT)


def input_grad_kernel(scal, tokens, one, two, vec, mixed_grad, result):
    hat, scale = norm_stats(tokens[...])
    grad = one[...] + two[...]
    result[...] = mixed_grad[...] + norm_back(hat, scale, piece(vec, 0), grad)


def total_square(value):
    return jnp.sum(jnp.sum(value * value, axis=0, keepdims=True), axis=1, keepdims=True)


def shard_sums_kernel(scal, first, in_shard, out_shard, small):
    total = total_square(first[:ROWS, :]) + total_square(in_shard[...]) + total_square(out_shard[...])
    small[...] = first[ROWS:, :]
    small[7:8, :] = jnp.broadcast_to(total, (1, D))


def shard_squares_kernel(scal, one, two, three, four, squares):
    whole = (one[...] + two[...]) + (three[...] + four[...])
    squares[...] = jnp.broadcast_to(whole[7:8, :1] + total_square(whole[:3, :HALF_VEC]), (8, 128))


def stage_kernel(scal, *refs):
    sources, targets, sems = refs[:15], refs[15:30], refs[30]
    copies = [
        pltpu.make_async_copy(source, target, sems.at[i])
        for i, (source, target) in enumerate(zip(sources, targets))
    ]
    for copy in copies:
        copy.start()
    for copy in copies:
        copy.wait()


def adamw_kernel(scal, squares, *refs):
    firsts, ins, outs, refs = refs[:4], refs[4:8], refs[8:12], refs[12:]
    states, clip, finals, news = refs[:15], refs[15], refs[16:31], refs[31:46]
    first, second, sems = refs[46:]
    send = lambda number: [
        pltpu.make_async_copy(news[i], finals[i], sems.at[i]) for i in range(3 * number, 3 * number + 3)
    ]
    mine = scal[0]
    norm = jnp.sqrt(squares[...])
    clip[...] = norm
    factor = (clip_limit / jnp.maximum(norm, clip_limit))[:1, :1]
    for r in range(SEQ):
        at = jnp.bitwise_xor(mine, r)
        first[at] = firsts[r][:ROWS, :]
        second[at, :ROWS] = ins[r][...]
        second[at, ROWS:] = outs[r][...]

    def update(number, spot, grad, rate, decay):
        held = [states[3 * number + i][spot] for i in range(3)]
        fresh = adamw_update(*held, factor * grad, rate, decay)
        for i in range(3):
            news[3 * number + i][spot] = fresh[i]

    def finish(number):
        for copy in send(number):
            copy.start()

    lines = [firsts[r][ROWS:, :HALF_VEC] for r in range(SEQ)]
    line = (lines[0] + lines[1]) + (lines[2] + lines[3])
    for i in range(3):
        for j in range(3):
            spot = (slice(3 * i + j, 3 * i + j + 1), slice(None))
            update(0, spot, line[i : i + 1, 128 * j : 128 * (j + 1)], vector_rate, 0.0)
    finish(0)
    every = slice(None)
    for part in range(3):
        grad = jnp.concatenate(
            [first[j][:, part * CH : part * CH + QUARTER] for j in range(SEQ)], axis=1
        )
        update(1, (every, slice(part * D, (part + 1) * D)), grad, matrix_rate, weight_decay)
    finish(1)
    for j in range(SEQ):
        grad = jnp.concatenate(
            [
                first[j][group * SUB : (group + 1) * SUB, part * CH + QUARTER : (part + 1) * CH]
                for group in range(SEQ)
                for part in range(3)
            ],
            axis=1,
        )
        update(2, (slice(j * SUB, (j + 1) * SUB), every), grad, matrix_rate, weight_decay)
    finish(2)
    for d in range(GROUPS):
        grad = jnp.concatenate(
            [second[j][:ROWS, d * ROWS : (d + 1) * ROWS] for j in range(SEQ)], axis=1
        )
        update(3, (every, slice(d * HALF_VEC, (d + 1) * HALF_VEC)), grad, matrix_rate, weight_decay)
    finish(3)
    for j in range(SEQ):
        update(
            4, (slice(j * ROWS, (j + 1) * ROWS), every), second[j][ROWS:, :], matrix_rate, weight_decay
        )
    finish(4)
    for number in range(5):
        for copy in send(number):
            copy.wait()


def adamw_update(weight, first, second, grad, rate, decay):
    new_first = beta_one * first + (1.0 - beta_one) * grad
    new_second = beta_two * second + (1.0 - beta_two) * grad * grad
    first_hat = new_first / (1.0 - beta_one**STEP)
    second_hat = new_second / (1.0 - beta_two**STEP)
    new_weight = weight - rate * (first_hat / (jnp.sqrt(second_hat) + adam_eps) + decay * weight)
    return (new_first, new_second, new_weight)


def ring_tables(count):
    evens = [2 * i for i in range(count // 2)]
    order = evens + [i + 1 for i in reversed(evens)]
    place = [0] * count
    for position, device in enumerate(order):
        place[device] = position
    right = [(order[i], order[(i + 1) % count]) for i in range(count)]
    left = [(b, a) for a, b in right]
    return order, place, right, left


class RingGather:
    def __init__(self, block, name, flip=False):
        _, _, self.right, self.left = ring_tables(GROUPS)
        if flip:
            self.right, self.left = self.left, self.right
        self.got, self.name, self.at, self.flip = {0: block}, name, 0, flip

    def step(self, after=()):
        places = (-self.at % GROUPS, self.at)
        if after:
            for place in set(places):
                self.got[place] = gate(self.got[place], after)
        forth, back = (self.got[place] for place in places)
        self.at += 1
        self.got[GROUPS - self.at] = move(forth, "dp", self.right, f"{self.name}_right_{self.at}")
        if self.at < HALF:
            self.got[self.at] = move(back, "dp", self.left, f"{self.name}_left_{self.at}")
        return [self.got[GROUPS - self.at]] + ([self.got[self.at]] if self.at < HALF else [])

    def halved(self, cut):
        top, rest = split_rows(self.got[GROUPS - self.at], self.got[self.at], cut)
        self.at += 1
        self.got[HALF] = move(top, "dp", self.right, f"{self.name}_right_{self.at}")
        self.got[GROUPS] = move(rest, "dp", self.left, f"{self.name}_left_{self.at}")
        return [self.got[HALF], self.got[GROUPS]]

    def blocks(self):
        blocks = [self.got[-k % GROUPS if self.flip else k] for k in range(GROUPS)]
        if GROUPS in self.got:
            blocks.insert(HALF + 1, self.got[GROUPS])
        return blocks


class RingScatter:
    def __init__(self, blocks, name, flip=False):
        _, _, self.right, self.left = ring_tables(GROUPS)
        self.blocks = blocks
        if flip:
            self.right, self.left = self.left, self.right
            self.blocks = [blocks[-k % GROUPS] for k in range(GROUPS)]
        self.name, self.back, self.at = name, None, HALF
        self.forth = move(self.blocks[HALF], "dp", self.right, f"{name}_right_1")

    def step(self, after=()):
        self.at -= 1
        ahead, back = self.blocks[self.at], self.blocks[GROUPS - self.at]
        if self.back is None:
            forth = plus(self.forth, ahead, after=after)
        else:
            forth, back = sums([(self.forth, ahead), (self.back, back)], after)
        number = HALF + 1 - self.at
        self.forth = move(forth, "dp", self.right, f"{self.name}_right_{number}")
        self.back = move(back, "dp", self.left, f"{self.name}_left_{number}")
        return [forth, back]

    def result(self, after=()):
        return plus(self.forth, self.back, self.blocks[0], after=after)


def move(block, axis, pairs, name):
    with jax.named_scope(name):
        return lax.ppermute(block, axis, pairs)


def swap(block, bits, name):
    return move(block, "seq", [(i, i ^ bits) for i in range(SEQ)], f"{name}_{bits}")


def gather_seq(block, name):
    across = swap(block, 2, name)
    core = swap(block, 1, name)
    return [block, core, across, swap(across, 1, f"{name}_2")]


def exchange_seq(parts, name):
    return [parts[0]] + [swap(parts[r], r, name) for r in range(1, SEQ)]


def scatter_core(parts, name):
    return parts[0], swap(parts[1], 1, f"{name}_own"), parts[2], swap(parts[3], 1, f"{name}_across")


def ordered(blocks, mine):
    stack = jnp.stack(blocks, axis=0)
    return [lax.dynamic_index_in_dim(stack, mine ^ j, 0, keepdims=False) for j in range(len(blocks))]


def local(
    tokens,
    cotangent,
    segment_ids,
    valid,
    vectors,
    vec_first,
    vec_second,
    w_qkv,
    qkv_first,
    qkv_second,
    w_proj,
    proj_first,
    proj_second,
    w_in,
    in_first,
    in_second,
    w_out,
    out_first,
    out_second,
):
    dp_parts = lax.axis_size("dp")
    ring = dp_parts == GROUPS
    mine = lax.axis_index("seq")
    home = lax.axis_index("dp")
    rows = w_qkv.shape[0]
    units = w_out.shape[0] // SEQ
    far, near = home // 2, home % 2
    position = jnp.where(near > 0, GROUPS - 1 - far, far)
    scal = jnp.stack([mine, position, jnp.full_like(mine, 1 if ring else 0)]).astype(jnp.int32)
    flat_in = tokens.reshape(CH, D)
    chunk, tall, square = shape(CH, D), shape(LEN, D, kind=bf16), shape(D, D, kind=bf16)

    if ring:
        first, packed = run(
            pack_first_kernel,
            scal,
            [w_qkv, w_proj, vectors.reshape(9, 128), segment_ids, valid, flat_in],
            [shape(ROWS + 8, D), shape(CH + 8, D)],
            scratch=[
                pltpu.VMEM((3, ROWS, CH), f32),
                pltpu.VMEM((SUB, D), f32),
                pltpu.VMEM((9, 128), f32),
                pltpu.VMEM((2, 1, CH), jnp.int32),
            ],
            sems=8,
            far_args=range(6),
            room=54,
            name="pack_first", work=3.0,
        )
        ring_first = RingGather(first, "first")
        for _ in range(HALF - 1):
            ring_first.step()
        ring_first.halved(CUT)
        firsts = ring_first.blocks()
        in_block, out_block = run(
            pack_second_kernel,
            scal,
            [w_in, w_out],
            [shape(ROWS, D)] * 2,
            name="pack_second", work=3.0,
            after=[firsts[GROUPS]],
        )
        ring_in = RingGather(in_block, "w_in")
        ring_out = RingGather(out_block, "w_out", flip=True)
        came = ring_in.step([firsts[HALF], firsts[HALF + 1]])
        came = came + ring_out.step([firsts[HALF], firsts[HALF + 1]])
    else:
        padded = jnp.pad(w_qkv, ((0, 0), (0, CH)))
        own = lambda part: lax.dynamic_slice_in_dim(padded, part * D + mine * QUARTER, CH, 1)
        first = jnp.concatenate([own(0), own(1), own(2)], axis=1)
        first = lax.all_gather(first, "dp", axis=0, tiled=True).reshape(GROUPS, ROWS, D)
        all_vec = lax.all_gather(vectors, "dp", axis=0, tiled=True).reshape(GROUPS, 3, HALF_VEC)
        first = jnp.concatenate([first, jnp.pad(all_vec, ((0, 0), (0, 5), (0, D - HALF_VEC)))], axis=1)
        firsts = [first[k] for k in range(GROUPS)]
        firsts[HALF : HALF + 1] = [first[HALF, :CUT], first[HALF, CUT:]]
        in_part = lax.dynamic_index_in_dim(
            w_in.reshape(rows, dp_parts, SEQ, units), mine, 2, keepdims=False
        ).reshape(rows, D)
        out_part = lax.dynamic_slice_in_dim(w_out, mine * units, units, 0)
        in_blocks, out_blocks = (
            list(lax.all_gather(part, "dp", axis=0, tiled=True).reshape(GROUPS, ROWS, D))
            for part in (in_part, out_part)
        )
        in_blocks[HALF : HALF + 1] = [in_blocks[HALF][:CUT], in_blocks[HALF][CUT:]]
        marks = jnp.where(valid > 0, segment_ids, -1).astype(f32)
        packed = jnp.concatenate([flat_in, jnp.pad(marks, ((0, 7), (0, D - CH)))], axis=0)
    toks = gather_seq(packed, "tokens")
    (grad_out,) = run(
        mask_kernel, scal, [cotangent.reshape(CH, D), valid], [chunk], name="mask", work=2.0, after=[toks[2]]
    )
    grads_row = gather_seq(grad_out, "cotangent")

    qkv_h, qkv_l, vec, proj = run(
        weights_kernel,
        scal,
        firsts,
        [square, square, shape(GROUPS, 8, HALF_VEC), shape(GROUPS * SUB, D)],
        name="weights", work=3.0,
    )
    if ring:
        proj_parts = gather_seq(proj, "w_proj")
    else:
        full = lax.all_gather(w_proj, "dp", axis=0, tiled=True).reshape(GROUPS, SEQ, SUB, D)
        proj_parts = [
            lax.dynamic_index_in_dim(full, mine ^ r, 1, keepdims=False).reshape(GROUPS * SUB, D)
            for r in range(SEQ)
        ]
    hat_h, hat_l, kcat, qturn, vcat, qpair, kturn, low_row, heads, lse = run(
        front_kernel,
        scal,
        toks + [qkv_h, qkv_l, vec],
        [
            tall,
            tall,
            shape(OWN, LEN, 256, kind=bf16),
            shape(OWN, 256, LEN, kind=bf16),
            shape(OWN, LEN, 256, kind=bf16),
            shape(OWN, LEN, 128, kind=bf16),
            shape(OWN, 128, LEN, kind=bf16),
            shape(8, LEN),
            shape(QUARTER, LEN),
            shape(OWN, 8, LEN),
        ],
        scratch=[pltpu.VMEM((OWN, 128, LEN), bf16), pltpu.VMEM((SEQ, 8, CH), f32)],
        name="front", work=14.0,
        after=[grads_row[2]],
    )
    if ring:
        heads = gate(heads, [proj_parts[2], *came])
        ring_in.step([lse])
        came = ring_in.step()
        came = came + ring_in.halved(CUT)
        ring_out.step(came)
        in_blocks = ring_in.blocks()
    across = swap(heads, 2, "heads")
    if ring:
        across = gate(across, came)
    all_heads = [heads, swap(heads, 1, "heads"), across, swap(across, 1, "heads_2")]
    wide = shape(D, CH, kind=bf16)
    split = shape(SEQ, CH, D, kind=bf16)
    proj_h, proj_l, heads_h, heads_l, norm_h, norm_l, mixed, hat_two, scale_two = run(
        proj_kernel,
        scal,
        toks + all_heads + proj_parts + [vec],
        [square, square, wide, wide, split, split, chunk, chunk, shape(CH, 128)],
        scratch=[pltpu.VMEM((D, D), f32), pltpu.VMEM((D, LEN), f32)],
        name="proj", work=8.0,
    )

    if ring:
        ring_out.step([norm_h])
        ring_out.step()
        out_blocks = ring_out.blocks()
    block = shape(ROWS, D)
    acts_h, acts_l, slope, in_wh, in_wl = run(
        hidden_kernel,
        scal,
        [norm_h, norm_l] + in_blocks + [vec],
        [tall, tall, shape(LEN, D), square, square],
        name="hidden", work=8.0,
    )
    done = run(
        out_grad_kernel,
        scal,
        [acts_h, acts_l] + grads_row,
        [tall, tall] + [block] * GROUPS,
        scratch=[pltpu.VMEM((D, D), f32)],
        name="out_grad", work=5.0,
    )
    out_h, out_l = done[:2]
    out_grads = list(done[2:])
    if ring:
        ring_out = RingScatter(out_grads, "out_grad")
    done = run(
        hidden_back_kernel,
        scal,
        [out_h, out_l, slope, in_wh, in_wl] + out_blocks,
        [tall, tall, square, square, shape(8, D)] + [chunk] * SEQ,
        name="hidden_back", work=11.0,
        after=out_grads[:1],
    )
    hid_h, hid_l, out_wh, out_wl, bias_sum = done[:5]
    parts = list(done[5:])
    if ring:
        parts[3] = gate(parts[3], ring_out.step([bias_sum]))
    norm_own, norm_near, norm_across, norm_far = scatter_core(parts, "norm_grad")
    norm_pair = plus(norm_across, norm_far)
    norm_last = swap(norm_pair, 2, "norm_grad")
    in_grads = list(
        run(
            in_grad_kernel,
            scal,
            [norm_h, norm_l, hid_h, hid_l],
            [block] * GROUPS,
            scratch=[pltpu.VMEM((D, D), f32)],
            name="in_grad", work=5.0,
            after=[norm_pair],
        )
    )
    if ring:
        ring_in = RingScatter(in_grads, "in_grad", flip=True)
        out_sent = ring_out.step()
        in_sent = ring_in.step()
    done = run(
        proj_back_kernel,
        scal,
        [norm_own, norm_near, norm_last, hat_two, scale_two, vec, grad_out, proj_h, proj_l],
        [chunk, shape(8, D)] + [shape(QUARTER, CH)] * SEQ,
        name="proj_back", work=5.0,
        after=out_sent + in_sent if ring else [],
    )
    mixed_grad, vector_sums = done[:2]
    head_grads = exchange_seq(list(done[2:]), "head_grad")
    if ring:
        out_sent = ring_out.step([mixed_grad])
        in_sent = ring_in.step([mixed_grad])
    out_parts = run(
        ffn_out_kernel,
        scal,
        [acts_h, acts_l, out_wh, out_wl],
        [chunk] * SEQ,
        name="ffn_out", work=7.0,
        after=[mixed_grad],
    )
    proj_grads = run(
        proj_grad_kernel,
        scal,
        [heads_h, heads_l, mixed_grad],
        [shape(GROUPS * SUB, D)] * SEQ,
        scratch=[pltpu.VMEM((D, D), f32)],
        name="proj_grad", work=4.0,
        after=[*head_grads[1:], *out_sent, *in_sent, out_parts[0]] if ring else [],
    )
    wait = [head_grads[3], head_grads[2]]
    out_own, out_near, out_across, out_far = scatter_core(out_parts, "output")
    if ring:
        proj_own, proj_near, proj_across, proj_far = scatter_core(proj_grads, "proj_grad")
        proj_pair, proj_base, out_pair, out_base = sums(
            [
                (proj_across, proj_far),
                (proj_own, proj_near),
                (out_across, out_far),
                (mixed, out_own, out_near),
            ],
            wait,
        )
        proj_last = swap(proj_pair, 2, "proj_grad")
    else:
        proj_base = proj_last = proj_grads[0]
        out_pair, out_base = plus(out_across, out_far), plus(mixed, out_own, out_near)
    joined_h, joined_l, joined_sums = run(
        back_kernel,
        scal,
        head_grads + [kcat, qturn, vcat, qpair, kturn, heads, lse, low_row],
        [tall, tall, shape(8, D)],
        scratch=[
            pltpu.VMEM((OWN, 256, LEN), bf16),
            pltpu.VMEM((OWN, LEN, 128), bf16),
            pltpu.VMEM((OWN, 8, LEN), f32),
            pltpu.VMEM((OWN, LEN, 128), f32),
            pltpu.VMEM((OWN, LEN, 128), f32),
            pltpu.VMEM((OWN, HEAD, LEN), f32),
        ],
        name="back", work=16.0,
        after=[proj_grads[0]],
    )
    if ring:
        shard_out = ring_out.result([joined_sums])
        in_sent = ring_in.step([joined_sums])
    done = run(
        qkv_grad_kernel,
        scal,
        [hat_h, hat_l, joined_h, joined_l, joined_sums, qkv_h, qkv_l, vec]
        + [proj_base, proj_last, vector_sums, bias_sum],
        [shape(ROWS + 8, D)] * GROUPS,
        scratch=[pltpu.VMEM((D, D), f32), pltpu.VMEM((GROUPS, 8, HALF_VEC), f32)],
        name="qkv_grad", work=1.0,
        after=[*in_sent, shard_out] if ring else [],
    )
    first_grads = list(done)
    if ring:
        shard_in = ring_in.result([first_grads[0]])
        out_all = gather_seq(shard_out, "out_shard")
        in_all = gather_seq(shard_in, "in_shard")
        first_grads[HALF] = gate(first_grads[HALF], [shard_in, out_all[2]])
        ring_first = RingScatter(first_grads, "first_grad")
        first_sent = ring_first.step([in_all[2]])
    pre_parts = run(
        pre_back_kernel,
        scal,
        [joined_h, joined_l, qkv_h, qkv_l],
        [chunk] * SEQ,
        name="pre_back", work=1.0,
        after=[shard_in, *first_sent] if ring else [],
    )
    pre_parts = list(pre_parts)
    out_top, out_bottom = split_rows(out_pair, out_pair, CH // 2)
    if ring:
        first_sent = ring_first.step()
        out_top = gate(out_top, [in_all[2]])
    top_last = swap(out_top, 2, "output_top")
    if ring:
        pre_parts[3] = gate(pre_parts[3], [*first_sent, top_last])
    pre_own, pre_near, pre_across, pre_far = scatter_core(pre_parts, "pre_grad")
    pre_pair, pre_base = sums([(pre_across, pre_far), (pre_own, pre_near)])
    pre_last = swap(pre_pair, 2, "pre_grad")
    states = [vectors, vec_first, vec_second, w_qkv, qkv_first, qkv_second, w_proj, proj_first, proj_second]
    states = states + [w_in, in_first, in_second, w_out, out_first, out_second]
    last_sent = ring_first.step([out_all[1], out_all[3]]) if ring else []
    if ring:
        held = [v.reshape(9, 128) for v in states[:3]] + states[3:]
        held = run(
            stage_kernel,
            scal,
            held,
            [shape(*v.shape) for v in held],
            sems=15,
            far_args=range(15),
            name="stage", work=3.0,
            after=[*last_sent, in_all[1], in_all[3]],
        )
        shard_first = ring_first.result([held[3]])
    (input_grad,) = run(
        input_grad_kernel,
        scal,
        [flat_in, pre_base, pre_last, vec, mixed_grad],
        [chunk],
        name="input_grad", work=3.0,
    )

    if ring:
        (small,) = run(
            shard_sums_kernel, scal, [shard_first, shard_in, shard_out], [shape(8, D)], name="shard_sums", work=1.0
        )
        shard_first = gate(shard_first, [pre_last])
        across = swap(shard_first, 2, "first_shard")
        core = swap(shard_first, 1, "first_shard")
        (squares,) = run(
            shard_squares_kernel,
            scal,
            [small] + [swap(small, bits, "small") for bits in (1, 2, 3)],
            [shape(8, 128)],
            name="shard_squares", work=1.0,
        )
        flipped = lambda bits: [(i, i ^ bits) for i in range(GROUPS)]
        one, two, three = (move(squares, "dp", flipped(bits), "squares") for bits in (1, 2, 3))
        squares = sum_pairs(squares, one, two, three)
        out_bottom = gate(out_bottom, [across, squares])
        across = gate(across, [squares, out_bottom])
        first_all = [shard_first, core, across, swap(across, 1, "first_shard_2")]
        squares = plus(squares, move(squares, "dp", flipped(4), "squares"), after=[input_grad])
        done = run(
            adamw_kernel,
            scal,
            [squares] + first_all + in_all + out_all + list(held),
            [shape(8, 128)] + [shape(*v.shape) for v in held],
            scratch=[pltpu.VMEM(v.shape, f32) for v in held]
            + [pltpu.VMEM((SEQ, ROWS, D), f32), pltpu.VMEM((SEQ, 2 * ROWS, D), f32)],
            sems=15,
            far_outs=range(1, 16),
            name="adamw", work=0.1,
        )
        new = [v.reshape(-1) for v in done[1:4]] + list(done[4:])
        clip_norm = done[0][0, 0]
    else:
        by_group = jnp.stack(first_grads)
        shard_first = lax.psum_scatter(
            by_group[:, :ROWS].reshape(D, D), "dp", scatter_dimension=0, tiled=True
        )
        proj_full = jnp.stack([p.reshape(GROUPS, SUB, D) for p in ordered(proj_grads, mine)], axis=1)
        proj_grad = lax.psum(
            lax.psum_scatter(proj_full.reshape(D, D), "dp", scatter_dimension=0, tiled=True), "seq"
        )
        all_vec = lax.psum(by_group[:, ROWS : ROWS + 3, :HALF_VEC], ("dp", "seq")).reshape(-1)
        vec_grad = lax.dynamic_slice_in_dim(all_vec, home * vectors.shape[0], vectors.shape[0])
        joined = lax.all_gather(shard_first, "seq", axis=0, tiled=False)
        qkv_grad = jnp.concatenate(
            [joined[j, :, i * CH : i * CH + QUARTER] for i in range(3) for j in range(SEQ)], axis=1
        )
        shard_in, shard_out = (
            lax.psum_scatter(jnp.concatenate(parts, axis=0), "dp", scatter_dimension=0, tiled=True)
            for parts in (in_grads, out_grads)
        )
        in_all = lax.all_gather(shard_in, "seq", axis=0, tiled=False)
        in_grad = in_all.reshape(SEQ, rows, dp_parts, units).transpose(1, 2, 0, 3).reshape(rows, -1)
        out_grad = lax.all_gather(shard_out, "seq", axis=0, tiled=True)
        total = sum(jnp.sum(g * g) for g in (qkv_grad, proj_grad, in_grad, out_grad, vec_grad))
        total = lax.psum(total, "dp")
        clip_norm = jnp.sqrt(total)
        factor = clip_limit / jnp.maximum(clip_norm, clip_limit)
        grads = (vec_grad, qkv_grad, proj_grad, in_grad, out_grad)
        new = []
        for number, grad in enumerate(grads):
            rate, decay = (matrix_rate, weight_decay) if number else (vector_rate, 0.0)
            new.extend(adamw_update(*states[3 * number : 3 * number + 3], factor * grad, rate, decay))
    (output,) = run(
        output_kernel,
        scal,
        [out_base, top_last, swap(out_bottom, 2, "output_bottom"), vec],
        [chunk],
        name="output", work=2.0,
    )
    return (output.reshape(tokens.shape), input_grad.reshape(tokens.shape), clip_norm, *new)


def solution(mesh):
    row = P("dp", "seq", None)
    mark = P("dp", "seq")
    vec = P("dp")
    mat = P("dp", None)
    return jax.shard_map(
        local,
        mesh=mesh,
        in_specs=(row, row, mark, mark) + (vec,) * 3 + (mat,) * 12,
        out_specs=(row, row, P()) + (vec,) * 3 + (mat,) * 12,
        check_vma=False,
    )
```
